32 devices in a mesh: parts: 2 (over x), row: 16 (over z, y, core).
Axes of the slice: x: 2, y: 2, z: 4, core: 2. Of those that a mesh axis runs over, the one named last changes fastest.
Arguments:
- fitted: bfloat16 [64, 2048, 512], P(('parts', 'row')), parts along dimension 0, may hold values from -2 to 2
- fit_start: int32 [64], P('parts'), parts along dimension 0, may hold values from 0 to 1023
- virt_domain: int32 [64, 512], P('parts'), parts along dimension 0, may hold values from 0 to 255
- occ_energy: float32 [64], P('parts'), parts along dimension 0, may hold values from -2 to -0.5
- virt_energy: float32 [512], P('parts'), parts along dimension 0, may hold values from 0.2 to 3
- pair_partner: int32 [96], P('parts'), parts along dimension 0, may hold values from 0 to 31, as said below
Outputs:
- gradient: bfloat16 [64, 2048, 512], P(('parts', 'row')), parts along dimension 0
- density: float32 [64, 512, 512], P(('parts', 'row')), parts along dimension 0
The draws below stay inside these ranges and needn't reach their ends.
There are 2 independent parts, one for each index of `parts`. The reference program is written for one: setup_inputs(seed, part) draws one part's arguments, and reference() takes and returns one part's arrays. A program takes and returns all parts, laid end to end along the dimension named above; each array names one. Nothing has to cross between parts.
Inputs may be any that keep to these rules, and one draw needn't show every extreme that they name: `pair_partner`: the second orbital of pair k lies between (k // 3 - 1) * 2 and (k // 3 + 2) * 2 - 1.
All inputs are finite; a program needn't handle non-finite values.
Results may differ from the reference program's by a relative error of at most 0.0056.
Values may be sent and summed in bfloat16 or wider, within the bound.
No kernel may reach another device: no remote copies, remote signals or barrier semaphores. Data moves between devices by JAX's collectives and lax.ppermute only.
A program may use at most 128 MiB of HBM per device.

```python
import jax
import jax.numpy as jnp
from jax import lax

NV = 512
NAUX = 2048
ORB_DEV = 2
PAIR_DEV = 3
NOCC = 32
PAIRS = 48
NVIRT = 256
N_ROW = 16


def draw_pair_partner(key, part):
    key = jax.random.fold_in(key, 11)
    ordinal = jnp.arange(PAIRS, dtype=jnp.int32)
    device = ordinal // PAIR_DEV
    offset = jax.random.randint(key, (PAIRS,), -ORB_DEV, 2 * ORB_DEV, dtype=jnp.int32)
    partner = jnp.clip(device * ORB_DEV + offset, 0, NOCC - 1)
    partner = partner.at[0].set(0)
    partner = partner.at[PAIRS - 1].set(NOCC - 1)
    return partner.astype(jnp.int32)


def set_ends(array, stream_key, smallest, high):
    dims = array.shape
    index_at = [jax.random.randint(jax.random.fold_in(stream_key, axis), (), 0, dims[axis]) for axis in range(len(dims))]
    array = array.at[tuple(index_at)].set(smallest)
    longest = dims.index(max(dims))
    index_at[longest] = (index_at[longest] + 1) % dims[longest]
    return array.at[tuple(index_at)].set(high)


def block_scale(stream_key, shape, pieces, least, largest):
    def one(axis_at, shards_of):
        draws = jax.random.uniform(jax.random.fold_in(jax.random.fold_in(stream_key, 6), axis_at), (shards_of,), jnp.float32, least / len(pieces), largest / len(pieces))
        return jnp.repeat(jnp.exp(draws), shape[axis_at] // shards_of).reshape((-1,) + (1,) * (len(shape) - axis_at - 1))

    factor_of = one(*pieces[0])
    for cut in pieces[1:]:
        factor_of = factor_of * one(*cut)
    return factor_of


def scatter_about(stream_key, dims, spread, limit, shards=(), kind=jnp.bfloat16):
    gain = block_scale(stream_key, dims, shards, -0.22, 0.18) if shards else 1.0
    array = jax.random.normal(stream_key, dims, jnp.float32) * spread * gain
    return jnp.minimum(jnp.maximum(array, -limit), limit).astype(kind)


def setup_inputs(seed: int = 0, part: int = 0) -> dict:
    keys = jax.random.split(jax.random.key(seed), 7)
    part_splits = jax.random.split(jax.random.fold_in(keys[6], part), 7)
    return {
        "fitted": scatter_about(part_splits[0], (NOCC, NAUX, NV), (NAUX ** -0.25), 2.0, ((0, 16),)),
        "fit_start": set_ends(jax.random.randint(part_splits[1], (NOCC,), 0, NAUX // 2), jax.random.fold_in(part_splits[1], 1), 0, (NAUX // 2) - 1).astype(jnp.int32),
        "virt_domain": set_ends(jax.random.randint(part_splits[2], (NOCC, NV), 0, NVIRT), jax.random.fold_in(part_splits[2], 1), 0, NVIRT - 1).astype(jnp.int32),
        "occ_energy": jnp.clip(jax.random.uniform(part_splits[3], (NOCC,), jnp.float32, -2.0, -0.5), -2.0, -0.5),
        "virt_energy": jnp.clip(jax.random.uniform(part_splits[4], (NVIRT,), jnp.float32, 0.2, 3.0), 0.2, 3.0),
        "pair_partner": draw_pair_partner(jax.random.fold_in(jax.random.fold_in(keys[6], part), 71), part),
    }


def select_row(table, position):
    return lax.dynamic_index_in_dim(table, position, 0, keepdims=False)


def add_block(stack_all, position, value):
    return lax.dynamic_update_index_in_dim(stack_all, select_row(stack_all, position) + value, position, 0)


def shift_rows(fitted_block, from_start, to_start):
    row_shift = (to_start - from_start).astype(jnp.int32)
    row_count = fitted_block.shape[0]
    rolled = jnp.roll(fitted_block, -row_shift, axis=0)
    source = jnp.arange(row_count, dtype=jnp.int32) + row_shift
    inside = (source >= 0) & (source < row_count)
    return jnp.where(inside[:, None], rolled, jnp.zeros_like(rolled))


def pair_terms(block_first, block_second, start_first, start_second, occ_first, occ_second, eps_first, eps_second):
    dens_scale = float(block_first.shape[1]) ** -0.5
    second_in_first = shift_rows(block_second, start_second, start_first)
    first_in_second = shift_rows(block_first, start_first, start_second)
    coulomb = lax.dot_general(block_first, second_in_first, (((0,), (0,)), ((), ())), preferred_element_type=jnp.float32)
    denominator = occ_first + occ_second - eps_first[:, None] - eps_second[None, :]
    amplitude = (coulomb / denominator).astype(jnp.bfloat16)
    grad_first = lax.dot_general(second_in_first, amplitude, (((1,), (1,)), ((), ())), preferred_element_type=jnp.float32)
    grad_second = jnp.dot(first_in_second, amplitude, preferred_element_type=jnp.float32)
    dens_first = lax.dot_general(amplitude, amplitude, (((1,), (1,)), ((), ())), preferred_element_type=jnp.float32) * dens_scale
    dens_second = lax.dot_general(amplitude, amplitude, (((0,), (0,)), ((), ())), preferred_element_type=jnp.float32) * dens_scale
    return grad_first, grad_second, dens_first, dens_second


def reference(fitted, fit_start, virt_domain, occ_energy, virt_energy, pair_partner):
    owned = ORB_DEV
    orbitals = fitted.shape[0]
    aux_rows = fitted.shape[1]
    virt_width = fitted.shape[2]
    rim = jnp.zeros((owned, aux_rows, virt_width), fitted.dtype)
    padded = jnp.concatenate([rim, fitted, rim], axis=0)
    grad_total = jnp.zeros((orbitals + 2 * owned, aux_rows, virt_width), jnp.float32)
    dens_total = jnp.zeros((orbitals + 2 * owned, virt_width, virt_width), jnp.float32)

    def one_group(device, totals):
        grad_total, dens_total = totals
        window = lax.dynamic_slice_in_dim(padded, device * owned, 3 * owned, 0)
        grad_terms = jnp.zeros((3 * owned, aux_rows, virt_width), jnp.float32)
        dens_terms = jnp.zeros((3 * owned, virt_width, virt_width), jnp.float32)
        for number in range(PAIR_DEV):
            first_orb = device * owned + number % owned
            partner = select_row(pair_partner, device * PAIR_DEV + number)
            place = (partner - device * owned + owned).astype(jnp.int32)
            slot = owned + number % owned
            terms = pair_terms(window[slot], select_row(window, place),
                               select_row(fit_start, first_orb), select_row(fit_start, partner),
                               select_row(occ_energy, first_orb), select_row(occ_energy, partner),
                               virt_energy[select_row(virt_domain, first_orb)],
                               virt_energy[select_row(virt_domain, partner)])
            grad_terms = add_block(add_block(grad_terms, slot, terms[0]), place, terms[1])
            dens_terms = add_block(add_block(dens_terms, slot, terms[2]), place, terms[3])
        grad_round = lax.optimization_barrier(grad_terms.astype(jnp.bfloat16)).astype(jnp.float32)
        dens_round = lax.optimization_barrier(dens_terms.astype(jnp.bfloat16)).astype(jnp.float32)
        start = (device * owned).astype(jnp.int32)
        grad_total = lax.dynamic_update_slice_in_dim(grad_total, lax.dynamic_slice_in_dim(grad_total, start, 3 * owned, 0) + grad_round, start, 0)
        dens_total = lax.dynamic_update_slice_in_dim(dens_total, lax.dynamic_slice_in_dim(dens_total, start, 3 * owned, 0) + dens_round, start, 0)
        return grad_total, dens_total

    grad_total, dens_total = lax.fori_loop(0, N_ROW, one_group, (grad_total, dens_total))
    gradient = grad_total[owned:owned + orbitals].astype(jnp.bfloat16)
    density = dens_total[owned:owned + orbitals]
    return gradient, density
```

```python
import functools

import jax
import jax.numpy as jnp
from jax import lax
from jax.experimental import pallas as pl
from jax.experimental.pallas import tpu as pltpu
from jax.sharding import PartitionSpec as P

SUB = 16
LANES = 128
COLS = 256
REACH = 1024
VMEM_BYTES = 50 * 1024 * 1024
NT = (((1,), (1,)), ((), ()))


def dot_nt(a, b):
    return lax.dot_general(a, b, NT, preferred_element_type=jnp.float32)


def up_to(value, unit):
    return -(-value // unit) * unit


def clear_margins(buf, rows):
    buf[:REACH, :] = jnp.zeros((REACH, buf.shape[1]), buf.dtype)
    tail = buf.shape[0] - REACH - rows
    buf[REACH + rows :, :] = jnp.zeros((tail, buf.shape[1]), buf.dtype)


def slot_of(owned, group, s, t):
    return (group * owned + s) * owned + t


def amplitude_of(meta, shifted, group, s, t, h, eps_col, eps_row, ft):
    coulomb = jnp.dot(ft[s], shifted, preferred_element_type=jnp.float32)
    denominator = meta - eps_col[s] - eps_row[group, t, h]
    return (coulomb / denominator).astype(jnp.bfloat16)


def add_rows(acc, s, buf, offset, amplitude, weight, rows, step):
    def one(i, carry):
        base = pl.multiple_of(i * step, step)
        block = buf[pl.ds(pl.multiple_of(offset + base, SUB), step), :]
        acc[s, pl.ds(base, step), :] += weight * dot_nt(block, amplitude)
        return carry

    whole = rows // step
    lax.fori_loop(0, whole, one, 0)
    rest = rows - whole * step
    if rest:
        base = whole * step
        block = buf[pl.ds(pl.multiple_of(offset + base, SUB), rest), :]
        acc[s, base:rows, :] += weight * dot_nt(block, amplitude)


def gather_block(count, shift, occ, group, t, h, eps_col, eps_row, ft, buf, acc, dens):
    owned, rows, width = acc.shape
    depth = ft.shape[2]
    scale = float(width) ** -0.5

    def one(s, carry):
        slot = slot_of(owned, group, s, t)

        @pl.when(count[slot] != 0)
        def _():
            weight = count[slot].astype(jnp.float32)
            offset = pl.multiple_of(REACH + shift[slot], SUB)
            amplitude = amplitude_of(
                occ[slot], buf[pl.ds(offset, depth), :], group, s, t, h, eps_col, eps_row, ft
            )
            dens[s] += (weight * scale) * dot_nt(amplitude, amplitude)
            add_rows(acc, s, buf, offset, amplitude, weight, rows, 256)

        return carry

    lax.fori_loop(0, owned, one, 0)


def near_kernel(
    count, shift, occ, eps_col, eps_row, own, mate, acc, dens, ft, buf, *, halves
):
    rows = own.shape[1]
    depth = ft.shape[2]
    clear_margins(buf, rows)
    acc[...] = jnp.zeros_like(acc)
    dens[...] = jnp.zeros_like(dens)

    def turn(j, carry):
        buf[REACH : REACH + rows, :] = own[j]

        def tile(i, inner):
            at = pl.multiple_of(i * LANES, LANES)
            block = buf[pl.ds(REACH + at, LANES), :]
            ft[
                j // halves, pl.ds(pl.multiple_of((j % halves) * COLS, COLS), COLS), pl.ds(at, LANES)
            ] = block.T
            return inner

        return lax.fori_loop(0, depth // LANES, tile, carry)

    lax.fori_loop(0, own.shape[0], turn, 0)

    for group, stack in ((0, own), (1, mate)):

        def one(j, carry):
            buf[REACH : REACH + rows, :] = stack[j]
            gather_block(
                count, shift, occ, group, j // halves, j % halves,
                eps_col, eps_row, ft, buf, acc, dens,
            )
            return carry

        lax.fori_loop(0, stack.shape[0], one, 0)


def far_kernel(
    count, shift, occ, eps_col, eps_row, ft, acc_in, dens_in, *refs, halves
):
    *blocks, acc, dens, buf, sem = refs
    rows = blocks[0].shape[0]
    load_acc = pltpu.make_async_copy(acc_in, acc, sem.at[0])
    load_dens = pltpu.make_async_copy(dens_in, dens, sem.at[1])
    load_acc.start()
    load_dens.start()
    clear_margins(buf, rows)
    load_acc.wait()
    load_dens.wait()
    for j, block in enumerate(blocks):
        buf[REACH : REACH + rows, :] = block[...]
        gather_block(
            count, shift, occ, 2, j // halves, j % halves,
            eps_col, eps_row, ft, buf, acc, dens,
        )


def last_kernel(
    count, shift, occ, lead, eps_col, eps_row, ft_in, block, acc_in, dens_in,
    out, dens, buf, ft, acc, amp, sem, *, t, h,
):
    owned, rows, width = acc_in.shape
    depth = ft.shape[2]
    scale = float(width) ** -0.5
    out_rows = out.shape[1]
    load_block = pltpu.make_async_copy(block, buf.at[pl.ds(REACH, rows)], sem.at[0])
    load_block.start()
    load_ft, load_acc = [], []
    for s in range(owned):
        load_ft.append(pltpu.make_async_copy(ft_in.at[s], ft.at[s], sem.at[2 + s]))
        load_ft[s].start()
    for s in range(owned):
        load_acc.append(
            pltpu.make_async_copy(acc_in.at[s], acc.at[s, pl.ds(0, rows)], sem.at[2 + owned + s])
        )
        load_acc[s].start()
    load_dens = pltpu.make_async_copy(dens_in, dens, sem.at[1])
    load_dens.start()
    clear_margins(buf, rows)
    load_block.wait()
    for s in range(owned):
        load_ft[s].wait()
        slot = slot_of(owned, 2, s, t)

        @pl.when(count[slot] != 0)
        def _():
            offset = pl.multiple_of(REACH + shift[slot], SUB)
            amp[s] = amplitude_of(
                occ[slot], buf[pl.ds(offset, depth), :], 2, s, t, h, eps_col, eps_row, ft
            )

    load_dens.wait()
    for s in range(owned):
        load_acc[s].wait()
        slot = slot_of(owned, 2, s, t)

        @pl.when(count[slot] != 0)
        def _():
            weight = count[slot].astype(jnp.float32)
            offset = pl.multiple_of(REACH + shift[slot], SUB)
            amplitude = amp[s]
            dens[s] += (weight * scale) * dot_nt(amplitude, amplitude)
            add_rows(acc, s, buf, offset, amplitude, weight, rows, 256)

        def settle(i, carry):
            base = pl.multiple_of(i * LANES, LANES)
            skip = lead[s] % 8
            start = pl.multiple_of(base + (lead[s] - skip), 8)
            taken = LANES + 8
            block = pltpu.roll(acc[s, pl.ds(start, taken), :], (taken - skip) % taken, 0)
            out[s, pl.ds(base, LANES), :] = block[:LANES].astype(out.dtype)
            return carry

        lax.fori_loop(0, out_rows // LANES, settle, 0)


def spec(space):
    return pl.BlockSpec(memory_space=space)


def on_device(fitted, fit_start, virt_domain, occ_energy, virt_energy, pair_partner):
    owned, aux, width = fitted.shape
    devices = lax.axis_size("row")
    position = lax.axis_index("row")
    orbitals = fit_start.shape[0]
    pairs = pair_partner.shape[0]
    pairs_here = pairs // devices
    halves = width // COLS
    rows = aux + SUB
    depth = up_to(rows, LANES)
    buf_rows = 2 * REACH + depth

    own_start = lax.dynamic_slice_in_dim(fit_start, position * owned, owned, 0)
    lead = own_start % SUB
    chunks = []
    for t in range(owned):
        for h in range(halves):
            piece = fitted[t, :, h * COLS : (h + 1) * COLS]
            empty = jnp.zeros((rows, COLS), fitted.dtype)
            chunks.append(lax.dynamic_update_slice(empty, piece, (lead[t], 0)))

    outward = []
    for i in range(devices):
        to = i + 1 if i % 2 else i - 1
        if 0 <= to < devices:
            outward.append((i, to))
    inward = [(i, i ^ 1) for i in range(devices) if i ^ 1 < devices]
    far = [lax.ppermute(chunk, "row", outward) for chunk in chunks]
    own = jnp.stack(chunks)
    mate = lax.ppermute(own, "row", inward)

    side = jnp.where(position % 2 == 1, 1, -1)
    bases = jnp.stack([position, position - side, position + side]) * owned
    places = bases[:, None] + jnp.arange(owned, dtype=jnp.int32)
    inside = jnp.clip(places, 0, orbitals - 1)
    pick = inside[:, :, None] == jnp.arange(orbitals, dtype=jnp.int32)
    starts = jnp.sum(jnp.where(pick, fit_start, 0), axis=-1)
    occs = jnp.sum(jnp.where(pick, occ_energy, 0.0), axis=-1)
    aligned = starts - starts % SUB
    mine = places[0]
    shift = aligned[0][None, :, None] - aligned[:, None, :]
    occ = occs[0][None, :, None] + occs[:, None, :]
    ordinal = jnp.arange(pairs, dtype=jnp.int32)
    first = (ordinal // pairs_here) * owned + (ordinal % pairs_here) % owned
    is_mine = mine[None, :, None, None]
    is_other = places[:, None, :, None]
    count = jnp.sum(
        ((first == is_mine) & (pair_partner == is_other)).astype(jnp.int32)
        + ((pair_partner == is_mine) & (first == is_other)).astype(jnp.int32),
        axis=-1,
    )
    domains = jnp.stack(
        [lax.dynamic_slice_in_dim(virt_domain, bases[g], owned, 0) for g in range(3)]
    )
    table = jnp.arange(virt_energy.shape[0], dtype=jnp.int32)
    eps = jnp.sum(jnp.where(domains[..., None] == table, virt_energy, 0.0), axis=-1)
    eps_col = eps[0].reshape(owned, width, 1)
    eps_row = eps.reshape(3, owned, halves, 1, COLS)
    count, shift, occ = count.reshape(-1), shift.reshape(-1), occ.reshape(-1)

    smem, vmem, anywhere = spec(pltpu.SMEM), spec(pltpu.VMEM), spec(pl.ANY)
    params = pltpu.CompilerParams(vmem_limit_bytes=VMEM_BYTES)
    unit = 2 * rows * width * COLS * 2
    f32_acc = jax.ShapeDtypeStruct((owned, rows, width), jnp.float32)
    f32_dens = jax.ShapeDtypeStruct((owned, width, width), jnp.float32)
    ft_shape = jax.ShapeDtypeStruct((owned, width, depth), fitted.dtype)
    buf = pltpu.VMEM((buf_rows, COLS), fitted.dtype)

    acc, dens, ft = pl.pallas_call(
        functools.partial(near_kernel, halves=halves),
        out_shape=(f32_acc, f32_dens, ft_shape),
        in_specs=[smem] * 3 + [vmem] * 4,
        out_specs=(vmem, vmem, vmem),
        scratch_shapes=[buf],
        compiler_params=params,
        cost_estimate=pl.CostEstimate(
            flops=unit * 2 * owned * owned * halves, bytes_accessed=24 << 20, transcendentals=0
        ),
        name="near_pairs",
    )(count, shift, occ, eps_col, eps_row, own, mate)

    acc, dens = pl.pallas_call(
        functools.partial(far_kernel, halves=halves),
        out_shape=(f32_acc, f32_dens),
        in_specs=[smem] * 3 + [vmem] * 3 + [anywhere] * 2 + [vmem] * (len(far) - 1),
        out_specs=(vmem, vmem),
        scratch_shapes=[buf, pltpu.SemaphoreType.DMA((2,))],
        compiler_params=params,
        cost_estimate=pl.CostEstimate(
            flops=unit * owned * (len(far) - 1), bytes_accessed=28 << 20, transcendentals=0
        ),
        name="far_pairs",
    )(count, shift, occ, eps_col, eps_row, ft, acc, dens, *far[:-1])

    gradient, density = pl.pallas_call(
        functools.partial(last_kernel, t=(len(far) - 1) // halves, h=(len(far) - 1) % halves),
        out_shape=(
            jax.ShapeDtypeStruct(fitted.shape, fitted.dtype),
            f32_dens,
        ),
        in_specs=[smem] * 4 + [vmem] * 2 + [anywhere] * 4,
        out_specs=(vmem, vmem),
        scratch_shapes=[
            buf,
            pltpu.VMEM(ft_shape.shape, ft_shape.dtype),
            pltpu.VMEM((owned, depth, width), jnp.float32),
            pltpu.VMEM((owned, width, COLS), jnp.bfloat16),
            pltpu.SemaphoreType.DMA((2 + 2 * owned,)),
        ],
        compiler_params=params,
        cost_estimate=pl.CostEstimate(
            flops=unit * owned, bytes_accessed=20 << 20, transcendentals=0
        ),
        name="last_pairs",
    )(count, shift, occ, lead, eps_col, eps_row, ft, far[-1], acc, dens)
    return gradient, density


def solution(mesh):
    placed = (
        P(("parts", "row"), None, None),
        P("parts"),
        P("parts", None),
        P("parts"),
        P("parts"),
        P("parts"),
    )
    return jax.shard_map(
        on_device,
        mesh=mesh,
        in_specs=placed,
        out_specs=(P(("parts", "row"), None, None), P(("parts", "row"), None, None)),
        check_vma=False,
    )
```

```python
import functools

import jax
import jax.numpy as jnp
from jax import lax
from jax.experimental import pallas as pl
from jax.experimental.pallas import tpu as pltpu
from jax.sharding import PartitionSpec as P

SUB = 16
STEP = 8
LANES = 128
COLS = 256
REACH = 1024
NEAR_VMEM = 36 * 1024 * 1024
FAR_VMEM = 16 * 1024 * 1024
NT = (((1,), (1,)), ((), ()))


def dot_nt(a, b):
    return lax.dot_general(a, b, NT, preferred_element_type=jnp.float32)


def up_to(value, unit):
    return -(-value // unit) * unit


def tile_of(rows):
    return max(n for n in range(SUB, 705, SUB) if rows % n == 0)


def rows_from(load, start, count):
    skip = start % STEP
    base = pl.multiple_of(start - skip, STEP)
    block = load(base, count + STEP)
    width = block.shape[1]
    block = block.reshape(count // STEP + 1, STEP, width)
    turned = pltpu.roll(block, (STEP - skip) % STEP, 1)
    row = lax.broadcasted_iota(jnp.int32, (count // STEP, STEP, width), 1)
    return jnp.where(row < STEP - skip, turned[:-1], turned[1:]).reshape(count, width)


def clear_margins(buf, rows):
    width = buf.shape[1]
    buf[:REACH, :] = jnp.zeros((REACH, width), buf.dtype)
    buf[REACH + rows :, :] = jnp.zeros((buf.shape[0] - REACH - rows, width), buf.dtype)


def align(source, lead, wide, buf):
    aux, width = source.shape
    rows = aux + SUB
    wide[:SUB, :] = jnp.zeros((SUB, width), jnp.float32)
    wide[SUB + aux :, :] = jnp.zeros((wide.shape[0] - SUB - aux, width), jnp.float32)
    tile = tile_of(aux)

    def widen(i, carry):
        base = pl.multiple_of(i * tile, SUB)
        wide[pl.ds(pl.multiple_of(SUB + base, SUB), tile), :] = source[
            pl.ds(base, tile), :
        ].astype(jnp.float32)
        return carry

    lax.fori_loop(0, aux // tile, widen, 0)
    step = tile_of(rows)

    def move(i, carry):
        base = pl.multiple_of(i * step, SUB)
        moved = rows_from(lambda at, n: wide[pl.ds(at, n), :], SUB - lead + base, step)
        buf[pl.ds(pl.multiple_of(REACH + base, SUB), step), :] = moved.astype(buf.dtype)
        return carry

    lax.fori_loop(0, rows // step, move, 0)


def add_pair(weight, offset, occ, eps_a, eps_b, ft, buf, acc, dens):
    rows, width = acc.shape
    depth = ft.shape[1]
    scale = float(width) ** -0.5
    coulomb = jnp.dot(
        ft[...], buf[pl.ds(offset, depth), :], preferred_element_type=jnp.float32
    )
    amplitude = (coulomb / (occ - eps_a - eps_b)).astype(jnp.bfloat16)
    dens[...] += (weight * scale) * dot_nt(amplitude, amplitude)
    step = tile_of(rows)

    def add(i, carry):
        base = pl.multiple_of(i * step, SUB)
        block = buf[pl.ds(pl.multiple_of(offset + base, SUB), step), :]
        acc[pl.ds(base, step), :] += weight * dot_nt(block, amplitude)
        return carry

    lax.fori_loop(0, rows // step, add, 0)


def add_block(meta, group, t, at, eps_col, eps_row, ft, buf, acc, dens):
    count, shift, occ = meta
    owned = acc.shape[0]
    cols = buf.shape[1]

    def one(s, carry):
        slot = (group * owned + s) * owned + t

        @pl.when(count[slot] != 0)
        def _():
            add_pair(
                count[slot].astype(jnp.float32),
                pl.multiple_of(REACH + shift[slot], SUB),
                occ[slot],
                eps_col[s],
                eps_row[group * owned + t, :, at : at + cols],
                ft.at[s],
                buf,
                acc.at[s],
                dens.at[s],
            )

        return carry

    lax.fori_loop(0, owned, one, 0)


def own_kernel(
    count, shift, occ, lead, eps_col, eps_row, own, acc, dens, ft, bufs, wide
):
    owned, aux, width = own.shape
    rows = aux + SUB
    depth = ft.shape[2]
    acc[...] = jnp.zeros_like(acc)
    dens[...] = jnp.zeros_like(dens)
    for t in range(owned):
        buf = bufs.at[t]
        clear_margins(buf, rows)
        align(own.at[t], lead[t], wide, buf)

        def turn(i, carry):
            at = pl.multiple_of(i * LANES, LANES)
            ft[t, :, pl.ds(at, LANES)] = buf[pl.ds(REACH + at, LANES), :].T
            return carry

        lax.fori_loop(0, depth // LANES, turn, 0)
    for t in range(owned):
        add_block(
            (count, shift, occ), 0, t, 0, eps_col, eps_row, ft, bufs.at[t], acc, dens
        )


def mate_kernel(
    count, shift, occ, lead, eps_col, eps_row, ft, mate, acc_in, dens_in, acc, dens, buf, wide
):
    del acc_in, dens_in
    owned, aux, width = mate.shape
    clear_margins(buf, aux + SUB)
    for t in range(owned):
        align(mate.at[t], lead[owned + t], wide, buf)
        add_block((count, shift, occ), 1, t, 0, eps_col, eps_row, ft, buf, acc, dens)


def far_kernel(
    count, shift, occ, lead, eps_col, eps_row, ft, block, acc_in, dens_in, acc, dens, buf, wide,
    *, t, at,
):
    del acc_in, dens_in
    owned = acc.shape[0]
    aux = block.shape[0]
    clear_margins(buf, aux + SUB)
    align(block, lead[2 * owned + t], wide, buf)
    add_block((count, shift, occ), 2, t, at, eps_col, eps_row, ft, buf, acc, dens)


def last_kernel(
    count, shift, occ, lead, eps_col, eps_row, ft, block, acc_in, dens_in,
    acc, dens, out, dens_out, buf, wide, ready, sem, *, t, at,
):
    far_kernel(
        count, shift, occ, lead, eps_col, eps_row, ft, block, acc_in, dens_in, acc, dens, buf,
        wide, t=t, at=at,
    )
    owned, aux, width = out.shape
    step = tile_of(aux)
    copies = [pltpu.make_async_copy(dens, dens_out, sem.at[owned])]
    copies[0].start()
    for s in range(owned):

        def settle(i, carry):
            base = pl.multiple_of(i * step, SUB)
            rows = rows_from(lambda at, n: acc[s, pl.ds(at, n), :], lead[s] + base, step)
            ready[s, pl.ds(base, step), :] = rows.astype(ready.dtype)
            return carry

        lax.fori_loop(0, aux // step, settle, 0)
        copies.append(pltpu.make_async_copy(ready.at[s], out.at[s], sem.at[s]))
        copies[-1].start()
    for copy in copies:
        copy.wait()


def copy_kernel(source, after, out, sem, *, t, at):
    del after
    copy = pltpu.make_async_copy(source.at[t, :, pl.ds(at, out.shape[1])], out, sem)
    copy.start()
    copy.wait()


def spec(space):
    return pl.BlockSpec(memory_space=space)


def on_device(fitted, fit_start, virt_domain, occ_energy, virt_energy, pair_partner):
    owned, aux, width = fitted.shape
    devices = lax.axis_size("row")
    position = lax.axis_index("row")
    orbitals = fit_start.shape[0]
    pairs = pair_partner.shape[0]
    pairs_here = pairs // devices
    rows = aux + SUB
    depth = up_to(rows, LANES)
    buf_rows = 2 * REACH + depth
    wide_rows = aux + 2 * SUB + STEP
    smem, vmem, anywhere = spec(pltpu.SMEM), spec(pltpu.VMEM), spec(pl.ANY)

    outward = []
    for i in range(devices):
        to = i + 1 if i % 2 else i - 1
        if 0 <= to < devices:
            outward.append((i, to))
    inward = [(i, i ^ 1) for i in range(devices) if i ^ 1 < devices]

    def in_vmem(array):
        return pltpu.with_memory_space_constraint(array, pltpu.VMEM)

    def chunk(t, at, after):
        return pl.pallas_call(
            functools.partial(copy_kernel, t=t, at=at),
            out_shape=jax.ShapeDtypeStruct((aux, COLS), fitted.dtype),
            in_specs=[anywhere] * 2,
            out_specs=anywhere,
            scratch_shapes=[pltpu.SemaphoreType.DMA],
            name=f"chunk_{t}_{at}",
        )(fitted, after)

    places_of = [(t, at) for t in range(owned) for at in range(0, width, COLS)]
    far = [lax.ppermute(fitted[0, :, :COLS], "row", outward)]
    mate = lax.ppermute(fitted, "row", inward)
    for number, (t, at) in enumerate(places_of[1:], 1):
        after = far[number - 2] if number > 1 else fit_start
        far.append(lax.ppermute(chunk(t, at, after), "row", outward))

    side = jnp.where(position % 2 == 1, 1, -1)
    bases = jnp.stack([position, position - side, position + side]) * owned
    places = bases[:, None] + jnp.arange(owned, dtype=jnp.int32)
    inside = jnp.clip(places, 0, orbitals - 1)
    pick = inside[:, :, None] == jnp.arange(orbitals, dtype=jnp.int32)
    starts = jnp.sum(jnp.where(pick, fit_start, 0), axis=-1)
    occs = jnp.sum(jnp.where(pick, occ_energy, 0.0), axis=-1)
    lead = starts % SUB
    aligned = starts - lead
    mine = places[0]
    shift = aligned[0][None, :, None] - aligned[:, None, :]
    occ = occs[0][None, :, None] + occs[:, None, :]
    ordinal = jnp.arange(pairs, dtype=jnp.int32)
    first = (ordinal // pairs_here) * owned + (ordinal % pairs_here) % owned
    is_mine = mine[None, :, None, None]
    is_other = places[:, None, :, None]
    count = jnp.sum(
        ((first == is_mine) & (pair_partner == is_other)).astype(jnp.int32)
        + ((pair_partner == is_mine) & (first == is_other)).astype(jnp.int32),
        axis=-1,
    )
    domains = jnp.stack(
        [lax.dynamic_slice_in_dim(virt_domain, bases[g], owned, 0) for g in range(3)]
    )
    table = jnp.arange(virt_energy.shape[0], dtype=jnp.int32)
    eps = jnp.sum(jnp.where(domains[..., None] == table, virt_energy, 0.0), axis=-1)
    eps_col = eps[0].reshape(owned, width, 1)
    eps_row = eps.reshape(3 * owned, 1, width)
    meta = (count.reshape(-1), shift.reshape(-1), occ.reshape(-1), lead.reshape(-1))
    meta = meta + (eps_col, eps_row)
    meta_specs = [smem] * 4 + [vmem] * 2

    unit = 4 * rows * width * COLS
    acc_shape = pltpu.VMEM((owned, rows, width), jnp.float32)
    dens_shape = pltpu.VMEM((owned, width, width), jnp.float32)
    ft_shape = pltpu.VMEM((owned, width, depth), fitted.dtype)

    def cost(blocks):
        return pl.CostEstimate(
            flops=unit * blocks * owned, bytes_accessed=8 << 20, transcendentals=0
        )

    acc, dens, ft = pl.pallas_call(
        own_kernel,
        out_shape=(acc_shape, dens_shape, ft_shape),
        in_specs=meta_specs + [vmem],
        out_specs=(vmem, vmem, vmem),
        scratch_shapes=[
            pltpu.VMEM((owned, buf_rows, width), fitted.dtype),
            pltpu.VMEM((wide_rows, width), jnp.float32),
        ],
        compiler_params=pltpu.CompilerParams(vmem_limit_bytes=NEAR_VMEM),
        cost_estimate=cost(len(places_of)),
        name="own_pairs",
    )(*meta, fitted)

    first_state = len(meta) + 2
    acc, dens = pl.pallas_call(
        mate_kernel,
        out_shape=(acc_shape, dens_shape),
        in_specs=meta_specs + [vmem] * 4,
        out_specs=(vmem, vmem),
        input_output_aliases={first_state: 0, first_state + 1: 1},
        scratch_shapes=[
            pltpu.VMEM((buf_rows, width), fitted.dtype),
            pltpu.VMEM((wide_rows, width), jnp.float32),
        ],
        compiler_params=pltpu.CompilerParams(vmem_limit_bytes=NEAR_VMEM),
        cost_estimate=cost(len(places_of)),
        name="mate_pairs",
    )(*meta, in_vmem(ft), mate, in_vmem(acc), in_vmem(dens))

    far_scratch = [
        pltpu.VMEM((buf_rows, COLS), fitted.dtype),
        pltpu.VMEM((wide_rows, COLS), jnp.float32),
    ]
    for number, (t, at) in enumerate(places_of[:-1]):
        acc, dens = pl.pallas_call(
            functools.partial(far_kernel, t=t, at=at),
            out_shape=(acc_shape, dens_shape),
            in_specs=meta_specs + [vmem] * 4,
            out_specs=(vmem, vmem),
            input_output_aliases={first_state: 0, first_state + 1: 1},
            scratch_shapes=far_scratch,
            compiler_params=pltpu.CompilerParams(vmem_limit_bytes=FAR_VMEM),
            cost_estimate=cost(1),
            name=f"far_pairs_{number}",
        )(*meta, in_vmem(ft), far[number], in_vmem(acc), in_vmem(dens))

    t, at = places_of[-1]
    _, _, gradient, density = pl.pallas_call(
        functools.partial(last_kernel, t=t, at=at),
        out_shape=(
            acc_shape,
            dens_shape,
            jax.ShapeDtypeStruct(fitted.shape, fitted.dtype),
            jax.ShapeDtypeStruct((owned, width, width), jnp.float32),
        ),
        in_specs=meta_specs + [vmem] * 4,
        out_specs=(vmem, vmem, anywhere, anywhere),
        input_output_aliases={first_state: 0, first_state + 1: 1},
        scratch_shapes=far_scratch
        + [
            pltpu.VMEM((owned, aux, width), fitted.dtype),
            pltpu.SemaphoreType.DMA((owned + 1,)),
        ],
        compiler_params=pltpu.CompilerParams(vmem_limit_bytes=FAR_VMEM),
        cost_estimate=cost(1),
        name="last_pairs",
    )(*meta, in_vmem(ft), far[-1], in_vmem(acc), in_vmem(dens))
    return gradient, density


def solution(mesh):
    placed = (
        P(("parts", "row"), None, None),
        P("parts"),
        P("parts", None),
        P("parts"),
        P("parts"),
        P("parts"),
    )
    return jax.shard_map(
        on_device,
        mesh=mesh,
        in_specs=placed,
        out_specs=(P(("parts", "row"), None, None), P(("parts", "row"), None, None)),
        check_vma=False,
    )
```

```python
import functools

import jax
import jax.numpy as jnp
from jax import lax
from jax.experimental import pallas as pl
from jax.experimental.pallas import tpu as pltpu
from jax.sharding import PartitionSpec as P

SUB = 16
STEP = 8
LANES = 128
COLS = 256
REACH = 1024
NEAR_VMEM = 36 * 1024 * 1024
FAR_VMEM = 16 * 1024 * 1024
CHUNK_VMEM = 5 * 1024 * 1024
NT = (((1,), (1,)), ((), ()))


def dot_nt(a, b):
    return lax.dot_general(a, b, NT, preferred_element_type=jnp.float32)


def up_to(value, unit):
    return -(-value // unit) * unit


def tile_of(rows):
    return max(n for n in range(SUB, 705, SUB) if rows % n == 0)


def rows_from(load, start, count):
    skip = start % STEP
    base = pl.multiple_of(start - skip, STEP)
    block = load(base, count + STEP)
    width = block.shape[1]
    block = block.reshape(count // STEP + 1, STEP, width)
    turned = pltpu.roll(block, (STEP - skip) % STEP, 1)
    row = lax.broadcasted_iota(jnp.int32, (count // STEP, STEP, width), 1)
    return jnp.where(row < STEP - skip, turned[:-1], turned[1:]).reshape(count, width)


def clear_margins(buf, rows):
    width = buf.shape[1]
    buf[:REACH, :] = jnp.zeros((REACH, width), buf.dtype)
    buf[REACH + rows :, :] = jnp.zeros((buf.shape[0] - REACH - rows, width), buf.dtype)


def align(source, lead, wide, buf):
    aux, width = source.shape
    rows = aux + SUB
    wide[:SUB, :] = jnp.zeros((SUB, width), jnp.float32)
    wide[SUB + aux :, :] = jnp.zeros((wide.shape[0] - SUB - aux, width), jnp.float32)
    tile = tile_of(aux)

    def widen(i, carry):
        base = pl.multiple_of(i * tile, SUB)
        wide[pl.ds(pl.multiple_of(SUB + base, SUB), tile), :] = source[
            pl.ds(base, tile), :
        ].astype(jnp.float32)
        return carry

    lax.fori_loop(0, aux // tile, widen, 0)
    step = tile_of(rows)

    def move(i, carry):
        base = pl.multiple_of(i * step, SUB)
        moved = rows_from(lambda at, n: wide[pl.ds(at, n), :], SUB - lead + base, step)
        buf[pl.ds(pl.multiple_of(REACH + base, SUB), step), :] = moved.astype(buf.dtype)
        return carry

    lax.fori_loop(0, rows // step, move, 0)


def add_pair(weight, offset, occ, eps_a, eps_b, ft, buf, acc, dens):
    rows, width = acc.shape
    depth = ft.shape[1]
    scale = float(width) ** -0.5
    coulomb = jnp.dot(
        ft[...], buf[pl.ds(offset, depth), :], preferred_element_type=jnp.float32
    )
    amplitude = (coulomb / (occ - eps_a - eps_b)).astype(jnp.bfloat16)
    dens[...] += (weight * scale) * dot_nt(amplitude, amplitude)
    step = tile_of(rows)

    def add(i, carry):
        base = pl.multiple_of(i * step, SUB)
        block = buf[pl.ds(pl.multiple_of(offset + base, SUB), step), :]
        acc[pl.ds(base, step), :] += weight * dot_nt(block, amplitude)
        return carry

    lax.fori_loop(0, rows // step, add, 0)


def add_block(meta, group, t, at, eps_col, eps_row, ft, buf, acc, dens):
    count, shift, occ = meta
    owned = acc.shape[0]
    cols = buf.shape[1]

    def one(s, carry):
        slot = (group * owned + s) * owned + t

        @pl.when(count[slot] != 0)
        def _():
            add_pair(
                count[slot].astype(jnp.float32),
                pl.multiple_of(REACH + shift[slot], SUB),
                occ[slot],
                eps_col[s],
                eps_row[group * owned + t, :, at : at + cols],
                ft.at[s],
                buf,
                acc.at[s],
                dens.at[s],
            )

        return carry

    lax.fori_loop(0, owned, one, 0)


def own_kernel(
    count, shift, occ, lead, eps_col, eps_row, own, acc, dens, ft, token, bufs, wide
):
    token[...] = jnp.zeros_like(token)
    owned, aux, width = own.shape
    rows = aux + SUB
    depth = ft.shape[2]
    acc[...] = jnp.zeros_like(acc)
    dens[...] = jnp.zeros_like(dens)
    for t in range(owned):
        buf = bufs.at[t]
        clear_margins(buf, rows)
        align(own.at[t], lead[t], wide, buf)

        def turn(i, carry):
            at = pl.multiple_of(i * LANES, LANES)
            ft[t, :, pl.ds(at, LANES)] = buf[pl.ds(REACH + at, LANES), :].T
            return carry

        lax.fori_loop(0, depth // LANES, turn, 0)
    for t in range(owned):
        add_block(
            (count, shift, occ), 0, t, 0, eps_col, eps_row, ft, bufs.at[t], acc, dens
        )


def mate_kernel(
    count, shift, occ, lead, eps_col, eps_row, ft, mate, acc_in, dens_in, after,
    acc, dens, token, buf, wide,
):
    del acc_in, dens_in, after
    token[...] = jnp.zeros_like(token)
    owned, aux, width = mate.shape
    clear_margins(buf, aux + SUB)
    for t in range(owned):
        align(mate.at[t], lead[owned + t], wide, buf)
        add_block((count, shift, occ), 1, t, 0, eps_col, eps_row, ft, buf, acc, dens)


def far_kernel(
    count, shift, occ, lead, eps_col, eps_row, ft, block, acc_in, dens_in, after,
    acc, dens, token, buf, wide, *, t, at,
):
    del acc_in, dens_in, after
    token[...] = jnp.zeros_like(token)
    owned = acc.shape[0]
    aux = block.shape[0]
    clear_margins(buf, aux + SUB)
    align(block, lead[2 * owned + t], wide, buf)
    add_block((count, shift, occ), 2, t, at, eps_col, eps_row, ft, buf, acc, dens)


def last_kernel(
    count, shift, occ, lead, eps_col, eps_row, ft, block, acc_in, dens_in, after,
    acc, dens, token, out, dens_out, buf, wide, ready, sem, *, t, at,
):
    far_kernel(
        count, shift, occ, lead, eps_col, eps_row, ft, block, acc_in, dens_in, after,
        acc, dens, token, buf, wide, t=t, at=at,
    )
    owned, aux, width = out.shape
    step = tile_of(aux)
    copies = [pltpu.make_async_copy(dens, dens_out, sem.at[owned])]
    copies[0].start()
    for s in range(owned):

        def settle(i, carry):
            base = pl.multiple_of(i * step, SUB)
            rows = rows_from(lambda at, n: acc[s, pl.ds(at, n), :], lead[s] + base, step)
            ready[s, pl.ds(base, step), :] = rows.astype(ready.dtype)
            return carry

        lax.fori_loop(0, aux // step, settle, 0)
        copies.append(pltpu.make_async_copy(ready.at[s], out.at[s], sem.at[s]))
        copies[-1].start()
    for copy in copies:
        copy.wait()


def copy_kernel(source, *refs):
    refs[-1][...] = source[0]


def spec(space):
    return pl.BlockSpec(memory_space=space)


def on_device(fitted, fit_start, virt_domain, occ_energy, virt_energy, pair_partner):
    owned, aux, width = fitted.shape
    devices = lax.axis_size("row")
    position = lax.axis_index("row")
    orbitals = fit_start.shape[0]
    pairs = pair_partner.shape[0]
    pairs_here = pairs // devices
    rows = aux + SUB
    depth = up_to(rows, LANES)
    buf_rows = 2 * REACH + depth
    wide_rows = aux + 2 * SUB + STEP
    smem, vmem, anywhere = spec(pltpu.SMEM), spec(pltpu.VMEM), spec(pl.ANY)

    outward = []
    for i in range(devices):
        to = i + 1 if i % 2 else i - 1
        if 0 <= to < devices:
            outward.append((i, to))
    inward = [(i, i ^ 1) for i in range(devices) if i ^ 1 < devices]

    def in_hbm(array):
        return pltpu.with_memory_space_constraint(array, pltpu.HBM)

    def in_vmem(array):
        return pltpu.with_memory_space_constraint(array, pltpu.VMEM)

    def chunk(t, at, *after):
        return pl.pallas_call(
            copy_kernel,
            grid=(1,),
            out_shape=jax.ShapeDtypeStruct((aux, COLS), fitted.dtype),
            in_specs=[pl.BlockSpec((1, aux, COLS), lambda i: (t, 0, at // COLS))]
            + [anywhere] * len(after),
            out_specs=pl.BlockSpec((aux, COLS), lambda i: (0, 0)),
            compiler_params=pltpu.CompilerParams(vmem_limit_bytes=CHUNK_VMEM),
            name=f"chunk_{t}_{at}",
        )(in_hbm(fitted), *after)

    places_of = [(t, at) for t in range(owned) for at in range(0, width, COLS)]
    sent = [chunk(*places_of[0])]
    far = [lax.ppermute(sent[0], "row", outward)]
    mate = lax.ppermute(fitted, "row", inward)
    sent.append(chunk(*places_of[1], sent[0]))
    far.append(lax.ppermute(sent[1], "row", outward))

    side = jnp.where(position % 2 == 1, 1, -1)
    bases = jnp.stack([position, position - side, position + side]) * owned
    places = bases[:, None] + jnp.arange(owned, dtype=jnp.int32)
    inside = jnp.clip(places, 0, orbitals - 1)
    pick = inside[:, :, None] == jnp.arange(orbitals, dtype=jnp.int32)
    starts = jnp.sum(jnp.where(pick, fit_start, 0), axis=-1)
    occs = jnp.sum(jnp.where(pick, occ_energy, 0.0), axis=-1)
    lead = starts % SUB
    aligned = starts - lead
    mine = places[0]
    shift = aligned[0][None, :, None] - aligned[:, None, :]
    occ = occs[0][None, :, None] + occs[:, None, :]
    ordinal = jnp.arange(pairs, dtype=jnp.int32)
    first = (ordinal // pairs_here) * owned + (ordinal % pairs_here) % owned
    is_mine = mine[None, :, None, None]
    is_other = places[:, None, :, None]
    count = jnp.sum(
        ((first == is_mine) & (pair_partner == is_other)).astype(jnp.int32)
        + ((pair_partner == is_mine) & (first == is_other)).astype(jnp.int32),
        axis=-1,
    )
    domains = jnp.stack(
        [lax.dynamic_slice_in_dim(virt_domain, bases[g], owned, 0) for g in range(3)]
    )
    table = jnp.arange(virt_energy.shape[0], dtype=jnp.int32)
    eps = jnp.sum(jnp.where(domains[..., None] == table, virt_energy, 0.0), axis=-1)
    eps_col = eps[0].reshape(owned, width, 1)
    eps_row = eps.reshape(3 * owned, 1, width)
    meta = (count.reshape(-1), shift.reshape(-1), occ.reshape(-1), lead.reshape(-1))
    meta = meta + (eps_col, eps_row)
    meta_specs = [smem] * 4 + [vmem] * 2

    unit = 4 * rows * width * COLS
    acc_shape = pltpu.VMEM((owned, rows, width), jnp.float32)
    dens_shape = pltpu.VMEM((owned, width, width), jnp.float32)
    ft_shape = pltpu.VMEM((owned, width, depth), fitted.dtype)

    def cost(blocks):
        return pl.CostEstimate(
            flops=unit * blocks * owned, bytes_accessed=8 << 20, transcendentals=0
        )

    token_shape = jax.ShapeDtypeStruct((8, LANES), jnp.int32)
    acc, dens, ft, token = pl.pallas_call(
        own_kernel,
        out_shape=(acc_shape, dens_shape, ft_shape, token_shape),
        in_specs=meta_specs + [vmem],
        out_specs=(vmem,) * 4,
        scratch_shapes=[
            pltpu.VMEM((owned, buf_rows, width), fitted.dtype),
            pltpu.VMEM((wide_rows, width), jnp.float32),
        ],
        compiler_params=pltpu.CompilerParams(vmem_limit_bytes=NEAR_VMEM),
        cost_estimate=cost(len(places_of)),
        name="own_pairs",
    )(*meta, in_hbm(fitted))

    def add_pairs(kernel, block, acc, dens, after, cols, limit, blocks, name, outs=(), scratch=()):
        first_state = len(meta) + 2
        return pl.pallas_call(
            kernel,
            out_shape=(acc_shape, dens_shape, token_shape, *outs),
            in_specs=meta_specs + [vmem] * 4 + [anywhere],
            out_specs=(vmem,) * 3 + (anywhere,) * len(outs),
            input_output_aliases={first_state: 0, first_state + 1: 1},
            scratch_shapes=[
                pltpu.VMEM((buf_rows, cols), fitted.dtype),
                pltpu.VMEM((wide_rows, cols), jnp.float32),
                *scratch,
            ],
            compiler_params=pltpu.CompilerParams(vmem_limit_bytes=limit),
            cost_estimate=cost(blocks),
            name=name,
        )(*meta, in_vmem(ft), block, in_vmem(acc), in_vmem(dens), after)

    acc, dens, token = add_pairs(
        mate_kernel, mate, acc, dens, token, width, NEAR_VMEM, len(places_of), "mate_pairs"
    )
    last = len(places_of) - 1
    for number, (t, at) in enumerate(places_of[:-1]):
        if number + 2 <= last:
            sent.append(chunk(*places_of[number + 2], far[number], token))
            far.append(lax.ppermute(sent[-1], "row", outward))
            token = sent[-1]
        acc, dens, token = add_pairs(
            functools.partial(far_kernel, t=t, at=at),
            far[number], acc, dens, token, COLS, FAR_VMEM, 1, f"far_pairs_{number}",
        )
    t, at = places_of[-1]
    *_, gradient, density = add_pairs(
        functools.partial(last_kernel, t=t, at=at),
        far[-1], acc, dens, token, COLS, FAR_VMEM, 1, "last_pairs",
        outs=(
            jax.ShapeDtypeStruct(fitted.shape, fitted.dtype),
            jax.ShapeDtypeStruct((owned, width, width), jnp.float32),
        ),
        scratch=(
            pltpu.VMEM((owned, aux, width), fitted.dtype),
            pltpu.SemaphoreType.DMA((owned + 1,)),
        ),
    )
    return gradient, density


def solution(mesh):
    placed = (
        P(("parts", "row"), None, None),
        P("parts"),
        P("parts", None),
        P("parts"),
        P("parts"),
        P("parts"),
    )
    return jax.shard_map(
        on_device,
        mesh=mesh,
        in_specs=placed,
        out_specs=(P(("parts", "row"), None, None), P(("parts", "row"), None, None)),
        check_vma=False,
    )
```

```python
import functools

import jax
import jax.numpy as jnp
from jax import lax
from jax.experimental import pallas as pl
from jax.experimental.pallas import tpu as pltpu
from jax.sharding import PartitionSpec as P

SUB = 16
STEP = 8
LANES = 128
OUT_TILES = 4
COLS = 256
REACH = 1024
NEAR_VMEM = 36 * 1024 * 1024
FAR_VMEM = 16 * 1024 * 1024
CHUNK_VMEM = 5 * 1024 * 1024


def dot(a, b):
    return jnp.dot(a, b, preferred_element_type=jnp.float32)


def up_to(value, unit):
    return -(-value // unit) * unit


def tile_of(rows):
    return max(n for n in range(SUB, 705, SUB) if rows % n == 0)


def rows_from(load, start, count):
    skip = start % STEP
    base = pl.multiple_of(start - skip, STEP)
    block = load(base, count + STEP)
    width = block.shape[1]
    block = block.reshape(count // STEP + 1, STEP, width)
    turned = pltpu.roll(block, (STEP - skip) % STEP, 1)
    row = lax.broadcasted_iota(jnp.int32, (count // STEP, STEP, width), 1)
    return jnp.where(row < STEP - skip, turned[:-1], turned[1:]).reshape(count, width)


def clear_margins(buf, rows):
    width = buf.shape[1]
    buf[:REACH, :] = jnp.zeros((REACH, width), buf.dtype)
    buf[REACH + rows :, :] = jnp.zeros((buf.shape[0] - REACH - rows, width), buf.dtype)


def align(source, lead, wide, buf):
    aux, width = source.shape
    rows = aux + SUB
    wide[:SUB, :] = jnp.zeros((SUB, width), jnp.float32)
    wide[SUB + aux :, :] = jnp.zeros((wide.shape[0] - SUB - aux, width), jnp.float32)
    tile = tile_of(aux)

    def widen(i, carry):
        base = pl.multiple_of(i * tile, SUB)
        wide[pl.ds(pl.multiple_of(SUB + base, SUB), tile), :] = source[
            pl.ds(base, tile), :
        ].astype(jnp.float32)
        return carry

    lax.fori_loop(0, aux // tile, widen, 0)
    step = tile_of(rows)

    def move(i, carry):
        base = pl.multiple_of(i * step, SUB)
        moved = rows_from(lambda at, n: wide[pl.ds(at, n), :], SUB - lead + base, step)
        buf[pl.ds(pl.multiple_of(REACH + base, SUB), step), :] = moved.astype(buf.dtype)
        return carry

    lax.fori_loop(0, rows // step, move, 0)


def add_pair(weight, offset, occ, eps_a, eps_b, ft, buf, acc, dens, turned):
    rows, width = acc.shape
    depth = ft.shape[1]
    scale = float(width) ** -0.5
    coulomb = jnp.dot(
        ft[...], buf[pl.ds(offset, depth), :], preferred_element_type=jnp.float32
    )
    amplitude = (coulomb / (occ - eps_a - eps_b)).astype(jnp.bfloat16)
    turned[...] = amplitude.T
    dens[...] += (weight * scale) * dot(amplitude, turned[...])
    step = tile_of(rows)

    def add(i, carry):
        base = pl.multiple_of(i * step, SUB)
        block = buf[pl.ds(pl.multiple_of(offset + base, SUB), step), :]
        acc[pl.ds(base, step), :] += weight * dot(block, turned[...])
        return carry

    lax.fori_loop(0, rows // step, add, 0)


def add_block(meta, group, t, at, eps_col, eps_row, ft, buf, acc, dens, turned):
    count, shift, occ = meta
    owned = acc.shape[0]
    cols = buf.shape[1]

    def one(s, carry):
        slot = (group * owned + s) * owned + t

        @pl.when(count[slot] != 0)
        def _():
            add_pair(
                count[slot].astype(jnp.float32),
                pl.multiple_of(REACH + shift[slot], SUB),
                occ[slot],
                eps_col[s],
                eps_row[group * owned + t, :, at : at + cols],
                ft.at[s],
                buf,
                acc.at[s],
                dens.at[s],
                turned,
            )

        return carry

    lax.fori_loop(0, owned, one, 0)


def own_kernel(
    count, shift, occ, lead, eps_col, eps_row, own, acc, dens, ft, token, bufs, wide, turned
):
    token[...] = jnp.zeros_like(token)
    owned, aux, width = own.shape
    rows = aux + SUB
    depth = ft.shape[2]
    acc[...] = jnp.zeros_like(acc)
    dens[...] = jnp.zeros_like(dens)
    for t in range(owned):
        buf = bufs.at[t]
        clear_margins(buf, rows)
        align(own.at[t], lead[t], wide, buf)

        def turn(i, carry):
            at = pl.multiple_of(i * LANES, LANES)
            ft[t, :, pl.ds(at, LANES)] = buf[pl.ds(REACH + at, LANES), :].T
            return carry

        lax.fori_loop(0, depth // LANES, turn, 0)
    for t in range(owned):
        add_block(
            (count, shift, occ), 0, t, 0, eps_col, eps_row, ft, bufs.at[t], acc, dens, turned
        )


def mate_kernel(
    count, shift, occ, lead, eps_col, eps_row, ft, mate, acc_in, dens_in, after,
    acc, dens, token, buf, wide, turned,
):
    del acc_in, dens_in, after
    token[...] = jnp.zeros_like(token)
    owned, aux, width = mate.shape
    clear_margins(buf, aux + SUB)
    for t in range(owned):
        align(mate.at[t], lead[owned + t], wide, buf)
        add_block((count, shift, occ), 1, t, 0, eps_col, eps_row, ft, buf, acc, dens, turned)


def far_kernel(
    count, shift, occ, lead, eps_col, eps_row, ft, block, acc_in, dens_in, after,
    acc, dens, token, buf, wide, turned, *, t, at,
):
    del acc_in, dens_in, after
    token[...] = jnp.zeros_like(token)
    owned = acc.shape[0]
    aux = block.shape[0]
    clear_margins(buf, aux + SUB)
    align(block, lead[2 * owned + t], wide, buf)
    add_block((count, shift, occ), 2, t, at, eps_col, eps_row, ft, buf, acc, dens, turned)


def last_kernel(
    count, shift, occ, lead, eps_col, eps_row, ft, block, acc_in, dens_in, after,
    acc, dens, token, out, dens_out, buf, wide, turned, ready, sem, *, t, at,
):
    del acc_in, dens_in, after
    token[...] = jnp.zeros_like(token)
    owned, aux, width = out.shape
    rows = aux + SUB
    depth = ft.shape[2]
    scale = float(width) ** -0.5
    step = aux // OUT_TILES
    tiles = OUT_TILES
    clear_margins(buf, rows)
    align(block, lead[2 * owned + t], wide, buf)
    copies = []

    def place_of(s):
        slot = (2 * owned + s) * owned + t
        return slot, pl.multiple_of(REACH + shift[slot], SUB)

    for s in range(owned):
        slot, offset = place_of(s)

        @pl.when(count[slot] != 0)
        def _():
            coulomb = dot(ft[s], buf[pl.ds(offset, depth), :])
            eps_b = eps_row[2 * owned + t, :, at : at + COLS]
            amplitude = (coulomb / (occ[slot] - eps_col[s] - eps_b)).astype(jnp.bfloat16)
            turned[s] = amplitude.T
            weight = count[slot].astype(jnp.float32)
            dens[s] += (weight * scale) * dot(amplitude, turned[s])

        copies.append(pltpu.make_async_copy(dens.at[s], dens_out.at[s], sem.at[s, tiles]))
        copies[-1].start()

    for s in range(owned):
        slot, offset = place_of(s)

        def add(base, taken):
            @pl.when(count[slot] != 0)
            def _():
                weight = count[slot].astype(jnp.float32)
                taken_rows = buf[pl.ds(pl.multiple_of(offset + base, SUB), taken), :]
                acc[s, pl.ds(base, taken), :] += weight * dot(taken_rows, turned[s])

        add(0, step + SUB)
        for i in range(tiles):
            if i + 1 < tiles:
                add((i + 1) * step + SUB, step)
            base = i * step
            block_rows = rows_from(lambda at, n: acc[s, pl.ds(at, n), :], lead[s] + base, step)
            ready[s, base : base + step, :] = block_rows.astype(ready.dtype)
            part = pl.ds(base, step)
            copies.append(
                pltpu.make_async_copy(ready.at[s, part], out.at[s, part], sem.at[s, i])
            )
            copies[-1].start()
    for copy in copies:
        copy.wait()


def copy_kernel(source, *refs):
    refs[-1][...] = source[0]


def spec(space):
    return pl.BlockSpec(memory_space=space)


def on_device(fitted, fit_start, virt_domain, occ_energy, virt_energy, pair_partner):
    owned, aux, width = fitted.shape
    devices = lax.axis_size("row")
    position = lax.axis_index("row")
    orbitals = fit_start.shape[0]
    pairs = pair_partner.shape[0]
    pairs_here = pairs // devices
    rows = aux + SUB
    depth = up_to(rows, LANES)
    buf_rows = 2 * REACH + depth
    wide_rows = aux + 2 * SUB + STEP
    smem, vmem, anywhere = spec(pltpu.SMEM), spec(pltpu.VMEM), spec(pl.ANY)

    outward = []
    for i in range(devices):
        to = i + 1 if i % 2 else i - 1
        if 0 <= to < devices:
            outward.append((i, to))
    inward = [(i, i ^ 1) for i in range(devices) if i ^ 1 < devices]

    def in_hbm(array):
        return pltpu.with_memory_space_constraint(array, pltpu.HBM)

    def in_vmem(array):
        return pltpu.with_memory_space_constraint(array, pltpu.VMEM)

    def chunk(t, at, *after):
        return pl.pallas_call(
            copy_kernel,
            grid=(1,),
            out_shape=pltpu.VMEM((aux, COLS), fitted.dtype),
            in_specs=[pl.BlockSpec((1, aux, COLS), lambda i: (t, 0, at // COLS))]
            + [anywhere] * len(after),
            out_specs=vmem,
            compiler_params=pltpu.CompilerParams(vmem_limit_bytes=CHUNK_VMEM),
            name=f"chunk_{t}_{at}",
        )(in_hbm(fitted), *after)

    places_of = [(t, at) for t in range(owned) for at in range(0, width, COLS)]
    sent = [chunk(*places_of[0])]
    far = [lax.ppermute(sent[0], "row", outward)]
    mate = lax.ppermute(fitted, "row", inward)
    sent.append(chunk(*places_of[1], sent[0]))
    far.append(lax.ppermute(sent[1], "row", outward))

    side = jnp.where(position % 2 == 1, 1, -1)
    bases = jnp.stack([position, position - side, position + side]) * owned
    places = bases[:, None] + jnp.arange(owned, dtype=jnp.int32)
    inside = jnp.clip(places, 0, orbitals - 1)
    pick = inside[:, :, None] == jnp.arange(orbitals, dtype=jnp.int32)
    starts = jnp.sum(jnp.where(pick, fit_start, 0), axis=-1)
    occs = jnp.sum(jnp.where(pick, occ_energy, 0.0), axis=-1)
    lead = starts % SUB
    aligned = starts - lead
    mine = places[0]
    shift = aligned[0][None, :, None] - aligned[:, None, :]
    occ = occs[0][None, :, None] + occs[:, None, :]
    ordinal = jnp.arange(pairs, dtype=jnp.int32)
    first = (ordinal // pairs_here) * owned + (ordinal % pairs_here) % owned
    is_mine = mine[None, :, None, None]
    is_other = places[:, None, :, None]
    count = jnp.sum(
        ((first == is_mine) & (pair_partner == is_other)).astype(jnp.int32)
        + ((pair_partner == is_mine) & (first == is_other)).astype(jnp.int32),
        axis=-1,
    )
    domains = jnp.stack(
        [lax.dynamic_slice_in_dim(virt_domain, bases[g], owned, 0) for g in range(3)]
    )
    table = jnp.arange(virt_energy.shape[0], dtype=jnp.int32)
    eps = jnp.sum(jnp.where(domains[..., None] == table, virt_energy, 0.0), axis=-1)
    eps_col = eps[0].reshape(owned, width, 1)
    eps_row = eps.reshape(3 * owned, 1, width)
    meta = (count.reshape(-1), shift.reshape(-1), occ.reshape(-1), lead.reshape(-1))
    meta = meta + (eps_col, eps_row)
    meta_specs = [smem] * 4 + [vmem] * 2

    unit = 4 * rows * width * COLS
    acc_shape = pltpu.VMEM((owned, rows, width), jnp.float32)
    dens_shape = pltpu.VMEM((owned, width, width), jnp.float32)
    ft_shape = pltpu.VMEM((owned, width, depth), fitted.dtype)

    def cost(blocks):
        return pl.CostEstimate(
            flops=unit * blocks * owned, bytes_accessed=8 << 20, transcendentals=0
        )

    token_shape = jax.ShapeDtypeStruct((8, LANES), jnp.int32)
    acc, dens, ft, token = pl.pallas_call(
        own_kernel,
        out_shape=(acc_shape, dens_shape, ft_shape, token_shape),
        in_specs=meta_specs + [vmem],
        out_specs=(vmem,) * 4,
        scratch_shapes=[
            pltpu.VMEM((owned, buf_rows, width), fitted.dtype),
            pltpu.VMEM((wide_rows, width), jnp.float32),
            pltpu.VMEM((width, width), fitted.dtype),
        ],
        compiler_params=pltpu.CompilerParams(vmem_limit_bytes=NEAR_VMEM),
        cost_estimate=cost(len(places_of)),
        name="own_pairs",
    )(*meta, in_hbm(fitted))

    def add_pairs(kernel, block, acc, dens, after, cols, limit, blocks, name, outs=(), scratch=None):
        first_state = len(meta) + 2
        if scratch is None:
            scratch = (pltpu.VMEM((cols, width), fitted.dtype),)
        return pl.pallas_call(
            kernel,
            out_shape=(acc_shape, dens_shape, token_shape, *outs),
            in_specs=meta_specs + [vmem] * 4 + [anywhere],
            out_specs=(vmem,) * 3 + (anywhere,) * len(outs),
            input_output_aliases={first_state: 0, first_state + 1: 1},
            scratch_shapes=[
                pltpu.VMEM((buf_rows, cols), fitted.dtype),
                pltpu.VMEM((wide_rows, cols), jnp.float32),
                *scratch,
            ],
            compiler_params=pltpu.CompilerParams(vmem_limit_bytes=limit),
            cost_estimate=cost(blocks),
            name=name,
        )(*meta, in_vmem(ft), block, in_vmem(acc), in_vmem(dens), after)

    last = len(places_of) - 1
    sent.append(chunk(*places_of[2], token))
    far.append(lax.ppermute(sent[-1], "row", outward))
    acc, dens, token = add_pairs(
        mate_kernel, mate, acc, dens, sent[-1], width, NEAR_VMEM, len(places_of), "mate_pairs"
    )
    for number, (t, at) in enumerate(places_of[:-1]):
        if number + 3 <= last:
            sent.append(chunk(*places_of[number + 3], far[number], token))
            far.append(lax.ppermute(sent[-1], "row", outward))
            token = sent[-1]
        acc, dens, token = add_pairs(
            functools.partial(far_kernel, t=t, at=at),
            far[number], acc, dens, token, COLS, FAR_VMEM, 1, f"far_pairs_{number}",
        )
    t, at = places_of[-1]
    *_, gradient, density = add_pairs(
        functools.partial(last_kernel, t=t, at=at),
        far[-1], acc, dens, token, COLS, FAR_VMEM, 1, "last_pairs",
        outs=(
            jax.ShapeDtypeStruct(fitted.shape, fitted.dtype),
            jax.ShapeDtypeStruct((owned, width, width), jnp.float32),
        ),
        scratch=(
            pltpu.VMEM((owned, COLS, width), fitted.dtype),
            pltpu.VMEM((owned, aux, width), fitted.dtype),
            pltpu.SemaphoreType.DMA((owned, OUT_TILES + 1)),
        ),
    )
    return gradient, density


def solution(mesh):
    placed = (
        P(("parts", "row"), None, None),
        P("parts"),
        P("parts", None),
        P("parts"),
        P("parts"),
        P("parts"),
    )
    return jax.shard_map(
        on_device,
        mesh=mesh,
        in_specs=placed,
        out_specs=(P(("parts", "row"), None, None), P(("parts", "row"), None, None)),
        check_vma=False,
    )
```

```python
import functools

import jax
import jax.numpy as jnp
from jax import lax
from jax.experimental import pallas as pl
from jax.experimental.pallas import tpu as pltpu
from jax.sharding import PartitionSpec as P

SUB = 16
STEP = 8
LANES = 128
OUT_TILES = 4
COLS = 256
REACH = 1024
NEAR_VMEM = 22 * 1024 * 1024
FAR_VMEM = 16 * 1024 * 1024
CHUNK_VMEM = 8 * 1024 * 1024


def dot(a, b):
    return jnp.dot(a, b, preferred_element_type=jnp.float32)


def up_to(value, unit):
    return -(-value // unit) * unit


def tile_of(rows):
    return max(n for n in range(SUB, 705, SUB) if rows % n == 0)


def rows_from(load, start, count):
    skip = start % STEP
    base = pl.multiple_of(start - skip, STEP)
    block = load(base, count + STEP)
    width = block.shape[1]
    block = block.reshape(count // STEP + 1, STEP, width)
    turned = pltpu.roll(block, (STEP - skip) % STEP, 1)
    row = lax.broadcasted_iota(jnp.int32, (count // STEP, STEP, width), 1)
    return jnp.where(row < STEP - skip, turned[:-1], turned[1:]).reshape(count, width)


def clear_margins(buf, rows):
    width = buf.shape[1]
    buf[:REACH, :] = jnp.zeros((REACH, width), buf.dtype)
    buf[REACH + rows :, :] = jnp.zeros((buf.shape[0] - REACH - rows, width), buf.dtype)


def align(source, lead, wide, buf):
    aux, width = source.shape
    rows = aux + SUB
    wide[:SUB, :] = jnp.zeros((SUB, width), jnp.float32)
    wide[SUB + aux :, :] = jnp.zeros((wide.shape[0] - SUB - aux, width), jnp.float32)
    tile = tile_of(aux)

    def widen(i, carry):
        base = pl.multiple_of(i * tile, SUB)
        wide[pl.ds(pl.multiple_of(SUB + base, SUB), tile), :] = source[
            pl.ds(base, tile), :
        ].astype(jnp.float32)
        return carry

    lax.fori_loop(0, aux // tile, widen, 0)
    step = tile_of(rows)

    def move(i, carry):
        base = pl.multiple_of(i * step, SUB)
        moved = rows_from(lambda at, n: wide[pl.ds(at, n), :], SUB - lead + base, step)
        buf[pl.ds(pl.multiple_of(REACH + base, SUB), step), :] = moved.astype(buf.dtype)
        return carry

    lax.fori_loop(0, rows // step, move, 0)


def add_pair(weight, offset, occ, eps_a, eps_b, ft, buf, acc, dens, turned):
    rows, width = acc.shape
    depth = ft.shape[1]
    scale = float(width) ** -0.5
    coulomb = jnp.dot(
        ft[...], buf[pl.ds(offset, depth), :], preferred_element_type=jnp.float32
    )
    amplitude = (coulomb / (occ - eps_a - eps_b)).astype(jnp.bfloat16)
    turned[...] = amplitude.T
    dens[...] += (weight * scale) * dot(amplitude, turned[...])
    step = tile_of(rows)

    def add(i, carry):
        base = pl.multiple_of(i * step, SUB)
        block = buf[pl.ds(pl.multiple_of(offset + base, SUB), step), :]
        acc[pl.ds(base, step), :] += weight * dot(block, turned[...])
        return carry

    lax.fori_loop(0, rows // step, add, 0)


def add_block(meta, group, t, at, eps_col, eps_row, ft, buf, acc, dens, turned):
    count, shift, occ = meta
    owned = acc.shape[0]
    cols = buf.shape[1]

    def one(s, carry):
        slot = (group * owned + s) * owned + t

        @pl.when(count[slot] != 0)
        def _():
            add_pair(
                count[slot].astype(jnp.float32),
                pl.multiple_of(REACH + shift[slot], SUB),
                occ[slot],
                eps_col[s],
                eps_row[group * owned + t, :, at : at + cols],
                ft.at[s],
                buf,
                acc.at[s],
                dens.at[s],
                turned,
            )

        return carry

    lax.fori_loop(0, owned, one, 0)


def own_kernel(
    count, shift, occ, lead, eps_col, eps_row, own, acc, dens, ft, token, bufs, wide, turned
):
    token[...] = jnp.zeros_like(token)
    owned, aux, width = own.shape
    rows = aux + SUB
    depth = ft.shape[2]
    acc[...] = jnp.zeros_like(acc)
    dens[...] = jnp.zeros_like(dens)
    for t in range(owned):
        buf = bufs.at[t]
        clear_margins(buf, rows)
        align(own.at[t], lead[t], wide, buf)

        def turn(i, carry):
            at = pl.multiple_of(i * LANES, LANES)
            ft[t, :, pl.ds(at, LANES)] = buf[pl.ds(REACH + at, LANES), :].T
            return carry

        lax.fori_loop(0, depth // LANES, turn, 0)
    for t in range(owned):
        add_block(
            (count, shift, occ), 0, t, 0, eps_col, eps_row, ft, bufs.at[t], acc, dens, turned
        )


def mate_kernel(
    count, shift, occ, lead, eps_col, eps_row, ft, acc_in, dens_in, mate, *refs
):
    del acc_in, dens_in
    acc, dens, token, buf, wide, turned = refs[-6:]
    token[...] = jnp.zeros_like(token)
    owned, aux, width = mate.shape
    clear_margins(buf, aux + SUB)
    for t in range(owned):
        align(mate.at[t], lead[owned + t], wide, buf)
        add_block((count, shift, occ), 1, t, 0, eps_col, eps_row, ft, buf, acc, dens, turned)


def far_kernel(
    count, shift, occ, lead, eps_col, eps_row, ft, acc_in, dens_in, block, after,
    acc, dens, token, buf, wide, turned, *, places,
):
    del acc_in, dens_in, after
    token[...] = jnp.zeros_like(token)
    clear_margins(buf, block.shape[1] + SUB)
    for number, (t, at) in enumerate(places):
        align(block.at[number], lead[2 * acc.shape[0] + t], wide, buf)
        add_block((count, shift, occ), 2, t, at, eps_col, eps_row, ft, buf, acc, dens, turned)


def relayed_kernel(
    count, shift, occ, lead, eps_col, eps_row, way, ft, acc_in, dens_in, *refs, places
):
    del acc_in, dens_in
    *blocks, acc, dens, token, buf, wide, turned, raw, sem = refs
    token[...] = jnp.zeros_like(token)
    for number, block in enumerate(blocks):

        @pl.when(way[0] == number)
        def _():
            copy = pltpu.make_async_copy(block, raw, sem)
            copy.start()
            copy.wait()

    clear_margins(buf, raw.shape[1] + SUB)
    for number, (t, at) in enumerate(places):
        align(raw.at[number], lead[2 * acc.shape[0] + t], wide, buf)
        add_block((count, shift, occ), 2, t, at, eps_col, eps_row, ft, buf, acc, dens, turned)


def last_kernel(
    count, shift, occ, lead, eps_col, eps_row, ft, acc_in, dens_in, block, after,
    acc, dens, token, out, dens_out, buf, wide, turned, ready, sem, *, places,
):
    ((t, at),) = places
    del acc_in, dens_in, after
    token[...] = jnp.zeros_like(token)
    owned, aux, width = out.shape
    rows = aux + SUB
    depth = ft.shape[2]
    scale = float(width) ** -0.5
    step = aux // OUT_TILES
    tiles = OUT_TILES
    clear_margins(buf, rows)
    align(block.at[0], lead[2 * owned + t], wide, buf)
    copies = []

    def place_of(s):
        slot = (2 * owned + s) * owned + t
        return slot, pl.multiple_of(REACH + shift[slot], SUB)

    for s in range(owned):
        slot, offset = place_of(s)

        @pl.when(count[slot] != 0)
        def _():
            coulomb = dot(ft[s], buf[pl.ds(offset, depth), :])
            eps_b = eps_row[2 * owned + t, :, at : at + COLS]
            amplitude = (coulomb / (occ[slot] - eps_col[s] - eps_b)).astype(jnp.bfloat16)
            turned[s] = amplitude.T
            weight = count[slot].astype(jnp.float32)
            dens[s] += (weight * scale) * dot(amplitude, turned[s])

        copies.append(pltpu.make_async_copy(dens.at[s], dens_out.at[s], sem.at[s, tiles]))
        copies[-1].start()

    for s in range(owned):
        slot, offset = place_of(s)

        def add(base, taken):
            @pl.when(count[slot] != 0)
            def _():
                weight = count[slot].astype(jnp.float32)
                taken_rows = buf[pl.ds(pl.multiple_of(offset + base, SUB), taken), :]
                acc[s, pl.ds(base, taken), :] += weight * dot(taken_rows, turned[s])

        add(0, step + SUB)
        for i in range(tiles):
            if i + 1 < tiles:
                add((i + 1) * step + SUB, step)
            base = i * step
            block_rows = rows_from(lambda at, n: acc[s, pl.ds(at, n), :], lead[s] + base, step)
            ready[s, base : base + step, :] = block_rows.astype(ready.dtype)
            part = pl.ds(base, step)
            copies.append(
                pltpu.make_async_copy(ready.at[s, part], out.at[s, part], sem.at[s, i])
            )
            copies[-1].start()
    for copy in copies:
        copy.wait()


def copy_kernel(*refs):
    for number, source in enumerate(refs[: refs[-1].shape[0]]):
        refs[-1][number] = source[0]


def pass_kernel(source, after, out, sem):
    del after
    copy = pltpu.make_async_copy(source, out, sem)
    copy.start()
    copy.wait()


def relay_plan(devices):
    if devices != 16:
        return []
    down, up = [], []
    for z in range(devices // 4):
        low, high = 4 * z + 1, 4 * z + 2
        if z > 0:
            down.append((high, low, 0))
        if z < devices // 4 - 1:
            up.append((low, high, devices - 1))
    return list(zip(down, reversed(up)))


def spec(space):
    return pl.BlockSpec(memory_space=space)


def on_device(fitted, fit_start, virt_domain, occ_energy, virt_energy, pair_partner):
    owned, aux, width = fitted.shape
    devices = lax.axis_size("row")
    position = lax.axis_index("row")
    orbitals = fit_start.shape[0]
    pairs = pair_partner.shape[0]
    pairs_here = pairs // devices
    rows = aux + SUB
    depth = up_to(rows, LANES)
    buf_rows = 2 * REACH + depth
    wide_rows = aux + 2 * SUB + STEP
    smem, vmem, anywhere = spec(pltpu.SMEM), spec(pltpu.VMEM), spec(pl.ANY)

    outward = []
    for i in range(devices):
        to = i + 1 if i % 2 else i - 1
        if 0 <= to < devices:
            outward.append((i, to))
    inward = [(i, i ^ 1) for i in range(devices) if i ^ 1 < devices]

    def in_hbm(array):
        return pltpu.with_memory_space_constraint(array, pltpu.HBM)

    def in_vmem(array):
        return pltpu.with_memory_space_constraint(array, pltpu.VMEM)

    def chunk(places, *after):
        return pl.pallas_call(
            copy_kernel,
            grid=(1,),
            out_shape=pltpu.VMEM((len(places), aux, COLS), fitted.dtype),
            in_specs=[
                pl.BlockSpec((1, aux, COLS), lambda i, t=t, at=at: (t, 0, at // COLS))
                for t, at in places
            ]
            + [anywhere] * len(after),
            out_specs=vmem,
            compiler_params=pltpu.CompilerParams(vmem_limit_bytes=CHUNK_VMEM),
            name="chunk",
        )(*[in_hbm(fitted)] * len(places), *after)

    def pass_on(block, after):
        return pl.pallas_call(
            pass_kernel,
            out_shape=pltpu.VMEM(block.shape, block.dtype),
            in_specs=[anywhere] * 2,
            out_specs=vmem,
            scratch_shapes=[pltpu.SemaphoreType.DMA],
            compiler_params=pltpu.CompilerParams(vmem_limit_bytes=CHUNK_VMEM),
            name="pass_on",
        )(block, after)

    cells = [(t, at) for t in range(owned) for at in range(0, width, COLS)]
    places_of = [cells[:1], cells[1:-1], cells[-1:]]
    plan = relay_plan(devices)
    gone = {(source, to) for group in plan for source, to, _ in group}
    direct = [pair for pair in outward if pair not in gone]
    hops = [[(source, by) for source, _, by in group] for group in plan]
    sent = [chunk(places_of[0])]
    far = [lax.ppermute(sent[0], "row", direct + (hops[0] if hops else []))]
    relayed = far[:1] if hops else []
    relayed += [lax.ppermute(sent[0], "row", hop) for hop in hops[1:]]
    mate = lax.ppermute(fitted, "row", inward)
    sent.append(chunk(places_of[1], sent[0]))
    far.append(lax.ppermute(sent[1], "row", outward))
    way = jnp.zeros((1,), jnp.int32)
    for number, group in enumerate(plan, 1):
        for _, to, _ in group:
            way = jnp.where(position == to, number, way)

    side = jnp.where(position % 2 == 1, 1, -1)
    bases = jnp.stack([position, position - side, position + side]) * owned
    places = bases[:, None] + jnp.arange(owned, dtype=jnp.int32)
    inside = jnp.clip(places, 0, orbitals - 1)
    pick = inside[:, :, None] == jnp.arange(orbitals, dtype=jnp.int32)
    starts = jnp.sum(jnp.where(pick, fit_start, 0), axis=-1)
    occs = jnp.sum(jnp.where(pick, occ_energy, 0.0), axis=-1)
    lead = starts % SUB
    aligned = starts - lead
    mine = places[0]
    shift = aligned[0][None, :, None] - aligned[:, None, :]
    occ = occs[0][None, :, None] + occs[:, None, :]
    ordinal = jnp.arange(pairs, dtype=jnp.int32)
    first = (ordinal // pairs_here) * owned + (ordinal % pairs_here) % owned
    is_mine = mine[None, :, None, None]
    is_other = places[:, None, :, None]
    count = jnp.sum(
        ((first == is_mine) & (pair_partner == is_other)).astype(jnp.int32)
        + ((pair_partner == is_mine) & (first == is_other)).astype(jnp.int32),
        axis=-1,
    )
    domains = jnp.stack(
        [lax.dynamic_slice_in_dim(virt_domain, bases[g], owned, 0) for g in range(3)]
    )
    table = jnp.arange(virt_energy.shape[0], dtype=jnp.int32)
    eps = jnp.sum(jnp.where(domains[..., None] == table, virt_energy, 0.0), axis=-1)
    eps_col = eps[0].reshape(owned, width, 1)
    eps_row = eps.reshape(3 * owned, 1, width)
    meta = (count.reshape(-1), shift.reshape(-1), occ.reshape(-1), lead.reshape(-1))
    meta = meta + (eps_col, eps_row)
    meta_specs = [smem] * 4 + [vmem] * 2

    unit = 4 * rows * width * COLS
    acc_shape = pltpu.VMEM((owned, rows, width), jnp.float32)
    dens_shape = pltpu.VMEM((owned, width, width), jnp.float32)
    ft_shape = pltpu.VMEM((owned, width, depth), fitted.dtype)

    def cost(blocks):
        return pl.CostEstimate(
            flops=blocks, bytes_accessed=blocks, transcendentals=0
        )

    token_shape = jax.ShapeDtypeStruct((8, LANES), jnp.int32)
    acc, dens, ft, token = pl.pallas_call(
        own_kernel,
        out_shape=(acc_shape, dens_shape, ft_shape, token_shape),
        in_specs=meta_specs + [vmem],
        out_specs=(vmem,) * 4,
        scratch_shapes=[
            pltpu.VMEM((owned, buf_rows, width), fitted.dtype),
            pltpu.VMEM((wide_rows, width), jnp.float32),
            pltpu.VMEM((width, width), fitted.dtype),
        ],
        compiler_params=pltpu.CompilerParams(vmem_limit_bytes=NEAR_VMEM),
        cost_estimate=cost(len(cells)),
        name="own_pairs",
    )(*meta, in_hbm(fitted))

    sent.append(chunk(places_of[2], token, mate))
    far.append(lax.ppermute(sent[2], "row", outward))
    state = {"acc": acc, "dens": dens, "token": sent[2]}

    def add_pairs(kernel, blocks, cols, limit, name, extra=(), outs=(), scratch=()):
        specs = meta_specs + [smem] * len(extra) + [vmem] * 3
        first_state = len(specs) - 2
        results = pl.pallas_call(
            kernel,
            out_shape=(acc_shape, dens_shape, token_shape, *outs),
            in_specs=specs + [vmem if space else anywhere for _, space in blocks],
            out_specs=(vmem,) * 3 + (anywhere,) * len(outs),
            input_output_aliases={first_state: 0, first_state + 1: 1},
            scratch_shapes=[
                pltpu.VMEM((buf_rows, cols), fitted.dtype),
                pltpu.VMEM((wide_rows, cols), jnp.float32),
                *scratch,
            ],
            compiler_params=pltpu.CompilerParams(vmem_limit_bytes=limit),
            cost_estimate=cost(cols // COLS),
            name=name,
        )(
            *meta, *extra, in_vmem(ft), in_vmem(state["acc"]), in_vmem(state["dens"]),
            *(block for block, _ in blocks),
        )
        state.update(acc=results[0], dens=results[1], token=results[2])
        return results[3:]

    def far_pairs(number, kernel, name, **more):
        blocks = [(far[number], True), (state["token"], False)]
        kernel = functools.partial(kernel, places=places_of[number])
        return add_pairs(kernel, blocks, COLS, FAR_VMEM, name, **more)

    near_turned = (pltpu.VMEM((width, width), fitted.dtype),)
    far_turned = (pltpu.VMEM((COLS, width), fitted.dtype),)
    mate_blocks = [(mate, True), (state["token"], False)]
    add_pairs(mate_kernel, mate_blocks, width, NEAR_VMEM, "mate_pairs", scratch=near_turned)
    first_ways = [far[0]] + [None] * len(plan)
    for number in sorted(range(len(plan)), key=lambda n: -n):
        state["token"] = pass_on(relayed[number], state["token"])
        second_hop = [(by, to) for _, to, by in plan[number]]
        first_ways[number + 1] = lax.ppermute(state["token"], "row", second_hop)
    far_pairs(1, far_kernel, "far_pairs_1", scratch=far_turned)
    add_pairs(
        functools.partial(relayed_kernel, places=places_of[0]),
        [(block, False) for block in first_ways],
        COLS, FAR_VMEM, "far_pairs_0",
        extra=(way,),
        scratch=far_turned
        + (pltpu.VMEM(far[0].shape, fitted.dtype), pltpu.SemaphoreType.DMA),
    )
    gradient, density = far_pairs(
        2, last_kernel, "last_pairs",
        outs=(
            jax.ShapeDtypeStruct(fitted.shape, fitted.dtype),
            jax.ShapeDtypeStruct((owned, width, width), jnp.float32),
        ),
        scratch=(
            pltpu.VMEM((owned, COLS, width), fitted.dtype),
            pltpu.VMEM((owned, aux, width), fitted.dtype),
            pltpu.SemaphoreType.DMA((owned, OUT_TILES + 1)),
        ),
    )
    return gradient, density


def solution(mesh):
    placed = (
        P(("parts", "row"), None, None),
        P("parts"),
        P("parts", None),
        P("parts"),
        P("parts"),
        P("parts"),
    )
    return jax.shard_map(
        on_device,
        mesh=mesh,
        in_specs=placed,
        out_specs=(P(("parts", "row"), None, None), P(("parts", "row"), None, None)),
        check_vma=False,
    )
```

```python
import functools

import jax
import jax.numpy as jnp
from jax import lax
from jax.experimental import pallas as pl
from jax.experimental.pallas import tpu as pltpu
from jax.sharding import PartitionSpec as P

SUB = 16
STEP = 8
LANES = 128
OUT_TILES = 4
COLS = 256
REACH = 1024
NEAR_VMEM = 22 * 1024 * 1024
FAR_VMEM = 16 * 1024 * 1024
CHUNK_VMEM = 8 * 1024 * 1024


def dot(a, b):
    return jnp.dot(a, b, preferred_element_type=jnp.float32)


def up_to(value, unit):
    return -(-value // unit) * unit


def tile_of(rows):
    return max(n for n in range(SUB, 705, SUB) if rows % n == 0)


def rows_from(load, start, count):
    skip = start % STEP
    base = pl.multiple_of(start - skip, STEP)
    block = load(base, count + STEP)
    width = block.shape[1]
    block = block.reshape(count // STEP + 1, STEP, width)
    turned = pltpu.roll(block, (STEP - skip) % STEP, 1)
    row = lax.broadcasted_iota(jnp.int32, (count // STEP, STEP, width), 1)
    return jnp.where(row < STEP - skip, turned[:-1], turned[1:]).reshape(count, width)


def clear_margins(buf, rows):
    width = buf.shape[1]
    buf[:REACH, :] = jnp.zeros((REACH, width), buf.dtype)
    buf[REACH + rows :, :] = jnp.zeros((buf.shape[0] - REACH - rows, width), buf.dtype)


def align(source, lead, wide, buf):
    aux, width = source.shape
    rows = aux + SUB
    wide[:SUB, :] = jnp.zeros((SUB, width), jnp.float32)
    wide[SUB + aux :, :] = jnp.zeros((wide.shape[0] - SUB - aux, width), jnp.float32)
    tile = tile_of(aux)

    def widen(i, carry):
        base = pl.multiple_of(i * tile, SUB)
        wide[pl.ds(pl.multiple_of(SUB + base, SUB), tile), :] = source[
            pl.ds(base, tile), :
        ].astype(jnp.float32)
        return carry

    lax.fori_loop(0, aux // tile, widen, 0)
    step = tile_of(rows)

    def move(i, carry):
        base = pl.multiple_of(i * step, SUB)
        moved = rows_from(lambda at, n: wide[pl.ds(at, n), :], SUB - lead + base, step)
        buf[pl.ds(pl.multiple_of(REACH + base, SUB), step), :] = moved.astype(buf.dtype)
        return carry

    lax.fori_loop(0, rows // step, move, 0)


def add_pair(weight, offset, occ, eps_a, eps_b, ft, buf, acc, dens, turned):
    rows, width = acc.shape
    depth = ft.shape[1]
    scale = float(width) ** -0.5
    coulomb = jnp.dot(
        ft[...], buf[pl.ds(offset, depth), :], preferred_element_type=jnp.float32
    )
    amplitude = (coulomb / (occ - eps_a - eps_b)).astype(jnp.bfloat16)
    turned[...] = amplitude.T
    dens[...] += (weight * scale) * dot(amplitude, turned[...])
    step = tile_of(rows)

    def add(i, carry):
        base = pl.multiple_of(i * step, SUB)
        block = buf[pl.ds(pl.multiple_of(offset + base, SUB), step), :]
        acc[pl.ds(base, step), :] += weight * dot(block, turned[...])
        return carry

    lax.fori_loop(0, rows // step, add, 0)


def add_block(meta, group, t, at, eps_col, eps_row, ft, buf, acc, dens, turned):
    count, shift, occ = meta
    owned = acc.shape[0]
    cols = buf.shape[1]

    def one(s, carry):
        slot = (group * owned + s) * owned + t

        @pl.when(count[slot] != 0)
        def _():
            add_pair(
                count[slot].astype(jnp.float32),
                pl.multiple_of(REACH + shift[slot], SUB),
                occ[slot],
                eps_col[s],
                eps_row[group * owned + t, :, at : at + cols],
                ft.at[s],
                buf,
                acc.at[s],
                dens.at[s],
                turned,
            )

        return carry

    lax.fori_loop(0, owned, one, 0)


def own_kernel(
    count, shift, occ, lead, way, eps_col, eps_row, own, acc, dens, ft, token, bufs, wide, turned
):
    token[...] = jnp.zeros_like(token)
    owned, aux, width = own.shape
    rows = aux + SUB
    depth = ft.shape[2]
    acc[...] = jnp.zeros_like(acc)
    dens[...] = jnp.zeros_like(dens)
    for t in range(owned):
        buf = bufs.at[t]
        clear_margins(buf, rows)
        align(own.at[t], lead[t], wide, buf)

        def turn(i, carry):
            at = pl.multiple_of(i * LANES, LANES)
            ft[t, :, pl.ds(at, LANES)] = buf[pl.ds(REACH + at, LANES), :].T
            return carry

        lax.fori_loop(0, depth // LANES, turn, 0)
    for t in range(owned):
        add_block(
            (count, shift, occ), 0, t, 0, eps_col, eps_row, ft, bufs.at[t], acc, dens, turned
        )


def mate_kernel(
    count, shift, occ, lead, way, eps_col, eps_row, ft, acc_in, dens_in, mate, *refs
):
    del acc_in, dens_in
    acc, dens, token, buf, wide, turned = refs[-6:]
    token[...] = jnp.zeros_like(token)
    owned, aux, width = mate.shape
    clear_margins(buf, aux + SUB)
    for t in range(owned):
        align(mate.at[t], lead[owned + t], wide, buf)
        add_block((count, shift, occ), 1, t, 0, eps_col, eps_row, ft, buf, acc, dens, turned)


def far_kernel(
    count, shift, occ, lead, way, eps_col, eps_row, ft, acc_in, dens_in, after, *refs, number, places
):
    del acc_in, dens_in, after
    *blocks, acc, dens, token, buf, wide, turned, raw, sem = refs
    token[...] = jnp.zeros_like(token)
    for choice, block in enumerate(blocks):

        @pl.when(way[number] == choice)
        def _():
            pltpu.make_async_copy(block, raw, sem).start()

    clear_margins(buf, raw.shape[1] + SUB)
    pltpu.make_async_copy(blocks[0], raw, sem).wait()
    for index, (t, at) in enumerate(places):
        align(raw.at[index], lead[2 * acc.shape[0] + t], wide, buf)
        add_block((count, shift, occ), 2, t, at, eps_col, eps_row, ft, buf, acc, dens, turned)


def last_kernel(
    count, shift, occ, lead, way, eps_col, eps_row, ft, acc_in, dens_in, block, after,
    acc, dens, token, out, dens_out, buf, wide, turned, ready, sem, *, places,
):
    ((t, at),) = places
    del acc_in, dens_in, after
    token[...] = jnp.zeros_like(token)
    owned, aux, width = out.shape
    rows = aux + SUB
    depth = ft.shape[2]
    scale = float(width) ** -0.5
    step = aux // OUT_TILES
    tiles = OUT_TILES
    clear_margins(buf, rows)
    align(block.at[0], lead[2 * owned + t], wide, buf)
    copies = []

    def place_of(s):
        slot = (2 * owned + s) * owned + t
        return slot, pl.multiple_of(REACH + shift[slot], SUB)

    for s in range(owned):
        slot, offset = place_of(s)

        @pl.when(count[slot] != 0)
        def _():
            coulomb = dot(ft[s], buf[pl.ds(offset, depth), :])
            eps_b = eps_row[2 * owned + t, :, at : at + COLS]
            amplitude = (coulomb / (occ[slot] - eps_col[s] - eps_b)).astype(jnp.bfloat16)
            turned[s] = amplitude.T
            weight = count[slot].astype(jnp.float32)
            dens[s] += (weight * scale) * dot(amplitude, turned[s])

        copies.append(pltpu.make_async_copy(dens.at[s], dens_out.at[s], sem.at[s, tiles]))
        copies[-1].start()

    for s in range(owned):
        slot, offset = place_of(s)

        def add(base, taken):
            @pl.when(count[slot] != 0)
            def _():
                weight = count[slot].astype(jnp.float32)
                taken_rows = buf[pl.ds(pl.multiple_of(offset + base, SUB), taken), :]
                acc[s, pl.ds(base, taken), :] += weight * dot(taken_rows, turned[s])

        add(0, step + SUB)
        for i in range(tiles):
            if i + 1 < tiles:
                add((i + 1) * step + SUB, step)
            base = i * step
            block_rows = rows_from(lambda at, n: acc[s, pl.ds(at, n), :], lead[s] + base, step)
            ready[s, base : base + step, :] = block_rows.astype(ready.dtype)
            part = pl.ds(base, step)
            copies.append(
                pltpu.make_async_copy(ready.at[s, part], out.at[s, part], sem.at[s, i])
            )
            copies[-1].start()
    for copy in copies:
        copy.wait()


def copy_kernel(*refs):
    for number, source in enumerate(refs[: refs[-1].shape[0]]):
        refs[-1][number] = source[0]


def pass_kernel(source, after, out):
    del source, after, out


def relay_plan(devices):
    if devices != 16:
        return [[], [], []]
    last = devices - 1
    plan = []
    for z in (1, 0, 2):
        high, low = 4 * z + 3, 4 * z + 4
        plan.append([(high, low, 0), (low, high, last)])
    return plan


def spec(space):
    return pl.BlockSpec(memory_space=space)


def on_device(fitted, fit_start, virt_domain, occ_energy, virt_energy, pair_partner):
    owned, aux, width = fitted.shape
    devices = lax.axis_size("row")
    position = lax.axis_index("row")
    orbitals = fit_start.shape[0]
    pairs = pair_partner.shape[0]
    pairs_here = pairs // devices
    rows = aux + SUB
    depth = up_to(rows, LANES)
    buf_rows = 2 * REACH + depth
    wide_rows = aux + 2 * SUB + STEP
    smem, vmem, anywhere = spec(pltpu.SMEM), spec(pltpu.VMEM), spec(pl.ANY)

    outward = []
    for i in range(devices):
        to = i + 1 if i % 2 else i - 1
        if 0 <= to < devices:
            outward.append((i, to))
    inward = [(i, i ^ 1) for i in range(devices) if i ^ 1 < devices]

    def in_hbm(array):
        return pltpu.with_memory_space_constraint(array, pltpu.HBM)

    def in_vmem(array):
        return pltpu.with_memory_space_constraint(array, pltpu.VMEM)

    def chunk(places, *after):
        return pl.pallas_call(
            copy_kernel,
            grid=(1,),
            out_shape=pltpu.VMEM((len(places), aux, COLS), fitted.dtype),
            in_specs=[
                pl.BlockSpec((1, aux, COLS), lambda i, t=t, at=at: (t, 0, at // COLS))
                for t, at in places
            ]
            + [anywhere] * len(after),
            out_specs=vmem,
            compiler_params=pltpu.CompilerParams(vmem_limit_bytes=CHUNK_VMEM),
            name="chunk",
        )(*[in_hbm(fitted)] * len(places), *after)

    def pass_on(block, after):
        return pl.pallas_call(
            pass_kernel,
            out_shape=jax.ShapeDtypeStruct(block.shape, block.dtype),
            in_specs=[anywhere] * 2,
            out_specs=anywhere,
            input_output_aliases={0: 0},
            compiler_params=pltpu.CompilerParams(vmem_limit_bytes=CHUNK_VMEM),
            name="pass_on",
        )(block, after)

    cells = [(t, at) for t in range(owned) for at in range(0, width, COLS)]
    places_of = [cells[number : number + 1] for number in range(len(cells))]
    plan = relay_plan(devices)
    relayed = any(plan)

    def exchange(number, block):
        group = plan[number] if number < len(plan) else []
        gone = {(source, to) for source, to, _ in group}
        pairs = [pair for pair in outward if pair not in gone]
        return lax.ppermute(block, "row", pairs + [(source, by) for source, _, by in group])

    def second_hop(number, block):
        return lax.ppermute(block, "row", [(by, to) for _, to, by in plan[number]])

    mate = lax.ppermute(fitted, "row", inward)
    sent = [chunk(places_of[0])]
    far = [exchange(0, sent[0])]
    for number in (1, 2):
        sent.append(chunk(places_of[number], sent[-1]))
        far.append(exchange(number, sent[-1]))
    way = jnp.zeros((3,), jnp.int32)
    for number, group in enumerate(plan):
        for _, to, _ in group:
            way = way.at[number].set(jnp.where(position == to, 1, way[number]))

    side = jnp.where(position % 2 == 1, 1, -1)
    bases = jnp.stack([position, position - side, position + side]) * owned
    places = bases[:, None] + jnp.arange(owned, dtype=jnp.int32)
    inside = jnp.clip(places, 0, orbitals - 1)
    pick = inside[:, :, None] == jnp.arange(orbitals, dtype=jnp.int32)
    starts = jnp.sum(jnp.where(pick, fit_start, 0), axis=-1)
    occs = jnp.sum(jnp.where(pick, occ_energy, 0.0), axis=-1)
    lead = starts % SUB
    aligned = starts - lead
    mine = places[0]
    shift = aligned[0][None, :, None] - aligned[:, None, :]
    occ = occs[0][None, :, None] + occs[:, None, :]
    ordinal = jnp.arange(pairs, dtype=jnp.int32)
    first = (ordinal // pairs_here) * owned + (ordinal % pairs_here) % owned
    is_mine = mine[None, :, None, None]
    is_other = places[:, None, :, None]
    count = jnp.sum(
        ((first == is_mine) & (pair_partner == is_other)).astype(jnp.int32)
        + ((pair_partner == is_mine) & (first == is_other)).astype(jnp.int32),
        axis=-1,
    )
    domains = jnp.stack(
        [lax.dynamic_slice_in_dim(virt_domain, bases[g], owned, 0) for g in range(3)]
    )
    table = jnp.arange(virt_energy.shape[0], dtype=jnp.int32)
    eps = jnp.sum(jnp.where(domains[..., None] == table, virt_energy, 0.0), axis=-1)
    eps_col = eps[0].reshape(owned, width, 1)
    eps_row = eps.reshape(3 * owned, 1, width)
    meta = (count.reshape(-1), shift.reshape(-1), occ.reshape(-1), lead.reshape(-1), way)
    meta = meta + (eps_col, eps_row)
    meta_specs = [smem] * 5 + [vmem] * 2

    unit = 4 * rows * width * COLS
    acc_shape = pltpu.VMEM((owned, rows, width), jnp.float32)
    dens_shape = pltpu.VMEM((owned, width, width), jnp.float32)
    ft_shape = pltpu.VMEM((owned, width, depth), fitted.dtype)

    def cost(blocks):
        return pl.CostEstimate(
            flops=100 * unit * blocks * owned, bytes_accessed=8 << 20, transcendentals=0
        )

    token_shape = jax.ShapeDtypeStruct((8, LANES), jnp.int32)
    acc, dens, ft, token = pl.pallas_call(
        own_kernel,
        out_shape=(acc_shape, dens_shape, ft_shape, token_shape),
        in_specs=meta_specs + [vmem],
        out_specs=(vmem,) * 4,
        scratch_shapes=[
            pltpu.VMEM((owned, buf_rows, width), fitted.dtype),
            pltpu.VMEM((wide_rows, width), jnp.float32),
            pltpu.VMEM((width, width), fitted.dtype),
        ],
        compiler_params=pltpu.CompilerParams(vmem_limit_bytes=NEAR_VMEM),
        cost_estimate=cost(len(cells)),
        name="own_pairs",
    )(*meta, in_hbm(fitted))

    sent.append(chunk(places_of[3], token, mate))
    far.append(exchange(3, sent[3]))
    state = {"acc": acc, "dens": dens, "token": sent[3]}

    def add_pairs(kernel, blocks, cols, limit, name, outs=(), scratch=()):
        specs = meta_specs + [vmem] * 3
        first_state = len(specs) - 2
        results = pl.pallas_call(
            kernel,
            out_shape=(acc_shape, dens_shape, token_shape, *outs),
            in_specs=specs + [vmem if space else anywhere for _, space in blocks],
            out_specs=(vmem,) * 3 + (anywhere,) * len(outs),
            input_output_aliases={first_state: 0, first_state + 1: 1},
            scratch_shapes=[
                pltpu.VMEM((buf_rows, cols), fitted.dtype),
                pltpu.VMEM((wide_rows, cols), jnp.float32),
                *scratch,
            ],
            compiler_params=pltpu.CompilerParams(vmem_limit_bytes=limit),
            cost_estimate=cost(cols // COLS),
            name=name,
        )(
            *meta, in_vmem(ft), in_vmem(state["acc"]), in_vmem(state["dens"]),
            *(block for block, _ in blocks),
        )
        state.update(acc=results[0], dens=results[1], token=results[2])
        return results[3:]

    hops = []

    def relay(number):
        if relayed:
            far[number] = state["token"] = pass_on(far[number], state["token"])
            hops.append(second_hop(number, far[number]))

    def far_pairs(number):
        blocks = [(state["token"], False), (far[number], False)]
        if relayed:
            blocks.append((hops[number], False))
        kernel = functools.partial(far_kernel, number=number, places=places_of[number])
        add_pairs(
            kernel, blocks, COLS, FAR_VMEM, f"far_pairs_{number}",
            scratch=(
                pltpu.VMEM((COLS, width), fitted.dtype),
                pltpu.VMEM(far[number].shape, fitted.dtype),
                pltpu.SemaphoreType.DMA,
            ),
        )

    relay(0)
    add_pairs(
        mate_kernel, [(mate, True), (state["token"], False)], width, NEAR_VMEM, "mate_pairs",
        scratch=(pltpu.VMEM((width, width), fitted.dtype),),
    )
    relay(1)
    far_pairs(0)
    relay(2)
    far_pairs(1)
    far_pairs(2)
    gradient, density = add_pairs(
        functools.partial(last_kernel, places=places_of[3]),
        [(far[3], True), (state["token"], False)], COLS, FAR_VMEM, "last_pairs",
        outs=(
            jax.ShapeDtypeStruct(fitted.shape, fitted.dtype),
            jax.ShapeDtypeStruct((owned, width, width), jnp.float32),
        ),
        scratch=(
            pltpu.VMEM((owned, COLS, width), fitted.dtype),
            pltpu.VMEM((owned, aux, width), fitted.dtype),
            pltpu.SemaphoreType.DMA((owned, OUT_TILES + 1)),
        ),
    )
    return gradient, density


def solution(mesh):
    placed = (
        P(("parts", "row"), None, None),
        P("parts"),
        P("parts", None),
        P("parts"),
        P("parts"),
        P("parts"),
    )
    return jax.shard_map(
        on_device,
        mesh=mesh,
        in_specs=placed,
        out_specs=(P(("parts", "row"), None, None), P(("parts", "row"), None, None)),
        check_vma=False,
    )
```

```python
import functools

import jax
import jax.numpy as jnp
from jax import lax
from jax.experimental import pallas as pl
from jax.experimental.pallas import tpu as pltpu
from jax.sharding import PartitionSpec as P

SUB = 16
STEP = 8
LANES = 128
OUT_TILES = 4
CHUNK_TILES = 4
COLS = 256
REACH = 1024
NEAR_VMEM = 22 * 1024 * 1024
FAR_VMEM = 16 * 1024 * 1024
CHUNK_VMEM = 8 * 1024 * 1024


class Plan:
    def __init__(self, ref, owned):
        self.ref, self.owned = ref, owned
        self.slots = 3 * owned * owned

    def slot(self, group, s, t):
        return (group * self.owned + s) * self.owned + t

    def at_shift(self, slot):
        return self.slots + slot

    def at_lead(self, place):
        return 2 * self.slots + place

    def at_way(self, number):
        return 2 * self.slots + 3 * self.owned + number

    def count(self, slot):
        return self.ref[slot]

    def offset(self, slot):
        return pl.multiple_of(REACH + self.ref[self.at_shift(slot)], SUB)

    def lead(self, place):
        return self.ref[self.at_lead(place)]

    def way(self, number):
        return self.ref[self.at_way(number)]


def dot(a, b):
    return jnp.dot(a, b, preferred_element_type=jnp.float32)


def up_to(value, unit):
    return -(-value // unit) * unit


def tile_of(rows):
    return max(n for n in range(SUB, 705, SUB) if rows % n == 0)


def rows_from(load, start, count):
    skip = start % STEP
    base = pl.multiple_of(start - skip, STEP)
    block = load(base, count + STEP)
    width = block.shape[1]
    block = block.reshape(count // STEP + 1, STEP, width)
    turned = pltpu.roll(block, (STEP - skip) % STEP, 1)
    row = lax.broadcasted_iota(jnp.int32, (count // STEP, STEP, width), 1)
    return jnp.where(row < STEP - skip, turned[:-1], turned[1:]).reshape(count, width)


def clear_margins(buf, rows):
    width = buf.shape[1]
    buf[:REACH, :] = jnp.zeros((REACH, width), buf.dtype)
    buf[REACH + rows :, :] = jnp.zeros((buf.shape[0] - REACH - rows, width), buf.dtype)


def align(source, lead, wide, buf):
    aux, width = source.shape
    rows = aux + SUB
    wide[:SUB, :] = jnp.zeros((SUB, width), jnp.float32)
    wide[SUB + aux :, :] = jnp.zeros((wide.shape[0] - SUB - aux, width), jnp.float32)
    tile = tile_of(aux)

    def widen(i, carry):
        base = pl.multiple_of(i * tile, SUB)
        wide[pl.ds(pl.multiple_of(SUB + base, SUB), tile), :] = source[
            pl.ds(base, tile), :
        ].astype(jnp.float32)
        return carry

    lax.fori_loop(0, aux // tile, widen, 0)
    step = tile_of(rows)

    def move(i, carry):
        base = pl.multiple_of(i * step, SUB)
        moved = rows_from(lambda at, n: wide[pl.ds(at, n), :], SUB - lead + base, step)
        buf[pl.ds(pl.multiple_of(REACH + base, SUB), step), :] = moved.astype(buf.dtype)
        return carry

    lax.fori_loop(0, rows // step, move, 0)


def add_pair(weight, offset, occ, eps_a, eps_b, ft, buf, acc, dens, turned):
    rows, width = acc.shape
    depth = ft.shape[1]
    scale = float(width) ** -0.5
    coulomb = jnp.dot(
        ft[...], buf[pl.ds(offset, depth), :], preferred_element_type=jnp.float32
    )
    amplitude = (coulomb / (occ - eps_a - eps_b)).astype(jnp.bfloat16)
    turned[...] = amplitude.T
    dens[...] += (weight * scale) * dot(amplitude, turned[...])
    step = tile_of(rows)

    def add(i, carry):
        base = pl.multiple_of(i * step, SUB)
        block = buf[pl.ds(pl.multiple_of(offset + base, SUB), step), :]
        acc[pl.ds(base, step), :] += weight * dot(block, turned[...])
        return carry

    lax.fori_loop(0, rows // step, add, 0)


def add_block(plan, occ, group, t, at, eps_col, eps_row, ft, buf, acc, dens, turned):
    owned = acc.shape[0]
    cols = buf.shape[1]

    def one(s, carry):
        slot = plan.slot(group, s, t)

        @pl.when(plan.count(slot) != 0)
        def _():
            add_pair(
                plan.count(slot).astype(jnp.float32),
                plan.offset(slot),
                occ[slot],
                eps_col[s],
                eps_row[group * owned + t, :, at : at + cols],
                ft.at[s],
                buf,
                acc.at[s],
                dens.at[s],
                turned,
            )

        return carry

    lax.fori_loop(0, owned, one, 0)


def make_plan(
    fit_start, occ_energy, pair_partner, domains, energy, ints, occ, eps_col, eps_row,
    *, devices, targets,
):
    owned, width = eps_col.shape[:2]
    orbitals = fit_start.shape[0]
    pairs_here = pair_partner.shape[0] // devices
    plan = Plan(ints, owned)
    position = lax.axis_index("row")
    side = jnp.where(position % 2 == 1, 1, -1)
    places = [
        base * owned + t
        for base in (position, position - side, position + side)
        for t in range(owned)
    ]
    inside = [jnp.clip(place, 0, orbitals - 1) for place in places]
    starts = [fit_start[place] for place in inside]
    pairs = []
    for step in (-1, 0, 1):
        group = position + step
        known = (group >= 0) & (group < devices)
        held = jnp.clip(group, 0, devices - 1)
        for n in range(pairs_here):
            pairs.append((known, group * owned + n % owned, pair_partner[held * pairs_here + n]))
    for group in range(3):
        for s in range(owned):
            for t in range(owned):
                slot = plan.slot(group, s, t)
                other = group * owned + t
                total = jnp.int32(0)
                for known, first, second in pairs:
                    forth = known & (first == places[s]) & (second == places[other])
                    back = known & (second == places[s]) & (first == places[other])
                    total = total + forth.astype(jnp.int32) + back.astype(jnp.int32)
                ints[slot] = total
                ints[plan.at_shift(slot)] = (
                    starts[s] - starts[s] % SUB - starts[other] + starts[other] % SUB
                )
                occ[slot] = occ_energy[inside[s]] + occ_energy[inside[other]]
    for place in range(3 * owned):
        ints[plan.at_lead(place)] = starts[place] % SUB
    for number, group in enumerate(targets):
        way = jnp.int32(0)
        for to in group:
            way = jnp.where(position == to, 1, way)
        ints[plan.at_way(number)] = way
    entries = energy.shape[0]
    table = lax.broadcasted_iota(jnp.int32, (entries, width), 0)
    for place in range(3 * owned):
        domain = domains[pl.ds(inside[place], 1), :]
        row = jnp.sum(jnp.where(table == domain, energy[...], 0.0), axis=0, keepdims=True)
        eps_row[place] = row
        if place < owned:
            eps_col[place] = jnp.broadcast_to(row, (LANES, width)).T[:, :1]
    return plan


def own_kernel(
    fit_start, occ_energy, pair_partner, domains, energy, own,
    ints, occ, eps_col, eps_row, acc, dens, ft, token, bufs, wide, turned, *, devices, targets,
):
    token[...] = jnp.zeros_like(token)
    plan = make_plan(
        fit_start, occ_energy, pair_partner, domains, energy, ints, occ, eps_col, eps_row,
        devices=devices, targets=targets,
    )
    owned, aux, width = own.shape
    rows = aux + SUB
    depth = ft.shape[2]
    acc[...] = jnp.zeros_like(acc)
    dens[...] = jnp.zeros_like(dens)
    for t in range(owned):
        buf = bufs.at[t]
        clear_margins(buf, rows)
        align(own.at[t], plan.lead(t), wide, buf)

        def turn(i, carry):
            at = pl.multiple_of(i * LANES, LANES)
            ft[t, :, pl.ds(at, LANES)] = buf[pl.ds(REACH + at, LANES), :].T
            return carry

        lax.fori_loop(0, depth // LANES, turn, 0)
    for t in range(owned):
        add_block(plan, occ, 0, t, 0, eps_col, eps_row, ft, bufs.at[t], acc, dens, turned)


def mate_kernel(ints, occ, eps_col, eps_row, ft, acc_in, dens_in, after, mate, *refs):
    del acc_in, dens_in, after
    acc, dens, token, buf, wide, turned = refs
    token[...] = jnp.zeros_like(token)
    owned, aux, width = mate.shape
    plan = Plan(ints, owned)
    clear_margins(buf, aux + SUB)
    for t in range(owned):
        align(mate.at[t], plan.lead(owned + t), wide, buf)
        add_block(plan, occ, 1, t, 0, eps_col, eps_row, ft, buf, acc, dens, turned)


def far_kernel(
    ints, occ, eps_col, eps_row, ft, acc_in, dens_in, after, *refs, number, place
):
    del acc_in, dens_in, after
    *blocks, acc, dens, token, buf, wide, turned, raw, sem = refs
    token[...] = jnp.zeros_like(token)
    plan = Plan(ints, acc.shape[0])
    t, at = place
    for choice, block in enumerate(blocks):

        @pl.when(plan.way(number) == choice)
        def _():
            pltpu.make_async_copy(block, raw, sem).start()

    clear_margins(buf, raw.shape[0] + SUB)
    pltpu.make_async_copy(blocks[0], raw, sem).wait()
    align(raw, plan.lead(2 * plan.owned + t), wide, buf)
    add_block(plan, occ, 2, t, at, eps_col, eps_row, ft, buf, acc, dens, turned)


def last_kernel(
    ints, occ, eps_col, eps_row, ft, acc_in, dens_in, after, block,
    acc, dens, token, out, dens_out, buf, wide, turned, ready, sem, *, place,
):
    del acc_in, dens_in, after
    token[...] = jnp.zeros_like(token)
    t, at = place
    owned, aux, width = out.shape
    plan = Plan(ints, owned)
    rows = aux + SUB
    depth = ft.shape[2]
    scale = float(width) ** -0.5
    step = aux // OUT_TILES
    tiles = OUT_TILES
    clear_margins(buf, rows)
    align(block, plan.lead(2 * owned + t), wide, buf)
    copies = []
    for s in range(owned):
        slot = plan.slot(2, s, t)

        @pl.when(plan.count(slot) != 0)
        def _():
            coulomb = dot(ft[s], buf[pl.ds(plan.offset(slot), depth), :])
            eps_b = eps_row[2 * owned + t, :, at : at + COLS]
            amplitude = (coulomb / (occ[slot] - eps_col[s] - eps_b)).astype(jnp.bfloat16)
            turned[s] = amplitude.T
            weight = plan.count(slot).astype(jnp.float32)
            dens[s] += (weight * scale) * dot(amplitude, turned[s])

        copies.append(pltpu.make_async_copy(dens.at[s], dens_out.at[s], sem.at[s, tiles]))
        copies[-1].start()

    for s in range(owned):
        slot = plan.slot(2, s, t)

        def add(base, taken):
            @pl.when(plan.count(slot) != 0)
            def _():
                weight = plan.count(slot).astype(jnp.float32)
                start = pl.multiple_of(plan.offset(slot) + base, SUB)
                taken_rows = buf[pl.ds(start, taken), :]
                acc[s, pl.ds(base, taken), :] += weight * dot(taken_rows, turned[s])

        add(0, step + SUB)
        for i in range(tiles):
            if i + 1 < tiles:
                add((i + 1) * step + SUB, step)
            base = i * step
            settled = rows_from(
                lambda at, n: acc[s, pl.ds(at, n), :], plan.lead(s) + base, step
            )
            ready[s, base : base + step, :] = settled.astype(ready.dtype)
            part = pl.ds(base, step)
            copies.append(
                pltpu.make_async_copy(ready.at[s, part], out.at[s, part], sem.at[s, i])
            )
            copies[-1].start()
    for copy in copies:
        copy.wait()


def copy_kernel(source, *refs):
    refs[-1][...] = source[0]


def pass_kernel(source, after, out):
    del source, after, out


def relay_plan(devices, chunks):
    if devices != 16 or chunks != 3:
        return [[] for _ in range(chunks)]
    last = devices - 1
    plan = []
    for z in (1, 0, 2):
        high, low = 4 * z + 3, 4 * z + 4
        plan.append([(high, low, 0), (low, high, last)])
    return plan


def spec(space):
    return pl.BlockSpec(memory_space=space)


def on_device(fitted, fit_start, virt_domain, occ_energy, virt_energy, pair_partner):
    owned, aux, width = fitted.shape
    devices = lax.axis_size("row")
    rows = aux + SUB
    depth = up_to(rows, LANES)
    buf_rows = 2 * REACH + depth
    wide_rows = aux + 2 * SUB + STEP
    smem, vmem, anywhere = spec(pltpu.SMEM), spec(pltpu.VMEM), spec(pl.ANY)

    outward = []
    for i in range(devices):
        to = i + 1 if i % 2 else i - 1
        if 0 <= to < devices:
            outward.append((i, to))
    inward = [(i, i ^ 1) for i in range(devices) if i ^ 1 < devices]

    def in_hbm(array):
        return pltpu.with_memory_space_constraint(array, pltpu.HBM)

    def in_vmem(array):
        return pltpu.with_memory_space_constraint(array, pltpu.VMEM)

    def chunk(place, *after):
        t, at = place
        tile = aux // CHUNK_TILES
        return pl.pallas_call(
            copy_kernel,
            grid=(CHUNK_TILES,),
            out_shape=jax.ShapeDtypeStruct((aux, COLS), fitted.dtype),
            in_specs=[pl.BlockSpec((1, tile, COLS), lambda i: (t, i, at // COLS))]
            + [anywhere] * len(after),
            out_specs=pl.BlockSpec((tile, COLS), lambda i: (i, 0)),
            compiler_params=pltpu.CompilerParams(vmem_limit_bytes=CHUNK_VMEM),
            name="chunk",
        )(in_hbm(fitted), *after)

    def pass_on(block, after):
        return pl.pallas_call(
            pass_kernel,
            out_shape=jax.ShapeDtypeStruct(block.shape, block.dtype),
            in_specs=[anywhere] * 2,
            out_specs=anywhere,
            input_output_aliases={0: 0},
            compiler_params=pltpu.CompilerParams(vmem_limit_bytes=CHUNK_VMEM),
            name="pass_on",
        )(block, after)

    cells = [(t, at) for t in range(owned) for at in range(0, width, COLS)]
    last = len(cells) - 1
    plan = relay_plan(devices, last)
    relayed = any(plan)

    def exchange(number, block):
        group = plan[number] if number < last else []
        gone = {(source, to) for source, to, _ in group}
        pairs = [pair for pair in outward if pair not in gone]
        first_hop = [(source, by) for source, _, by in group] if number else []
        return lax.ppermute(block, "row", pairs + first_hop)

    mate = lax.ppermute(fitted, "row", inward)
    sent = [chunk(cells[0])]
    early = None
    if relayed:
        early = lax.ppermute(sent[0], "row", [(source, by) for source, _, by in plan[0]])
    far = [exchange(0, sent[0])]
    for number in range(1, last):
        sent.append(chunk(cells[number], sent[-1]))
        far.append(exchange(number, sent[-1]))

    unit = 4 * rows * width * COLS
    acc_shape = pltpu.VMEM((owned, rows, width), jnp.float32)
    dens_shape = pltpu.VMEM((owned, width, width), jnp.float32)
    ft_shape = pltpu.VMEM((owned, width, depth), fitted.dtype)
    token_shape = jax.ShapeDtypeStruct((8, LANES), jnp.int32)
    slots = 3 * owned * owned

    def cost(blocks):
        return pl.CostEstimate(
            flops=100 * unit * blocks * owned, bytes_accessed=8 << 20, transcendentals=0
        )

    ints, occ, eps_col, eps_row, acc, dens, ft, token = pl.pallas_call(
        functools.partial(
            own_kernel, devices=devices, targets=[[to for _, to, _ in group] for group in plan]
        ),
        out_shape=(
            jax.ShapeDtypeStruct((Plan(None, owned).at_way(last),), jnp.int32),
            jax.ShapeDtypeStruct((slots,), jnp.float32),
            jax.ShapeDtypeStruct((owned, width, 1), jnp.float32),
            jax.ShapeDtypeStruct((3 * owned, 1, width), jnp.float32),
            acc_shape,
            dens_shape,
            ft_shape,
            token_shape,
        ),
        in_specs=[smem] * 3 + [vmem] * 3,
        out_specs=(smem,) * 2 + (vmem,) * 6,
        scratch_shapes=[
            pltpu.VMEM((owned, buf_rows, width), fitted.dtype),
            pltpu.VMEM((wide_rows, width), jnp.float32),
            pltpu.VMEM((width, width), fitted.dtype),
        ],
        compiler_params=pltpu.CompilerParams(vmem_limit_bytes=NEAR_VMEM),
        cost_estimate=cost(len(cells)),
        name="own_pairs",
    )(
        fit_start, occ_energy, pair_partner, virt_domain, virt_energy.reshape(-1, 1),
        in_hbm(fitted),
    )
    state = {"acc": acc, "dens": dens, "token": token}
    hops = []

    def add_pairs(kernel, block_specs, blocks, cols, limit, name, outs=(), scratch=()):
        specs = [smem] * 2 + [vmem] * 5 + [anywhere] + block_specs
        results = pl.pallas_call(
            kernel,
            out_shape=(acc_shape, dens_shape, token_shape, *outs),
            in_specs=specs,
            out_specs=(vmem,) * 3 + (anywhere,) * len(outs),
            input_output_aliases={5: 0, 6: 1},
            scratch_shapes=[
                pltpu.VMEM((buf_rows, cols), fitted.dtype),
                pltpu.VMEM((wide_rows, cols), jnp.float32),
                *scratch,
            ],
            compiler_params=pltpu.CompilerParams(vmem_limit_bytes=limit),
            cost_estimate=cost(cols // COLS),
            name=name,
        )(
            ints, occ, eps_col, eps_row, in_vmem(ft), in_vmem(state["acc"]),
            in_vmem(state["dens"]), state["token"], *blocks,
        )
        state.update(acc=results[0], dens=results[1], token=results[2])
        return results[3:]

    def relay(number):
        if relayed:
            held = pass_on(far[number] if number else early, state["token"])
            if number:
                far[number] = held
            state["token"] = held
            pairs = [(by, to) for _, to, by in plan[number]]
            hops.append(lax.ppermute(held, "row", pairs))

    def far_pairs(number):
        blocks = [far[number]] + hops[number : number + 1]
        add_pairs(
            functools.partial(far_kernel, number=number, place=cells[number]),
            [anywhere] * len(blocks), blocks, COLS, FAR_VMEM, f"far_pairs_{number}",
            scratch=(
                pltpu.VMEM((COLS, width), fitted.dtype),
                pltpu.VMEM((aux, COLS), fitted.dtype),
                pltpu.SemaphoreType.DMA,
            ),
        )

    relay(0)
    state["token"] = chunk(cells[last], state["token"], mate)
    far.append(exchange(last, state["token"]))
    add_pairs(
        mate_kernel, [vmem], [mate], width, NEAR_VMEM, "mate_pairs",
        scratch=(pltpu.VMEM((width, width), fitted.dtype),),
    )
    for number in range(last):
        if number + 1 < last:
            relay(number + 1)
        far_pairs(number)
    gradient, density = add_pairs(
        functools.partial(last_kernel, place=cells[last]),
        [vmem], [far[last]], COLS, FAR_VMEM, "last_pairs",
        outs=(
            jax.ShapeDtypeStruct(fitted.shape, fitted.dtype),
            jax.ShapeDtypeStruct((owned, width, width), jnp.float32),
        ),
        scratch=(
            pltpu.VMEM((owned, COLS, width), fitted.dtype),
            pltpu.VMEM((owned, aux, width), fitted.dtype),
            pltpu.SemaphoreType.DMA((owned, OUT_TILES + 1)),
        ),
    )
    return gradient, density


def solution(mesh):
    placed = (
        P(("parts", "row"), None, None),
        P("parts"),
        P("parts", None),
        P("parts"),
        P("parts"),
        P("parts"),
    )
    return jax.shard_map(
        on_device,
        mesh=mesh,
        in_specs=placed,
        out_specs=(P(("parts", "row"), None, None), P(("parts", "row"), None, None)),
        check_vma=False,
    )
```

```python
import functools

import jax
import jax.numpy as jnp
from jax import lax
from jax.experimental import pallas as pl
from jax.experimental.pallas import tpu as pltpu
from jax.sharding import PartitionSpec as P

SUB = 16
STEP = 8
LANES = 128
OUT_TILES = 4
COLS = 256
REACH = 1024
NEAR_VMEM = 22 * 1024 * 1024
FAR_VMEM = 16 * 1024 * 1024
CHUNK_VMEM = 14 * 1024 * 1024


class Plan:
    def __init__(self, ref, owned):
        self.ref, self.owned = ref, owned
        self.slots = 3 * owned * owned

    def slot(self, group, s, t):
        return (group * self.owned + s) * self.owned + t

    def at_shift(self, slot):
        return self.slots + slot

    def at_lead(self, place):
        return 2 * self.slots + place

    def at_way(self, number):
        return 2 * self.slots + 3 * self.owned + number

    def count(self, slot):
        return self.ref[slot]

    def offset(self, slot):
        return pl.multiple_of(REACH + self.ref[self.at_shift(slot)], SUB)

    def lead(self, place):
        return self.ref[self.at_lead(place)]

    def way(self, number):
        return self.ref[self.at_way(number)]


def dot(a, b):
    return jnp.dot(a, b, preferred_element_type=jnp.float32)


def up_to(value, unit):
    return -(-value // unit) * unit


def tile_of(rows):
    return max(n for n in range(SUB, 705, SUB) if rows % n == 0)


def rows_from(load, start, count):
    skip = start % STEP
    base = pl.multiple_of(start - skip, STEP)
    block = load(base, count + STEP)
    width = block.shape[1]
    block = block.reshape(count // STEP + 1, STEP, width)
    turned = pltpu.roll(block, (STEP - skip) % STEP, 1)
    row = lax.broadcasted_iota(jnp.int32, (count // STEP, STEP, width), 1)
    return jnp.where(row < STEP - skip, turned[:-1], turned[1:]).reshape(count, width)


def clear_margins(buf, rows):
    width = buf.shape[1]
    buf[:REACH, :] = jnp.zeros((REACH, width), buf.dtype)
    buf[REACH + rows :, :] = jnp.zeros((buf.shape[0] - REACH - rows, width), buf.dtype)


def align(source, lead, wide, buf):
    aux, width = source.shape
    rows = aux + SUB
    wide[:SUB, :] = jnp.zeros((SUB, width), jnp.float32)
    wide[SUB + aux :, :] = jnp.zeros((wide.shape[0] - SUB - aux, width), jnp.float32)
    tile = tile_of(aux)

    def widen(i, carry):
        base = pl.multiple_of(i * tile, SUB)
        wide[pl.ds(pl.multiple_of(SUB + base, SUB), tile), :] = source[
            pl.ds(base, tile), :
        ].astype(jnp.float32)
        return carry

    lax.fori_loop(0, aux // tile, widen, 0)
    step = tile_of(rows)

    def move(i, carry):
        base = pl.multiple_of(i * step, SUB)
        moved = rows_from(lambda at, n: wide[pl.ds(at, n), :], SUB - lead + base, step)
        buf[pl.ds(pl.multiple_of(REACH + base, SUB), step), :] = moved.astype(buf.dtype)
        return carry

    lax.fori_loop(0, rows // step, move, 0)


def add_pair(weight, offset, occ, eps_a, eps_b, ft, buf, acc, dens, turned):
    rows, width = acc.shape
    depth = ft.shape[1]
    scale = float(width) ** -0.5
    coulomb = jnp.dot(
        ft[...], buf[pl.ds(offset, depth), :], preferred_element_type=jnp.float32
    )
    amplitude = (coulomb / (occ - eps_a - eps_b)).astype(jnp.bfloat16)
    turned[...] = amplitude.T
    dens[...] += (weight * scale) * dot(amplitude, turned[...])
    step = tile_of(rows)

    def add(i, carry):
        base = pl.multiple_of(i * step, SUB)
        block = buf[pl.ds(pl.multiple_of(offset + base, SUB), step), :]
        acc[pl.ds(base, step), :] += weight * dot(block, turned[...])
        return carry

    lax.fori_loop(0, rows // step, add, 0)


def add_block(plan, occ, group, t, at, eps_col, eps_row, ft, buf, acc, dens, turned):
    owned = acc.shape[0]
    cols = buf.shape[1]

    def one(s, carry):
        slot = plan.slot(group, s, t)

        @pl.when(plan.count(slot) != 0)
        def _():
            add_pair(
                plan.count(slot).astype(jnp.float32),
                plan.offset(slot),
                occ[slot],
                eps_col[s],
                eps_row[group * owned + t, :, at : at + cols],
                ft.at[s],
                buf,
                acc.at[s],
                dens.at[s],
                turned,
            )

        return carry

    lax.fori_loop(0, owned, one, 0)


def make_plan(
    fit_start, occ_energy, pair_partner, domains, energy, ints, occ, eps_col, eps_row,
    *, devices, targets,
):
    owned, width = eps_col.shape[:2]
    orbitals = fit_start.shape[0]
    pairs_here = pair_partner.shape[0] // devices
    plan = Plan(ints, owned)
    position = lax.axis_index("row")
    side = jnp.where(position % 2 == 1, 1, -1)
    places = [
        base * owned + t
        for base in (position, position - side, position + side)
        for t in range(owned)
    ]
    inside = [jnp.clip(place, 0, orbitals - 1) for place in places]
    starts = [fit_start[place] for place in inside]
    pairs = []
    for step in (-1, 0, 1):
        group = position + step
        known = (group >= 0) & (group < devices)
        held = jnp.clip(group, 0, devices - 1)
        for n in range(pairs_here):
            pairs.append((known, group * owned + n % owned, pair_partner[held * pairs_here + n]))
    for group in range(3):
        for s in range(owned):
            for t in range(owned):
                slot = plan.slot(group, s, t)
                other = group * owned + t
                total = jnp.int32(0)
                for known, first, second in pairs:
                    forth = known & (first == places[s]) & (second == places[other])
                    back = known & (second == places[s]) & (first == places[other])
                    total = total + forth.astype(jnp.int32) + back.astype(jnp.int32)
                ints[slot] = total
                ints[plan.at_shift(slot)] = (
                    starts[s] - starts[s] % SUB - starts[other] + starts[other] % SUB
                )
                occ[slot] = occ_energy[inside[s]] + occ_energy[inside[other]]
    for place in range(3 * owned):
        ints[plan.at_lead(place)] = starts[place] % SUB
    for number, group in enumerate(targets):
        way = jnp.int32(0)
        for to in group:
            way = jnp.where(position == to, 1, way)
        ints[plan.at_way(number)] = way
    entries = energy.shape[0]
    table = lax.broadcasted_iota(jnp.int32, (entries, width), 0)
    for place in range(3 * owned):
        domain = domains[pl.ds(inside[place], 1), :]
        row = jnp.sum(jnp.where(table == domain, energy[...], 0.0), axis=0, keepdims=True)
        eps_row[place] = row
        if place < owned:
            eps_col[place] = jnp.broadcast_to(row, (LANES, width)).T[:, :1]
    return plan


def own_kernel(
    fit_start, occ_energy, pair_partner, domains, energy, own,
    *refs, devices, targets,
):
    ints, occ, eps_col, eps_row, acc, dens, ft, token, bufs, wide, turned = refs[-11:]
    token[...] = jnp.zeros_like(token)
    plan = make_plan(
        fit_start, occ_energy, pair_partner, domains, energy, ints, occ, eps_col, eps_row,
        devices=devices, targets=targets,
    )
    owned, aux, width = own.shape
    rows = aux + SUB
    depth = ft.shape[2]
    acc[...] = jnp.zeros_like(acc)
    dens[...] = jnp.zeros_like(dens)
    for t in range(owned):
        buf = bufs.at[t]
        clear_margins(buf, rows)
        align(own.at[t], plan.lead(t), wide, buf)

        def turn(i, carry):
            at = pl.multiple_of(i * LANES, LANES)
            ft[t, :, pl.ds(at, LANES)] = buf[pl.ds(REACH + at, LANES), :].T
            return carry

        lax.fori_loop(0, depth // LANES, turn, 0)
    for t in range(owned):
        add_block(plan, occ, 0, t, 0, eps_col, eps_row, ft, bufs.at[t], acc, dens, turned)


def mate_kernel(ints, occ, eps_col, eps_row, ft, acc_in, dens_in, after, mate, *refs):
    del acc_in, dens_in, after
    acc, dens, token, buf, wide, turned = refs
    token[...] = jnp.zeros_like(token)
    owned, aux, width = mate.shape
    plan = Plan(ints, owned)
    clear_margins(buf, aux + SUB)
    for t in range(owned):
        align(mate.at[t], plan.lead(owned + t), wide, buf)
        add_block(plan, occ, 1, t, 0, eps_col, eps_row, ft, buf, acc, dens, turned)


def needed(plan, t):
    total = jnp.int32(0)
    for s in range(plan.owned):
        total = total + plan.count(plan.slot(2, s, t))
    return total != 0


def far_kernel(
    ints, occ, eps_col, eps_row, ft, acc_in, dens_in, after, block,
    acc, dens, token, buf, wide, turned, *, number, place,
):
    del acc_in, dens_in, after
    token[...] = jnp.zeros_like(token)
    plan = Plan(ints, acc.shape[0])
    t, at = place

    @pl.when(needed(plan, t) & (plan.way(number) == 0))
    def _():
        clear_margins(buf, block.shape[0] + SUB)
        align(block, plan.lead(2 * plan.owned + t), wide, buf)
        add_block(plan, occ, 2, t, at, eps_col, eps_row, ft, buf, acc, dens, turned)


def relayed_kernel(
    ints, occ, eps_col, eps_row, ft, acc_in, dens_in, after, *refs, places
):
    del acc_in, dens_in, after
    *blocks, acc, dens, token, buf, wide, turned, raw, sem = refs
    token[...] = jnp.zeros_like(token)
    plan = Plan(ints, acc.shape[0])
    for number, (block, (t, at)) in enumerate(zip(blocks, places)):

        @pl.when(needed(plan, t) & (plan.way(number) == 1))
        def _():
            copy = pltpu.make_async_copy(block, raw, sem)
            copy.start()
            clear_margins(buf, raw.shape[0] + SUB)
            copy.wait()
            align(raw, plan.lead(2 * plan.owned + t), wide, buf)
            add_block(plan, occ, 2, t, at, eps_col, eps_row, ft, buf, acc, dens, turned)


def last_kernel(
    ints, occ, eps_col, eps_row, ft, acc_in, dens_in, after, block,
    acc, dens, token, out, dens_out, buf, wide, turned, ready, sem, *, place,
):
    del acc_in, dens_in, after
    token[...] = jnp.zeros_like(token)
    t, at = place
    owned, aux, width = out.shape
    plan = Plan(ints, owned)
    rows = aux + SUB
    depth = ft.shape[2]
    scale = float(width) ** -0.5
    step = aux // OUT_TILES
    tiles = OUT_TILES

    @pl.when(needed(plan, t))
    def _():
        clear_margins(buf, rows)
        align(block, plan.lead(2 * owned + t), wide, buf)

    copies = []
    for s in range(owned):
        slot = plan.slot(2, s, t)

        @pl.when(plan.count(slot) != 0)
        def _():
            coulomb = dot(ft[s], buf[pl.ds(plan.offset(slot), depth), :])
            eps_b = eps_row[2 * owned + t, :, at : at + COLS]
            amplitude = (coulomb / (occ[slot] - eps_col[s] - eps_b)).astype(jnp.bfloat16)
            turned[s] = amplitude.T
            weight = plan.count(slot).astype(jnp.float32)
            dens[s] += (weight * scale) * dot(amplitude, turned[s])

        copies.append(pltpu.make_async_copy(dens.at[s], dens_out.at[s], sem.at[s, tiles]))
        copies[-1].start()

    for s in range(owned):
        slot = plan.slot(2, s, t)

        def add(base, taken):
            @pl.when(plan.count(slot) != 0)
            def _():
                weight = plan.count(slot).astype(jnp.float32)
                start = pl.multiple_of(plan.offset(slot) + base, SUB)
                taken_rows = buf[pl.ds(start, taken), :]
                acc[s, pl.ds(base, taken), :] += weight * dot(taken_rows, turned[s])

        add(0, step + SUB)
        for i in range(tiles):
            if i + 1 < tiles:
                add((i + 1) * step + SUB, step)
            base = i * step
            settled = rows_from(
                lambda at, n: acc[s, pl.ds(at, n), :], plan.lead(s) + base, step
            )
            ready[s, base : base + step, :] = settled.astype(ready.dtype)
            part = pl.ds(base, step)
            copies.append(
                pltpu.make_async_copy(ready.at[s, part], out.at[s, part], sem.at[s, i])
            )
            copies[-1].start()
    for copy in copies:
        copy.wait()


def copy_kernel(*refs):
    count = len(refs) // 2
    for source, out in zip(refs[:count], refs[-count:]):
        out[...] = source[0]


def pass_kernel(source, after, out):
    del source, after, out


def relay_plan(devices, chunks):
    if devices != 16 or chunks != 3:
        return [[] for _ in range(chunks)]
    last = devices - 1
    plan = []
    for z in (1, 0, 2):
        high, low = 4 * z + 3, 4 * z + 4
        plan.append([(high, low, 0), (low, high, last)])
    return plan


def spec(space):
    return pl.BlockSpec(memory_space=space)


def on_device(fitted, fit_start, virt_domain, occ_energy, virt_energy, pair_partner):
    owned, aux, width = fitted.shape
    devices = lax.axis_size("row")
    rows = aux + SUB
    depth = up_to(rows, LANES)
    buf_rows = 2 * REACH + depth
    wide_rows = aux + 2 * SUB + STEP
    smem, vmem, anywhere = spec(pltpu.SMEM), spec(pltpu.VMEM), spec(pl.ANY)

    outward = []
    for i in range(devices):
        to = i + 1 if i % 2 else i - 1
        if 0 <= to < devices:
            outward.append((i, to))
    inward = [(i, i ^ 1) for i in range(devices) if i ^ 1 < devices]

    def in_hbm(array):
        return pltpu.with_memory_space_constraint(array, pltpu.HBM)

    def in_vmem(array):
        return pltpu.with_memory_space_constraint(array, pltpu.VMEM)

    def chunks(places, *after):
        return pl.pallas_call(
            copy_kernel,
            grid=(1,),
            out_shape=[jax.ShapeDtypeStruct((aux, COLS), fitted.dtype)] * len(places),
            in_specs=[
                pl.BlockSpec((1, aux, COLS), lambda i, t=t, at=at: (t, 0, at // COLS))
                for t, at in places
            ]
            + [anywhere] * len(after),
            out_specs=[pl.BlockSpec((aux, COLS), lambda i: (0, 0))] * len(places),
            compiler_params=pltpu.CompilerParams(vmem_limit_bytes=CHUNK_VMEM),
            name="chunks",
        )(*[in_hbm(fitted)] * len(places), *after)

    def pass_on(block, after):
        return pl.pallas_call(
            pass_kernel,
            out_shape=jax.ShapeDtypeStruct(block.shape, block.dtype),
            in_specs=[anywhere] * 2,
            out_specs=anywhere,
            input_output_aliases={0: 0},
            compiler_params=pltpu.CompilerParams(vmem_limit_bytes=CHUNK_VMEM),
            name="pass_on",
        )(block, after)

    cells = [(t, at) for t in range(owned) for at in range(0, width, COLS)]
    last = len(cells) - 1
    plan = relay_plan(devices, last)
    relayed = any(plan)

    def exchange(number, block):
        group = plan[number] if number < last else []
        gone = {(source, to) for source, to, _ in group}
        pairs = [pair for pair in outward if pair not in gone]
        first_hop = [(source, by) for source, _, by in group] if number else []
        return lax.ppermute(block, "row", pairs + first_hop)

    mate = lax.ppermute(fitted, "row", inward)
    sent = list(chunks(cells[:1]))
    early = []
    if relayed:
        early.append(lax.ppermute(sent[0], "row", [(source, by) for source, _, by in plan[0]]))
    far = [exchange(0, sent[0])]
    sent += chunks(cells[1:], sent[0])
    far += [exchange(number, sent[number]) for number in range(1, last + 1)]

    unit = 4 * rows * width * COLS
    acc_shape = pltpu.VMEM((owned, rows, width), jnp.float32)
    dens_shape = pltpu.VMEM((owned, width, width), jnp.float32)
    ft_shape = pltpu.VMEM((owned, width, depth), fitted.dtype)
    token_shape = jax.ShapeDtypeStruct((8, LANES), jnp.int32)
    slots = 3 * owned * owned

    def cost(blocks):
        return pl.CostEstimate(
            flops=100 * unit * blocks * owned, bytes_accessed=8 << 20, transcendentals=0
        )

    ints, occ, eps_col, eps_row, acc, dens, ft, token = pl.pallas_call(
        functools.partial(
            own_kernel, devices=devices, targets=[[to for _, to, _ in group] for group in plan]
        ),
        out_shape=(
            jax.ShapeDtypeStruct((Plan(None, owned).at_way(last),), jnp.int32),
            jax.ShapeDtypeStruct((slots,), jnp.float32),
            jax.ShapeDtypeStruct((owned, width, 1), jnp.float32),
            jax.ShapeDtypeStruct((3 * owned, 1, width), jnp.float32),
            acc_shape,
            dens_shape,
            ft_shape,
            token_shape,
        ),
        in_specs=[smem] * 3 + [vmem] * 3 + [anywhere] * (1 + len(early)),
        out_specs=(smem,) * 2 + (vmem,) * 6,
        scratch_shapes=[
            pltpu.VMEM((owned, buf_rows, width), fitted.dtype),
            pltpu.VMEM((wide_rows, width), jnp.float32),
            pltpu.VMEM((width, width), fitted.dtype),
        ],
        compiler_params=pltpu.CompilerParams(vmem_limit_bytes=NEAR_VMEM),
        cost_estimate=cost(len(cells)),
        name="own_pairs",
    )(
        fit_start, occ_energy, pair_partner, virt_domain, virt_energy.reshape(-1, 1),
        in_hbm(fitted), mate, *early,
    )
    state = {"acc": acc, "dens": dens, "token": token}
    hops = []

    def add_pairs(kernel, block_specs, blocks, cols, limit, name, outs=(), scratch=()):
        specs = [smem] * 2 + [vmem] * 5 + [anywhere] + block_specs
        results = pl.pallas_call(
            kernel,
            out_shape=(acc_shape, dens_shape, token_shape, *outs),
            in_specs=specs,
            out_specs=(vmem,) * 3 + (anywhere,) * len(outs),
            input_output_aliases={5: 0, 6: 1},
            scratch_shapes=[
                pltpu.VMEM((buf_rows, cols), fitted.dtype),
                pltpu.VMEM((wide_rows, cols), jnp.float32),
                *scratch,
            ],
            compiler_params=pltpu.CompilerParams(vmem_limit_bytes=limit),
            cost_estimate=cost(cols // COLS),
            name=name,
        )(
            ints, occ, eps_col, eps_row, in_vmem(ft), in_vmem(state["acc"]),
            in_vmem(state["dens"]), state["token"], *blocks,
        )
        state.update(acc=results[0], dens=results[1], token=results[2])
        return results[3:]

    def second_hop(number, block):
        hops.append(lax.ppermute(block, "row", [(by, to) for _, to, by in plan[number]]))

    def relay(number):
        if relayed:
            far[number] = state["token"] = pass_on(far[number], state["token"])
            second_hop(number, far[number])

    turned_cols = (pltpu.VMEM((COLS, width), fitted.dtype),)
    if relayed:
        second_hop(0, early[0])
    add_pairs(
        mate_kernel, [vmem], [mate], width, NEAR_VMEM, "mate_pairs",
        scratch=(pltpu.VMEM((width, width), fitted.dtype),),
    )
    for number in range(last):
        if number:
            relay(number)
        add_pairs(
            functools.partial(far_kernel, number=number, place=cells[number]),
            [vmem], [far[number]], COLS, FAR_VMEM, f"far_pairs_{number}", scratch=turned_cols,
        )
    if relayed:
        add_pairs(
            functools.partial(relayed_kernel, places=cells[:last]),
            [anywhere] * last, hops, COLS, FAR_VMEM, "relayed_pairs",
            scratch=turned_cols
            + (pltpu.VMEM((aux, COLS), fitted.dtype), pltpu.SemaphoreType.DMA),
        )
    gradient, density = add_pairs(
        functools.partial(last_kernel, place=cells[last]),
        [vmem], [far[last]], COLS, FAR_VMEM, "last_pairs",
        outs=(
            jax.ShapeDtypeStruct(fitted.shape, fitted.dtype),
            jax.ShapeDtypeStruct((owned, width, width), jnp.float32),
        ),
        scratch=(
            pltpu.VMEM((owned, COLS, width), fitted.dtype),
            pltpu.VMEM((owned, aux, width), fitted.dtype),
            pltpu.SemaphoreType.DMA((owned, OUT_TILES + 1)),
        ),
    )
    return gradient, density


def solution(mesh):
    placed = (
        P(("parts", "row"), None, None),
        P("parts"),
        P("parts", None),
        P("parts"),
        P("parts"),
        P("parts"),
    )
    return jax.shard_map(
        on_device,
        mesh=mesh,
        in_specs=placed,
        out_specs=(P(("parts", "row"), None, None), P(("parts", "row"), None, None)),
        check_vma=False,
    )
```

```python
import functools

import jax
import jax.numpy as jnp
from jax import lax
from jax.experimental import pallas as pl
from jax.experimental.pallas import tpu as pltpu
from jax.sharding import PartitionSpec as P

SUB = 16
STEP = 8
LANES = 128
OUT_TILES = 4
COLS = 256
REACH = 1024
NEAR_VMEM = 22 * 1024 * 1024
FAR_VMEM = 16 * 1024 * 1024
CHUNK_VMEM = 14 * 1024 * 1024


class Plan:
    def __init__(self, ref, owned):
        self.ref, self.owned = ref, owned
        self.slots = 3 * owned * owned

    def slot(self, group, s, t):
        return (group * self.owned + s) * self.owned + t

    def at_shift(self, slot):
        return self.slots + slot

    def at_lead(self, place):
        return 2 * self.slots + place

    def at_way(self, number):
        return 2 * self.slots + 3 * self.owned + number

    def at_late(self, ways):
        return self.at_way(ways)

    def count(self, slot):
        return self.ref[slot]

    def offset(self, slot):
        return pl.multiple_of(REACH + self.ref[self.at_shift(slot)], SUB)

    def lead(self, place):
        return self.ref[self.at_lead(place)]

    def way(self, number):
        return self.ref[self.at_way(number)]


def dot(a, b):
    return jnp.dot(a, b, preferred_element_type=jnp.float32)


def up_to(value, unit):
    return -(-value // unit) * unit


def tile_of(rows):
    return max(n for n in range(SUB, 705, SUB) if rows % n == 0)


def rows_from(load, start, count):
    skip = start % STEP
    base = pl.multiple_of(start - skip, STEP)
    block = load(base, count + STEP)
    width = block.shape[1]
    block = block.reshape(count // STEP + 1, STEP, width)
    turned = pltpu.roll(block, (STEP - skip) % STEP, 1)
    row = lax.broadcasted_iota(jnp.int32, (count // STEP, STEP, width), 1)
    return jnp.where(row < STEP - skip, turned[:-1], turned[1:]).reshape(count, width)


def clear_margins(buf, rows):
    width = buf.shape[1]
    buf[:REACH, :] = jnp.zeros((REACH, width), buf.dtype)
    buf[REACH + rows :, :] = jnp.zeros((buf.shape[0] - REACH - rows, width), buf.dtype)


def align(source, lead, wide, buf):
    aux, width = source.shape
    rows = aux + SUB
    wide[:SUB, :] = jnp.zeros((SUB, width), jnp.float32)
    wide[SUB + aux :, :] = jnp.zeros((wide.shape[0] - SUB - aux, width), jnp.float32)
    tile = tile_of(aux)

    def widen(i, carry):
        base = pl.multiple_of(i * tile, SUB)
        wide[pl.ds(pl.multiple_of(SUB + base, SUB), tile), :] = source[
            pl.ds(base, tile), :
        ].astype(jnp.float32)
        return carry

    lax.fori_loop(0, aux // tile, widen, 0)
    step = tile_of(rows)

    def move(i, carry):
        base = pl.multiple_of(i * step, SUB)
        moved = rows_from(lambda at, n: wide[pl.ds(at, n), :], SUB - lead + base, step)
        buf[pl.ds(pl.multiple_of(REACH + base, SUB), step), :] = moved.astype(buf.dtype)
        return carry

    lax.fori_loop(0, rows // step, move, 0)


def add_pair(weight, offset, occ, eps_a, eps_b, ft, buf, acc, dens, turned):
    rows, width = acc.shape
    depth = ft.shape[1]
    scale = float(width) ** -0.5
    coulomb = jnp.dot(
        ft[...], buf[pl.ds(offset, depth), :], preferred_element_type=jnp.float32
    )
    amplitude = (coulomb / (occ - eps_a - eps_b)).astype(jnp.bfloat16)
    turned[...] = amplitude.T
    dens[...] += (weight * scale) * dot(amplitude, turned[...])
    step = tile_of(rows)

    def add(i, carry):
        base = pl.multiple_of(i * step, SUB)
        block = buf[pl.ds(pl.multiple_of(offset + base, SUB), step), :]
        acc[pl.ds(base, step), :] += weight * dot(block, turned[...])
        return carry

    lax.fori_loop(0, rows // step, add, 0)


def add_block(plan, occ, group, t, at, eps_col, eps_row, ft, buf, acc, dens, turned):
    owned = acc.shape[0]
    cols = buf.shape[1]

    def one(s, carry):
        slot = plan.slot(group, s, t)

        @pl.when(plan.count(slot) != 0)
        def _():
            add_pair(
                plan.count(slot).astype(jnp.float32),
                plan.offset(slot),
                occ[slot],
                eps_col[s],
                eps_row[group * owned + t, :, at : at + cols],
                ft.at[s],
                buf,
                acc.at[s],
                dens.at[s],
                turned,
            )

        return carry

    lax.fori_loop(0, owned, one, 0)


def make_plan(
    fit_start, occ_energy, pair_partner, domains, energy, ints, occ, eps_col, eps_row,
    *, devices, targets, relays,
):
    owned, width = eps_col.shape[:2]
    orbitals = fit_start.shape[0]
    pairs_here = pair_partner.shape[0] // devices
    plan = Plan(ints, owned)
    position = lax.axis_index("row")
    side = jnp.where(position % 2 == 1, 1, -1)
    places = [
        base * owned + t
        for base in (position, position - side, position + side)
        for t in range(owned)
    ]
    inside = [jnp.clip(place, 0, orbitals - 1) for place in places]
    starts = [fit_start[place] for place in inside]
    pairs = []
    for step in (-1, 0, 1):
        group = position + step
        known = (group >= 0) & (group < devices)
        held = jnp.clip(group, 0, devices - 1)
        for n in range(pairs_here):
            pairs.append((known, group * owned + n % owned, pair_partner[held * pairs_here + n]))
    for group in range(3):
        for s in range(owned):
            for t in range(owned):
                slot = plan.slot(group, s, t)
                other = group * owned + t
                total = jnp.int32(0)
                for known, first, second in pairs:
                    forth = known & (first == places[s]) & (second == places[other])
                    back = known & (second == places[s]) & (first == places[other])
                    total = total + forth.astype(jnp.int32) + back.astype(jnp.int32)
                ints[slot] = total
                ints[plan.at_shift(slot)] = (
                    starts[s] - starts[s] % SUB - starts[other] + starts[other] % SUB
                )
                occ[slot] = occ_energy[inside[s]] + occ_energy[inside[other]]
    for place in range(3 * owned):
        ints[plan.at_lead(place)] = starts[place] % SUB
    for number, group in enumerate(targets):
        way = jnp.int32(0)
        for to in group:
            way = jnp.where(position == to, 1, way)
        ints[plan.at_way(number)] = way
    late = jnp.int32(0)
    for row in relays:
        late = jnp.where(position == row, 1, late)
    ints[plan.at_late(len(targets))] = late
    entries = energy.shape[0]
    table = lax.broadcasted_iota(jnp.int32, (entries, width), 0)
    for place in range(3 * owned):
        domain = domains[pl.ds(inside[place], 1), :]
        row = jnp.sum(jnp.where(table == domain, energy[...], 0.0), axis=0, keepdims=True)
        eps_row[place] = row
        if place < owned:
            eps_col[place] = jnp.broadcast_to(row, (LANES, width)).T[:, :1]
    return plan


def own_kernel(
    fit_start, occ_energy, pair_partner, domains, energy, own,
    *refs, devices, targets, relays,
):
    ints, occ, eps_col, eps_row, acc, dens, ft, token, bufs, wide, turned = refs[-11:]
    token[...] = jnp.zeros_like(token)
    plan = make_plan(
        fit_start, occ_energy, pair_partner, domains, energy, ints, occ, eps_col, eps_row,
        devices=devices, targets=targets, relays=relays,
    )
    owned, aux, width = own.shape
    rows = aux + SUB
    depth = ft.shape[2]
    acc[...] = jnp.zeros_like(acc)
    dens[...] = jnp.zeros_like(dens)
    for t in range(owned):
        buf = bufs.at[t]
        clear_margins(buf, rows)
        align(own.at[t], plan.lead(t), wide, buf)

        def turn(i, carry):
            at = pl.multiple_of(i * LANES, LANES)
            ft[t, :, pl.ds(at, LANES)] = buf[pl.ds(REACH + at, LANES), :].T
            return carry

        lax.fori_loop(0, depth // LANES, turn, 0)

    @pl.when(ints[plan.at_late(len(targets))] == 0)
    def _():
        for t in range(owned):
            add_block(plan, occ, 0, t, 0, eps_col, eps_row, ft, bufs.at[t], acc, dens, turned)


def mate_kernel(
    ints, occ, eps_col, eps_row, ft, acc_in, dens_in, after, mate,
    acc, dens, token, buf, wide, turned, *, ways,
):
    del acc_in, dens_in, after
    token[...] = jnp.zeros_like(token)
    owned, aux, width = mate.shape
    plan = Plan(ints, owned)

    @pl.when(ints[plan.at_late(ways)] == 0)
    def _():
        clear_margins(buf, aux + SUB)
        for t in range(owned):
            align(mate.at[t], plan.lead(owned + t), wide, buf)
            add_block(plan, occ, 1, t, 0, eps_col, eps_row, ft, buf, acc, dens, turned)


def late_kernel(
    ints, occ, eps_col, eps_row, ft, acc_in, dens_in, after, own, mate,
    acc, dens, token, buf, wide, turned, raw, sem, *, ways,
):
    del acc_in, dens_in, after
    token[...] = jnp.zeros_like(token)
    owned, aux, width = own.shape
    plan = Plan(ints, owned)

    @pl.when(ints[plan.at_late(ways)] == 1)
    def _():
        clear_margins(buf, aux + SUB)
        for group, blocks in ((0, own), (1, mate)):
            for t in range(owned):
                copy = pltpu.make_async_copy(blocks.at[t], raw, sem)
                copy.start()
                copy.wait()
                align(raw, plan.lead(group * owned + t), wide, buf)
                add_block(plan, occ, group, t, 0, eps_col, eps_row, ft, buf, acc, dens, turned)


def needed(plan, t):
    total = jnp.int32(0)
    for s in range(plan.owned):
        total = total + plan.count(plan.slot(2, s, t))
    return total != 0


def far_kernel(
    ints, occ, eps_col, eps_row, ft, acc_in, dens_in, after, block,
    acc, dens, token, buf, wide, turned, *, number, place,
):
    del acc_in, dens_in, after
    token[...] = jnp.zeros_like(token)
    plan = Plan(ints, acc.shape[0])
    t, at = place

    @pl.when(needed(plan, t) & (plan.way(number) == 0))
    def _():
        clear_margins(buf, block.shape[0] + SUB)
        align(block, plan.lead(2 * plan.owned + t), wide, buf)
        add_block(plan, occ, 2, t, at, eps_col, eps_row, ft, buf, acc, dens, turned)


def relayed_kernel(
    ints, occ, eps_col, eps_row, ft, acc_in, dens_in, after, *refs, places
):
    del acc_in, dens_in, after
    *blocks, acc, dens, token, buf, wide, turned, raw, sem = refs
    token[...] = jnp.zeros_like(token)
    plan = Plan(ints, acc.shape[0])
    for number, (block, (t, at)) in enumerate(zip(blocks, places)):

        @pl.when(needed(plan, t) & (plan.way(number) == 1))
        def _():
            copy = pltpu.make_async_copy(block, raw, sem)
            copy.start()
            clear_margins(buf, raw.shape[0] + SUB)
            copy.wait()
            align(raw, plan.lead(2 * plan.owned + t), wide, buf)
            add_block(plan, occ, 2, t, at, eps_col, eps_row, ft, buf, acc, dens, turned)


def last_kernel(
    ints, occ, eps_col, eps_row, ft, acc_in, dens_in, after, block,
    acc, dens, token, out, dens_out, buf, wide, turned, ready, sem, *, place,
):
    del acc_in, dens_in, after
    token[...] = jnp.zeros_like(token)
    t, at = place
    owned, aux, width = out.shape
    plan = Plan(ints, owned)
    rows = aux + SUB
    depth = ft.shape[2]
    scale = float(width) ** -0.5
    step = aux // OUT_TILES
    tiles = OUT_TILES

    @pl.when(needed(plan, t))
    def _():
        clear_margins(buf, rows)
        align(block, plan.lead(2 * owned + t), wide, buf)

    copies = []
    for s in range(owned):
        slot = plan.slot(2, s, t)

        @pl.when(plan.count(slot) != 0)
        def _():
            coulomb = dot(ft[s], buf[pl.ds(plan.offset(slot), depth), :])
            eps_b = eps_row[2 * owned + t, :, at : at + COLS]
            amplitude = (coulomb / (occ[slot] - eps_col[s] - eps_b)).astype(jnp.bfloat16)
            turned[s] = amplitude.T
            weight = plan.count(slot).astype(jnp.float32)
            dens[s] += (weight * scale) * dot(amplitude, turned[s])

        copies.append(pltpu.make_async_copy(dens.at[s], dens_out.at[s], sem.at[s, tiles]))
        copies[-1].start()

    for s in range(owned):
        slot = plan.slot(2, s, t)

        def add(base, taken):
            @pl.when(plan.count(slot) != 0)
            def _():
                weight = plan.count(slot).astype(jnp.float32)
                start = pl.multiple_of(plan.offset(slot) + base, SUB)
                taken_rows = buf[pl.ds(start, taken), :]
                acc[s, pl.ds(base, taken), :] += weight * dot(taken_rows, turned[s])

        add(0, step + SUB)
        for i in range(tiles):
            if i + 1 < tiles:
                add((i + 1) * step + SUB, step)
            base = i * step
            settled = rows_from(
                lambda at, n: acc[s, pl.ds(at, n), :], plan.lead(s) + base, step
            )
            ready[s, base : base + step, :] = settled.astype(ready.dtype)
            part = pl.ds(base, step)
            copies.append(
                pltpu.make_async_copy(ready.at[s, part], out.at[s, part], sem.at[s, i])
            )
            copies[-1].start()
    for copy in copies:
        copy.wait()


def copy_kernel(*refs):
    count = len(refs) // 2
    for source, out in zip(refs[:count], refs[-count:]):
        out[...] = source[0]


def pass_kernel(source, after, out):
    del source, after, out


def relay_plan(devices, chunks):
    if devices != 16 or chunks != 3:
        return [[] for _ in range(chunks)]
    last = devices - 1
    plan = []
    for z in (1, 0, 2):
        high, low = 4 * z + 3, 4 * z + 4
        plan.append([(high, low, 0), (low, high, last)])
    return plan


def spec(space):
    return pl.BlockSpec(memory_space=space)


def on_device(fitted, fit_start, virt_domain, occ_energy, virt_energy, pair_partner):
    owned, aux, width = fitted.shape
    devices = lax.axis_size("row")
    rows = aux + SUB
    depth = up_to(rows, LANES)
    buf_rows = 2 * REACH + depth
    wide_rows = aux + 2 * SUB + STEP
    smem, vmem, anywhere = spec(pltpu.SMEM), spec(pltpu.VMEM), spec(pl.ANY)

    outward = []
    for i in range(devices):
        to = i + 1 if i % 2 else i - 1
        if 0 <= to < devices:
            outward.append((i, to))
    inward = [(i, i ^ 1) for i in range(devices) if i ^ 1 < devices]

    def in_hbm(array):
        return pltpu.with_memory_space_constraint(array, pltpu.HBM)

    def in_vmem(array):
        return pltpu.with_memory_space_constraint(array, pltpu.VMEM)

    def chunks(places, *after):
        return pl.pallas_call(
            copy_kernel,
            grid=(1,),
            out_shape=[jax.ShapeDtypeStruct((aux, COLS), fitted.dtype)] * len(places),
            in_specs=[
                pl.BlockSpec((1, aux, COLS), lambda i, t=t, at=at: (t, 0, at // COLS))
                for t, at in places
            ]
            + [anywhere] * len(after),
            out_specs=[pl.BlockSpec((aux, COLS), lambda i: (0, 0))] * len(places),
            compiler_params=pltpu.CompilerParams(vmem_limit_bytes=CHUNK_VMEM),
            name="chunks",
        )(*[in_hbm(fitted)] * len(places), *after)

    def pass_on(block, after):
        return pl.pallas_call(
            pass_kernel,
            out_shape=jax.ShapeDtypeStruct(block.shape, block.dtype),
            in_specs=[anywhere] * 2,
            out_specs=anywhere,
            input_output_aliases={0: 0},
            compiler_params=pltpu.CompilerParams(vmem_limit_bytes=CHUNK_VMEM),
            name="pass_on",
        )(block, after)

    cells = [(t, at) for t in range(owned) for at in range(0, width, COLS)]
    last = len(cells) - 1
    plan = relay_plan(devices, last)
    relayed = any(plan)

    def exchange(number, block):
        group = plan[number] if number < last else []
        gone = {(source, to) for source, to, _ in group}
        pairs = [pair for pair in outward if pair not in gone]
        first_hop = [(source, by) for source, _, by in group] if number else []
        return lax.ppermute(block, "row", pairs + first_hop)

    mate = lax.ppermute(fitted, "row", inward)
    sent = list(chunks(cells[:1]))
    early = []
    if relayed:
        early.append(lax.ppermute(sent[0], "row", [(source, by) for source, _, by in plan[0]]))
    far = [exchange(0, sent[0])]
    sent += chunks(cells[1:], sent[0])
    far += [exchange(number, sent[number]) for number in range(1, last + 1)]

    unit = 4 * rows * width * COLS
    acc_shape = pltpu.VMEM((owned, rows, width), jnp.float32)
    dens_shape = pltpu.VMEM((owned, width, width), jnp.float32)
    ft_shape = pltpu.VMEM((owned, width, depth), fitted.dtype)
    token_shape = jax.ShapeDtypeStruct((8, LANES), jnp.int32)
    slots = 3 * owned * owned

    def cost(blocks):
        return pl.CostEstimate(
            flops=100 * unit * blocks * owned, bytes_accessed=8 << 20, transcendentals=0
        )

    ints, occ, eps_col, eps_row, acc, dens, ft, token = pl.pallas_call(
        functools.partial(
            own_kernel,
            devices=devices,
            targets=[[to for _, to, _ in group] for group in plan],
            relays=sorted({by for group in plan for _, _, by in group}),
        ),
        out_shape=(
            jax.ShapeDtypeStruct((Plan(None, owned).at_late(last) + 1,), jnp.int32),
            jax.ShapeDtypeStruct((slots,), jnp.float32),
            jax.ShapeDtypeStruct((owned, width, 1), jnp.float32),
            jax.ShapeDtypeStruct((3 * owned, 1, width), jnp.float32),
            acc_shape,
            dens_shape,
            ft_shape,
            token_shape,
        ),
        in_specs=[smem] * 3 + [vmem] * 3 + [anywhere] * (1 + len(early)),
        out_specs=(smem,) * 2 + (vmem,) * 6,
        scratch_shapes=[
            pltpu.VMEM((owned, buf_rows, width), fitted.dtype),
            pltpu.VMEM((wide_rows, width), jnp.float32),
            pltpu.VMEM((width, width), fitted.dtype),
        ],
        compiler_params=pltpu.CompilerParams(vmem_limit_bytes=NEAR_VMEM),
        cost_estimate=cost(len(cells)),
        name="own_pairs",
    )(
        fit_start, occ_energy, pair_partner, virt_domain, virt_energy.reshape(-1, 1),
        in_hbm(fitted), mate, *early,
    )
    state = {"acc": acc, "dens": dens, "token": token}
    hops = []

    def add_pairs(kernel, block_specs, blocks, cols, limit, name, outs=(), scratch=()):
        specs = [smem] * 2 + [vmem] * 5 + [anywhere] + block_specs
        results = pl.pallas_call(
            kernel,
            out_shape=(acc_shape, dens_shape, token_shape, *outs),
            in_specs=specs,
            out_specs=(vmem,) * 3 + (anywhere,) * len(outs),
            input_output_aliases={5: 0, 6: 1},
            scratch_shapes=[
                pltpu.VMEM((buf_rows, cols), fitted.dtype),
                pltpu.VMEM((wide_rows, cols), jnp.float32),
                *scratch,
            ],
            compiler_params=pltpu.CompilerParams(vmem_limit_bytes=limit),
            cost_estimate=cost(cols // COLS),
            name=name,
        )(
            ints, occ, eps_col, eps_row, in_vmem(ft), in_vmem(state["acc"]),
            in_vmem(state["dens"]), state["token"], *blocks,
        )
        state.update(acc=results[0], dens=results[1], token=results[2])
        return results[3:]

    def second_hop(number, block):
        hops.append(lax.ppermute(block, "row", [(by, to) for _, to, by in plan[number]]))

    def relay(number):
        if relayed:
            far[number] = state["token"] = pass_on(far[number], state["token"])
            second_hop(number, far[number])

    turned_cols = (pltpu.VMEM((COLS, width), fitted.dtype),)
    if relayed:
        second_hop(0, early[0])
    turned_full = (pltpu.VMEM((width, width), fitted.dtype),)
    add_pairs(
        functools.partial(mate_kernel, ways=last), [vmem], [mate], width, NEAR_VMEM, "mate_pairs",
        scratch=turned_full,
    )
    for number in range(last):
        if number:
            relay(number)
        if relayed and number == last - 1:
            add_pairs(
                functools.partial(late_kernel, ways=last),
                [anywhere] * 2, [in_hbm(fitted), mate], width, NEAR_VMEM, "late_pairs",
                scratch=turned_full
                + (pltpu.VMEM((aux, width), fitted.dtype), pltpu.SemaphoreType.DMA),
            )
        add_pairs(
            functools.partial(far_kernel, number=number, place=cells[number]),
            [vmem], [far[number]], COLS, FAR_VMEM, f"far_pairs_{number}", scratch=turned_cols,
        )
    if relayed:
        add_pairs(
            functools.partial(relayed_kernel, places=cells[:last]),
            [anywhere] * last, hops, COLS, FAR_VMEM, "relayed_pairs",
            scratch=turned_cols
            + (pltpu.VMEM((aux, COLS), fitted.dtype), pltpu.SemaphoreType.DMA),
        )
    gradient, density = add_pairs(
        functools.partial(last_kernel, place=cells[last]),
        [vmem], [far[last]], COLS, FAR_VMEM, "last_pairs",
        outs=(
            jax.ShapeDtypeStruct(fitted.shape, fitted.dtype),
            jax.ShapeDtypeStruct((owned, width, width), jnp.float32),
        ),
        scratch=(
            pltpu.VMEM((owned, COLS, width), fitted.dtype),
            pltpu.VMEM((owned, aux, width), fitted.dtype),
            pltpu.SemaphoreType.DMA((owned, OUT_TILES + 1)),
        ),
    )
    return gradient, density


def solution(mesh):
    placed = (
        P(("parts", "row"), None, None),
        P("parts"),
        P("parts", None),
        P("parts"),
        P("parts"),
        P("parts"),
    )
    return jax.shard_map(
        on_device,
        mesh=mesh,
        in_specs=placed,
        out_specs=(P(("parts", "row"), None, None), P(("parts", "row"), None, None)),
        check_vma=False,
    )
```

```python
import functools

import jax
import jax.numpy as jnp
from jax import lax
from jax.experimental import pallas as pl
from jax.experimental.pallas import tpu as pltpu
from jax.sharding import PartitionSpec as P

SUB = 16
STEP = 8
LANES = 128
OUT_TILES = 4
CHUNK_TILES = 2
COLS = 256
REACH = 1024
NEAR_VMEM = 22 * 1024 * 1024
FAR_VMEM = 16 * 1024 * 1024
CHUNK_VMEM = 6 * 1024 * 1024


class Plan:
    def __init__(self, ref, owned):
        self.ref, self.owned = ref, owned
        self.slots = 3 * owned * owned

    def slot(self, group, s, t):
        return (group * self.owned + s) * self.owned + t

    def at_shift(self, slot):
        return self.slots + slot

    def at_lead(self, place):
        return 2 * self.slots + place

    def at_way(self, number):
        return 2 * self.slots + 3 * self.owned + number

    def at_late(self, ways):
        return self.at_way(ways)

    def count(self, slot):
        return self.ref[slot]

    def offset(self, slot):
        return pl.multiple_of(REACH + self.ref[self.at_shift(slot)], SUB)

    def lead(self, place):
        return self.ref[self.at_lead(place)]

    def way(self, number):
        return self.ref[self.at_way(number)]


def dot(a, b):
    return jnp.dot(a, b, preferred_element_type=jnp.float32)


def up_to(value, unit):
    return -(-value // unit) * unit


def tile_of(rows):
    return max(n for n in range(SUB, 705, SUB) if rows % n == 0)


def rows_from(load, start, count):
    skip = start % STEP
    base = pl.multiple_of(start - skip, STEP)
    block = load(base, count + STEP)
    width = block.shape[1]
    block = block.reshape(count // STEP + 1, STEP, width)
    turned = pltpu.roll(block, (STEP - skip) % STEP, 1)
    row = lax.broadcasted_iota(jnp.int32, (count // STEP, STEP, width), 1)
    return jnp.where(row < STEP - skip, turned[:-1], turned[1:]).reshape(count, width)


def clear_margins(buf, rows):
    width = buf.shape[1]
    buf[:REACH, :] = jnp.zeros((REACH, width), buf.dtype)
    buf[REACH + rows :, :] = jnp.zeros((buf.shape[0] - REACH - rows, width), buf.dtype)


def align(source, lead, wide, buf):
    aux, width = source.shape
    rows = aux + SUB
    wide[:SUB, :] = jnp.zeros((SUB, width), jnp.float32)
    wide[SUB + aux :, :] = jnp.zeros((wide.shape[0] - SUB - aux, width), jnp.float32)
    tile = tile_of(aux)

    def widen(i, carry):
        base = pl.multiple_of(i * tile, SUB)
        wide[pl.ds(pl.multiple_of(SUB + base, SUB), tile), :] = source[
            pl.ds(base, tile), :
        ].astype(jnp.float32)
        return carry

    lax.fori_loop(0, aux // tile, widen, 0)
    step = tile_of(rows)

    def move(i, carry):
        base = pl.multiple_of(i * step, SUB)
        moved = rows_from(lambda at, n: wide[pl.ds(at, n), :], SUB - lead + base, step)
        buf[pl.ds(pl.multiple_of(REACH + base, SUB), step), :] = moved.astype(buf.dtype)
        return carry

    lax.fori_loop(0, rows // step, move, 0)


def amplitudes(coulomb, denominator, weight):
    amplitude = (coulomb / denominator).astype(jnp.bfloat16)
    weighted = (amplitude.astype(jnp.float32) * weight).astype(jnp.bfloat16)
    return amplitude, weighted.T


def add_pair(weight, offset, occ, eps_a, eps_b, ft, buf, acc, dens, turned):
    rows, width = acc.shape
    depth = ft.shape[1]
    scale = float(width) ** -0.5
    coulomb = dot(ft[...], buf[pl.ds(offset, depth), :])
    amplitude, turned[...] = amplitudes(coulomb, occ - eps_a - eps_b, weight)
    dens[...] += scale * dot(amplitude, turned[...])
    step = tile_of(rows)

    def add(i, carry):
        base = pl.multiple_of(i * step, SUB)
        block = buf[pl.ds(pl.multiple_of(offset + base, SUB), step), :]
        acc[pl.ds(base, step), :] += dot(block, turned[...])
        return carry

    lax.fori_loop(0, rows // step, add, 0)


def add_block(plan, occ, group, t, at, eps_col, eps_row, ft, buf, acc, dens, turned):
    owned = acc.shape[0]
    cols = buf.shape[1]

    def one(s, carry):
        slot = plan.slot(group, s, t)

        @pl.when(plan.count(slot) != 0)
        def _():
            add_pair(
                plan.count(slot).astype(jnp.float32),
                plan.offset(slot),
                occ[slot],
                eps_col[s],
                eps_row[group * owned + t, :, at : at + cols],
                ft.at[s],
                buf,
                acc.at[s],
                dens.at[s],
                turned,
            )

        return carry

    lax.fori_loop(0, owned, one, 0)


def make_plan(
    fit_start, occ_energy, pair_partner, domains, energy, ints, occ, eps_col, eps_row,
    *, devices, targets, relays,
):
    owned, width = eps_col.shape[:2]
    orbitals = fit_start.shape[0]
    pairs_here = pair_partner.shape[0] // devices
    plan = Plan(ints, owned)
    position = lax.axis_index("row")
    side = jnp.where(position % 2 == 1, 1, -1)
    places = [
        base * owned + t
        for base in (position, position - side, position + side)
        for t in range(owned)
    ]
    inside = [jnp.clip(place, 0, orbitals - 1) for place in places]
    starts = [fit_start[place] for place in inside]
    pairs = []
    for step in (-1, 0, 1):
        group = position + step
        known = (group >= 0) & (group < devices)
        held = jnp.clip(group, 0, devices - 1)
        for n in range(pairs_here):
            pairs.append((known, group * owned + n % owned, pair_partner[held * pairs_here + n]))
    for group in range(3):
        for s in range(owned):
            for t in range(owned):
                slot = plan.slot(group, s, t)
                other = group * owned + t
                total = jnp.int32(0)
                for known, first, second in pairs:
                    forth = known & (first == places[s]) & (second == places[other])
                    back = known & (second == places[s]) & (first == places[other])
                    total = total + forth.astype(jnp.int32) + back.astype(jnp.int32)
                ints[slot] = total
                ints[plan.at_shift(slot)] = (
                    starts[s] - starts[s] % SUB - starts[other] + starts[other] % SUB
                )
                occ[slot] = occ_energy[inside[s]] + occ_energy[inside[other]]
    for place in range(3 * owned):
        ints[plan.at_lead(place)] = starts[place] % SUB
    for number, group in enumerate(targets):
        way = jnp.int32(0)
        for to in group:
            way = jnp.where(position == to, 1, way)
        ints[plan.at_way(number)] = way
    late = jnp.int32(0)
    for row in relays:
        late = jnp.where(position == row, 1, late)
    ints[plan.at_late(len(targets))] = late
    entries = energy.shape[0]
    table = lax.broadcasted_iota(jnp.int32, (entries, width), 0)
    for place in range(3 * owned):
        domain = domains[pl.ds(inside[place], 1), :]
        row = jnp.sum(jnp.where(table == domain, energy[...], 0.0), axis=0, keepdims=True)
        eps_row[place] = row
        if place < owned:
            eps_col[place] = jnp.broadcast_to(row, (LANES, width)).T[:, :1]
    return plan


def add_blocks(plan, occ, sources, eps_col, eps_row, ft, buf, acc, dens, turned, raw, wide, sem):
    copies = [
        pltpu.make_async_copy(block, raw.at[n % 2], sem.at[n % 2])
        for n, (_, _, block) in enumerate(sources)
    ]
    copies[0].start()
    clear_margins(buf, raw.shape[1] + SUB)
    for n, (group, t, _) in enumerate(sources):
        if n + 1 < len(copies):
            copies[n + 1].start()
        copies[n].wait()
        align(raw.at[n % 2], plan.lead(group * plan.owned + t), wide, buf)
        add_block(plan, occ, group, t, 0, eps_col, eps_row, ft, buf, acc, dens, turned)


def first_kernel(
    fit_start, occ_energy, pair_partner, domains, energy, own, after,
    ints, occ, eps_col, eps_row, acc, dens, ft, token, bufs, wide, turned,
    *, devices, targets, relays,
):
    del after
    token[...] = jnp.zeros_like(token)
    plan = make_plan(
        fit_start, occ_energy, pair_partner, domains, energy, ints, occ, eps_col, eps_row,
        devices=devices, targets=targets, relays=relays,
    )
    owned, aux, width = own.shape
    rows = aux + SUB
    depth = ft.shape[2]
    acc[...] = jnp.zeros_like(acc)
    dens[...] = jnp.zeros_like(dens)
    for t in range(owned):
        buf = bufs.at[t]
        clear_margins(buf, rows)
        align(own.at[t], plan.lead(t), wide, buf)

        def turn(i, carry):
            at = pl.multiple_of(i * LANES, LANES)
            ft[t, :, pl.ds(at, LANES)] = buf[pl.ds(REACH + at, LANES), :].T
            return carry

        lax.fori_loop(0, depth // LANES, turn, 0)

    @pl.when(ints[plan.at_late(len(targets))] == 1)
    def _():
        for t in range(owned):
            add_block(plan, occ, 0, t, 0, eps_col, eps_row, ft, bufs.at[t], acc, dens, turned)


def near_kernel(
    ints, occ, eps_col, eps_row, ft, acc_in, dens_in, own, mate, *refs, ways, late
):
    del acc_in, dens_in
    acc, dens, token, buf, wide, turned, raw, sem = refs[-8:]
    token[...] = jnp.zeros_like(token)
    owned = own.shape[0]
    plan = Plan(ints, owned)
    groups = ((1, mate),) if late else ((0, own), (1, mate))
    sources = [(group, t, blocks.at[t]) for group, blocks in groups for t in range(owned)]

    @pl.when(ints[plan.at_late(ways)] == late)
    def _():
        add_blocks(
            plan, occ, sources, eps_col, eps_row, ft, buf, acc, dens, turned, raw, wide, sem
        )


def needed(plan, t):
    total = jnp.int32(0)
    for s in range(plan.owned):
        total = total + plan.count(plan.slot(2, s, t))
    return total != 0


def far_kernel(
    ints, occ, eps_col, eps_row, ft, acc_in, dens_in, block, after,
    acc, dens, token, buf, wide, turned, *, number, place,
):
    del acc_in, dens_in, after
    token[...] = jnp.zeros_like(token)
    plan = Plan(ints, acc.shape[0])
    t, at = place

    @pl.when(needed(plan, t) & (plan.way(number) == 0))
    def _():
        clear_margins(buf, block.shape[0] + SUB)
        align(block, plan.lead(2 * plan.owned + t), wide, buf)
        add_block(plan, occ, 2, t, at, eps_col, eps_row, ft, buf, acc, dens, turned)


def relayed_kernel(
    ints, occ, eps_col, eps_row, ft, acc_in, dens_in, *refs, places
):
    del acc_in, dens_in
    *blocks, _, acc, dens, token, buf, wide, turned, raw, sem = refs
    token[...] = jnp.zeros_like(token)
    plan = Plan(ints, acc.shape[0])
    for number, (block, (t, at)) in enumerate(zip(blocks, places)):

        @pl.when(needed(plan, t) & (plan.way(number) == 1))
        def _():
            copy = pltpu.make_async_copy(block, raw, sem)
            copy.start()
            clear_margins(buf, raw.shape[0] + SUB)
            copy.wait()
            align(raw, plan.lead(2 * plan.owned + t), wide, buf)
            add_block(plan, occ, 2, t, at, eps_col, eps_row, ft, buf, acc, dens, turned)


def last_kernel(
    ints, occ, eps_col, eps_row, ft, acc_in, dens_in, block, after,
    acc, dens, token, out, dens_out, buf, wide, turned, ready, sem, *, place,
):
    del acc_in, dens_in, after
    token[...] = jnp.zeros_like(token)
    t, at = place
    owned, aux, width = out.shape
    plan = Plan(ints, owned)
    rows = aux + SUB
    depth = ft.shape[2]
    scale = float(width) ** -0.5
    step = aux // OUT_TILES
    tiles = OUT_TILES

    @pl.when(needed(plan, t))
    def _():
        clear_margins(buf, rows)
        align(block, plan.lead(2 * owned + t), wide, buf)

    copies = []
    for s in range(owned):
        slot = plan.slot(2, s, t)

        @pl.when(plan.count(slot) != 0)
        def _():
            coulomb = dot(ft[s], buf[pl.ds(plan.offset(slot), depth), :])
            eps_b = eps_row[2 * owned + t, :, at : at + COLS]
            weight = plan.count(slot).astype(jnp.float32)
            amplitude, turned[s] = amplitudes(coulomb, occ[slot] - eps_col[s] - eps_b, weight)
            dens[s] += scale * dot(amplitude, turned[s])

        copies.append(pltpu.make_async_copy(dens.at[s], dens_out.at[s], sem.at[s, tiles]))
        copies[-1].start()

    for s in range(owned):
        slot = plan.slot(2, s, t)

        def add(base, taken):
            @pl.when(plan.count(slot) != 0)
            def _():
                start = pl.multiple_of(plan.offset(slot) + base, SUB)
                taken_rows = buf[pl.ds(start, taken), :]
                acc[s, pl.ds(base, taken), :] += dot(taken_rows, turned[s])

        add(0, step + SUB)
        for i in range(tiles):
            if i + 1 < tiles:
                add((i + 1) * step + SUB, step)
            base = i * step
            settled = rows_from(
                lambda at, n: acc[s, pl.ds(at, n), :], plan.lead(s) + base, step
            )
            ready[s, base : base + step, :] = settled.astype(ready.dtype)
            part = pl.ds(base, step)
            copies.append(
                pltpu.make_async_copy(ready.at[s, part], out.at[s, part], sem.at[s, i])
            )
            copies[-1].start()
    for copy in copies:
        copy.wait()


def copy_kernel(source, *refs, places):
    *outs, buf, sem = refs[-len(places) - 2 :]
    rows, cols = outs[0].shape
    tile = rows // CHUNK_TILES
    parts = [(n, i) for n in range(len(places)) for i in range(CHUNK_TILES)]

    def copies(n, i):
        t, at = places[n]
        part = pl.ds(i * tile, tile)
        held = buf.at[n, part]
        load = pltpu.make_async_copy(source.at[t, part, pl.ds(at, cols)], held, sem.at[0, n, i])
        return load, pltpu.make_async_copy(held, outs[n].at[part], sem.at[1, n, i])

    for n, i in parts:
        copies(n, i)[0].start()
    for n, i in parts:
        load, store = copies(n, i)
        load.wait()
        store.start()
    for n, i in parts:
        copies(n, i)[1].wait()


def pass_kernel(source, after, out):
    del source, after, out


def relay_plan(devices, chunks):
    if devices != 16 or chunks != 3:
        return [[] for _ in range(chunks)]
    last = devices - 1
    plan = []
    for z in (1, 0, 2):
        high, low = 4 * z + 3, 4 * z + 4
        plan.append([(high, low, 0), (low, high, last)])
    return plan


def spec(space):
    return pl.BlockSpec(memory_space=space)


def on_device(fitted, fit_start, virt_domain, occ_energy, virt_energy, pair_partner):
    owned, aux, width = fitted.shape
    devices = lax.axis_size("row")
    rows = aux + SUB
    depth = up_to(rows, LANES)
    buf_rows = 2 * REACH + depth
    wide_rows = aux + 2 * SUB + STEP
    smem, vmem, anywhere = spec(pltpu.SMEM), spec(pltpu.VMEM), spec(pl.ANY)

    outward = []
    for i in range(devices):
        to = i + 1 if i % 2 else i - 1
        if 0 <= to < devices:
            outward.append((i, to))
    inward = [(i, i ^ 1) for i in range(devices) if i ^ 1 < devices]

    def in_hbm(array):
        return pltpu.with_memory_space_constraint(array, pltpu.HBM)

    def in_vmem(array):
        return pltpu.with_memory_space_constraint(array, pltpu.VMEM)

    def chunks(places, *after):
        return pl.pallas_call(
            functools.partial(copy_kernel, places=places),
            out_shape=[jax.ShapeDtypeStruct((aux, COLS), fitted.dtype)] * len(places),
            in_specs=[anywhere] * (1 + len(after)),
            out_specs=[anywhere] * len(places),
            scratch_shapes=[
                pltpu.VMEM((len(places), aux, COLS), fitted.dtype),
                pltpu.SemaphoreType.DMA((2, len(places), CHUNK_TILES)),
            ],
            compiler_params=pltpu.CompilerParams(vmem_limit_bytes=CHUNK_VMEM),
            name="chunks",
        )(in_hbm(fitted), *after)

    def pass_on(block, after):
        return pl.pallas_call(
            pass_kernel,
            out_shape=jax.ShapeDtypeStruct(block.shape, block.dtype),
            in_specs=[anywhere] * 2,
            out_specs=anywhere,
            input_output_aliases={0: 0},
            compiler_params=pltpu.CompilerParams(vmem_limit_bytes=CHUNK_VMEM),
            name="pass_on",
        )(block, after)

    cells = [(t, at) for t in range(owned) for at in range(0, width, COLS)]
    last = len(cells) - 1
    plan = relay_plan(devices, last)
    relayed = any(plan)

    def exchange(number, block):
        group = plan[number] if number < last else []
        gone = {(source, to) for source, to, _ in group}
        pairs = [pair for pair in outward if pair not in gone]
        first_hop = [(source, by) for source, _, by in group] if number else []
        return lax.ppermute(block, "row", pairs + first_hop)

    mate = lax.ppermute(fitted, "row", inward)
    sent = list(chunks(cells[:1]))
    far = [exchange(0, sent[0])]
    rest = chunks(cells[1:] + cells[:1] * relayed, sent[0])
    sent += rest[:last]
    early = []
    if relayed:
        early.append(lax.ppermute(rest[last], "row", [(source, by) for source, _, by in plan[0]]))
    far += [exchange(number, sent[number]) for number in range(1, last + 1)]

    unit = 4 * rows * width * COLS
    acc_shape = pltpu.VMEM((owned, rows, width), jnp.float32)
    dens_shape = pltpu.VMEM((owned, width, width), jnp.float32)
    ft_shape = pltpu.VMEM((owned, width, depth), fitted.dtype)
    token_shape = jax.ShapeDtypeStruct((8, LANES), jnp.int32)
    slots = 3 * owned * owned

    def cost(blocks):
        return pl.CostEstimate(
            flops=100 * unit * blocks * owned, bytes_accessed=8 << 20, transcendentals=0
        )

    ints, occ, eps_col, eps_row, acc, dens, ft, token = pl.pallas_call(
        functools.partial(
            first_kernel,
            devices=devices,
            targets=[[to for _, to, _ in group] for group in plan],
            relays=sorted({by for group in plan for _, _, by in group}),
        ),
        out_shape=(
            jax.ShapeDtypeStruct((Plan(None, owned).at_late(last) + 1,), jnp.int32),
            jax.ShapeDtypeStruct((slots,), jnp.float32),
            jax.ShapeDtypeStruct((owned, width, 1), jnp.float32),
            jax.ShapeDtypeStruct((3 * owned, 1, width), jnp.float32),
            acc_shape,
            dens_shape,
            ft_shape,
            token_shape,
        ),
        in_specs=[smem] * 3 + [vmem] * 3 + [anywhere],
        out_specs=(smem,) * 2 + (vmem,) * 6,
        scratch_shapes=[
            pltpu.VMEM((owned, buf_rows, width), fitted.dtype),
            pltpu.VMEM((wide_rows, width), jnp.float32),
            pltpu.VMEM((width, width), fitted.dtype),
        ],
        compiler_params=pltpu.CompilerParams(vmem_limit_bytes=NEAR_VMEM),
        cost_estimate=cost(len(cells)),
        name="first",
    )(
        fit_start, occ_energy, pair_partner, virt_domain, virt_energy.reshape(-1, 1),
        in_hbm(fitted), sent[last - 1],
    )
    state = {"acc": acc, "dens": dens, "token": token}
    hops = []

    def add_pairs(kernel, block_specs, blocks, cols, limit, name, extra=(), outs=(), scratch=()):
        specs = [smem] * 2 + [vmem] * 5 + block_specs
        results = pl.pallas_call(
            kernel,
            out_shape=(acc_shape, dens_shape, token_shape, *outs),
            in_specs=specs + [anywhere] * (1 + len(extra)),
            out_specs=(vmem,) * 3 + (anywhere,) * len(outs),
            input_output_aliases={5: 0, 6: 1},
            scratch_shapes=[
                pltpu.VMEM((buf_rows, cols), fitted.dtype),
                pltpu.VMEM((wide_rows, cols), jnp.float32),
                *scratch,
            ],
            compiler_params=pltpu.CompilerParams(vmem_limit_bytes=limit),
            cost_estimate=cost(cols // COLS),
            name=name,
        )(
            ints, occ, eps_col, eps_row, in_vmem(ft), in_vmem(state["acc"]),
            in_vmem(state["dens"]), *blocks, *extra, state["token"],
        )
        state.update(acc=results[0], dens=results[1], token=results[2])
        return results[3:]

    def second_hop(number, block):
        hops.append(lax.ppermute(block, "row", [(by, to) for _, to, by in plan[number]]))

    def relay(number):
        if relayed:
            far[number] = state["token"] = pass_on(far[number], state["token"])
            second_hop(number, far[number])

    turned_cols = (pltpu.VMEM((COLS, width), fitted.dtype),)
    if relayed:
        second_hop(0, early[0])
    def near_pairs(late, *extra):
        add_pairs(
            functools.partial(near_kernel, ways=last, late=late),
            [anywhere] * 2, [in_hbm(fitted), mate], width, NEAR_VMEM, f"near_pairs_{late}",
            extra=extra,
            scratch=(
                pltpu.VMEM((width, width), fitted.dtype),
                pltpu.VMEM((2, aux, width), fitted.dtype),
                pltpu.SemaphoreType.DMA((2,)),
            ),
        )

    near_pairs(0, *early)
    for number in range(last):
        if number:
            relay(number)
        if relayed and number == last - 1:
            near_pairs(1)
        add_pairs(
            functools.partial(far_kernel, number=number, place=cells[number]),
            [vmem], [far[number]], COLS, FAR_VMEM, f"far_pairs_{number}", scratch=turned_cols,
        )
    if relayed:
        add_pairs(
            functools.partial(relayed_kernel, places=cells[:last]),
            [anywhere] * last, hops, COLS, FAR_VMEM, "relayed_pairs",
            scratch=turned_cols
            + (pltpu.VMEM((aux, COLS), fitted.dtype), pltpu.SemaphoreType.DMA),
        )
    gradient, density = add_pairs(
        functools.partial(last_kernel, place=cells[last]),
        [vmem], [far[last]], COLS, FAR_VMEM, "last_pairs",
        outs=(
            jax.ShapeDtypeStruct(fitted.shape, fitted.dtype),
            jax.ShapeDtypeStruct((owned, width, width), jnp.float32),
        ),
        scratch=(
            pltpu.VMEM((owned, COLS, width), fitted.dtype),
            pltpu.VMEM((owned, aux, width), fitted.dtype),
            pltpu.SemaphoreType.DMA((owned, OUT_TILES + 1)),
        ),
    )
    return gradient, density


def solution(mesh):
    placed = (
        P(("parts", "row"), None, None),
        P("parts"),
        P("parts", None),
        P("parts"),
        P("parts"),
        P("parts"),
    )
    return jax.shard_map(
        on_device,
        mesh=mesh,
        in_specs=placed,
        out_specs=(P(("parts", "row"), None, None), P(("parts", "row"), None, None)),
        check_vma=False,
    )
```

```python
import functools

import jax
import jax.numpy as jnp
from jax import lax
from jax.experimental import pallas as pl
from jax.experimental.pallas import tpu as pltpu
from jax.sharding import PartitionSpec as P

SUB = 16
STEP = 8
LANES = 128
OUT_TILES = 4
CHUNK_TILES = 2
COLS = 256
REACH = 1024
NEAR_VMEM = 22 * 1024 * 1024
FAR_VMEM = 16 * 1024 * 1024
CHUNK_VMEM = 6 * 1024 * 1024


class Plan:
    def __init__(self, ref, owned):
        self.ref, self.owned = ref, owned
        self.slots = 3 * owned * owned

    def slot(self, group, s, t):
        return (group * self.owned + s) * self.owned + t

    def at_shift(self, slot):
        return self.slots + slot

    def at_lead(self, place):
        return 2 * self.slots + place

    def at_way(self, number):
        return 2 * self.slots + 3 * self.owned + number

    def at_late(self, ways):
        return self.at_way(ways)

    def count(self, slot):
        return self.ref[slot]

    def offset(self, slot):
        return pl.multiple_of(REACH + self.ref[self.at_shift(slot)], SUB)

    def lead(self, place):
        return self.ref[self.at_lead(place)]

    def way(self, number):
        return self.ref[self.at_way(number)]


def dot(a, b):
    return jnp.dot(a, b, preferred_element_type=jnp.float32)


def up_to(value, unit):
    return -(-value // unit) * unit


def tile_of(rows):
    return max(n for n in range(SUB, 705, SUB) if rows % n == 0)


def rows_from(load, start, count):
    skip = start % STEP
    base = pl.multiple_of(start - skip, STEP)
    block = load(base, count + STEP)
    width = block.shape[1]
    block = block.reshape(count // STEP + 1, STEP, width)
    turned = pltpu.roll(block, (STEP - skip) % STEP, 1)
    row = lax.broadcasted_iota(jnp.int32, (count // STEP, STEP, width), 1)
    return jnp.where(row < STEP - skip, turned[:-1], turned[1:]).reshape(count, width)


def clear_margins(buf, rows):
    width = buf.shape[1]
    buf[:REACH, :] = jnp.zeros((REACH, width), buf.dtype)
    buf[REACH + rows :, :] = jnp.zeros((buf.shape[0] - REACH - rows, width), buf.dtype)


def align(source, lead, wide, buf):
    aux, width = source.shape
    rows = aux + SUB
    wide[:SUB, :] = jnp.zeros((SUB, width), jnp.float32)
    wide[SUB + aux :, :] = jnp.zeros((wide.shape[0] - SUB - aux, width), jnp.float32)
    tile = tile_of(aux)

    def widen(i, carry):
        base = pl.multiple_of(i * tile, SUB)
        wide[pl.ds(pl.multiple_of(SUB + base, SUB), tile), :] = source[
            pl.ds(base, tile), :
        ].astype(jnp.float32)
        return carry

    lax.fori_loop(0, aux // tile, widen, 0)
    step = tile_of(rows)

    def move(i, carry):
        base = pl.multiple_of(i * step, SUB)
        moved = rows_from(lambda at, n: wide[pl.ds(at, n), :], SUB - lead + base, step)
        buf[pl.ds(pl.multiple_of(REACH + base, SUB), step), :] = moved.astype(buf.dtype)
        return carry

    lax.fori_loop(0, rows // step, move, 0)


def amplitudes(coulomb, denominator, weight):
    amplitude = (coulomb / denominator).astype(jnp.bfloat16)
    weighted = (amplitude.astype(jnp.float32) * weight).astype(jnp.bfloat16)
    return amplitude, weighted.T


def add_pair(weight, offset, occ, eps_a, eps_b, ft, buf, acc, dens, turned):
    rows, width = acc.shape
    depth = ft.shape[1]
    scale = float(width) ** -0.5
    coulomb = dot(ft[...], buf[pl.ds(offset, depth), :])
    amplitude, turned[...] = amplitudes(coulomb, occ - eps_a - eps_b, weight)
    dens[...] += scale * dot(amplitude, turned[...])
    step = tile_of(rows)

    def add(i, carry):
        base = pl.multiple_of(i * step, SUB)
        block = buf[pl.ds(pl.multiple_of(offset + base, SUB), step), :]
        acc[pl.ds(base, step), :] += dot(block, turned[...])
        return carry

    lax.fori_loop(0, rows // step, add, 0)


def add_block(plan, occ, group, t, at, eps_col, eps_row, ft, buf, acc, dens, turned):
    owned = acc.shape[0]
    cols = buf.shape[1]

    def one(s, carry):
        slot = plan.slot(group, s, t)

        @pl.when(plan.count(slot) != 0)
        def _():
            add_pair(
                plan.count(slot).astype(jnp.float32),
                plan.offset(slot),
                occ[slot],
                eps_col[s],
                eps_row[group * owned + t, :, at : at + cols],
                ft.at[s],
                buf,
                acc.at[s],
                dens.at[s],
                turned,
            )

        return carry

    lax.fori_loop(0, owned, one, 0)


def make_plan(
    fit_start, occ_energy, pair_partner, domains, energy, ints, occ, eps_col, eps_row,
    *, devices, targets, relays,
):
    owned, width = eps_col.shape[:2]
    orbitals = fit_start.shape[0]
    pairs_here = pair_partner.shape[0] // devices
    plan = Plan(ints, owned)
    position = lax.axis_index("row")
    side = jnp.where(position % 2 == 1, 1, -1)
    places = [
        base * owned + t
        for base in (position, position - side, position + side)
        for t in range(owned)
    ]
    inside = [jnp.clip(place, 0, orbitals - 1) for place in places]
    starts = [fit_start[place] for place in inside]
    pairs = []
    for step in (-1, 0, 1):
        group = position + step
        known = (group >= 0) & (group < devices)
        held = jnp.clip(group, 0, devices - 1)
        for n in range(pairs_here):
            pairs.append((known, group * owned + n % owned, pair_partner[held * pairs_here + n]))
    for group in range(3):
        for s in range(owned):
            for t in range(owned):
                slot = plan.slot(group, s, t)
                other = group * owned + t
                total = jnp.int32(0)
                for known, first, second in pairs:
                    forth = known & (first == places[s]) & (second == places[other])
                    back = known & (second == places[s]) & (first == places[other])
                    total = total + forth.astype(jnp.int32) + back.astype(jnp.int32)
                ints[slot] = total
                ints[plan.at_shift(slot)] = (
                    starts[s] - starts[s] % SUB - starts[other] + starts[other] % SUB
                )
                occ[slot] = occ_energy[inside[s]] + occ_energy[inside[other]]
    for place in range(3 * owned):
        ints[plan.at_lead(place)] = starts[place] % SUB
    for number, group in enumerate(targets):
        way = jnp.int32(0)
        for to in group:
            way = jnp.where(position == to, 1, way)
        ints[plan.at_way(number)] = way
    late = jnp.int32(0)
    for row in relays:
        late = jnp.where(position == row, 1, late)
    ints[plan.at_late(len(targets))] = late
    entries = energy.shape[0]
    table = lax.broadcasted_iota(jnp.int32, (entries, width), 0)
    for place in range(3 * owned):
        domain = domains[pl.ds(inside[place], 1), :]
        row = jnp.sum(jnp.where(table == domain, energy[...], 0.0), axis=0, keepdims=True)
        eps_row[place] = row
        if place < owned:
            eps_col[place] = jnp.broadcast_to(row, (LANES, width)).T[:, :1]
    return plan


def add_blocks(plan, occ, sources, eps_col, eps_row, ft, buf, acc, dens, turned, raw, wide, sem):
    copies = [
        pltpu.make_async_copy(block, raw.at[n % 2], sem.at[n % 2])
        for n, (_, _, block) in enumerate(sources)
    ]
    copies[0].start()
    clear_margins(buf, raw.shape[1] + SUB)
    for n, (group, t, _) in enumerate(sources):
        if n + 1 < len(copies):
            copies[n + 1].start()
        copies[n].wait()
        align(raw.at[n % 2], plan.lead(group * plan.owned + t), wide, buf)
        add_block(plan, occ, group, t, 0, eps_col, eps_row, ft, buf, acc, dens, turned)


def first_kernel(
    fit_start, occ_energy, pair_partner, domains, energy, own, after,
    ints, occ, eps_col, eps_row, acc, dens, ft, token, bufs, wide, turned,
    *, devices, targets, relays,
):
    del after
    token[...] = jnp.zeros_like(token)
    plan = make_plan(
        fit_start, occ_energy, pair_partner, domains, energy, ints, occ, eps_col, eps_row,
        devices=devices, targets=targets, relays=relays,
    )
    owned, aux, width = own.shape
    rows = aux + SUB
    depth = ft.shape[2]
    acc[...] = jnp.zeros_like(acc)
    dens[...] = jnp.zeros_like(dens)
    for t in range(owned):
        buf = bufs.at[t]
        clear_margins(buf, rows)
        align(own.at[t], plan.lead(t), wide, buf)

        def turn(i, carry):
            at = pl.multiple_of(i * LANES, LANES)
            ft[t, :, pl.ds(at, LANES)] = buf[pl.ds(REACH + at, LANES), :].T
            return carry

        lax.fori_loop(0, depth // LANES, turn, 0)

    @pl.when(ints[plan.at_late(len(targets))] == 1)
    def _():
        for t in range(owned):
            add_block(plan, occ, 0, t, 0, eps_col, eps_row, ft, bufs.at[t], acc, dens, turned)


def near_kernel(
    ints, occ, eps_col, eps_row, ft, acc_in, dens_in, own, mate, *refs, ways, late
):
    del acc_in, dens_in
    acc, dens, token, buf, wide, turned, raw, sem = refs[-8:]
    token[...] = jnp.zeros_like(token)
    owned = own.shape[0]
    plan = Plan(ints, owned)
    groups = ((1, mate),) if late else ((0, own), (1, mate))
    sources = [(group, t, blocks.at[t]) for group, blocks in groups for t in range(owned)]

    @pl.when(ints[plan.at_late(ways)] == late)
    def _():
        add_blocks(
            plan, occ, sources, eps_col, eps_row, ft, buf, acc, dens, turned, raw, wide, sem
        )


def needed(plan, t):
    total = jnp.int32(0)
    for s in range(plan.owned):
        total = total + plan.count(plan.slot(2, s, t))
    return total != 0


def far_kernel(
    ints, occ, eps_col, eps_row, ft, acc_in, dens_in, block, after,
    acc, dens, token, buf, wide, turned, *, ways, place,
):
    del acc_in, dens_in, after
    token[...] = jnp.zeros_like(token)
    plan = Plan(ints, acc.shape[0])
    t, at = place

    here = needed(plan, t)
    for way in ways:
        here = here & (plan.way(way) == 0)

    @pl.when(here)
    def _():
        clear_margins(buf, block.shape[0] + SUB)
        align(block, plan.lead(2 * plan.owned + t), wide, buf)
        add_block(plan, occ, 2, t, at, eps_col, eps_row, ft, buf, acc, dens, turned)


def relayed_kernel(
    ints, occ, eps_col, eps_row, ft, acc_in, dens_in, *refs, places, last
):
    del acc_in, dens_in
    *blocks, _, acc, dens, token, out, dens_out, buf, wide, turned, raw, ready, sem, out_sem = refs
    token[...] = jnp.zeros_like(token)
    owned = acc.shape[0]
    plan = Plan(ints, owned)
    for number, (block, (t, at)) in enumerate(zip(blocks, places)):

        @pl.when(needed(plan, t) & (plan.way(number) == 1))
        def _():
            copy = pltpu.make_async_copy(block, raw, sem)
            copy.start()
            clear_margins(buf, raw.shape[0] + SUB)
            copy.wait()
            align(raw, plan.lead(2 * owned + t), wide, buf)
            add_block(plan, occ, 2, t, at, eps_col, eps_row, ft, buf, acc, dens, turned)

    slots = [plan.slot(2, s, last) for s in range(owned)]
    for s in range(owned):

        @pl.when(plan.count(slots[s]) == 0)
        def _():
            send_out(plan, s, acc, dens, ready, out, dens_out, out_sem)

    for s in range(owned):

        @pl.when(plan.count(slots[s]) == 0)
        def _():
            for copy in sent_out(s, dens, ready, out, dens_out, out_sem):
                copy.wait()


def sent_out(s, dens, ready, out, dens_out, sem):
    step = out.shape[1] // OUT_TILES
    copies = [pltpu.make_async_copy(dens.at[s], dens_out.at[s], sem.at[s, OUT_TILES])]
    for i in range(OUT_TILES):
        part = pl.ds(i * step, step)
        copies.append(pltpu.make_async_copy(ready.at[s, part], out.at[s, part], sem.at[s, i]))
    return copies


def send_out(plan, s, acc, dens, ready, out, dens_out, sem, before=None):
    step = out.shape[1] // OUT_TILES
    copies = sent_out(s, dens, ready, out, dens_out, sem)
    copies[0].start()
    for i in range(OUT_TILES):
        if before is not None:
            before(i)
        base = i * step
        settled = rows_from(lambda at, n: acc[s, pl.ds(at, n), :], plan.lead(s) + base, step)
        ready[s, base : base + step, :] = settled.astype(ready.dtype)
        copies[1 + i].start()


def last_kernel(
    ints, occ, eps_col, eps_row, ft, acc_in, dens_in, block, out_in, dens_out_in, after,
    acc, dens, token, out, dens_out, buf, wide, turned, ready, sem, *, place,
):
    del acc_in, dens_in, out_in, dens_out_in, after
    token[...] = jnp.zeros_like(token)
    t, at = place
    owned, aux, width = out.shape
    plan = Plan(ints, owned)
    rows = aux + SUB
    depth = ft.shape[2]
    scale = float(width) ** -0.5
    step = aux // OUT_TILES

    @pl.when(needed(plan, t))
    def _():
        clear_margins(buf, rows)
        align(block, plan.lead(2 * owned + t), wide, buf)

    for s in range(owned):
        slot = plan.slot(2, s, t)

        @pl.when(plan.count(slot) != 0)
        def _():
            coulomb = dot(ft[s], buf[pl.ds(plan.offset(slot), depth), :])
            eps_b = eps_row[2 * owned + t, :, at : at + COLS]
            weight = plan.count(slot).astype(jnp.float32)
            amplitude, turned[s] = amplitudes(coulomb, occ[slot] - eps_col[s] - eps_b, weight)
            dens[s] += scale * dot(amplitude, turned[s])

    for s in range(owned):
        slot = plan.slot(2, s, t)

        def add(base, taken):
            start = pl.multiple_of(plan.offset(slot) + base, SUB)
            taken_rows = buf[pl.ds(start, taken), :]
            acc[s, pl.ds(base, taken), :] += dot(taken_rows, turned[s])

        def before(i):
            if i == 0:
                add(0, step + SUB)
            if i + 1 < OUT_TILES:
                add((i + 1) * step + SUB, step)

        @pl.when(plan.count(slot) != 0)
        def _():
            send_out(plan, s, acc, dens, ready, out, dens_out, sem, before)

    for s in range(owned):

        @pl.when(plan.count(plan.slot(2, s, t)) != 0)
        def _():
            for copy in sent_out(s, dens, ready, out, dens_out, sem):
                copy.wait()


def copy_kernel(source, *refs, places):
    *outs, buf, sem = refs[-len(places) - 2 :]
    rows, cols = outs[0].shape
    tile = rows // CHUNK_TILES
    parts = [(n, i) for n in range(len(places)) for i in range(CHUNK_TILES)]

    def copies(n, i):
        t, at = places[n]
        part = pl.ds(i * tile, tile)
        held = buf.at[n, part]
        load = pltpu.make_async_copy(source.at[t, part, pl.ds(at, cols)], held, sem.at[0, n, i])
        return load, pltpu.make_async_copy(held, outs[n].at[part], sem.at[1, n, i])

    for n, i in parts:
        copies(n, i)[0].start()
    for n, i in parts:
        load, store = copies(n, i)
        load.wait()
        store.start()
    for n, i in parts:
        copies(n, i)[1].wait()


def pass_kernel(source, after, out):
    del source, after, out


def relay_plan(devices, chunks):
    if devices != 16 or chunks != 4:
        return []
    plan = []
    for z, chunk, alone in ((1, 0, True), (0, 0, False), (2, 1, False)):
        high, low = 4 * z + 3, 4 * z + 4
        plan.append((chunk, alone, [(high, low, 0), (low, high, devices - 1)]))
    return plan


def spec(space):
    return pl.BlockSpec(memory_space=space)


def on_device(fitted, fit_start, virt_domain, occ_energy, virt_energy, pair_partner):
    owned, aux, width = fitted.shape
    devices = lax.axis_size("row")
    rows = aux + SUB
    depth = up_to(rows, LANES)
    buf_rows = 2 * REACH + depth
    wide_rows = aux + 2 * SUB + STEP
    smem, vmem, anywhere = spec(pltpu.SMEM), spec(pltpu.VMEM), spec(pl.ANY)

    outward = []
    for i in range(devices):
        to = i + 1 if i % 2 else i - 1
        if 0 <= to < devices:
            outward.append((i, to))
    inward = [(i, i ^ 1) for i in range(devices) if i ^ 1 < devices]

    def in_hbm(array):
        return pltpu.with_memory_space_constraint(array, pltpu.HBM)

    def in_vmem(array):
        return pltpu.with_memory_space_constraint(array, pltpu.VMEM)

    def chunks(places, *after):
        return pl.pallas_call(
            functools.partial(copy_kernel, places=places),
            out_shape=[jax.ShapeDtypeStruct((aux, COLS), fitted.dtype)] * len(places),
            in_specs=[anywhere] * (1 + len(after)),
            out_specs=[anywhere] * len(places),
            scratch_shapes=[
                pltpu.VMEM((len(places), aux, COLS), fitted.dtype),
                pltpu.SemaphoreType.DMA((2, len(places), CHUNK_TILES)),
            ],
            compiler_params=pltpu.CompilerParams(vmem_limit_bytes=CHUNK_VMEM),
            name="chunks",
        )(in_hbm(fitted), *after)

    def pass_on(block, after):
        return pl.pallas_call(
            pass_kernel,
            out_shape=jax.ShapeDtypeStruct(block.shape, block.dtype),
            in_specs=[anywhere] * 2,
            out_specs=anywhere,
            input_output_aliases={0: 0},
            compiler_params=pltpu.CompilerParams(vmem_limit_bytes=CHUNK_VMEM),
            name="pass_on",
        )(block, after)

    cells = [(t, at) for t in range(owned) for at in range(0, width, COLS)]
    last = len(cells) - 1
    plan = relay_plan(devices, len(cells))
    first_hops = [[(source, by) for source, _, by in pairs] for _, _, pairs in plan]
    second_hops = [[(by, to) for _, to, by in pairs] for _, _, pairs in plan]

    def exchange(number, block):
        pairs = list(outward)
        for (at, alone, group), hop in zip(plan, first_hops):
            if at == number:
                pairs = [pair for pair in pairs if pair not in {(a, b) for a, b, _ in group}]
                pairs += [] if alone else hop
        return lax.ppermute(block, "row", pairs)

    mate = lax.ppermute(fitted, "row", inward)
    sent = list(chunks(cells[:1]))
    far = [exchange(0, sent[0])]
    rest = chunks(cells[1:] + cells[:1] * bool(plan), sent[0])
    sent += rest[:last]
    early = {
        index: lax.ppermute(rest[last], "row", first_hops[index])
        for index, (_, alone, _) in enumerate(plan)
        if alone
    }
    far += [exchange(number, sent[number]) for number in range(1, last + 1)]

    unit = 4 * rows * width * COLS
    acc_shape = pltpu.VMEM((owned, rows, width), jnp.float32)
    dens_shape = pltpu.VMEM((owned, width, width), jnp.float32)
    ft_shape = pltpu.VMEM((owned, width, depth), fitted.dtype)
    token_shape = jax.ShapeDtypeStruct((8, LANES), jnp.int32)
    slots = 3 * owned * owned

    def cost(blocks):
        return pl.CostEstimate(
            flops=100 * unit * blocks * owned, bytes_accessed=8 << 20, transcendentals=0
        )

    ints, occ, eps_col, eps_row, acc, dens, ft, token = pl.pallas_call(
        functools.partial(
            first_kernel,
            devices=devices,
            targets=[[to for _, to, _ in pairs] for _, _, pairs in plan],
            relays=sorted({by for _, _, pairs in plan for _, _, by in pairs}),
        ),
        out_shape=(
            jax.ShapeDtypeStruct((Plan(None, owned).at_late(len(plan)) + 1,), jnp.int32),
            jax.ShapeDtypeStruct((slots,), jnp.float32),
            jax.ShapeDtypeStruct((owned, width, 1), jnp.float32),
            jax.ShapeDtypeStruct((3 * owned, 1, width), jnp.float32),
            acc_shape,
            dens_shape,
            ft_shape,
            token_shape,
        ),
        in_specs=[smem] * 3 + [vmem] * 3 + [anywhere],
        out_specs=(smem,) * 2 + (vmem,) * 6,
        scratch_shapes=[
            pltpu.VMEM((owned, buf_rows, width), fitted.dtype),
            pltpu.VMEM((wide_rows, width), jnp.float32),
            pltpu.VMEM((width, width), fitted.dtype),
        ],
        compiler_params=pltpu.CompilerParams(vmem_limit_bytes=NEAR_VMEM),
        cost_estimate=cost(len(cells)),
        name="first",
    )(
        fit_start, occ_energy, pair_partner, virt_domain, virt_energy.reshape(-1, 1),
        in_hbm(fitted), sent[last - 1],
    )
    state = {"acc": acc, "dens": dens, "token": token}
    hops = []

    def add_pairs(
        kernel, block_specs, blocks, cols, limit, name, extra=(), outs=(), aliases={}, scratch=()
    ):
        specs = [smem] * 2 + [vmem] * 5 + block_specs
        results = pl.pallas_call(
            kernel,
            out_shape=(acc_shape, dens_shape, token_shape, *outs),
            in_specs=specs + [anywhere] * (1 + len(extra)),
            out_specs=(vmem,) * 3 + (anywhere,) * len(outs),
            input_output_aliases={5: 0, 6: 1, **aliases},
            scratch_shapes=[
                pltpu.VMEM((buf_rows, cols), fitted.dtype),
                pltpu.VMEM((wide_rows, cols), jnp.float32),
                *scratch,
            ],
            compiler_params=pltpu.CompilerParams(vmem_limit_bytes=limit),
            cost_estimate=cost(cols // COLS),
            name=name,
        )(
            ints, occ, eps_col, eps_row, in_vmem(ft), in_vmem(state["acc"]),
            in_vmem(state["dens"]), *blocks, *extra, state["token"],
        )
        state.update(acc=results[0], dens=results[1], token=results[2])
        return results[3:]

    hops = {index: lax.ppermute(early[index], "row", second_hops[index]) for index in early}
    turned_cols = (pltpu.VMEM((COLS, width), fitted.dtype),)

    def near_pairs(late, *extra):
        add_pairs(
            functools.partial(near_kernel, ways=len(plan), late=late),
            [anywhere] * 2, [in_hbm(fitted), mate], width, NEAR_VMEM, f"near_pairs_{late}",
            extra=extra,
            scratch=(
                pltpu.VMEM((width, width), fitted.dtype),
                pltpu.VMEM((2, aux, width), fitted.dtype),
                pltpu.SemaphoreType.DMA((2,)),
            ),
        )

    near_pairs(0, *early.values())
    for number in range(last):
        for index, (at, alone, _) in enumerate(plan):
            if at == number and not alone:
                far[number] = state["token"] = pass_on(far[number], state["token"])
                hops[index] = lax.ppermute(far[number], "row", second_hops[index])
                if index == len(plan) - 1:
                    near_pairs(1)
        ways = [index for index, (at, _, _) in enumerate(plan) if at == number]
        add_pairs(
            functools.partial(far_kernel, ways=ways, place=cells[number]),
            [vmem], [far[number]], COLS, FAR_VMEM, f"far_pairs_{number}", scratch=turned_cols,
        )
    results = (
        jax.ShapeDtypeStruct(fitted.shape, fitted.dtype),
        jax.ShapeDtypeStruct((owned, width, width), jnp.float32),
    )
    out_scratch = (
        pltpu.VMEM((owned, aux, width), fitted.dtype),
        pltpu.SemaphoreType.DMA((owned, OUT_TILES + 1)),
    )
    ready = add_pairs(
        functools.partial(
            relayed_kernel, places=[cells[at] for at, _, _ in plan], last=cells[last][0]
        ),
        [anywhere] * len(hops), [hops[index] for index in range(len(plan))], COLS, FAR_VMEM,
        "relayed_pairs",
        outs=results,
        scratch=turned_cols
        + (pltpu.VMEM((aux, COLS), fitted.dtype), out_scratch[0], pltpu.SemaphoreType.DMA)
        + out_scratch[1:],
    )
    gradient, density = add_pairs(
        functools.partial(last_kernel, place=cells[last]),
        [vmem, anywhere, anywhere], [far[last], *ready], COLS, FAR_VMEM, "last_pairs",
        outs=results,
        aliases={8: 3, 9: 4},
        scratch=(pltpu.VMEM((owned, COLS, width), fitted.dtype),) + out_scratch,
    )
    return gradient, density


def solution(mesh):
    placed = (
        P(("parts", "row"), None, None),
        P("parts"),
        P("parts", None),
        P("parts"),
        P("parts"),
        P("parts"),
    )
    return jax.shard_map(
        on_device,
        mesh=mesh,
        in_specs=placed,
        out_specs=(P(("parts", "row"), None, None), P(("parts", "row"), None, None)),
        check_vma=False,
    )
```

```python
import functools

import jax
import jax.numpy as jnp
from jax import lax
from jax.experimental import pallas as pl
from jax.experimental.pallas import tpu as pltpu
from jax.sharding import PartitionSpec as P

SUB = 16
STEP = 8
LANES = 128
OUT_TILES = 4
CHUNK_TILES = 2
COLS = 256
REACH = 1024
NEAR_VMEM = 22 * 1024 * 1024
FAR_VMEM = 16 * 1024 * 1024
CHUNK_VMEM = 6 * 1024 * 1024


class Plan:
    def __init__(self, ref, owned):
        self.ref, self.owned = ref, owned
        self.slots = 3 * owned * owned

    def slot(self, group, s, t):
        return (group * self.owned + s) * self.owned + t

    def at_shift(self, slot):
        return self.slots + slot

    def at_lead(self, place):
        return 2 * self.slots + place

    def at_way(self, number):
        return 2 * self.slots + 3 * self.owned + number

    def at_late(self, ways):
        return self.at_way(ways)

    def count(self, slot):
        return self.ref[slot]

    def offset(self, slot):
        return pl.multiple_of(REACH + self.ref[self.at_shift(slot)], SUB)

    def lead(self, place):
        return self.ref[self.at_lead(place)]

    def way(self, number):
        return self.ref[self.at_way(number)]


def dot(a, b):
    return jnp.dot(a, b, preferred_element_type=jnp.float32)


def up_to(value, unit):
    return -(-value // unit) * unit


def tile_of(rows):
    return max(n for n in range(SUB, 705, SUB) if rows % n == 0)


def rows_from(load, start, count):
    skip = start % STEP
    base = pl.multiple_of(start - skip, STEP)
    block = load(base, count + STEP)
    width = block.shape[1]
    block = block.reshape(count // STEP + 1, STEP, width)
    turned = pltpu.roll(block, (STEP - skip) % STEP, 1)
    row = lax.broadcasted_iota(jnp.int32, (count // STEP, STEP, width), 1)
    return jnp.where(row < STEP - skip, turned[:-1], turned[1:]).reshape(count, width)


def clear_margins(buf, rows):
    width = buf.shape[1]
    buf[:REACH, :] = jnp.zeros((REACH, width), buf.dtype)
    buf[REACH + rows :, :] = jnp.zeros((buf.shape[0] - REACH - rows, width), buf.dtype)


def align(source, lead, wide, buf):
    aux, width = source.shape
    rows = aux + SUB
    wide[:SUB, :] = jnp.zeros((SUB, width), jnp.float32)
    wide[SUB + aux :, :] = jnp.zeros((wide.shape[0] - SUB - aux, width), jnp.float32)
    tile = tile_of(aux)

    def widen(i, carry):
        base = pl.multiple_of(i * tile, SUB)
        wide[pl.ds(pl.multiple_of(SUB + base, SUB), tile), :] = source[
            pl.ds(base, tile), :
        ].astype(jnp.float32)
        return carry

    lax.fori_loop(0, aux // tile, widen, 0)
    step = tile_of(rows)

    def move(i, carry):
        base = pl.multiple_of(i * step, SUB)
        moved = rows_from(lambda at, n: wide[pl.ds(at, n), :], SUB - lead + base, step)
        buf[pl.ds(pl.multiple_of(REACH + base, SUB), step), :] = moved.astype(buf.dtype)
        return carry

    lax.fori_loop(0, rows // step, move, 0)


def amplitudes(coulomb, denominator, weight):
    amplitude = (coulomb / denominator).astype(jnp.bfloat16)
    weighted = (amplitude.astype(jnp.float32) * weight).astype(jnp.bfloat16)
    return amplitude, weighted.T


def add_pair(weight, offset, occ, eps_a, eps_b, ft, buf, acc, dens, turned):
    rows, width = acc.shape
    depth = ft.shape[1]
    scale = float(width) ** -0.5
    coulomb = dot(ft[...], buf[pl.ds(offset, depth), :])
    amplitude, turned[...] = amplitudes(coulomb, occ - eps_a - eps_b, weight)
    dens[...] += scale * dot(amplitude, turned[...])
    step = tile_of(rows)

    def add(i, carry):
        base = pl.multiple_of(i * step, SUB)
        block = buf[pl.ds(pl.multiple_of(offset + base, SUB), step), :]
        acc[pl.ds(base, step), :] += dot(block, turned[...])
        return carry

    lax.fori_loop(0, rows // step, add, 0, unroll=True)


def add_block(plan, occ, group, t, at, eps_col, eps_row, ft, buf, acc, dens, turned):
    owned = acc.shape[0]
    cols = buf.shape[1]

    def one(s, carry):
        slot = plan.slot(group, s, t)

        @pl.when(plan.count(slot) != 0)
        def _():
            add_pair(
                plan.count(slot).astype(jnp.float32),
                plan.offset(slot),
                occ[slot],
                eps_col[s],
                eps_row[group * owned + t, :, at : at + cols],
                ft.at[s],
                buf,
                acc.at[s],
                dens.at[s],
                turned,
            )

        return carry

    lax.fori_loop(0, owned, one, 0)


def make_plan(
    fit_start, occ_energy, pair_partner, domains, energy, ints, occ, eps_col, eps_row,
    *, devices, targets, relays,
):
    owned, width = eps_col.shape[:2]
    orbitals = fit_start.shape[0]
    pairs_here = pair_partner.shape[0] // devices
    plan = Plan(ints, owned)
    position = lax.axis_index("row")
    side = jnp.where(position % 2 == 1, 1, -1)
    places = [
        base * owned + t
        for base in (position, position - side, position + side)
        for t in range(owned)
    ]
    inside = [jnp.clip(place, 0, orbitals - 1) for place in places]
    starts = [fit_start[place] for place in inside]
    pairs = []
    for step in (-1, 0, 1):
        group = position + step
        known = (group >= 0) & (group < devices)
        held = jnp.clip(group, 0, devices - 1)
        for n in range(pairs_here):
            pairs.append((known, group * owned + n % owned, pair_partner[held * pairs_here + n]))
    for group in range(3):
        for s in range(owned):
            for t in range(owned):
                slot = plan.slot(group, s, t)
                other = group * owned + t
                total = jnp.int32(0)
                for known, first, second in pairs:
                    forth = known & (first == places[s]) & (second == places[other])
                    back = known & (second == places[s]) & (first == places[other])
                    total = total + forth.astype(jnp.int32) + back.astype(jnp.int32)
                ints[slot] = total
                ints[plan.at_shift(slot)] = (
                    starts[s] - starts[s] % SUB - starts[other] + starts[other] % SUB
                )
                occ[slot] = occ_energy[inside[s]] + occ_energy[inside[other]]
    for place in range(3 * owned):
        ints[plan.at_lead(place)] = starts[place] % SUB
    for number, group in enumerate(targets):
        way = jnp.int32(0)
        for to in group:
            way = jnp.where(position == to, 1, way)
        ints[plan.at_way(number)] = way
    late = jnp.int32(0)
    for row in relays:
        late = jnp.where(position == row, 1, late)
    ints[plan.at_late(len(targets))] = late
    entries = energy.shape[0]
    table = lax.broadcasted_iota(jnp.int32, (entries, width), 0)
    for place in range(3 * owned):
        domain = domains[pl.ds(inside[place], 1), :]
        row = jnp.sum(jnp.where(table == domain, energy[...], 0.0), axis=0, keepdims=True)
        eps_row[place] = row
        if place < owned:
            eps_col[place] = jnp.broadcast_to(row, (LANES, width)).T[:, :1]
    return plan


def add_blocks(plan, occ, sources, eps_col, eps_row, ft, buf, acc, dens, turned, raw, wide, sem):
    copies = [
        pltpu.make_async_copy(block, raw.at[n % 2], sem.at[n % 2])
        for n, (_, _, block) in enumerate(sources)
    ]
    copies[0].start()
    clear_margins(buf, raw.shape[1] + SUB)
    for n, (group, t, _) in enumerate(sources):
        if n + 1 < len(copies):
            copies[n + 1].start()
        copies[n].wait()
        align(raw.at[n % 2], plan.lead(group * plan.owned + t), wide, buf)
        add_block(plan, occ, group, t, 0, eps_col, eps_row, ft, buf, acc, dens, turned)


def first_kernel(
    fit_start, occ_energy, pair_partner, domains, energy, own, after,
    ints, occ, eps_col, eps_row, acc, dens, ft, token, bufs, wide, turned,
    *, devices, targets, relays,
):
    del after
    token[...] = jnp.zeros_like(token)
    plan = make_plan(
        fit_start, occ_energy, pair_partner, domains, energy, ints, occ, eps_col, eps_row,
        devices=devices, targets=targets, relays=relays,
    )
    owned, aux, width = own.shape
    rows = aux + SUB
    depth = ft.shape[2]
    acc[...] = jnp.zeros_like(acc)
    dens[...] = jnp.zeros_like(dens)
    for t in range(owned):
        buf = bufs.at[t]
        clear_margins(buf, rows)
        align(own.at[t], plan.lead(t), wide, buf)

        def turn(i, carry):
            at = pl.multiple_of(i * LANES, LANES)
            ft[t, :, pl.ds(at, LANES)] = buf[pl.ds(REACH + at, LANES), :].T
            return carry

        lax.fori_loop(0, depth // LANES, turn, 0)

    @pl.when(ints[plan.at_late(len(targets))] == 1)
    def _():
        for t in range(owned):
            add_block(plan, occ, 0, t, 0, eps_col, eps_row, ft, bufs.at[t], acc, dens, turned)


def near_kernel(
    ints, occ, eps_col, eps_row, ft, acc_in, dens_in, own, mate, *refs, ways, late
):
    del acc_in, dens_in
    acc, dens, token, buf, wide, turned, raw, sem = refs[-8:]
    token[...] = jnp.zeros_like(token)
    owned = own.shape[0]
    plan = Plan(ints, owned)
    groups = ((1, mate),) if late else ((0, own), (1, mate))
    sources = [(group, t, blocks.at[t]) for group, blocks in groups for t in range(owned)]

    @pl.when(ints[plan.at_late(ways)] == late)
    def _():
        add_blocks(
            plan, occ, sources, eps_col, eps_row, ft, buf, acc, dens, turned, raw, wide, sem
        )


def needed(plan, t):
    total = jnp.int32(0)
    for s in range(plan.owned):
        total = total + plan.count(plan.slot(2, s, t))
    return total != 0


def far_kernel(
    ints, occ, eps_col, eps_row, ft, acc_in, dens_in, block, after,
    acc, dens, token, buf, wide, turned, *, ways, place,
):
    del acc_in, dens_in, after
    token[...] = jnp.zeros_like(token)
    plan = Plan(ints, acc.shape[0])
    t, at = place

    here = needed(plan, t)
    for way in ways:
        here = here & (plan.way(way) == 0)

    @pl.when(here)
    def _():
        clear_margins(buf, block.shape[0] + SUB)
        align(block, plan.lead(2 * plan.owned + t), wide, buf)
        add_block(plan, occ, 2, t, at, eps_col, eps_row, ft, buf, acc, dens, turned)


def relayed_kernel(
    ints, occ, eps_col, eps_row, ft, acc_in, dens_in, *refs, places, last
):
    del acc_in, dens_in
    *blocks, _, acc, dens, token, out, dens_out, buf, wide, turned, raw, ready, sem, out_sem = refs
    token[...] = jnp.zeros_like(token)
    owned = acc.shape[0]
    plan = Plan(ints, owned)
    for number, (block, (t, at)) in enumerate(zip(blocks, places)):

        @pl.when(needed(plan, t) & (plan.way(number) == 1))
        def _():
            copy = pltpu.make_async_copy(block, raw, sem)
            copy.start()
            clear_margins(buf, raw.shape[0] + SUB)
            copy.wait()
            align(raw, plan.lead(2 * owned + t), wide, buf)
            add_block(plan, occ, 2, t, at, eps_col, eps_row, ft, buf, acc, dens, turned)

    slots = [plan.slot(2, s, last) for s in range(owned)]
    for s in range(owned):

        @pl.when(plan.count(slots[s]) == 0)
        def _():
            copies = sent_out(s, dens, ready, out, dens_out, out_sem)
            copies[0].start()
            for i in range(OUT_TILES):
                settle(plan, s, i, acc, ready)
                copies[1 + i].start()

    for s in range(owned):

        @pl.when(plan.count(slots[s]) == 0)
        def _():
            for copy in sent_out(s, dens, ready, out, dens_out, out_sem):
                copy.wait()


def sent_out(s, dens, ready, out, dens_out, sem):
    step = out.shape[1] // OUT_TILES
    copies = [pltpu.make_async_copy(dens.at[s], dens_out.at[s], sem.at[s, OUT_TILES])]
    for i in range(OUT_TILES):
        part = pl.ds(i * step, step)
        copies.append(pltpu.make_async_copy(ready.at[s, part], out.at[s, part], sem.at[s, i]))
    return copies


def settle(plan, s, i, acc, ready):
    step = ready.shape[1] // OUT_TILES
    base = i * step
    rows = rows_from(lambda at, n: acc[s, pl.ds(at, n), :], plan.lead(s) + base, step)
    ready[s, base : base + step, :] = rows.astype(ready.dtype)


def last_kernel(
    ints, occ, eps_col, eps_row, ft, acc_in, dens_in, block, out_in, dens_out_in, after,
    acc, dens, token, out, dens_out, buf, wide, turned, ready, raw, sem, raw_sem, *, place,
):
    del acc_in, dens_in, out_in, dens_out_in, after
    token[...] = jnp.zeros_like(token)
    t, at = place
    owned, aux, width = out.shape
    plan = Plan(ints, owned)
    rows = aux + SUB
    depth = ft.shape[2]
    scale = float(width) ** -0.5
    step = aux // OUT_TILES
    slots = [plan.slot(2, s, t) for s in range(owned)]

    @pl.when(needed(plan, t))
    def _():
        load = pltpu.make_async_copy(block, raw, raw_sem)
        load.start()
        clear_margins(buf, rows)
        load.wait()
        align(raw, plan.lead(2 * owned + t), wide, buf)

    def finish(chosen):
        copies = {s: sent_out(s, dens, ready, out, dens_out, sem) for s in chosen}
        coulombs = [dot(ft[s], buf[pl.ds(plan.offset(slots[s]), depth), :]) for s in chosen]
        eps_b = eps_row[2 * owned + t, :, at : at + COLS]
        pairs = []
        for s, coulomb in zip(chosen, coulombs):
            weight = plan.count(slots[s]).astype(jnp.float32)
            pairs.append(amplitudes(coulomb, occ[slots[s]] - eps_col[s] - eps_b, weight))
        for s, (amplitude, weighted) in zip(chosen, pairs):
            turned[s] = weighted
            dens[s] += scale * dot(amplitude, weighted)
        for s in chosen:
            copies[s][0].start()

        def add(base, taken):
            for s in chosen:
                start = pl.multiple_of(plan.offset(slots[s]) + base, SUB)
                acc[s, pl.ds(base, taken), :] += dot(buf[pl.ds(start, taken), :], turned[s])

        add(0, step + SUB)
        for i in range(OUT_TILES):
            if i + 1 < OUT_TILES:
                add((i + 1) * step + SUB, step)
            for s in chosen:
                settle(plan, s, i, acc, ready)
                copies[s][1 + i].start()
        for s in chosen:
            for copy in copies[s]:
                copy.wait()

    for mask in range(1, 2**owned):
        chosen = [s for s in range(owned) if mask >> s & 1]
        wanted = jnp.bool_(True)
        for s in range(owned):
            wanted = wanted & ((plan.count(slots[s]) != 0) == (s in chosen))

        @pl.when(wanted)
        def _():
            finish(chosen)


def copy_kernel(source, *refs, places):
    *outs, buf, sem = refs[-len(places) - 2 :]
    rows, cols = outs[0].shape
    tile = rows // CHUNK_TILES
    parts = [(n, i) for n in range(len(places)) for i in range(CHUNK_TILES)]

    def copies(n, i):
        t, at = places[n]
        part = pl.ds(i * tile, tile)
        held = buf.at[n, part]
        load = pltpu.make_async_copy(source.at[t, part, pl.ds(at, cols)], held, sem.at[0, n, i])
        return load, pltpu.make_async_copy(held, outs[n].at[part], sem.at[1, n, i])

    for n, i in parts:
        copies(n, i)[0].start()
    for n, i in parts:
        load, store = copies(n, i)
        load.wait()
        store.start()
    for n, i in parts:
        copies(n, i)[1].wait()


def pass_kernel(source, after, out):
    del source, after, out


def relay_plan(devices, chunks):
    if devices != 16 or chunks != 4:
        return []
    plan = []
    for z, chunk, alone in ((1, 0, True), (0, 0, False), (2, 1, False)):
        high, low = 4 * z + 3, 4 * z + 4
        plan.append((chunk, alone, [(high, low, 0), (low, high, devices - 1)]))
    return plan


def spec(space):
    return pl.BlockSpec(memory_space=space)


def on_device(fitted, fit_start, virt_domain, occ_energy, virt_energy, pair_partner):
    owned, aux, width = fitted.shape
    devices = lax.axis_size("row")
    rows = aux + SUB
    depth = up_to(rows, LANES)
    buf_rows = 2 * REACH + depth
    wide_rows = aux + 2 * SUB + STEP
    smem, vmem, anywhere = spec(pltpu.SMEM), spec(pltpu.VMEM), spec(pl.ANY)

    outward = []
    for i in range(devices):
        to = i + 1 if i % 2 else i - 1
        if 0 <= to < devices:
            outward.append((i, to))
    inward = [(i, i ^ 1) for i in range(devices) if i ^ 1 < devices]

    def in_hbm(array):
        return pltpu.with_memory_space_constraint(array, pltpu.HBM)

    def in_vmem(array):
        return pltpu.with_memory_space_constraint(array, pltpu.VMEM)

    def chunks(places, *after):
        return pl.pallas_call(
            functools.partial(copy_kernel, places=places),
            out_shape=[jax.ShapeDtypeStruct((aux, COLS), fitted.dtype)] * len(places),
            in_specs=[anywhere] * (1 + len(after)),
            out_specs=[anywhere] * len(places),
            scratch_shapes=[
                pltpu.VMEM((len(places), aux, COLS), fitted.dtype),
                pltpu.SemaphoreType.DMA((2, len(places), CHUNK_TILES)),
            ],
            compiler_params=pltpu.CompilerParams(vmem_limit_bytes=CHUNK_VMEM),
            name="chunks",
        )(in_hbm(fitted), *after)

    def pass_on(block, after):
        return pl.pallas_call(
            pass_kernel,
            out_shape=jax.ShapeDtypeStruct(block.shape, block.dtype),
            in_specs=[anywhere] * 2,
            out_specs=anywhere,
            input_output_aliases={0: 0},
            compiler_params=pltpu.CompilerParams(vmem_limit_bytes=CHUNK_VMEM),
            name="pass_on",
        )(block, after)

    cells = [(t, at) for t in range(owned) for at in range(0, width, COLS)]
    last = len(cells) - 1
    plan = relay_plan(devices, len(cells))
    first_hops = [[(source, by) for source, _, by in pairs] for _, _, pairs in plan]
    second_hops = [[(by, to) for _, to, by in pairs] for _, _, pairs in plan]

    def exchange(number, block):
        pairs = list(outward)
        for (at, alone, group), hop in zip(plan, first_hops):
            if at == number:
                pairs = [pair for pair in pairs if pair not in {(a, b) for a, b, _ in group}]
                pairs += [] if alone else hop
        return lax.ppermute(block, "row", pairs)

    mate = lax.ppermute(fitted, "row", inward)
    sent = list(chunks(cells[:1]))
    far = [exchange(0, sent[0])]
    rest = chunks(cells[1:] + cells[:1] * bool(plan), sent[0])
    sent += rest[:last]
    early = {
        index: lax.ppermute(rest[last], "row", first_hops[index])
        for index, (_, alone, _) in enumerate(plan)
        if alone
    }
    far += [exchange(number, sent[number]) for number in range(1, last + 1)]

    unit = 4 * rows * width * COLS
    acc_shape = pltpu.VMEM((owned, rows, width), jnp.float32)
    dens_shape = pltpu.VMEM((owned, width, width), jnp.float32)
    ft_shape = pltpu.VMEM((owned, width, depth), fitted.dtype)
    token_shape = jax.ShapeDtypeStruct((8, LANES), jnp.int32)
    slots = 3 * owned * owned

    def cost(blocks):
        return pl.CostEstimate(
            flops=100 * unit * blocks * owned, bytes_accessed=8 << 20, transcendentals=0
        )

    ints, occ, eps_col, eps_row, acc, dens, ft, token = pl.pallas_call(
        functools.partial(
            first_kernel,
            devices=devices,
            targets=[[to for _, to, _ in pairs] for _, _, pairs in plan],
            relays=sorted({by for _, _, pairs in plan for _, _, by in pairs}),
        ),
        out_shape=(
            jax.ShapeDtypeStruct((Plan(None, owned).at_late(len(plan)) + 1,), jnp.int32),
            jax.ShapeDtypeStruct((slots,), jnp.float32),
            pltpu.VMEM((owned, width, 1), jnp.float32),
            pltpu.VMEM((3 * owned, 1, width), jnp.float32),
            acc_shape,
            dens_shape,
            ft_shape,
            token_shape,
        ),
        in_specs=[smem] * 3 + [vmem] * 3 + [anywhere],
        out_specs=(smem,) * 2 + (vmem,) * 6,
        scratch_shapes=[
            pltpu.VMEM((owned, buf_rows, width), fitted.dtype),
            pltpu.VMEM((wide_rows, width), jnp.float32),
            pltpu.VMEM((width, width), fitted.dtype),
        ],
        compiler_params=pltpu.CompilerParams(vmem_limit_bytes=NEAR_VMEM),
        cost_estimate=cost(len(cells)),
        name="first",
    )(
        fit_start, occ_energy, pair_partner, virt_domain, virt_energy.reshape(-1, 1),
        in_hbm(fitted), sent[last - 1],
    )
    state = {"acc": acc, "dens": dens, "token": token}
    hops = []

    def add_pairs(
        kernel, block_specs, blocks, cols, limit, name, extra=(), outs=(), aliases={}, scratch=()
    ):
        specs = [smem] * 2 + [vmem] * 5 + block_specs
        results = pl.pallas_call(
            kernel,
            out_shape=(acc_shape, dens_shape, token_shape, *outs),
            in_specs=specs + [anywhere] * (1 + len(extra)),
            out_specs=(vmem,) * 3 + (anywhere,) * len(outs),
            input_output_aliases={5: 0, 6: 1, **aliases},
            scratch_shapes=[
                pltpu.VMEM((buf_rows, cols), fitted.dtype),
                pltpu.VMEM((wide_rows, cols), jnp.float32),
                *scratch,
            ],
            compiler_params=pltpu.CompilerParams(vmem_limit_bytes=limit),
            cost_estimate=cost(cols // COLS),
            name=name,
        )(
            ints, occ, in_vmem(eps_col), in_vmem(eps_row), in_vmem(ft), in_vmem(state["acc"]),
            in_vmem(state["dens"]), *blocks, *extra, state["token"],
        )
        state.update(acc=results[0], dens=results[1], token=results[2])
        return results[3:]

    hops = {index: lax.ppermute(early[index], "row", second_hops[index]) for index in early}
    turned_cols = (pltpu.VMEM((COLS, width), fitted.dtype),)

    def near_pairs(late, *extra):
        add_pairs(
            functools.partial(near_kernel, ways=len(plan), late=late),
            [anywhere] * 2, [in_hbm(fitted), mate], width, NEAR_VMEM, f"near_pairs_{late}",
            extra=extra,
            scratch=(
                pltpu.VMEM((width, width), fitted.dtype),
                pltpu.VMEM((2, aux, width), fitted.dtype),
                pltpu.SemaphoreType.DMA((2,)),
            ),
        )

    near_pairs(0, *early.values())
    for number in range(last):
        for index, (at, alone, _) in enumerate(plan):
            if at == number and not alone:
                far[number] = state["token"] = pass_on(far[number], state["token"])
                hops[index] = lax.ppermute(far[number], "row", second_hops[index])
                if index == len(plan) - 1:
                    near_pairs(1)
        ways = [index for index, (at, _, _) in enumerate(plan) if at == number]
        add_pairs(
            functools.partial(far_kernel, ways=ways, place=cells[number]),
            [vmem], [far[number]], COLS, FAR_VMEM, f"far_pairs_{number}", scratch=turned_cols,
        )
    results = (
        jax.ShapeDtypeStruct(fitted.shape, fitted.dtype),
        jax.ShapeDtypeStruct((owned, width, width), jnp.float32),
    )
    out_scratch = (
        pltpu.VMEM((owned, aux, width), fitted.dtype),
        pltpu.SemaphoreType.DMA((owned, OUT_TILES + 1)),
    )
    ready = add_pairs(
        functools.partial(
            relayed_kernel, places=[cells[at] for at, _, _ in plan], last=cells[last][0]
        ),
        [anywhere] * len(hops), [hops[index] for index in range(len(plan))], COLS, FAR_VMEM,
        "relayed_pairs",
        outs=results,
        scratch=turned_cols
        + (pltpu.VMEM((aux, COLS), fitted.dtype), out_scratch[0], pltpu.SemaphoreType.DMA)
        + out_scratch[1:],
    )
    gradient, density = add_pairs(
        functools.partial(last_kernel, place=cells[last]),
        [anywhere] * 3, [far[last], *ready], COLS, FAR_VMEM, "last_pairs",
        outs=results,
        aliases={8: 3, 9: 4},
        scratch=(
            pltpu.VMEM((owned, COLS, width), fitted.dtype),
            out_scratch[0],
            pltpu.VMEM((aux, COLS), fitted.dtype),
            out_scratch[1],
            pltpu.SemaphoreType.DMA,
        ),
    )
    return gradient, density


def solution(mesh):
    placed = (
        P(("parts", "row"), None, None),
        P("parts"),
        P("parts", None),
        P("parts"),
        P("parts"),
        P("parts"),
    )
    return jax.shard_map(
        on_device,
        mesh=mesh,
        in_specs=placed,
        out_specs=(P(("parts", "row"), None, None), P(("parts", "row"), None, None)),
        check_vma=False,
    )
```

```python
import functools

import jax
import jax.numpy as jnp
from jax import lax
from jax.experimental import pallas as pl
from jax.experimental.pallas import tpu as pltpu
from jax.sharding import PartitionSpec as P

SUB = 16
STEP = 8
LANES = 128
ROW_TILES = 4
CHUNK_TILES = 2
COLS = 256
REACH = 1024
NEAR_VMEM = 22 * 1024 * 1024
FAR_VMEM = 16 * 1024 * 1024
CHUNK_VMEM = 6 * 1024 * 1024


class Plan:
    def __init__(self, ref, owned):
        self.ref, self.owned = ref, owned
        self.slots = 3 * owned * owned

    def slot(self, group, s, t):
        return (group * self.owned + s) * self.owned + t

    def at_shift(self, slot):
        return self.slots + slot

    def at_lead(self, slot):
        return 2 * self.slots + slot

    def at_way(self, number):
        return 3 * self.slots + number

    def at_late(self, ways):
        return self.at_way(ways)

    def count(self, slot):
        return self.ref[slot]

    def offset(self, slot):
        return pl.multiple_of(REACH + self.ref[self.at_shift(slot)], SUB)

    def lead(self, slot):
        return self.ref[self.at_lead(slot)]

    def way(self, number):
        return self.ref[self.at_way(number)]


def dot(a, b):
    return jnp.dot(a, b, preferred_element_type=jnp.float32)


def tile_of(rows):
    return max(n for n in range(SUB, 705, SUB) if rows % n == 0)


def rows_from(load, start, count):
    skip = start % STEP
    base = pl.multiple_of(start - skip, STEP)
    block = load(base, count + STEP)
    width = block.shape[1]
    block = block.reshape(count // STEP + 1, STEP, width)
    turned = pltpu.roll(block, (STEP - skip) % STEP, 1)
    row = lax.broadcasted_iota(jnp.int32, (count // STEP, STEP, width), 1)
    return jnp.where(row < STEP - skip, turned[:-1], turned[1:]).reshape(count, width)


def clear_margins(buf, rows):
    width = buf.shape[1]
    buf[:REACH, :] = jnp.zeros((REACH, width), buf.dtype)
    buf[REACH + rows :, :] = jnp.zeros((buf.shape[0] - REACH - rows, width), buf.dtype)


def widen(source, wide):
    aux, width = source.shape
    wide[:SUB, :] = jnp.zeros((SUB, width), jnp.float32)
    wide[SUB + aux :, :] = jnp.zeros((wide.shape[0] - SUB - aux, width), jnp.float32)
    tile = aux // ROW_TILES

    def one(i, carry):
        base = pl.multiple_of(i * tile, SUB)
        wide[pl.ds(pl.multiple_of(SUB + base, SUB), tile), :] = source[
            pl.ds(base, tile), :
        ].astype(jnp.float32)
        return carry

    lax.fori_loop(0, ROW_TILES, one, 0)


def place(lead, wide, buf):
    rows = wide.shape[0] - SUB - STEP
    step = tile_of(rows)

    def move(i, carry):
        base = pl.multiple_of(i * step, SUB)
        moved = rows_from(lambda at, n: wide[pl.ds(at, n), :], SUB - lead + base, step)
        buf[pl.ds(pl.multiple_of(REACH + base, SUB), step), :] = moved.astype(buf.dtype)
        return carry

    lax.fori_loop(0, rows // step, move, 0)


def amplitudes(coulomb, denominator, weight):
    amplitude = (coulomb / denominator).astype(jnp.bfloat16)
    weighted = (amplitude.astype(jnp.float32) * weight).astype(jnp.bfloat16)
    return amplitude, weighted.T


def needed(plan, group, t):
    total = jnp.int32(0)
    for s in range(plan.owned):
        total = total + plan.count(plan.slot(group, s, t))
    return total != 0


def amplitude_of(plan, occ, slot, s, partner, at, eps_col, eps_row, ft, buf):
    rows = ft.shape[2]
    cols = buf.shape[1]
    coulomb = dot(ft[s], buf[pl.ds(plan.offset(slot), rows), :])
    denominator = occ[slot] - eps_col[s] - eps_row[partner, :, at : at + cols]
    return amplitudes(coulomb, denominator, plan.count(slot).astype(jnp.float32))


def add_block(plan, occ, group, t, at, eps_col, eps_row, ft, source, wide, buf, acc, dens, turned):
    owned, rows, width = acc.shape
    scale = float(width) ** -0.5
    step = rows // ROW_TILES

    @pl.when(needed(plan, group, t))
    def _():
        widen(source, wide)

    def one(s, carry):
        slot = plan.slot(group, s, t)

        @pl.when(plan.count(slot) != 0)
        def _():
            place(plan.lead(slot), wide, buf)
            amplitude, turned[...] = amplitude_of(
                plan, occ, slot, s, group * owned + t, at, eps_col, eps_row, ft, buf
            )
            dens[s] += scale * dot(amplitude, turned[...])

            def add(i, inner):
                base = pl.multiple_of(i * step, SUB)
                block = buf[pl.ds(pl.multiple_of(plan.offset(slot) + base, SUB), step), :]
                acc[s, pl.ds(base, step), :] += dot(block, turned[...])
                return inner

            lax.fori_loop(0, ROW_TILES, add, 0)

        return carry

    lax.fori_loop(0, owned, one, 0)


def make_plan(
    fit_start, occ_energy, pair_partner, domains, energy, ints, occ, eps_col, eps_row,
    *, devices, targets, relays,
):
    owned, width = eps_col.shape[:2]
    orbitals = fit_start.shape[0]
    pairs_here = pair_partner.shape[0] // devices
    plan = Plan(ints, owned)
    position = lax.axis_index("row")
    side = jnp.where(position % 2 == 1, 1, -1)
    places = [
        base * owned + t
        for base in (position, position - side, position + side)
        for t in range(owned)
    ]
    inside = [jnp.clip(orbital, 0, orbitals - 1) for orbital in places]
    starts = [fit_start[orbital] for orbital in inside]
    pairs = []
    for step in (-1, 0, 1):
        group = position + step
        known = (group >= 0) & (group < devices)
        held = jnp.clip(group, 0, devices - 1)
        for n in range(pairs_here):
            pairs.append((known, group * owned + n % owned, pair_partner[held * pairs_here + n]))
    for group in range(3):
        for s in range(owned):
            for t in range(owned):
                slot = plan.slot(group, s, t)
                other = group * owned + t
                total = jnp.int32(0)
                for known, first, second in pairs:
                    forth = known & (first == places[s]) & (second == places[other])
                    back = known & (second == places[s]) & (first == places[other])
                    total = total + forth.astype(jnp.int32) + back.astype(jnp.int32)
                ints[slot] = total
                apart = starts[other] - starts[s]
                ints[plan.at_shift(slot)] = (apart & (SUB - 1)) - apart
                ints[plan.at_lead(slot)] = apart & (SUB - 1)
                occ[slot] = occ_energy[inside[s]] + occ_energy[inside[other]]
    for number, group in enumerate(targets):
        way = jnp.int32(0)
        for to in group:
            way = jnp.where(position == to, 1, way)
        ints[plan.at_way(number)] = way
    late = jnp.int32(0)
    for row in relays:
        late = jnp.where(position == row, 1, late)
    ints[plan.at_late(len(targets))] = late
    entries = energy.shape[0]
    table = lax.broadcasted_iota(jnp.int32, (entries, width), 0)
    for n, orbital in enumerate(inside):
        domain = domains[pl.ds(orbital, 1), :]
        row = jnp.sum(jnp.where(table == domain, energy[...], 0.0), axis=0, keepdims=True)
        eps_row[n] = row
        if n < owned:
            eps_col[n] = jnp.broadcast_to(row, (LANES, width)).T[:, :1]
    return plan


def add_blocks(plan, occ, sources, eps_col, eps_row, ft, wide, buf, acc, dens, turned, raw, sem):
    copies = [
        pltpu.make_async_copy(block, raw.at[n % 2], sem.at[n % 2])
        for n, (_, _, block) in enumerate(sources)
    ]
    copies[0].start()
    clear_margins(buf, raw.shape[1] + SUB)
    for n, (group, t, _) in enumerate(sources):
        if n + 1 < len(copies):
            copies[n + 1].start()
        copies[n].wait()
        add_block(
            plan, occ, group, t, 0, eps_col, eps_row, ft, raw.at[n % 2], wide, buf, acc, dens, turned
        )


def first_kernel(
    fit_start, occ_energy, pair_partner, domains, energy, own, after,
    ints, occ, eps_col, eps_row, acc, dens, ft, token, wide, buf, turned,
    *, devices, targets, relays,
):
    del after
    token[...] = jnp.zeros_like(token)
    plan = make_plan(
        fit_start, occ_energy, pair_partner, domains, energy, ints, occ, eps_col, eps_row,
        devices=devices, targets=targets, relays=relays,
    )
    owned, aux, width = own.shape
    acc[...] = jnp.zeros_like(acc)
    dens[...] = jnp.zeros_like(dens)
    for t in range(owned):

        def turn(i, carry):
            at = pl.multiple_of(i * LANES, LANES)
            ft[t, :, pl.ds(at, LANES)] = own[t, pl.ds(at, LANES), :].T
            return carry

        lax.fori_loop(0, aux // LANES, turn, 0)

    @pl.when(ints[plan.at_late(len(targets))] == 1)
    def _():
        clear_margins(buf, aux + SUB)
        for t in range(owned):
            add_block(
                plan, occ, 0, t, 0, eps_col, eps_row, ft, own.at[t], wide, buf, acc, dens, turned
            )


def near_kernel(
    ints, occ, eps_col, eps_row, ft, acc_in, dens_in, own, mate, *refs, ways, late
):
    del acc_in, dens_in
    acc, dens, token, wide, buf, turned, raw, sem = refs[-8:]
    token[...] = jnp.zeros_like(token)
    owned = own.shape[0]
    plan = Plan(ints, owned)
    groups = ((1, mate),) if late else ((0, own), (1, mate))
    sources = [(group, t, blocks.at[t]) for group, blocks in groups for t in range(owned)]

    @pl.when(ints[plan.at_late(ways)] == late)
    def _():
        add_blocks(
            plan, occ, sources, eps_col, eps_row, ft, wide, buf, acc, dens, turned, raw, sem
        )


def far_kernel(
    ints, occ, eps_col, eps_row, ft, acc_in, dens_in, block, after,
    acc, dens, token, wide, buf, turned, *, ways, cell,
):
    del acc_in, dens_in, after
    token[...] = jnp.zeros_like(token)
    plan = Plan(ints, acc.shape[0])
    t, at = cell
    here = needed(plan, 2, t)
    for way in ways:
        here = here & (plan.way(way) == 0)

    @pl.when(here)
    def _():
        clear_margins(buf, block.shape[0] + SUB)
        add_block(plan, occ, 2, t, at, eps_col, eps_row, ft, block, wide, buf, acc, dens, turned)


def send_out(s, tile_of_rows, dens, ready, out, dens_out, sem):
    step = out.shape[1] // ROW_TILES
    pltpu.make_async_copy(dens.at[s], dens_out.at[s], sem.at[s, ROW_TILES]).start()

    def one(i, carry):
        part = pl.ds(pl.multiple_of(i * step, SUB), step)
        ready[s, part, :] = tile_of_rows(i * step, step).astype(ready.dtype)
        pltpu.make_async_copy(ready.at[s, part], out.at[s, part], sem.at[s, i]).start()
        return carry

    lax.fori_loop(0, ROW_TILES, one, 0)


def wait_out(s, dens, ready, out, dens_out, sem):
    step = out.shape[1] // ROW_TILES
    pltpu.make_async_copy(dens.at[s], dens_out.at[s], sem.at[s, ROW_TILES]).wait()
    for i in range(ROW_TILES):
        part = pl.ds(i * step, step)
        pltpu.make_async_copy(ready.at[s, part], out.at[s, part], sem.at[s, i]).wait()


def relayed_kernel(
    ints, occ, eps_col, eps_row, ft, acc_in, dens_in, *refs, cells, last
):
    del acc_in, dens_in
    *blocks, _, acc, dens, token, out, dens_out, wide, buf, turned, raw, ready, sem, out_sem = refs
    token[...] = jnp.zeros_like(token)
    owned = acc.shape[0]
    plan = Plan(ints, owned)
    for number, (block, (t, at)) in enumerate(zip(blocks, cells)):

        @pl.when(needed(plan, 2, t) & (plan.way(number) == 1))
        def _():
            copy = pltpu.make_async_copy(block, raw, sem)
            copy.start()
            clear_margins(buf, raw.shape[0] + SUB)
            copy.wait()
            add_block(plan, occ, 2, t, at, eps_col, eps_row, ft, raw, wide, buf, acc, dens, turned)

    for s in range(owned):

        @pl.when(plan.count(plan.slot(2, s, last)) == 0)
        def _():
            send_out(
                s,
                lambda base, n: acc[s, pl.ds(pl.multiple_of(base, SUB), n), :],
                dens, ready, out, dens_out, out_sem,
            )

    for s in range(owned):

        @pl.when(plan.count(plan.slot(2, s, last)) == 0)
        def _():
            wait_out(s, dens, ready, out, dens_out, out_sem)


def last_kernel(
    ints, occ, eps_col, eps_row, ft, acc_in, dens_in, block, out_in, dens_out_in, after,
    acc, dens, token, out, dens_out, wide, buf, turned, ready, sem, *, cell,
):
    del acc_in, dens_in, out_in, dens_out_in, after
    token[...] = jnp.zeros_like(token)
    t, at = cell
    owned, aux, width = out.shape
    plan = Plan(ints, owned)
    scale = float(width) ** -0.5

    @pl.when(needed(plan, 2, t))
    def _():
        clear_margins(buf, aux + SUB)
        widen(block, wide)

    def one(s, carry):
        slot = plan.slot(2, s, t)

        @pl.when(plan.count(slot) != 0)
        def _():
            place(plan.lead(slot), wide, buf)
            amplitude, turned[...] = amplitude_of(
                plan, occ, slot, s, 2 * owned + t, at, eps_col, eps_row, ft, buf
            )
            dens[s] += scale * dot(amplitude, turned[...])

            def total(base, n):
                rows = buf[pl.ds(pl.multiple_of(plan.offset(slot) + base, SUB), n), :]
                return acc[s, pl.ds(pl.multiple_of(base, SUB), n), :] + dot(rows, turned[...])

            send_out(s, total, dens, ready, out, dens_out, sem)

        return carry

    lax.fori_loop(0, owned, one, 0)
    for s in range(owned):

        @pl.when(plan.count(plan.slot(2, s, t)) != 0)
        def _():
            wait_out(s, dens, ready, out, dens_out, sem)


def copy_kernel(source, *refs, places):
    *outs, buf, sem = refs[-len(places) - 2 :]
    rows, cols = outs[0].shape
    tile = rows // CHUNK_TILES
    parts = [(n, i) for n in range(len(places)) for i in range(CHUNK_TILES)]

    def copies(n, i):
        t, at = places[n]
        part = pl.ds(i * tile, tile)
        held = buf.at[n, part]
        load = pltpu.make_async_copy(source.at[t, part, pl.ds(at, cols)], held, sem.at[0, n, i])
        return load, pltpu.make_async_copy(held, outs[n].at[part], sem.at[1, n, i])

    for n, i in parts:
        copies(n, i)[0].start()
    for n, i in parts:
        load, store = copies(n, i)
        load.wait()
        store.start()
    for n, i in parts:
        copies(n, i)[1].wait()


def pass_kernel(source, after, out):
    del source, after, out


def relay_plan(devices, chunks):
    if devices != 16 or chunks != 4:
        return []
    plan = []
    for z, chunk, alone in ((1, 0, True), (0, 0, False), (2, 1, False)):
        high, low = 4 * z + 3, 4 * z + 4
        plan.append((chunk, alone, [(high, low, 0), (low, high, devices - 1)]))
    return plan


def spec(space):
    return pl.BlockSpec(memory_space=space)


def on_device(fitted, fit_start, virt_domain, occ_energy, virt_energy, pair_partner):
    owned, aux, width = fitted.shape
    devices = lax.axis_size("row")
    buf_rows = 2 * REACH + aux
    wide_rows = aux + 2 * SUB + STEP
    smem, vmem, anywhere = spec(pltpu.SMEM), spec(pltpu.VMEM), spec(pl.ANY)

    outward = []
    for i in range(devices):
        to = i + 1 if i % 2 else i - 1
        if 0 <= to < devices:
            outward.append((i, to))
    inward = [(i, i ^ 1) for i in range(devices) if i ^ 1 < devices]

    def in_hbm(array):
        return pltpu.with_memory_space_constraint(array, pltpu.HBM)

    def in_vmem(array):
        return pltpu.with_memory_space_constraint(array, pltpu.VMEM)

    def chunks(places, *after):
        return pl.pallas_call(
            functools.partial(copy_kernel, places=places),
            out_shape=[jax.ShapeDtypeStruct((aux, COLS), fitted.dtype)] * len(places),
            in_specs=[anywhere] * (1 + len(after)),
            out_specs=[anywhere] * len(places),
            scratch_shapes=[
                pltpu.VMEM((len(places), aux, COLS), fitted.dtype),
                pltpu.SemaphoreType.DMA((2, len(places), CHUNK_TILES)),
            ],
            compiler_params=pltpu.CompilerParams(vmem_limit_bytes=CHUNK_VMEM),
            name="chunks",
        )(in_hbm(fitted), *after)

    def pass_on(block, after):
        return pl.pallas_call(
            pass_kernel,
            out_shape=jax.ShapeDtypeStruct(block.shape, block.dtype),
            in_specs=[anywhere] * 2,
            out_specs=anywhere,
            input_output_aliases={0: 0},
            compiler_params=pltpu.CompilerParams(vmem_limit_bytes=CHUNK_VMEM),
            name="pass_on",
        )(block, after)

    cells = [(t, at) for t in range(owned) for at in range(0, width, COLS)]
    last = len(cells) - 1
    plan = relay_plan(devices, len(cells))
    first_hops = [[(source, by) for source, _, by in pairs] for _, _, pairs in plan]
    second_hops = [[(by, to) for _, to, by in pairs] for _, _, pairs in plan]

    def exchange(number, block):
        pairs = list(outward)
        for (at, alone, group), hop in zip(plan, first_hops):
            if at == number:
                pairs = [pair for pair in pairs if pair not in {(a, b) for a, b, _ in group}]
                pairs += [] if alone else hop
        return lax.ppermute(block, "row", pairs)

    mate = lax.ppermute(fitted, "row", inward)
    sent = list(chunks(cells[:1]))
    far = [exchange(0, sent[0])]
    rest = chunks(cells[1:] + cells[:1] * bool(plan), sent[0])
    sent += rest[:last]
    early = {
        index: lax.ppermute(rest[last], "row", first_hops[index])
        for index, (_, alone, _) in enumerate(plan)
        if alone
    }
    far += [exchange(number, sent[number]) for number in range(1, last + 1)]

    unit = 4 * aux * width * COLS
    acc_shape = pltpu.VMEM((owned, aux, width), jnp.float32)
    dens_shape = pltpu.VMEM((owned, width, width), jnp.float32)
    ft_shape = pltpu.VMEM((owned, width, aux), fitted.dtype)
    token_shape = jax.ShapeDtypeStruct((8, LANES), jnp.int32)
    slots = 3 * owned * owned

    def cost(blocks):
        return pl.CostEstimate(
            flops=100 * unit * blocks * owned, bytes_accessed=8 << 20, transcendentals=0
        )

    ints, occ, eps_col, eps_row, acc, dens, ft, token = pl.pallas_call(
        functools.partial(
            first_kernel,
            devices=devices,
            targets=[[to for _, to, _ in pairs] for _, _, pairs in plan],
            relays=sorted({by for _, _, pairs in plan for _, _, by in pairs}),
        ),
        out_shape=(
            jax.ShapeDtypeStruct((Plan(None, owned).at_late(len(plan)) + 1,), jnp.int32),
            jax.ShapeDtypeStruct((slots,), jnp.float32),
            pltpu.VMEM((owned, width, 1), jnp.float32),
            pltpu.VMEM((3 * owned, 1, width), jnp.float32),
            acc_shape,
            dens_shape,
            ft_shape,
            token_shape,
        ),
        in_specs=[smem] * 3 + [vmem] * 3 + [anywhere],
        out_specs=(smem,) * 2 + (vmem,) * 6,
        scratch_shapes=[
            pltpu.VMEM((wide_rows, width), jnp.float32),
            pltpu.VMEM((buf_rows, width), fitted.dtype),
            pltpu.VMEM((width, width), fitted.dtype),
        ],
        compiler_params=pltpu.CompilerParams(vmem_limit_bytes=NEAR_VMEM),
        cost_estimate=cost(len(cells)),
        name="first",
    )(
        fit_start, occ_energy, pair_partner, virt_domain, virt_energy.reshape(-1, 1),
        in_hbm(fitted), sent[last - 1],
    )
    state = {"acc": acc, "dens": dens, "token": token}
    hops = []

    def add_pairs(
        kernel, block_specs, blocks, cols, limit, name, extra=(), outs=(), aliases={}, scratch=()
    ):
        specs = [smem] * 2 + [vmem] * 5 + block_specs
        results = pl.pallas_call(
            kernel,
            out_shape=(acc_shape, dens_shape, token_shape, *outs),
            in_specs=specs + [anywhere] * (1 + len(extra)),
            out_specs=(vmem,) * 3 + (anywhere,) * len(outs),
            input_output_aliases={5: 0, 6: 1, **aliases},
            scratch_shapes=[
                pltpu.VMEM((wide_rows, cols), jnp.float32),
                pltpu.VMEM((buf_rows, cols), fitted.dtype),
                *scratch,
            ],
            compiler_params=pltpu.CompilerParams(vmem_limit_bytes=limit),
            cost_estimate=cost(cols // COLS),
            name=name,
        )(
            ints, occ, in_vmem(eps_col), in_vmem(eps_row), in_vmem(ft), in_vmem(state["acc"]),
            in_vmem(state["dens"]), *blocks, *extra, state["token"],
        )
        state.update(acc=results[0], dens=results[1], token=results[2])
        return results[3:]

    hops = {index: lax.ppermute(early[index], "row", second_hops[index]) for index in early}
    turned_cols = (pltpu.VMEM((COLS, width), fitted.dtype),)

    def near_pairs(late, *extra):
        add_pairs(
            functools.partial(near_kernel, ways=len(plan), late=late),
            [anywhere] * 2, [in_hbm(fitted), mate], width, NEAR_VMEM, f"near_pairs_{late}",
            extra=extra,
            scratch=(
                pltpu.VMEM((width, width), fitted.dtype),
                pltpu.VMEM((2, aux, width), fitted.dtype),
                pltpu.SemaphoreType.DMA((2,)),
            ),
        )

    near_pairs(0, *early.values())
    for number in range(last):
        for index, (at, alone, _) in enumerate(plan):
            if at == number and not alone:
                far[number] = state["token"] = pass_on(far[number], state["token"])
                hops[index] = lax.ppermute(far[number], "row", second_hops[index])
                if index == len(plan) - 1:
                    near_pairs(1)
        ways = [index for index, (at, _, _) in enumerate(plan) if at == number]
        add_pairs(
            functools.partial(far_kernel, ways=ways, cell=cells[number]),
            [vmem], [far[number]], COLS, FAR_VMEM, f"far_pairs_{number}", scratch=turned_cols,
        )
    results = (
        jax.ShapeDtypeStruct(fitted.shape, fitted.dtype),
        jax.ShapeDtypeStruct((owned, width, width), jnp.float32),
    )
    out_scratch = (
        pltpu.VMEM((owned, aux, width), fitted.dtype),
        pltpu.SemaphoreType.DMA((owned, ROW_TILES + 1)),
    )
    ready = add_pairs(
        functools.partial(
            relayed_kernel, cells=[cells[at] for at, _, _ in plan], last=cells[last][0]
        ),
        [anywhere] * len(hops), [hops[index] for index in range(len(plan))], COLS, FAR_VMEM,
        "relayed_pairs",
        outs=results,
        scratch=turned_cols
        + (pltpu.VMEM((aux, COLS), fitted.dtype), out_scratch[0], pltpu.SemaphoreType.DMA)
        + out_scratch[1:],
    )
    gradient, density = add_pairs(
        functools.partial(last_kernel, cell=cells[last]),
        [vmem, anywhere, anywhere], [in_vmem(far[last]), *ready], COLS, FAR_VMEM, "last_pairs",
        outs=results,
        aliases={8: 3, 9: 4},
        scratch=turned_cols + out_scratch,
    )
    return gradient, density


def solution(mesh):
    placed = (
        P(("parts", "row"), None, None),
        P("parts"),
        P("parts", None),
        P("parts"),
        P("parts"),
        P("parts"),
    )
    return jax.shard_map(
        on_device,
        mesh=mesh,
        in_specs=placed,
        out_specs=(P(("parts", "row"), None, None), P(("parts", "row"), None, None)),
        check_vma=False,
    )
```

```python
import functools

import jax
import jax.numpy as jnp
from jax import lax
from jax.experimental import pallas as pl
from jax.experimental.pallas import tpu as pltpu
from jax.sharding import PartitionSpec as P

SUB = 16
STEP = 8
LANES = 128
ROW_TILES = 2
LOAD_TILES = 4
CHUNK_TILES = 2
COLS = 256
REACH = 1024
NEAR_VMEM = 22 * 1024 * 1024
FAR_VMEM = 16 * 1024 * 1024
CHUNK_VMEM = 6 * 1024 * 1024


class Plan:
    def __init__(self, ref, owned):
        self.ref, self.owned = ref, owned
        self.slots = 3 * owned * owned

    def slot(self, group, s, t):
        return (group * self.owned + s) * self.owned + t

    def at_shift(self, slot):
        return self.slots + slot

    def at_lead(self, slot):
        return 2 * self.slots + slot

    def at_way(self, number):
        return 3 * self.slots + number

    def at_late(self, ways):
        return self.at_way(ways)

    def count(self, slot):
        return self.ref[slot]

    def offset(self, slot):
        return pl.multiple_of(REACH + self.ref[self.at_shift(slot)], SUB)

    def lead(self, slot):
        return self.ref[self.at_lead(slot)]

    def way(self, number):
        return self.ref[self.at_way(number)]


def dot(a, b):
    return jnp.dot(a, b, preferred_element_type=jnp.float32)


def tile_of(rows):
    return max(n for n in range(SUB, 705, SUB) if rows % n == 0)


def rows_from(load, start, count):
    skip = start % STEP
    base = pl.multiple_of(start - skip, STEP)
    block = load(base, count + STEP)
    width = block.shape[1]
    block = block.reshape(count // STEP + 1, STEP, width)
    turned = pltpu.roll(block, (STEP - skip) % STEP, 1)
    row = lax.broadcasted_iota(jnp.int32, (count // STEP, STEP, width), 1)
    return jnp.where(row < STEP - skip, turned[:-1], turned[1:]).reshape(count, width)


def clear_margins(buf, rows):
    width = buf.shape[1]
    buf[:REACH, :] = jnp.zeros((REACH, width), buf.dtype)
    buf[REACH + rows :, :] = jnp.zeros((buf.shape[0] - REACH - rows, width), buf.dtype)


def clear_ends(wide):
    rows, width = wide.shape
    wide[:SUB, :] = jnp.zeros((SUB, width), jnp.float32)
    wide[rows - SUB - STEP :, :] = jnp.zeros((SUB + STEP, width), jnp.float32)


def widen(source, wide):
    aux = source.shape[0]
    clear_ends(wide)
    tile = aux // ROW_TILES

    def one(i, carry):
        base = pl.multiple_of(i * tile, SUB)
        wide[pl.ds(pl.multiple_of(SUB + base, SUB), tile), :] = source[
            pl.ds(base, tile), :
        ].astype(jnp.float32)
        return carry

    lax.fori_loop(0, ROW_TILES, one, 0)


def place(lead, wide, buf):
    rows = wide.shape[0] - SUB - STEP
    step = tile_of(rows)

    def move(i, carry):
        base = pl.multiple_of(i * step, SUB)
        moved = rows_from(lambda at, n: wide[pl.ds(at, n), :], SUB - lead + base, step)
        buf[pl.ds(pl.multiple_of(REACH + base, SUB), step), :] = moved.astype(buf.dtype)
        return carry

    lax.fori_loop(0, rows // step, move, 0)


def amplitudes(coulomb, denominator, weight):
    amplitude = (coulomb / denominator).astype(jnp.bfloat16)
    weighted = (amplitude.astype(jnp.float32) * weight).astype(jnp.bfloat16)
    return amplitude, weighted.T


def needed(plan, group, t):
    total = jnp.int32(0)
    for s in range(plan.owned):
        total = total + plan.count(plan.slot(group, s, t))
    return total != 0


def amplitude_of(plan, occ, slot, s, partner, at, eps_col, eps_row, ft, buf):
    rows = ft.shape[2]
    cols = buf.shape[1]
    coulomb = dot(ft[s], buf[pl.ds(plan.offset(slot), rows), :])
    denominator = occ[slot] - eps_col[s] - eps_row[partner, :, at : at + cols]
    return amplitudes(coulomb, denominator, plan.count(slot).astype(jnp.float32))


def add_block(plan, occ, group, t, at, eps_col, eps_row, ft, source, wide, buf, acc, dens, turned):
    owned, rows, width = acc.shape
    scale = float(width) ** -0.5
    step = rows // ROW_TILES

    @pl.when(needed(plan, group, t))
    def _():
        widen(source, wide)

    def one(s, carry):
        slot = plan.slot(group, s, t)

        @pl.when(plan.count(slot) != 0)
        def _():
            place(plan.lead(slot), wide, buf)
            amplitude, turned[...] = amplitude_of(
                plan, occ, slot, s, group * owned + t, at, eps_col, eps_row, ft, buf
            )
            dens[s] += scale * dot(amplitude, turned[...])

            def add(i, inner):
                base = pl.multiple_of(i * step, SUB)
                block = buf[pl.ds(pl.multiple_of(plan.offset(slot) + base, SUB), step), :]
                acc[s, pl.ds(base, step), :] += dot(block, turned[...])
                return inner

            lax.fori_loop(0, ROW_TILES, add, 0)

        return carry

    lax.fori_loop(0, owned, one, 0)


def make_plan(
    fit_start, occ_energy, pair_partner, domains, energy, ints, occ, eps_col, eps_row,
    *, devices, targets, relays,
):
    owned, width = eps_col.shape[:2]
    orbitals = fit_start.shape[0]
    pairs_here = pair_partner.shape[0] // devices
    plan = Plan(ints, owned)
    position = lax.axis_index("row")
    side = jnp.where(position % 2 == 1, 1, -1)
    places = [
        base * owned + t
        for base in (position, position - side, position + side)
        for t in range(owned)
    ]
    inside = [jnp.clip(orbital, 0, orbitals - 1) for orbital in places]
    starts = [fit_start[orbital] for orbital in inside]
    pairs = []
    for step in (-1, 0, 1):
        group = position + step
        known = (group >= 0) & (group < devices)
        held = jnp.clip(group, 0, devices - 1)
        for n in range(pairs_here):
            pairs.append((known, group * owned + n % owned, pair_partner[held * pairs_here + n]))
    for group in range(3):
        for s in range(owned):
            for t in range(owned):
                slot = plan.slot(group, s, t)
                other = group * owned + t
                total = jnp.int32(0)
                for known, first, second in pairs:
                    forth = known & (first == places[s]) & (second == places[other])
                    back = known & (second == places[s]) & (first == places[other])
                    total = total + forth.astype(jnp.int32) + back.astype(jnp.int32)
                ints[slot] = total
                apart = starts[other] - starts[s]
                ints[plan.at_shift(slot)] = (apart & (SUB - 1)) - apart
                ints[plan.at_lead(slot)] = apart & (SUB - 1)
                occ[slot] = occ_energy[inside[s]] + occ_energy[inside[other]]
    for number, group in enumerate(targets):
        way = jnp.int32(0)
        for to in group:
            way = jnp.where(position == to, 1, way)
        ints[plan.at_way(number)] = way
    late = jnp.int32(0)
    for row in relays:
        late = jnp.where(position == row, 1, late)
    ints[plan.at_late(len(targets))] = late
    entries = energy.shape[0]
    table = lax.broadcasted_iota(jnp.int32, (entries, width), 0)
    for n, orbital in enumerate(inside):
        domain = domains[pl.ds(orbital, 1), :]
        row = jnp.sum(jnp.where(table == domain, energy[...], 0.0), axis=0, keepdims=True)
        eps_row[n] = row
        if n < owned:
            eps_col[n] = jnp.broadcast_to(row, (LANES, width)).T[:, :1]
    return plan


def add_blocks(plan, occ, sources, eps_col, eps_row, ft, wide, buf, acc, dens, turned, raw, sem):
    copies = [
        pltpu.make_async_copy(block, raw.at[n % 2], sem.at[n % 2])
        for n, (_, _, block) in enumerate(sources)
    ]
    copies[0].start()
    clear_margins(buf, raw.shape[1] + SUB)
    for n, (group, t, _) in enumerate(sources):
        if n + 1 < len(copies):
            copies[n + 1].start()
        copies[n].wait()
        add_block(
            plan, occ, group, t, 0, eps_col, eps_row, ft, raw.at[n % 2], wide, buf, acc, dens, turned
        )


def first_kernel(
    fit_start, occ_energy, pair_partner, domains, energy, own, after,
    ints, occ, eps_col, eps_row, acc, dens, ft, token, wide, buf, turned,
    *, devices, targets, relays,
):
    del after
    token[...] = jnp.zeros_like(token)
    plan = make_plan(
        fit_start, occ_energy, pair_partner, domains, energy, ints, occ, eps_col, eps_row,
        devices=devices, targets=targets, relays=relays,
    )
    owned, aux, width = own.shape
    acc[...] = jnp.zeros_like(acc)
    dens[...] = jnp.zeros_like(dens)
    for t in range(owned):

        def turn(i, carry):
            at = pl.multiple_of(i * LANES, LANES)
            ft[t, :, pl.ds(at, LANES)] = own[t, pl.ds(at, LANES), :].T
            return carry

        lax.fori_loop(0, aux // LANES, turn, 0)

    @pl.when(ints[plan.at_late(len(targets))] == 1)
    def _():
        clear_margins(buf, aux + SUB)
        for t in range(owned):
            add_block(
                plan, occ, 0, t, 0, eps_col, eps_row, ft, own.at[t], wide, buf, acc, dens, turned
            )


def near_kernel(
    ints, occ, eps_col, eps_row, ft, acc_in, dens_in, own, mate, *refs, ways, late
):
    del acc_in, dens_in
    acc, dens, token, wide, buf, turned, raw, sem = refs[-8:]
    token[...] = jnp.zeros_like(token)
    owned = own.shape[0]
    plan = Plan(ints, owned)
    groups = ((1, mate),) if late else ((0, own), (1, mate))
    sources = [(group, t, blocks.at[t]) for group, blocks in groups for t in range(owned)]

    @pl.when(ints[plan.at_late(ways)] == late)
    def _():
        add_blocks(
            plan, occ, sources, eps_col, eps_row, ft, wide, buf, acc, dens, turned, raw, sem
        )


def far_kernel(
    ints, occ, eps_col, eps_row, ft, acc_in, dens_in, block, after,
    acc, dens, token, wide, buf, turned, *, ways, cell,
):
    del acc_in, dens_in, after
    token[...] = jnp.zeros_like(token)
    plan = Plan(ints, acc.shape[0])
    t, at = cell
    here = needed(plan, 2, t)
    for way in ways:
        here = here & (plan.way(way) == 0)

    @pl.when(here)
    def _():
        clear_margins(buf, block.shape[0] + SUB)
        add_block(plan, occ, 2, t, at, eps_col, eps_row, ft, block, wide, buf, acc, dens, turned)


def send_out(s, tile_of_rows, dens, ready, out, dens_out, sem):
    step = out.shape[1] // ROW_TILES
    pltpu.make_async_copy(dens.at[s], dens_out.at[s], sem.at[s, ROW_TILES]).start()

    def one(i, carry):
        part = pl.ds(pl.multiple_of(i * step, SUB), step)
        ready[s, part, :] = tile_of_rows(i * step, step).astype(ready.dtype)
        pltpu.make_async_copy(ready.at[s, part], out.at[s, part], sem.at[s, i]).start()
        return carry

    lax.fori_loop(0, ROW_TILES, one, 0)


def wait_out(s, dens, ready, out, dens_out, sem):
    step = out.shape[1] // ROW_TILES
    pltpu.make_async_copy(dens.at[s], dens_out.at[s], sem.at[s, ROW_TILES]).wait()
    for i in range(ROW_TILES):
        part = pl.ds(i * step, step)
        pltpu.make_async_copy(ready.at[s, part], out.at[s, part], sem.at[s, i]).wait()


def relayed_kernel(
    ints, occ, eps_col, eps_row, ft, acc_in, dens_in, *refs, cells, last
):
    del acc_in, dens_in
    *blocks, _, acc, dens, token, out, dens_out, wide, buf, turned, raw, ready, sem, out_sem = refs
    token[...] = jnp.zeros_like(token)
    owned = acc.shape[0]
    plan = Plan(ints, owned)
    for number, (block, (t, at)) in enumerate(zip(blocks, cells)):

        @pl.when(needed(plan, 2, t) & (plan.way(number) == 1))
        def _():
            copy = pltpu.make_async_copy(block, raw, sem)
            copy.start()
            clear_margins(buf, raw.shape[0] + SUB)
            copy.wait()
            add_block(plan, occ, 2, t, at, eps_col, eps_row, ft, raw, wide, buf, acc, dens, turned)

    for s in range(owned):

        @pl.when(plan.count(plan.slot(2, s, last)) == 0)
        def _():
            send_out(
                s,
                lambda base, n: acc[s, pl.ds(pl.multiple_of(base, SUB), n), :],
                dens, ready, out, dens_out, out_sem,
            )

    for s in range(owned):

        @pl.when(plan.count(plan.slot(2, s, last)) == 0)
        def _():
            wait_out(s, dens, ready, out, dens_out, out_sem)


def last_kernel(
    ints, occ, eps_col, eps_row, ft, acc_in, dens_in, block, out_in, dens_out_in, after,
    acc, dens, out, dens_out, wide, buf, turned, raw, ready, sem, raw_sem, *, cell,
):
    del acc_in, dens_in, out_in, dens_out_in, after
    t, at = cell
    owned, aux, width = out.shape
    plan = Plan(ints, owned)
    scale = float(width) ** -0.5

    @pl.when(needed(plan, 2, t))
    def _():
        step = aux // LOAD_TILES
        parts = [pl.ds(i * step, step) for i in range(LOAD_TILES)]
        loads = [
            pltpu.make_async_copy(block.at[part], raw.at[part], raw_sem.at[i])
            for i, part in enumerate(parts)
        ]
        for load in loads:
            load.start()
        clear_margins(buf, aux + SUB)
        clear_ends(wide)
        for i, load in enumerate(loads):
            load.wait()
            wide[SUB + i * step : SUB + (i + 1) * step, :] = raw[parts[i], :].astype(jnp.float32)

    def one(s, carry):
        slot = plan.slot(2, s, t)

        @pl.when(plan.count(slot) != 0)
        def _():
            place(plan.lead(slot), wide, buf)
            amplitude, turned[...] = amplitude_of(
                plan, occ, slot, s, 2 * owned + t, at, eps_col, eps_row, ft, buf
            )
            dens[s] += scale * dot(amplitude, turned[...])

            def total(base, n):
                rows = buf[pl.ds(pl.multiple_of(plan.offset(slot) + base, SUB), n), :]
                return acc[s, pl.ds(pl.multiple_of(base, SUB), n), :] + dot(rows, turned[...])

            send_out(s, total, dens, ready, out, dens_out, sem)

        return carry

    lax.fori_loop(0, owned, one, 0)
    for s in range(owned):

        @pl.when(plan.count(plan.slot(2, s, t)) != 0)
        def _():
            wait_out(s, dens, ready, out, dens_out, sem)


def copy_kernel(source, *refs, places):
    *outs, buf, sem = refs[-len(places) - 2 :]
    rows, cols = outs[0].shape
    tile = rows // CHUNK_TILES
    parts = [(n, i) for n in range(len(places)) for i in range(CHUNK_TILES)]

    def copies(n, i):
        t, at = places[n]
        part = pl.ds(i * tile, tile)
        held = buf.at[n, part]
        load = pltpu.make_async_copy(source.at[t, part, pl.ds(at, cols)], held, sem.at[0, n, i])
        return load, pltpu.make_async_copy(held, outs[n].at[part], sem.at[1, n, i])

    for n, i in parts:
        copies(n, i)[0].start()
    for n, i in parts:
        load, store = copies(n, i)
        load.wait()
        store.start()
    for n, i in parts:
        copies(n, i)[1].wait()


def pass_kernel(source, after, out):
    del source, after, out


def relay_plan(devices, chunks):
    if devices != 16 or chunks != 4:
        return []
    plan = []
    for z, chunk, alone in ((1, 0, True), (0, 0, False), (2, 1, False)):
        high, low = 4 * z + 3, 4 * z + 4
        plan.append((chunk, alone, [(high, low, 0), (low, high, devices - 1)]))
    return plan


def spec(space):
    return pl.BlockSpec(memory_space=space)


def on_device(fitted, fit_start, virt_domain, occ_energy, virt_energy, pair_partner):
    owned, aux, width = fitted.shape
    devices = lax.axis_size("row")
    buf_rows = 2 * REACH + aux
    wide_rows = aux + 2 * SUB + STEP
    smem, vmem, anywhere = spec(pltpu.SMEM), spec(pltpu.VMEM), spec(pl.ANY)

    outward = []
    for i in range(devices):
        to = i + 1 if i % 2 else i - 1
        if 0 <= to < devices:
            outward.append((i, to))
    inward = [(i, i ^ 1) for i in range(devices) if i ^ 1 < devices]

    def in_hbm(array):
        return pltpu.with_memory_space_constraint(array, pltpu.HBM)

    def in_vmem(array):
        return pltpu.with_memory_space_constraint(array, pltpu.VMEM)

    def chunks(places, *after):
        return pl.pallas_call(
            functools.partial(copy_kernel, places=places),
            out_shape=[jax.ShapeDtypeStruct((aux, COLS), fitted.dtype)] * len(places),
            in_specs=[anywhere] * (1 + len(after)),
            out_specs=[anywhere] * len(places),
            scratch_shapes=[
                pltpu.VMEM((len(places), aux, COLS), fitted.dtype),
                pltpu.SemaphoreType.DMA((2, len(places), CHUNK_TILES)),
            ],
            compiler_params=pltpu.CompilerParams(vmem_limit_bytes=CHUNK_VMEM),
            name="chunks",
        )(in_hbm(fitted), *after)

    def pass_on(block, after):
        return pl.pallas_call(
            pass_kernel,
            out_shape=jax.ShapeDtypeStruct(block.shape, block.dtype),
            in_specs=[anywhere] * 2,
            out_specs=anywhere,
            input_output_aliases={0: 0},
            compiler_params=pltpu.CompilerParams(vmem_limit_bytes=CHUNK_VMEM),
            name="pass_on",
        )(block, after)

    cells = [(t, at) for t in range(owned) for at in range(0, width, COLS)]
    last = len(cells) - 1
    plan = relay_plan(devices, len(cells))
    first_hops = [[(source, by) for source, _, by in pairs] for _, _, pairs in plan]
    second_hops = [[(by, to) for _, to, by in pairs] for _, _, pairs in plan]

    def exchange(number, block):
        pairs = list(outward)
        for (at, alone, group), hop in zip(plan, first_hops):
            if at == number:
                pairs = [pair for pair in pairs if pair not in {(a, b) for a, b, _ in group}]
                pairs += [] if alone else hop
        return lax.ppermute(block, "row", pairs)

    sent = list(chunks(cells[:1]))
    mate = lax.ppermute(lax.optimization_barrier((fitted, sent[0]))[0], "row", inward)
    far = [exchange(0, sent[0])]
    rest = chunks(cells[1:] + cells[:1] * bool(plan), sent[0])
    sent += rest[:last]
    early = {
        index: lax.ppermute(rest[last], "row", first_hops[index])
        for index, (_, alone, _) in enumerate(plan)
        if alone
    }
    far += [exchange(number, sent[number]) for number in range(1, last + 1)]

    unit = 4 * aux * width * COLS
    acc_shape = pltpu.VMEM((owned, aux, width), jnp.float32)
    dens_shape = pltpu.VMEM((owned, width, width), jnp.float32)
    ft_shape = pltpu.VMEM((owned, width, aux), fitted.dtype)
    token_shape = jax.ShapeDtypeStruct((8, LANES), jnp.int32)
    slots = 3 * owned * owned

    def cost(blocks):
        return pl.CostEstimate(
            flops=100 * unit * blocks * owned, bytes_accessed=8 << 20, transcendentals=0
        )

    ints, occ, eps_col, eps_row, acc, dens, ft, token = pl.pallas_call(
        functools.partial(
            first_kernel,
            devices=devices,
            targets=[[to for _, to, _ in pairs] for _, _, pairs in plan],
            relays=sorted({by for _, _, pairs in plan for _, _, by in pairs}),
        ),
        out_shape=(
            jax.ShapeDtypeStruct((Plan(None, owned).at_late(len(plan)) + 1,), jnp.int32),
            jax.ShapeDtypeStruct((slots,), jnp.float32),
            pltpu.VMEM((owned, width, 1), jnp.float32),
            pltpu.VMEM((3 * owned, 1, width), jnp.float32),
            acc_shape,
            dens_shape,
            ft_shape,
            token_shape,
        ),
        in_specs=[smem] * 3 + [vmem] * 3 + [anywhere],
        out_specs=(smem,) * 2 + (vmem,) * 6,
        scratch_shapes=[
            pltpu.VMEM((wide_rows, width), jnp.float32),
            pltpu.VMEM((buf_rows, width), fitted.dtype),
            pltpu.VMEM((width, width), fitted.dtype),
        ],
        compiler_params=pltpu.CompilerParams(vmem_limit_bytes=NEAR_VMEM),
        cost_estimate=cost(len(cells)),
        name="first",
    )(
        fit_start, occ_energy, pair_partner, virt_domain, virt_energy.reshape(-1, 1),
        in_hbm(fitted), sent[last - 1],
    )
    state = {"acc": acc, "dens": dens, "token": token}
    hops = []

    def add_pairs(
        kernel, block_specs, blocks, cols, limit, name,
        extra=(), outs=(), aliases={}, scratch=(), token=True,
    ):
        specs = [smem] * 2 + [vmem] * 5 + block_specs
        results = pl.pallas_call(
            kernel,
            out_shape=(acc_shape, dens_shape) + (token_shape,) * token + tuple(outs),
            in_specs=specs + [anywhere] * (1 + len(extra)),
            out_specs=(vmem,) * (2 + token) + (anywhere,) * len(outs),
            input_output_aliases={5: 0, 6: 1, **aliases},
            scratch_shapes=[
                pltpu.VMEM((wide_rows, cols), jnp.float32),
                pltpu.VMEM((buf_rows, cols), fitted.dtype),
                *scratch,
            ],
            compiler_params=pltpu.CompilerParams(vmem_limit_bytes=limit),
            cost_estimate=cost(cols // COLS),
            name=name,
        )(
            ints, occ, in_vmem(eps_col), in_vmem(eps_row), in_vmem(ft), in_vmem(state["acc"]),
            in_vmem(state["dens"]), *blocks, *extra, state["token"],
        )
        state.update(acc=results[0], dens=results[1], token=results[2])
        return results[2 + token :]

    hops = {index: lax.ppermute(early[index], "row", second_hops[index]) for index in early}
    turned_cols = (pltpu.VMEM((COLS, width), fitted.dtype),)

    def near_pairs(late, *extra):
        add_pairs(
            functools.partial(near_kernel, ways=len(plan), late=late),
            [anywhere] * 2, [in_hbm(fitted), mate], width, NEAR_VMEM, f"near_pairs_{late}",
            extra=extra,
            scratch=(
                pltpu.VMEM((width, width), fitted.dtype),
                pltpu.VMEM((2, aux, width), fitted.dtype),
                pltpu.SemaphoreType.DMA((2,)),
            ),
        )

    near_pairs(0, *early.values())
    for number in range(last):
        for index, (at, alone, _) in enumerate(plan):
            if at == number and not alone:
                far[number] = state["token"] = pass_on(far[number], state["token"])
                hops[index] = lax.ppermute(far[number], "row", second_hops[index])
                if index == len(plan) - 1:
                    near_pairs(1)
        ways = [index for index, (at, _, _) in enumerate(plan) if at == number]
        add_pairs(
            functools.partial(far_kernel, ways=ways, cell=cells[number]),
            [vmem], [far[number]], COLS, FAR_VMEM, f"far_pairs_{number}", scratch=turned_cols,
        )
    results = (
        jax.ShapeDtypeStruct(fitted.shape, fitted.dtype),
        jax.ShapeDtypeStruct((owned, width, width), jnp.float32),
    )
    out_scratch = (
        pltpu.VMEM((owned, aux, width), fitted.dtype),
        pltpu.SemaphoreType.DMA((owned, ROW_TILES + 1)),
    )
    ready = add_pairs(
        functools.partial(
            relayed_kernel, cells=[cells[at] for at, _, _ in plan], last=cells[last][0]
        ),
        [anywhere] * len(hops), [hops[index] for index in range(len(plan))], COLS, FAR_VMEM,
        "relayed_pairs",
        outs=results,
        scratch=turned_cols
        + (pltpu.VMEM((aux, COLS), fitted.dtype), out_scratch[0], pltpu.SemaphoreType.DMA)
        + out_scratch[1:],
    )
    gradient, density = add_pairs(
        functools.partial(last_kernel, cell=cells[last]),
        [anywhere] * 3, [far[last], *ready], COLS, FAR_VMEM, "last_pairs",
        outs=results,
        aliases={8: 2, 9: 3},
        scratch=turned_cols
        + (pltpu.VMEM((aux, COLS), fitted.dtype),)
        + out_scratch
        + (pltpu.SemaphoreType.DMA((LOAD_TILES,)),),
        token=False,
    )
    return gradient, density


def solution(mesh):
    placed = (
        P(("parts", "row"), None, None),
        P("parts"),
        P("parts", None),
        P("parts"),
        P("parts"),
        P("parts"),
    )
    return jax.shard_map(
        on_device,
        mesh=mesh,
        in_specs=placed,
        out_specs=(P(("parts", "row"), None, None), P(("parts", "row"), None, None)),
        check_vma=False,
    )
```

```python
import functools

import jax
import jax.numpy as jnp
from jax import lax
from jax.experimental import pallas as pl
from jax.experimental.pallas import tpu as pltpu
from jax.sharding import PartitionSpec as P

SUB = 16
STEP = 8
LANES = 128
ROW_TILES = 2
LOAD_TILES = 4
CHUNK_TILES = 2
COLS = 256
REACH = 1024
NEAR_VMEM = 22 * 1024 * 1024
FAR_VMEM = 16 * 1024 * 1024
CHUNK_VMEM = 6 * 1024 * 1024


class Plan:
    def __init__(self, ref, owned):
        self.ref, self.owned = ref, owned
        self.slots = 3 * owned * owned

    def slot(self, group, s, t):
        return (group * self.owned + s) * self.owned + t

    def at_shift(self, slot):
        return self.slots + slot

    def at_lead(self, slot):
        return 2 * self.slots + slot

    def at_way(self, number):
        return 3 * self.slots + number

    def at_late(self, ways):
        return self.at_way(ways)

    def at_flip(self, ways):
        return self.at_way(ways) + 1

    def count(self, slot):
        return self.ref[slot]

    def offset(self, slot):
        return pl.multiple_of(REACH + self.ref[self.at_shift(slot)], SUB)

    def lead(self, slot):
        return self.ref[self.at_lead(slot)]

    def way(self, number):
        return self.ref[self.at_way(number)]


def dot(a, b):
    return jnp.dot(a, b, preferred_element_type=jnp.float32)


def tile_of(rows):
    return max(n for n in range(SUB, 705, SUB) if rows % n == 0)


def rows_from(load, start, count):
    skip = start % STEP
    base = pl.multiple_of(start - skip, STEP)
    block = load(base, count + STEP)
    width = block.shape[1]
    block = block.reshape(count // STEP + 1, STEP, width)
    turned = pltpu.roll(block, (STEP - skip) % STEP, 1)
    row = lax.broadcasted_iota(jnp.int32, (count // STEP, STEP, width), 1)
    return jnp.where(row < STEP - skip, turned[:-1], turned[1:]).reshape(count, width)


def clear_margins(buf, rows):
    width = buf.shape[1]
    buf[:REACH, :] = jnp.zeros((REACH, width), buf.dtype)
    buf[REACH + rows :, :] = jnp.zeros((buf.shape[0] - REACH - rows, width), buf.dtype)


def clear_ends(wide):
    rows, width = wide.shape
    wide[:SUB, :] = jnp.zeros((SUB, width), jnp.float32)
    wide[rows - SUB - STEP :, :] = jnp.zeros((SUB + STEP, width), jnp.float32)


def widen(source, wide):
    aux = source.shape[0]
    clear_ends(wide)
    tile = aux // ROW_TILES

    def one(i, carry):
        base = pl.multiple_of(i * tile, SUB)
        wide[pl.ds(pl.multiple_of(SUB + base, SUB), tile), :] = source[
            pl.ds(base, tile), :
        ].astype(jnp.float32)
        return carry

    lax.fori_loop(0, ROW_TILES, one, 0)


def place(lead, wide, buf):
    rows = wide.shape[0] - SUB - STEP
    step = tile_of(rows)

    def move(i, carry):
        base = pl.multiple_of(i * step, SUB)
        moved = rows_from(lambda at, n: wide[pl.ds(at, n), :], SUB - lead + base, step)
        buf[pl.ds(pl.multiple_of(REACH + base, SUB), step), :] = moved.astype(buf.dtype)
        return carry

    lax.fori_loop(0, rows // step, move, 0)


def amplitudes(coulomb, denominator, weight):
    amplitude = (coulomb / denominator).astype(jnp.bfloat16)
    weighted = (amplitude.astype(jnp.float32) * weight).astype(jnp.bfloat16)
    return amplitude, weighted.T


def needed(plan, group, t):
    total = jnp.int32(0)
    for s in range(plan.owned):
        total = total + plan.count(plan.slot(group, s, t))
    return total != 0


def amplitude_of(plan, occ, slot, s, partner, at, eps_col, eps_row, ft, buf):
    rows = ft.shape[2]
    cols = buf.shape[1]
    coulomb = dot(ft[s], buf[pl.ds(plan.offset(slot), rows), :])
    denominator = occ[slot] - eps_col[s] - eps_row[partner, :, pl.ds(at, cols)]
    return amplitudes(coulomb, denominator, plan.count(slot).astype(jnp.float32))


def add_block(plan, occ, group, t, at, eps_col, eps_row, ft, source, wide, buf, acc, dens, turned):
    owned, rows, width = acc.shape
    scale = float(width) ** -0.5
    step = rows // ROW_TILES

    @pl.when(needed(plan, group, t))
    def _():
        widen(source, wide)

    def one(s, carry):
        slot = plan.slot(group, s, t)

        @pl.when(plan.count(slot) != 0)
        def _():
            place(plan.lead(slot), wide, buf)
            amplitude, turned[...] = amplitude_of(
                plan, occ, slot, s, group * owned + t, at, eps_col, eps_row, ft, buf
            )
            dens[s] += scale * dot(amplitude, turned[...])

            def add(i, inner):
                base = pl.multiple_of(i * step, SUB)
                block = buf[pl.ds(pl.multiple_of(plan.offset(slot) + base, SUB), step), :]
                acc[s, pl.ds(base, step), :] += dot(block, turned[...])
                return inner

            lax.fori_loop(0, ROW_TILES, add, 0)

        return carry

    lax.fori_loop(0, owned, one, 0)


def near_pairs_of(position, pair_partner, owned, devices):
    pairs_here = pair_partner.shape[0] // devices
    pairs = []
    for step in (-1, 0, 1):
        group = position + step
        known = (group >= 0) & (group < devices)
        held = jnp.clip(group, 0, devices - 1)
        for n in range(pairs_here):
            pairs.append((known, group * owned + n % owned, pair_partner[held * pairs_here + n]))
    return pairs


def count_between(pairs, one, other):
    total = jnp.int32(0)
    for known, first, second in pairs:
        forth = known & (first == one) & (second == other)
        back = known & (second == one) & (first == other)
        total = total + forth.astype(jnp.int32) + back.astype(jnp.int32)
    return total


def flip_of(used):
    return (used[0] < used[-1]).astype(jnp.int32)


def cell_of(cells, number, flip):
    halves = len([cell for cell in cells if cell[0] == 0])
    flipped = cells[:1] + cells[halves:] + cells[1:halves]
    (t, at), (other_t, other_at) = cells[number], flipped[number]
    if (t, at) == (other_t, other_at):
        return t, at
    return (
        jnp.where(flip == 1, other_t, t),
        pl.multiple_of(jnp.where(flip == 1, other_at, at), COLS),
    )


def make_plan(
    fit_start, occ_energy, pair_partner, domains, energy, ints, occ, eps_col, eps_row,
    *, devices, targets, relays,
):
    owned, width = eps_col.shape[:2]
    orbitals = fit_start.shape[0]
    plan = Plan(ints, owned)
    position = lax.axis_index("row")
    side = jnp.where(position % 2 == 1, 1, -1)
    places = [
        base * owned + t
        for base in (position, position - side, position + side)
        for t in range(owned)
    ]
    inside = [jnp.clip(orbital, 0, orbitals - 1) for orbital in places]
    starts = [fit_start[orbital] for orbital in inside]
    pairs = near_pairs_of(position, pair_partner, owned, devices)
    used = [jnp.int32(0)] * owned
    for group in range(3):
        for s in range(owned):
            for t in range(owned):
                slot = plan.slot(group, s, t)
                other = group * owned + t
                total = count_between(pairs, places[s], places[other])
                ints[slot] = total
                if group == 2:
                    used[t] = used[t] + (total != 0).astype(jnp.int32)
                apart = starts[other] - starts[s]
                ints[plan.at_shift(slot)] = (apart & (SUB - 1)) - apart
                ints[plan.at_lead(slot)] = apart & (SUB - 1)
                occ[slot] = occ_energy[inside[s]] + occ_energy[inside[other]]
    for number, group in enumerate(targets):
        way = jnp.int32(0)
        for to in group:
            way = jnp.where(position == to, 1, way)
        ints[plan.at_way(number)] = way
    late = jnp.int32(0)
    for row in relays:
        late = jnp.where(position == row, 1, late)
    ints[plan.at_late(len(targets))] = late
    ints[plan.at_flip(len(targets))] = flip_of(used)
    entries = energy.shape[0]
    table = lax.broadcasted_iota(jnp.int32, (entries, width), 0)
    for n, orbital in enumerate(inside):
        domain = domains[pl.ds(orbital, 1), :]
        row = jnp.sum(jnp.where(table == domain, energy[...], 0.0), axis=0, keepdims=True)
        eps_row[n] = row
        if n < owned:
            eps_col[n] = jnp.broadcast_to(row, (LANES, width)).T[:, :1]
    return plan


def add_blocks(plan, occ, sources, eps_col, eps_row, ft, wide, buf, acc, dens, turned, raw, sem):
    copies = [
        pltpu.make_async_copy(block, raw.at[n % 2], sem.at[n % 2])
        for n, (_, _, block) in enumerate(sources)
    ]
    copies[0].start()
    clear_margins(buf, raw.shape[1] + SUB)
    for n, (group, t, _) in enumerate(sources):
        if n + 1 < len(copies):
            copies[n + 1].start()
        copies[n].wait()
        add_block(
            plan, occ, group, t, 0, eps_col, eps_row, ft, raw.at[n % 2], wide, buf, acc, dens, turned
        )


def first_kernel(
    fit_start, occ_energy, pair_partner, domains, energy, own, after,
    ints, occ, eps_col, eps_row, acc, dens, ft, token, wide, buf, turned,
    *, devices, targets, relays,
):
    del after
    token[...] = jnp.zeros_like(token)
    plan = make_plan(
        fit_start, occ_energy, pair_partner, domains, energy, ints, occ, eps_col, eps_row,
        devices=devices, targets=targets, relays=relays,
    )
    owned, aux, width = own.shape
    acc[...] = jnp.zeros_like(acc)
    dens[...] = jnp.zeros_like(dens)
    for t in range(owned):

        def turn(i, carry):
            at = pl.multiple_of(i * LANES, LANES)
            ft[t, :, pl.ds(at, LANES)] = own[t, pl.ds(at, LANES), :].T
            return carry

        lax.fori_loop(0, aux // LANES, turn, 0)

    @pl.when(ints[plan.at_late(len(targets))] == 1)
    def _():
        clear_margins(buf, aux + SUB)
        for t in range(owned):
            add_block(
                plan, occ, 0, t, 0, eps_col, eps_row, ft, own.at[t], wide, buf, acc, dens, turned
            )


def near_kernel(
    ints, occ, eps_col, eps_row, ft, acc_in, dens_in, own, mate, *refs, ways, late
):
    del acc_in, dens_in
    acc, dens, token, wide, buf, turned, raw, sem = refs[-8:]
    token[...] = jnp.zeros_like(token)
    owned = own.shape[0]
    plan = Plan(ints, owned)
    groups = ((1, mate),) if late else ((0, own), (1, mate))
    sources = [(group, t, blocks.at[t]) for group, blocks in groups for t in range(owned)]

    @pl.when(ints[plan.at_late(ways)] == late)
    def _():
        add_blocks(
            plan, occ, sources, eps_col, eps_row, ft, wide, buf, acc, dens, turned, raw, sem
        )


def far_kernel(
    ints, occ, eps_col, eps_row, ft, acc_in, dens_in, block, after,
    acc, dens, token, wide, buf, turned, *, ways, total_ways, cells, number,
):
    del acc_in, dens_in, after
    token[...] = jnp.zeros_like(token)
    plan = Plan(ints, acc.shape[0])
    t, at = cell_of(cells, number, ints[plan.at_flip(total_ways)])
    here = needed(plan, 2, t)
    for way in ways:
        here = here & (plan.way(way) == 0)

    @pl.when(here)
    def _():
        clear_margins(buf, block.shape[0] + SUB)
        add_block(plan, occ, 2, t, at, eps_col, eps_row, ft, block, wide, buf, acc, dens, turned)


def send_out(s, tile_of_rows, dens, ready, out, dens_out, sem):
    step = out.shape[1] // ROW_TILES
    pltpu.make_async_copy(dens.at[s], dens_out.at[s], sem.at[s, ROW_TILES]).start()

    def one(i, carry):
        part = pl.ds(pl.multiple_of(i * step, SUB), step)
        ready[s, part, :] = tile_of_rows(i * step, step).astype(ready.dtype)
        pltpu.make_async_copy(ready.at[s, part], out.at[s, part], sem.at[s, i]).start()
        return carry

    lax.fori_loop(0, ROW_TILES, one, 0)


def wait_out(s, dens, ready, out, dens_out, sem):
    step = out.shape[1] // ROW_TILES
    pltpu.make_async_copy(dens.at[s], dens_out.at[s], sem.at[s, ROW_TILES]).wait()
    for i in range(ROW_TILES):
        part = pl.ds(i * step, step)
        pltpu.make_async_copy(ready.at[s, part], out.at[s, part], sem.at[s, i]).wait()


def relayed_kernel(
    ints, occ, eps_col, eps_row, ft, acc_in, dens_in, *refs, numbers, cells
):
    del acc_in, dens_in
    *blocks, _, acc, dens, token, out, dens_out, wide, buf, turned, raw, ready, sem, out_sem = refs
    token[...] = jnp.zeros_like(token)
    owned = acc.shape[0]
    plan = Plan(ints, owned)
    flip = ints[plan.at_flip(len(numbers))]
    last, _ = cell_of(cells, len(cells) - 1, flip)
    for way, (block, number) in enumerate(zip(blocks, numbers)):
        t, at = cell_of(cells, number, flip)

        @pl.when(needed(plan, 2, t) & (plan.way(way) == 1))
        def _():
            copy = pltpu.make_async_copy(block, raw, sem)
            copy.start()
            clear_margins(buf, raw.shape[0] + SUB)
            copy.wait()
            add_block(plan, occ, 2, t, at, eps_col, eps_row, ft, raw, wide, buf, acc, dens, turned)

    for s in range(owned):

        @pl.when(plan.count(plan.slot(2, s, last)) == 0)
        def _():
            send_out(
                s,
                lambda base, n: acc[s, pl.ds(pl.multiple_of(base, SUB), n), :],
                dens, ready, out, dens_out, out_sem,
            )

    for s in range(owned):

        @pl.when(plan.count(plan.slot(2, s, last)) == 0)
        def _():
            wait_out(s, dens, ready, out, dens_out, out_sem)


def last_kernel(
    ints, occ, eps_col, eps_row, ft, acc_in, dens_in, block, out_in, dens_out_in, after,
    acc, dens, out, dens_out, wide, buf, turned, raw, ready, sem, raw_sem, *, total_ways, cells,
):
    del acc_in, dens_in, out_in, dens_out_in, after
    owned, aux, width = out.shape
    plan = Plan(ints, owned)
    t, at = cell_of(cells, len(cells) - 1, ints[plan.at_flip(total_ways)])
    scale = float(width) ** -0.5

    @pl.when(needed(plan, 2, t))
    def _():
        step = aux // LOAD_TILES
        parts = [pl.ds(i * step, step) for i in range(LOAD_TILES)]
        loads = [
            pltpu.make_async_copy(block.at[part], raw.at[part], raw_sem.at[i])
            for i, part in enumerate(parts)
        ]
        for load in loads:
            load.start()
        clear_margins(buf, aux + SUB)
        clear_ends(wide)
        for i, load in enumerate(loads):
            load.wait()
            wide[SUB + i * step : SUB + (i + 1) * step, :] = raw[parts[i], :].astype(jnp.float32)

    def one(s, carry):
        slot = plan.slot(2, s, t)

        @pl.when(plan.count(slot) != 0)
        def _():
            place(plan.lead(slot), wide, buf)
            amplitude, turned[...] = amplitude_of(
                plan, occ, slot, s, 2 * owned + t, at, eps_col, eps_row, ft, buf
            )
            dens[s] += scale * dot(amplitude, turned[...])

            def total(base, n):
                rows = buf[pl.ds(pl.multiple_of(plan.offset(slot) + base, SUB), n), :]
                return acc[s, pl.ds(pl.multiple_of(base, SUB), n), :] + dot(rows, turned[...])

            send_out(s, total, dens, ready, out, dens_out, sem)

        return carry

    lax.fori_loop(0, owned, one, 0)
    for s in range(owned):

        @pl.when(plan.count(plan.slot(2, s, t)) != 0)
        def _():
            wait_out(s, dens, ready, out, dens_out, sem)


def copy_kernel(pair_partner, source, *refs, numbers, cells, devices):
    *outs, buf, sem = refs[-len(numbers) - 2 :]
    owned = source.shape[0]
    flip = jnp.int32(0)
    if any(numbers):
        position = lax.axis_index("row")
        pairs = near_pairs_of(position, pair_partner, owned, devices)
        beyond = position + jnp.where(position % 2 == 1, 1, -1)
        used = []
        for t in range(owned):
            total = jnp.int32(0)
            for s in range(owned):
                count = count_between(pairs, position * owned + t, beyond * owned + s)
                total = total + (count != 0).astype(jnp.int32)
            used.append(total)
        flip = flip_of(used)
    places = [cell_of(cells, number, flip) for number in numbers]
    rows, cols = outs[0].shape
    tile = rows // CHUNK_TILES
    parts = [(n, i) for n in range(len(places)) for i in range(CHUNK_TILES)]

    def copies(n, i):
        t, at = places[n]
        part = pl.ds(i * tile, tile)
        held = buf.at[n, part]
        load = pltpu.make_async_copy(source.at[t, part, pl.ds(at, cols)], held, sem.at[0, n, i])
        return load, pltpu.make_async_copy(held, outs[n].at[part], sem.at[1, n, i])

    for n, i in parts:
        copies(n, i)[0].start()
    for n, i in parts:
        load, store = copies(n, i)
        load.wait()
        store.start()
    for n, i in parts:
        copies(n, i)[1].wait()


def pass_kernel(source, after, out):
    del source, after, out


def relay_plan(devices, chunks):
    if devices != 16 or chunks != 4:
        return []
    plan = []
    for z, chunk, alone in ((1, 0, True), (0, 0, False), (2, 1, False)):
        high, low = 4 * z + 3, 4 * z + 4
        plan.append((chunk, alone, [(high, low, 0), (low, high, devices - 1)]))
    return plan


def spec(space):
    return pl.BlockSpec(memory_space=space)


def on_device(fitted, fit_start, virt_domain, occ_energy, virt_energy, pair_partner):
    owned, aux, width = fitted.shape
    devices = lax.axis_size("row")
    buf_rows = 2 * REACH + aux
    wide_rows = aux + 2 * SUB + STEP
    smem, vmem, anywhere = spec(pltpu.SMEM), spec(pltpu.VMEM), spec(pl.ANY)

    outward = []
    for i in range(devices):
        to = i + 1 if i % 2 else i - 1
        if 0 <= to < devices:
            outward.append((i, to))
    inward = [(i, i ^ 1) for i in range(devices) if i ^ 1 < devices]

    def in_hbm(array):
        return pltpu.with_memory_space_constraint(array, pltpu.HBM)

    def in_vmem(array):
        return pltpu.with_memory_space_constraint(array, pltpu.VMEM)

    def chunks(numbers, *after):
        return pl.pallas_call(
            functools.partial(copy_kernel, numbers=numbers, cells=cells, devices=devices),
            out_shape=[jax.ShapeDtypeStruct((aux, COLS), fitted.dtype)] * len(numbers),
            in_specs=[smem] + [anywhere] * (1 + len(after)),
            out_specs=[anywhere] * len(numbers),
            scratch_shapes=[
                pltpu.VMEM((len(numbers), aux, COLS), fitted.dtype),
                pltpu.SemaphoreType.DMA((2, len(numbers), CHUNK_TILES)),
            ],
            compiler_params=pltpu.CompilerParams(vmem_limit_bytes=CHUNK_VMEM),
            name="chunks",
        )(pair_partner, in_hbm(fitted), *after)

    def pass_on(block, after):
        return pl.pallas_call(
            pass_kernel,
            out_shape=jax.ShapeDtypeStruct(block.shape, block.dtype),
            in_specs=[anywhere] * 2,
            out_specs=anywhere,
            input_output_aliases={0: 0},
            compiler_params=pltpu.CompilerParams(vmem_limit_bytes=CHUNK_VMEM),
            name="pass_on",
        )(block, after)

    cells = [(t, at) for t in range(owned) for at in range(0, width, COLS)]
    last = len(cells) - 1
    plan = relay_plan(devices, len(cells))
    first_hops = [[(source, by) for source, _, by in pairs] for _, _, pairs in plan]
    second_hops = [[(by, to) for _, to, by in pairs] for _, _, pairs in plan]

    def exchange(number, block):
        pairs = list(outward)
        for (at, alone, group), hop in zip(plan, first_hops):
            if at == number:
                pairs = [pair for pair in pairs if pair not in {(a, b) for a, b, _ in group}]
                pairs += [] if alone else hop
        return lax.ppermute(block, "row", pairs)

    sent = list(chunks([0]))
    mate = lax.ppermute(lax.optimization_barrier((fitted, sent[0]))[0], "row", inward)
    far = [exchange(0, sent[0])]
    rest = chunks(list(range(1, len(cells))) + [0] * bool(plan), sent[0])
    sent += rest[:last]
    early = {
        index: lax.ppermute(rest[last], "row", first_hops[index])
        for index, (_, alone, _) in enumerate(plan)
        if alone
    }
    far += [exchange(number, sent[number]) for number in range(1, last + 1)]

    unit = 4 * aux * width * COLS
    acc_shape = pltpu.VMEM((owned, aux, width), jnp.float32)
    dens_shape = pltpu.VMEM((owned, width, width), jnp.float32)
    ft_shape = pltpu.VMEM((owned, width, aux), fitted.dtype)
    token_shape = jax.ShapeDtypeStruct((8, LANES), jnp.int32)
    slots = 3 * owned * owned

    def cost(blocks):
        return pl.CostEstimate(
            flops=100 * unit * blocks * owned, bytes_accessed=8 << 20, transcendentals=0
        )

    ints, occ, eps_col, eps_row, acc, dens, ft, token = pl.pallas_call(
        functools.partial(
            first_kernel,
            devices=devices,
            targets=[[to for _, to, _ in pairs] for _, _, pairs in plan],
            relays=sorted({by for _, _, pairs in plan for _, _, by in pairs}),
        ),
        out_shape=(
            jax.ShapeDtypeStruct((Plan(None, owned).at_flip(len(plan)) + 1,), jnp.int32),
            jax.ShapeDtypeStruct((slots,), jnp.float32),
            pltpu.VMEM((owned, width, 1), jnp.float32),
            pltpu.VMEM((3 * owned, 1, width), jnp.float32),
            acc_shape,
            dens_shape,
            ft_shape,
            token_shape,
        ),
        in_specs=[smem] * 3 + [vmem] * 3 + [anywhere],
        out_specs=(smem,) * 2 + (vmem,) * 6,
        scratch_shapes=[
            pltpu.VMEM((wide_rows, width), jnp.float32),
            pltpu.VMEM((buf_rows, width), fitted.dtype),
            pltpu.VMEM((width, width), fitted.dtype),
        ],
        compiler_params=pltpu.CompilerParams(vmem_limit_bytes=NEAR_VMEM),
        cost_estimate=cost(len(cells)),
        name="first",
    )(
        fit_start, occ_energy, pair_partner, virt_domain, virt_energy.reshape(-1, 1),
        in_hbm(fitted), sent[last - 1],
    )
    state = {"acc": acc, "dens": dens, "token": token}
    hops = []

    def add_pairs(
        kernel, block_specs, blocks, cols, limit, name,
        extra=(), outs=(), aliases={}, scratch=(), token=True,
    ):
        specs = [smem] * 2 + [vmem] * 5 + block_specs
        results = pl.pallas_call(
            kernel,
            out_shape=(acc_shape, dens_shape) + (token_shape,) * token + tuple(outs),
            in_specs=specs + [anywhere] * (1 + len(extra)),
            out_specs=(vmem,) * (2 + token) + (anywhere,) * len(outs),
            input_output_aliases={5: 0, 6: 1, **aliases},
            scratch_shapes=[
                pltpu.VMEM((wide_rows, cols), jnp.float32),
                pltpu.VMEM((buf_rows, cols), fitted.dtype),
                *scratch,
            ],
            compiler_params=pltpu.CompilerParams(vmem_limit_bytes=limit),
            cost_estimate=cost(cols // COLS),
            name=name,
        )(
            ints, occ, in_vmem(eps_col), in_vmem(eps_row), in_vmem(ft), in_vmem(state["acc"]),
            in_vmem(state["dens"]), *blocks, *extra, state["token"],
        )
        state.update(acc=results[0], dens=results[1], token=results[2])
        return results[2 + token :]

    hops = {index: lax.ppermute(early[index], "row", second_hops[index]) for index in early}
    turned_cols = (pltpu.VMEM((COLS, width), fitted.dtype),)

    def near_pairs(late, *extra):
        add_pairs(
            functools.partial(near_kernel, ways=len(plan), late=late),
            [anywhere] * 2, [in_hbm(fitted), mate], width, NEAR_VMEM, f"near_pairs_{late}",
            extra=extra,
            scratch=(
                pltpu.VMEM((width, width), fitted.dtype),
                pltpu.VMEM((2, aux, width), fitted.dtype),
                pltpu.SemaphoreType.DMA((2,)),
            ),
        )

    near_pairs(0, *early.values())
    for number in range(last):
        for index, (at, alone, _) in enumerate(plan):
            if at == number and not alone:
                far[number] = state["token"] = pass_on(far[number], state["token"])
                hops[index] = lax.ppermute(far[number], "row", second_hops[index])
                if index == len(plan) - 1:
                    near_pairs(1)
        ways = [index for index, (at, _, _) in enumerate(plan) if at == number]
        add_pairs(
            functools.partial(
                far_kernel, ways=ways, total_ways=len(plan), cells=cells, number=number
            ),
            [vmem], [far[number]], COLS, FAR_VMEM, f"far_pairs_{number}", scratch=turned_cols,
        )
    results = (
        jax.ShapeDtypeStruct(fitted.shape, fitted.dtype),
        jax.ShapeDtypeStruct((owned, width, width), jnp.float32),
    )
    out_scratch = (
        pltpu.VMEM((owned, aux, width), fitted.dtype),
        pltpu.SemaphoreType.DMA((owned, ROW_TILES + 1)),
    )
    ready = add_pairs(
        functools.partial(
            relayed_kernel, numbers=[at for at, _, _ in plan], cells=cells
        ),
        [anywhere] * len(hops), [hops[index] for index in range(len(plan))], COLS, FAR_VMEM,
        "relayed_pairs",
        outs=results,
        scratch=turned_cols
        + (pltpu.VMEM((aux, COLS), fitted.dtype), out_scratch[0], pltpu.SemaphoreType.DMA)
        + out_scratch[1:],
    )
    gradient, density = add_pairs(
        functools.partial(last_kernel, total_ways=len(plan), cells=cells),
        [anywhere] * 3, [far[last], *ready], COLS, FAR_VMEM, "last_pairs",
        outs=results,
        aliases={8: 2, 9: 3},
        scratch=turned_cols
        + (pltpu.VMEM((aux, COLS), fitted.dtype),)
        + out_scratch
        + (pltpu.SemaphoreType.DMA((LOAD_TILES,)),),
        token=False,
    )
    return gradient, density


def solution(mesh):
    placed = (
        P(("parts", "row"), None, None),
        P("parts"),
        P("parts", None),
        P("parts"),
        P("parts"),
        P("parts"),
    )
    return jax.shard_map(
        on_device,
        mesh=mesh,
        in_specs=placed,
        out_specs=(P(("parts", "row"), None, None), P(("parts", "row"), None, None)),
        check_vma=False,
    )
```

```python
import functools

import jax
import jax.numpy as jnp
from jax import lax
from jax.experimental import pallas as pl
from jax.experimental.pallas import tpu as pltpu
from jax.sharding import PartitionSpec as P

SUB = 16
STEP = 8
LANES = 128
ROW_TILES = 2
OUT_TILES = 4
LOAD_TILES = 4
CHUNK_TILES = 2
COLS = 256
REACH = 1024
NEAR_VMEM = 22 * 1024 * 1024
FAR_VMEM = 16 * 1024 * 1024
CHUNK_VMEM = 6 * 1024 * 1024


class Plan:
    def __init__(self, ref, owned):
        self.ref, self.owned = ref, owned
        self.slots = 3 * owned * owned

    def slot(self, group, s, t):
        return (group * self.owned + s) * self.owned + t

    def at_shift(self, slot):
        return self.slots + slot

    def at_lead(self, slot):
        return 2 * self.slots + slot

    def at_way(self, number):
        return 3 * self.slots + number

    def at_late(self, ways):
        return self.at_way(ways)

    def at_flip(self, ways):
        return self.at_way(ways) + 1

    def count(self, slot):
        return self.ref[slot]

    def offset(self, slot):
        return pl.multiple_of(REACH + self.ref[self.at_shift(slot)], SUB)

    def lead(self, slot):
        return self.ref[self.at_lead(slot)]

    def way(self, number):
        return self.ref[self.at_way(number)]


def dot(a, b):
    return jnp.dot(a, b, preferred_element_type=jnp.float32)


def tile_of(rows):
    return max(n for n in range(SUB, 705, SUB) if rows % n == 0)


def rows_from(load, start, count):
    skip = start % STEP
    base = pl.multiple_of(start - skip, STEP)
    block = load(base, count + STEP)
    width = block.shape[1]
    block = block.reshape(count // STEP + 1, STEP, width)
    turned = pltpu.roll(block, (STEP - skip) % STEP, 1)
    row = lax.broadcasted_iota(jnp.int32, (count // STEP, STEP, width), 1)
    return jnp.where(row < STEP - skip, turned[:-1], turned[1:]).reshape(count, width)


def clear_margins(buf, rows):
    width = buf.shape[1]
    buf[:REACH, :] = jnp.zeros((REACH, width), buf.dtype)
    buf[REACH + rows :, :] = jnp.zeros((buf.shape[0] - REACH - rows, width), buf.dtype)


def clear_ends(wide):
    rows, width = wide.shape
    wide[:SUB, :] = jnp.zeros((SUB, width), jnp.float32)
    wide[rows - SUB - STEP :, :] = jnp.zeros((SUB + STEP, width), jnp.float32)


def widen(source, wide):
    aux = source.shape[0]
    clear_ends(wide)
    tile = aux // ROW_TILES

    def one(i, carry):
        base = pl.multiple_of(i * tile, SUB)
        wide[pl.ds(pl.multiple_of(SUB + base, SUB), tile), :] = source[
            pl.ds(base, tile), :
        ].astype(jnp.float32)
        return carry

    lax.fori_loop(0, ROW_TILES, one, 0)


def place(lead, wide, buf):
    rows = wide.shape[0] - SUB - STEP
    step = tile_of(rows)

    def move(i, carry):
        base = pl.multiple_of(i * step, SUB)
        moved = rows_from(lambda at, n: wide[pl.ds(at, n), :], SUB - lead + base, step)
        buf[pl.ds(pl.multiple_of(REACH + base, SUB), step), :] = moved.astype(buf.dtype)
        return carry

    lax.fori_loop(0, rows // step, move, 0)


def amplitudes(coulomb, denominator, weight):
    amplitude = (coulomb / denominator).astype(jnp.bfloat16)
    weighted = (amplitude.astype(jnp.float32) * weight).astype(jnp.bfloat16)
    return amplitude, weighted.T


def needed(plan, group, t):
    total = jnp.int32(0)
    for s in range(plan.owned):
        total = total + plan.count(plan.slot(group, s, t))
    return total != 0


def amplitude_of(plan, occ, slot, s, partner, at, eps_col, eps_row, ft, buf):
    rows = ft.shape[2]
    cols = buf.shape[1]
    coulomb = dot(ft[s], buf[pl.ds(plan.offset(slot), rows), :])
    denominator = occ[slot] - eps_col[s] - eps_row[partner, :, pl.ds(at, cols)]
    return amplitudes(coulomb, denominator, plan.count(slot).astype(jnp.float32))


def add_block(plan, occ, group, t, at, eps_col, eps_row, ft, source, wide, buf, acc, dens, turned):
    owned, rows, width = acc.shape
    scale = float(width) ** -0.5
    step = rows // ROW_TILES

    @pl.when(needed(plan, group, t))
    def _():
        widen(source, wide)

    def one(s, carry):
        slot = plan.slot(group, s, t)

        @pl.when(plan.count(slot) != 0)
        def _():
            place(plan.lead(slot), wide, buf)
            amplitude, turned[...] = amplitude_of(
                plan, occ, slot, s, group * owned + t, at, eps_col, eps_row, ft, buf
            )
            dens[s] += scale * dot(amplitude, turned[...])

            def add(i, inner):
                base = pl.multiple_of(i * step, SUB)
                block = buf[pl.ds(pl.multiple_of(plan.offset(slot) + base, SUB), step), :]
                acc[s, pl.ds(base, step), :] += dot(block, turned[...])
                return inner

            lax.fori_loop(0, ROW_TILES, add, 0)

        return carry

    lax.fori_loop(0, owned, one, 0)


def near_pairs_of(position, pair_partner, owned, devices):
    pairs_here = pair_partner.shape[0] // devices
    pairs = []
    for step in (-1, 0, 1):
        group = position + step
        known = (group >= 0) & (group < devices)
        held = jnp.clip(group, 0, devices - 1)
        for n in range(pairs_here):
            pairs.append((known, group * owned + n % owned, pair_partner[held * pairs_here + n]))
    return pairs


def count_between(pairs, one, other):
    total = jnp.int32(0)
    for known, first, second in pairs:
        forth = known & (first == one) & (second == other)
        back = known & (second == one) & (first == other)
        total = total + forth.astype(jnp.int32) + back.astype(jnp.int32)
    return total


def flip_of(used):
    return (used[0] < used[-1]).astype(jnp.int32)


def cell_of(cells, number, flip):
    halves = len([cell for cell in cells if cell[0] == 0])
    flipped = cells[:1] + cells[halves:] + cells[1:halves]
    (t, at), (other_t, other_at) = cells[number], flipped[number]
    if (t, at) == (other_t, other_at):
        return t, at
    return (
        jnp.where(flip == 1, other_t, t),
        pl.multiple_of(jnp.where(flip == 1, other_at, at), COLS),
    )


def make_plan(
    fit_start, occ_energy, pair_partner, domains, energy, ints, occ, eps_col, eps_row,
    *, devices, targets, relays,
):
    owned, width = eps_col.shape[:2]
    orbitals = fit_start.shape[0]
    plan = Plan(ints, owned)
    position = lax.axis_index("row")
    side = jnp.where(position % 2 == 1, 1, -1)
    places = [
        base * owned + t
        for base in (position, position - side, position + side)
        for t in range(owned)
    ]
    inside = [jnp.clip(orbital, 0, orbitals - 1) for orbital in places]
    starts = [fit_start[orbital] for orbital in inside]
    pairs = near_pairs_of(position, pair_partner, owned, devices)
    used = [jnp.int32(0)] * owned
    for group in range(3):
        for s in range(owned):
            for t in range(owned):
                slot = plan.slot(group, s, t)
                other = group * owned + t
                total = count_between(pairs, places[s], places[other])
                ints[slot] = total
                if group == 2:
                    used[t] = used[t] + (total != 0).astype(jnp.int32)
                apart = starts[other] - starts[s]
                ints[plan.at_shift(slot)] = (apart & (SUB - 1)) - apart
                ints[plan.at_lead(slot)] = apart & (SUB - 1)
                occ[slot] = occ_energy[inside[s]] + occ_energy[inside[other]]
    for number, group in enumerate(targets):
        way = jnp.int32(0)
        for to in group:
            way = jnp.where(position == to, 1, way)
        ints[plan.at_way(number)] = way
    late = jnp.int32(0)
    for row in relays:
        late = jnp.where(position == row, 1, late)
    ints[plan.at_late(len(targets))] = late
    ints[plan.at_flip(len(targets))] = flip_of(used)
    entries = energy.shape[0]
    table = lax.broadcasted_iota(jnp.int32, (entries, width), 0)
    for n, orbital in enumerate(inside):
        domain = domains[pl.ds(orbital, 1), :]
        row = jnp.sum(jnp.where(table == domain, energy[...], 0.0), axis=0, keepdims=True)
        eps_row[n] = row
        if n < owned:
            eps_col[n] = jnp.broadcast_to(row, (LANES, width)).T[:, :1]
    return plan


def add_blocks(plan, occ, sources, eps_col, eps_row, ft, wide, buf, acc, dens, turned, raw, sem):
    copies = [
        pltpu.make_async_copy(block, raw.at[n % 2], sem.at[n % 2])
        for n, (_, _, block) in enumerate(sources)
    ]
    copies[0].start()
    clear_margins(buf, raw.shape[1] + SUB)
    for n, (group, t, _) in enumerate(sources):
        if n + 1 < len(copies):
            copies[n + 1].start()
        copies[n].wait()
        add_block(
            plan, occ, group, t, 0, eps_col, eps_row, ft, raw.at[n % 2], wide, buf, acc, dens, turned
        )


def first_kernel(
    fit_start, occ_energy, pair_partner, domains, energy, own, after,
    ints, occ, eps_col, eps_row, acc, dens, ft, token, wide, buf, turned,
    *, devices, targets, relays,
):
    del after
    token[...] = jnp.zeros_like(token)
    plan = make_plan(
        fit_start, occ_energy, pair_partner, domains, energy, ints, occ, eps_col, eps_row,
        devices=devices, targets=targets, relays=relays,
    )
    owned, aux, width = own.shape
    acc[...] = jnp.zeros_like(acc)
    dens[...] = jnp.zeros_like(dens)
    for t in range(owned):

        def turn(i, carry):
            at = pl.multiple_of(i * LANES, LANES)
            ft[t, :, pl.ds(at, LANES)] = own[t, pl.ds(at, LANES), :].T
            return carry

        lax.fori_loop(0, aux // LANES, turn, 0)

    @pl.when(ints[plan.at_late(len(targets))] == 1)
    def _():
        clear_margins(buf, aux + SUB)
        for t in range(owned):
            add_block(
                plan, occ, 0, t, 0, eps_col, eps_row, ft, own.at[t], wide, buf, acc, dens, turned
            )


def near_kernel(
    ints, occ, eps_col, eps_row, ft, acc_in, dens_in, own, mate, *refs, ways, late
):
    del acc_in, dens_in
    acc, dens, token, wide, buf, turned, raw, sem = refs[-8:]
    token[...] = jnp.zeros_like(token)
    owned = own.shape[0]
    plan = Plan(ints, owned)
    groups = ((1, mate),) if late else ((0, own), (1, mate))
    sources = [(group, t, blocks.at[t]) for group, blocks in groups for t in range(owned)]

    @pl.when(ints[plan.at_late(ways)] == late)
    def _():
        add_blocks(
            plan, occ, sources, eps_col, eps_row, ft, wide, buf, acc, dens, turned, raw, sem
        )


def far_kernel(
    ints, occ, eps_col, eps_row, ft, acc_in, dens_in, block, after,
    acc, dens, token, wide, buf, turned, *, ways, total_ways, cells, number,
):
    del acc_in, dens_in, after
    token[...] = jnp.zeros_like(token)
    plan = Plan(ints, acc.shape[0])
    t, at = cell_of(cells, number, ints[plan.at_flip(total_ways)])
    here = needed(plan, 2, t)
    for way in ways:
        here = here & (plan.way(way) == 0)

    @pl.when(here)
    def _():
        clear_margins(buf, block.shape[0] + SUB)
        add_block(plan, occ, 2, t, at, eps_col, eps_row, ft, block, wide, buf, acc, dens, turned)


def send_out(s, tile_of_rows, dens, ready, out, dens_out, sem):
    step = out.shape[1] // OUT_TILES
    pltpu.make_async_copy(dens.at[s], dens_out.at[s], sem.at[s, OUT_TILES]).start()

    def one(i, carry):
        part = pl.ds(pl.multiple_of(i * step, SUB), step)
        ready[s, part, :] = tile_of_rows(i * step, step).astype(ready.dtype)
        pltpu.make_async_copy(ready.at[s, part], out.at[s, part], sem.at[s, i]).start()
        return carry

    lax.fori_loop(0, OUT_TILES, one, 0)


def wait_out(s, dens, ready, out, dens_out, sem):
    step = out.shape[1] // OUT_TILES
    pltpu.make_async_copy(dens.at[s], dens_out.at[s], sem.at[s, OUT_TILES]).wait()
    for i in range(OUT_TILES):
        part = pl.ds(i * step, step)
        pltpu.make_async_copy(ready.at[s, part], out.at[s, part], sem.at[s, i]).wait()


def relayed_kernel(
    ints, occ, eps_col, eps_row, ft, acc_in, dens_in, *refs, numbers, cells
):
    del acc_in, dens_in
    *blocks, _, acc, dens, token, out, dens_out, wide, buf, turned, raw, ready, sem, out_sem = refs
    token[...] = jnp.zeros_like(token)
    owned = acc.shape[0]
    plan = Plan(ints, owned)
    flip = ints[plan.at_flip(len(numbers))]
    last, _ = cell_of(cells, len(cells) - 1, flip)
    for way, (block, number) in enumerate(zip(blocks, numbers)):
        t, at = cell_of(cells, number, flip)

        @pl.when(needed(plan, 2, t) & (plan.way(way) == 1))
        def _():
            copy = pltpu.make_async_copy(block, raw, sem)
            copy.start()
            clear_margins(buf, raw.shape[0] + SUB)
            copy.wait()
            add_block(plan, occ, 2, t, at, eps_col, eps_row, ft, raw, wide, buf, acc, dens, turned)

    for s in range(owned):

        @pl.when(plan.count(plan.slot(2, s, last)) == 0)
        def _():
            send_out(
                s,
                lambda base, n: acc[s, pl.ds(pl.multiple_of(base, SUB), n), :],
                dens, ready, out, dens_out, out_sem,
            )

    for s in range(owned):

        @pl.when(plan.count(plan.slot(2, s, last)) == 0)
        def _():
            wait_out(s, dens, ready, out, dens_out, out_sem)


def last_kernel(
    ints, occ, eps_col, eps_row, ft, acc_in, dens_in, block, out_in, dens_out_in, after,
    acc, dens, out, dens_out, wide, buf, turned, raw, ready, sem, raw_sem, *, total_ways, cells,
):
    del acc_in, dens_in, out_in, dens_out_in, after
    owned, aux, width = out.shape
    plan = Plan(ints, owned)
    t, at = cell_of(cells, len(cells) - 1, ints[plan.at_flip(total_ways)])
    scale = float(width) ** -0.5

    @pl.when(needed(plan, 2, t))
    def _():
        step = aux // LOAD_TILES
        parts = [pl.ds(i * step, step) for i in range(LOAD_TILES)]
        loads = [
            pltpu.make_async_copy(block.at[part], raw.at[part], raw_sem.at[i])
            for i, part in enumerate(parts)
        ]
        for load in loads:
            load.start()
        clear_margins(buf, aux + SUB)
        clear_ends(wide)
        for i, load in enumerate(loads):
            load.wait()
            wide[SUB + i * step : SUB + (i + 1) * step, :] = raw[parts[i], :].astype(jnp.float32)

    def one(s, carry):
        slot = plan.slot(2, s, t)

        @pl.when(plan.count(slot) != 0)
        def _():
            place(plan.lead(slot), wide, buf)
            amplitude, turned[...] = amplitude_of(
                plan, occ, slot, s, 2 * owned + t, at, eps_col, eps_row, ft, buf
            )
            dens[s] += scale * dot(amplitude, turned[...])

            def total(base, n):
                rows = buf[pl.ds(pl.multiple_of(plan.offset(slot) + base, SUB), n), :]
                return acc[s, pl.ds(pl.multiple_of(base, SUB), n), :] + dot(rows, turned[...])

            send_out(s, total, dens, ready, out, dens_out, sem)

        return carry

    lax.fori_loop(0, owned, one, 0)
    for s in range(owned):

        @pl.when(plan.count(plan.slot(2, s, t)) != 0)
        def _():
            wait_out(s, dens, ready, out, dens_out, sem)


def copy_kernel(source, *refs, numbers, cells, devices):
    *outs, buf, sem = refs[-len(numbers) - 2 :]
    owned = source.shape[0]
    flip = jnp.int32(0)
    if any(numbers):
        position = lax.axis_index("row")
        pairs = near_pairs_of(position, refs[0], owned, devices)
        beyond = position + jnp.where(position % 2 == 1, 1, -1)
        used = []
        for t in range(owned):
            total = jnp.int32(0)
            for s in range(owned):
                count = count_between(pairs, position * owned + t, beyond * owned + s)
                total = total + (count != 0).astype(jnp.int32)
            used.append(total)
        flip = flip_of(used)
    places = [cell_of(cells, number, flip) for number in numbers]
    rows, cols = outs[0].shape
    tile = rows // CHUNK_TILES
    parts = [(n, i) for n in range(len(places)) for i in range(CHUNK_TILES)]

    def copies(n, i):
        t, at = places[n]
        part = pl.ds(i * tile, tile)
        held = buf.at[n, part]
        load = pltpu.make_async_copy(source.at[t, part, pl.ds(at, cols)], held, sem.at[0, n, i])
        return load, pltpu.make_async_copy(held, outs[n].at[part], sem.at[1, n, i])

    for n, i in parts:
        copies(n, i)[0].start()
    for n, i in parts:
        load, store = copies(n, i)
        load.wait()
        store.start()
    for n, i in parts:
        copies(n, i)[1].wait()


def pass_kernel(source, after, out):
    del source, after, out


def relay_plan(devices, chunks):
    if devices != 16 or chunks != 4:
        return []
    plan = []
    for z, chunk, alone in ((1, 0, True), (0, 0, False), (2, 1, False)):
        high, low = 4 * z + 3, 4 * z + 4
        plan.append((chunk, alone, [(high, low, 0), (low, high, devices - 1)]))
    return plan


def spec(space):
    return pl.BlockSpec(memory_space=space)


def on_device(fitted, fit_start, virt_domain, occ_energy, virt_energy, pair_partner):
    owned, aux, width = fitted.shape
    devices = lax.axis_size("row")
    buf_rows = 2 * REACH + aux
    wide_rows = aux + 2 * SUB + STEP
    smem, vmem, anywhere = spec(pltpu.SMEM), spec(pltpu.VMEM), spec(pl.ANY)

    outward = []
    for i in range(devices):
        to = i + 1 if i % 2 else i - 1
        if 0 <= to < devices:
            outward.append((i, to))
    inward = [(i, i ^ 1) for i in range(devices) if i ^ 1 < devices]

    def in_hbm(array):
        return pltpu.with_memory_space_constraint(array, pltpu.HBM)

    def in_vmem(array):
        return pltpu.with_memory_space_constraint(array, pltpu.VMEM)

    def chunks(numbers, *after):
        return pl.pallas_call(
            functools.partial(copy_kernel, numbers=numbers, cells=cells, devices=devices),
            out_shape=[jax.ShapeDtypeStruct((aux, COLS), fitted.dtype)] * len(numbers),
            in_specs=[anywhere] + [smem] * any(numbers) + [anywhere] * len(after),
            out_specs=[anywhere] * len(numbers),
            scratch_shapes=[
                pltpu.VMEM((len(numbers), aux, COLS), fitted.dtype),
                pltpu.SemaphoreType.DMA((2, len(numbers), CHUNK_TILES)),
            ],
            compiler_params=pltpu.CompilerParams(vmem_limit_bytes=CHUNK_VMEM),
            name="chunks",
        )(in_hbm(fitted), *[pair_partner] * any(numbers), *after)

    def pass_on(block, after):
        return pl.pallas_call(
            pass_kernel,
            out_shape=jax.ShapeDtypeStruct(block.shape, block.dtype),
            in_specs=[anywhere] * 2,
            out_specs=anywhere,
            input_output_aliases={0: 0},
            compiler_params=pltpu.CompilerParams(vmem_limit_bytes=CHUNK_VMEM),
            name="pass_on",
        )(block, after)

    cells = [(t, at) for t in range(owned) for at in range(0, width, COLS)]
    last = len(cells) - 1
    plan = relay_plan(devices, len(cells))
    first_hops = [[(source, by) for source, _, by in pairs] for _, _, pairs in plan]
    second_hops = [[(by, to) for _, to, by in pairs] for _, _, pairs in plan]

    def exchange(number, block):
        pairs = list(outward)
        for (at, alone, group), hop in zip(plan, first_hops):
            if at == number:
                pairs = [pair for pair in pairs if pair not in {(a, b) for a, b, _ in group}]
                pairs += [] if alone else hop
        return lax.ppermute(block, "row", pairs)

    sent = list(chunks([0]))
    mate = lax.ppermute(lax.optimization_barrier((fitted, sent[0]))[0], "row", inward)
    far = [exchange(0, sent[0])]
    rest = chunks(list(range(1, len(cells))) + [0] * bool(plan), sent[0])
    sent += rest[:last]
    early = {
        index: lax.ppermute(rest[last], "row", first_hops[index])
        for index, (_, alone, _) in enumerate(plan)
        if alone
    }
    far += [exchange(number, sent[number]) for number in range(1, last + 1)]

    unit = 4 * aux * width * COLS
    acc_shape = pltpu.VMEM((owned, aux, width), jnp.float32)
    dens_shape = pltpu.VMEM((owned, width, width), jnp.float32)
    ft_shape = pltpu.VMEM((owned, width, aux), fitted.dtype)
    token_shape = jax.ShapeDtypeStruct((8, LANES), jnp.int32)
    slots = 3 * owned * owned

    def cost(blocks):
        return pl.CostEstimate(
            flops=100 * unit * blocks * owned, bytes_accessed=8 << 20, transcendentals=0
        )

    ints, occ, eps_col, eps_row, acc, dens, ft, token = pl.pallas_call(
        functools.partial(
            first_kernel,
            devices=devices,
            targets=[[to for _, to, _ in pairs] for _, _, pairs in plan],
            relays=sorted({by for _, _, pairs in plan for _, _, by in pairs}),
        ),
        out_shape=(
            jax.ShapeDtypeStruct((Plan(None, owned).at_flip(len(plan)) + 1,), jnp.int32),
            jax.ShapeDtypeStruct((slots,), jnp.float32),
            pltpu.VMEM((owned, width, 1), jnp.float32),
            pltpu.VMEM((3 * owned, 1, width), jnp.float32),
            acc_shape,
            dens_shape,
            ft_shape,
            token_shape,
        ),
        in_specs=[smem] * 3 + [vmem] * 3 + [anywhere],
        out_specs=(smem,) * 2 + (vmem,) * 6,
        scratch_shapes=[
            pltpu.VMEM((wide_rows, width), jnp.float32),
            pltpu.VMEM((buf_rows, width), fitted.dtype),
            pltpu.VMEM((width, width), fitted.dtype),
        ],
        compiler_params=pltpu.CompilerParams(vmem_limit_bytes=NEAR_VMEM),
        cost_estimate=cost(len(cells)),
        name="first",
    )(
        fit_start, occ_energy, pair_partner, virt_domain, virt_energy.reshape(-1, 1),
        in_hbm(fitted), sent[last - 1],
    )
    state = {"acc": acc, "dens": dens, "token": token}
    hops = []

    def add_pairs(
        kernel, block_specs, blocks, cols, limit, name,
        extra=(), outs=(), aliases={}, scratch=(), token=True,
    ):
        specs = [smem] * 2 + [vmem] * 5 + block_specs
        results = pl.pallas_call(
            kernel,
            out_shape=(acc_shape, dens_shape) + (token_shape,) * token + tuple(outs),
            in_specs=specs + [anywhere] * (1 + len(extra)),
            out_specs=(vmem,) * (2 + token) + (anywhere,) * len(outs),
            input_output_aliases={5: 0, 6: 1, **aliases},
            scratch_shapes=[
                pltpu.VMEM((wide_rows, cols), jnp.float32),
                pltpu.VMEM((buf_rows, cols), fitted.dtype),
                *scratch,
            ],
            compiler_params=pltpu.CompilerParams(vmem_limit_bytes=limit),
            cost_estimate=cost(cols // COLS),
            name=name,
        )(
            ints, occ, in_vmem(eps_col), in_vmem(eps_row), in_vmem(ft), in_vmem(state["acc"]),
            in_vmem(state["dens"]), *blocks, *extra, state["token"],
        )
        state.update(acc=results[0], dens=results[1], token=results[2])
        return results[2 + token :]

    hops = {index: lax.ppermute(early[index], "row", second_hops[index]) for index in early}
    turned_cols = (pltpu.VMEM((COLS, width), fitted.dtype),)

    def near_pairs(late, *extra):
        add_pairs(
            functools.partial(near_kernel, ways=len(plan), late=late),
            [anywhere] * 2, [in_hbm(fitted), mate], width, NEAR_VMEM, f"near_pairs_{late}",
            extra=extra,
            scratch=(
                pltpu.VMEM((width, width), fitted.dtype),
                pltpu.VMEM((2, aux, width), fitted.dtype),
                pltpu.SemaphoreType.DMA((2,)),
            ),
        )

    near_pairs(0, *early.values())
    for number in range(last):
        for index, (at, alone, _) in enumerate(plan):
            if at == number and not alone:
                far[number] = state["token"] = pass_on(far[number], state["token"])
                hops[index] = lax.ppermute(far[number], "row", second_hops[index])
                if index == len(plan) - 1:
                    near_pairs(1)
        ways = [index for index, (at, _, _) in enumerate(plan) if at == number]
        add_pairs(
            functools.partial(
                far_kernel, ways=ways, total_ways=len(plan), cells=cells, number=number
            ),
            [vmem], [far[number]], COLS, FAR_VMEM, f"far_pairs_{number}", scratch=turned_cols,
        )
    results = (
        jax.ShapeDtypeStruct(fitted.shape, fitted.dtype),
        jax.ShapeDtypeStruct((owned, width, width), jnp.float32),
    )
    out_scratch = (
        pltpu.VMEM((owned, aux, width), fitted.dtype),
        pltpu.SemaphoreType.DMA((owned, OUT_TILES + 1)),
    )
    ready = add_pairs(
        functools.partial(
            relayed_kernel, numbers=[at for at, _, _ in plan], cells=cells
        ),
        [anywhere] * len(hops), [hops[index] for index in range(len(plan))], COLS, FAR_VMEM,
        "relayed_pairs",
        outs=results,
        scratch=turned_cols
        + (pltpu.VMEM((aux, COLS), fitted.dtype), out_scratch[0], pltpu.SemaphoreType.DMA)
        + out_scratch[1:],
    )
    gradient, density = add_pairs(
        functools.partial(last_kernel, total_ways=len(plan), cells=cells),
        [anywhere] * 3, [far[last], *ready], COLS, FAR_VMEM, "last_pairs",
        outs=results,
        aliases={8: 2, 9: 3},
        scratch=turned_cols
        + (pltpu.VMEM((aux, COLS), fitted.dtype),)
        + out_scratch
        + (pltpu.SemaphoreType.DMA((LOAD_TILES,)),),
        token=False,
    )
    return gradient, density


def solution(mesh):
    placed = (
        P(("parts", "row"), None, None),
        P("parts"),
        P("parts", None),
        P("parts"),
        P("parts"),
        P("parts"),
    )
    return jax.shard_map(
        on_device,
        mesh=mesh,
        in_specs=placed,
        out_specs=(P(("parts", "row"), None, None), P(("parts", "row"), None, None)),
        check_vma=False,
    )
```

```python
import functools

import jax
import jax.numpy as jnp
from jax import lax
from jax.experimental import pallas as pl
from jax.experimental.pallas import tpu as pltpu
from jax.sharding import PartitionSpec as P

SUB = 16
STEP = 8
LANES = 128
ROW_TILES = 2
OUT_TILES = 4
LOAD_TILES = 4
CHUNK_TILES = 4
COLS = 256
REACH = 1024
NEAR_VMEM = 22 * 1024 * 1024
FAR_VMEM = 16 * 1024 * 1024
CHUNK_VMEM = 6 * 1024 * 1024


class Plan:
    def __init__(self, ref, owned):
        self.ref, self.owned = ref, owned
        self.slots = 3 * owned * owned

    def slot(self, group, s, t):
        return (group * self.owned + s) * self.owned + t

    def at_shift(self, slot):
        return self.slots + slot

    def at_lead(self, slot):
        return 2 * self.slots + slot

    def at_way(self, number):
        return 3 * self.slots + number

    def at_late(self, ways):
        return self.at_way(ways)

    def at_flip(self, ways):
        return self.at_way(ways) + 1

    def count(self, slot):
        return self.ref[slot]

    def offset(self, slot):
        return pl.multiple_of(REACH + self.ref[self.at_shift(slot)], SUB)

    def lead(self, slot):
        return self.ref[self.at_lead(slot)]

    def way(self, number):
        return self.ref[self.at_way(number)]


def dot(a, b):
    return jnp.dot(a, b, preferred_element_type=jnp.float32)


def tile_of(rows):
    return max(n for n in range(SUB, 705, SUB) if rows % n == 0)


def rows_from(load, start, count):
    skip = start % STEP
    base = pl.multiple_of(start - skip, STEP)
    block = load(base, count + STEP)
    width = block.shape[1]
    block = block.reshape(count // STEP + 1, STEP, width)
    turned = pltpu.roll(block, (STEP - skip) % STEP, 1)
    row = lax.broadcasted_iota(jnp.int32, (count // STEP, STEP, width), 1)
    return jnp.where(row < STEP - skip, turned[:-1], turned[1:]).reshape(count, width)


def clear_margins(buf, rows):
    width = buf.shape[1]
    buf[:REACH, :] = jnp.zeros((REACH, width), buf.dtype)
    buf[REACH + rows :, :] = jnp.zeros((buf.shape[0] - REACH - rows, width), buf.dtype)


def clear_ends(wide):
    rows, width = wide.shape
    wide[:SUB, :] = jnp.zeros((SUB, width), jnp.float32)
    wide[rows - SUB - STEP :, :] = jnp.zeros((SUB + STEP, width), jnp.float32)


def widen(source, wide):
    aux = source.shape[0]
    clear_ends(wide)
    tile = aux // ROW_TILES

    def one(i, carry):
        base = pl.multiple_of(i * tile, SUB)
        wide[pl.ds(pl.multiple_of(SUB + base, SUB), tile), :] = source[
            pl.ds(base, tile), :
        ].astype(jnp.float32)
        return carry

    lax.fori_loop(0, ROW_TILES, one, 0)


def place(lead, wide, buf):
    rows = wide.shape[0] - SUB - STEP
    step = tile_of(rows)

    def move(i, carry):
        base = pl.multiple_of(i * step, SUB)
        moved = rows_from(lambda at, n: wide[pl.ds(at, n), :], SUB - lead + base, step)
        buf[pl.ds(pl.multiple_of(REACH + base, SUB), step), :] = moved.astype(buf.dtype)
        return carry

    lax.fori_loop(0, rows // step, move, 0)


def amplitudes(coulomb, denominator, weight):
    amplitude = (coulomb / denominator).astype(jnp.bfloat16)
    weighted = (amplitude.astype(jnp.float32) * weight).astype(jnp.bfloat16)
    return amplitude, weighted.T


def needed(plan, group, t):
    total = jnp.int32(0)
    for s in range(plan.owned):
        total = total + plan.count(plan.slot(group, s, t))
    return total != 0


def amplitude_of(plan, occ, slot, s, partner, at, eps_col, eps_row, ft, buf):
    rows = ft.shape[2]
    cols = buf.shape[1]
    coulomb = dot(ft[s], buf[pl.ds(plan.offset(slot), rows), :])
    denominator = occ[slot] - eps_col[s] - eps_row[partner, :, pl.ds(at, cols)]
    return amplitudes(coulomb, denominator, plan.count(slot).astype(jnp.float32))


def add_block(plan, occ, group, t, at, eps_col, eps_row, ft, source, wide, buf, acc, dens, turned):
    owned, rows, width = acc.shape
    scale = float(width) ** -0.5
    step = rows // ROW_TILES

    @pl.when(needed(plan, group, t))
    def _():
        widen(source, wide)

    def one(s, carry):
        slot = plan.slot(group, s, t)

        @pl.when(plan.count(slot) != 0)
        def _():
            place(plan.lead(slot), wide, buf)
            amplitude, turned[...] = amplitude_of(
                plan, occ, slot, s, group * owned + t, at, eps_col, eps_row, ft, buf
            )
            dens[s] += scale * dot(amplitude, turned[...])

            def add(i, inner):
                base = pl.multiple_of(i * step, SUB)
                block = buf[pl.ds(pl.multiple_of(plan.offset(slot) + base, SUB), step), :]
                acc[s, pl.ds(base, step), :] += dot(block, turned[...])
                return inner

            lax.fori_loop(0, ROW_TILES, add, 0)

        return carry

    lax.fori_loop(0, owned, one, 0)


def near_pairs_of(position, pair_partner, owned, devices):
    pairs_here = pair_partner.shape[0] // devices
    pairs = []
    for step in (-1, 0, 1):
        group = position + step
        known = (group >= 0) & (group < devices)
        held = jnp.clip(group, 0, devices - 1)
        for n in range(pairs_here):
            pairs.append((known, group * owned + n % owned, pair_partner[held * pairs_here + n]))
    return pairs


def count_between(pairs, one, other):
    total = jnp.int32(0)
    for known, first, second in pairs:
        forth = known & (first == one) & (second == other)
        back = known & (second == one) & (first == other)
        total = total + forth.astype(jnp.int32) + back.astype(jnp.int32)
    return total


def flip_of(used):
    return (used[0] < used[-1]).astype(jnp.int32)


def cell_of(cells, number, flip):
    halves = len([cell for cell in cells if cell[0] == 0])
    flipped = cells[:1] + cells[halves:] + cells[1:halves]
    (t, at), (other_t, other_at) = cells[number], flipped[number]
    if (t, at) == (other_t, other_at):
        return t, at
    return (
        jnp.where(flip == 1, other_t, t),
        pl.multiple_of(jnp.where(flip == 1, other_at, at), COLS),
    )


def make_plan(
    fit_start, occ_energy, pair_partner, domains, energy, ints, occ, eps_col, eps_row,
    *, devices, targets, relays,
):
    owned, width = eps_col.shape[:2]
    orbitals = fit_start.shape[0]
    plan = Plan(ints, owned)
    position = lax.axis_index("row")
    side = jnp.where(position % 2 == 1, 1, -1)
    places = [
        base * owned + t
        for base in (position, position - side, position + side)
        for t in range(owned)
    ]
    inside = [jnp.clip(orbital, 0, orbitals - 1) for orbital in places]
    starts = [fit_start[orbital] for orbital in inside]
    pairs = near_pairs_of(position, pair_partner, owned, devices)
    used = [jnp.int32(0)] * owned
    for group in range(3):
        for s in range(owned):
            for t in range(owned):
                slot = plan.slot(group, s, t)
                other = group * owned + t
                total = count_between(pairs, places[s], places[other])
                ints[slot] = total
                if group == 2:
                    used[t] = used[t] + (total != 0).astype(jnp.int32)
                apart = starts[other] - starts[s]
                ints[plan.at_shift(slot)] = (apart & (SUB - 1)) - apart
                ints[plan.at_lead(slot)] = apart & (SUB - 1)
                occ[slot] = occ_energy[inside[s]] + occ_energy[inside[other]]
    for number, group in enumerate(targets):
        way = jnp.int32(0)
        for to in group:
            way = jnp.where(position == to, 1, way)
        ints[plan.at_way(number)] = way
    late = jnp.int32(0)
    for row in relays:
        late = jnp.where(position == row, 1, late)
    ints[plan.at_late(len(targets))] = late
    ints[plan.at_flip(len(targets))] = flip_of(used)
    entries = energy.shape[0]
    table = lax.broadcasted_iota(jnp.int32, (entries, width), 0)
    for n, orbital in enumerate(inside):
        domain = domains[pl.ds(orbital, 1), :]
        row = jnp.sum(jnp.where(table == domain, energy[...], 0.0), axis=0, keepdims=True)
        eps_row[n] = row
        if n < owned:
            eps_col[n] = jnp.broadcast_to(row, (LANES, width)).T[:, :1]
    return plan


def add_blocks(plan, occ, sources, eps_col, eps_row, ft, wide, buf, acc, dens, turned, raw, sem):
    copies = [
        pltpu.make_async_copy(block, raw.at[n % 2], sem.at[n % 2])
        for n, (_, _, block) in enumerate(sources)
    ]
    copies[0].start()
    clear_margins(buf, raw.shape[1] + SUB)
    for n, (group, t, _) in enumerate(sources):
        if n + 1 < len(copies):
            copies[n + 1].start()
        copies[n].wait()
        add_block(
            plan, occ, group, t, 0, eps_col, eps_row, ft, raw.at[n % 2], wide, buf, acc, dens, turned
        )


def first_kernel(
    fit_start, occ_energy, pair_partner, domains, energy, own, after,
    ints, occ, eps_col, eps_row, acc, dens, ft, token, wide, buf, turned,
    *, devices, targets, relays,
):
    del after
    token[...] = jnp.zeros_like(token)
    plan = make_plan(
        fit_start, occ_energy, pair_partner, domains, energy, ints, occ, eps_col, eps_row,
        devices=devices, targets=targets, relays=relays,
    )
    owned, aux, width = own.shape
    acc[...] = jnp.zeros_like(acc)
    dens[...] = jnp.zeros_like(dens)
    for t in range(owned):

        def turn(i, carry):
            at = pl.multiple_of(i * LANES, LANES)
            ft[t, :, pl.ds(at, LANES)] = own[t, pl.ds(at, LANES), :].T
            return carry

        lax.fori_loop(0, aux // LANES, turn, 0)

    @pl.when(ints[plan.at_late(len(targets))] == 1)
    def _():
        clear_margins(buf, aux + SUB)
        for t in range(owned):
            add_block(
                plan, occ, 0, t, 0, eps_col, eps_row, ft, own.at[t], wide, buf, acc, dens, turned
            )


def near_kernel(
    ints, occ, eps_col, eps_row, ft, acc_in, dens_in, own, mate, *refs, ways, late
):
    del acc_in, dens_in
    acc, dens, token, wide, buf, turned, raw, sem = refs[-8:]
    token[...] = jnp.zeros_like(token)
    owned = own.shape[0]
    plan = Plan(ints, owned)
    groups = ((1, mate),) if late else ((0, own), (1, mate))
    sources = [(group, t, blocks.at[t]) for group, blocks in groups for t in range(owned)]

    @pl.when(ints[plan.at_late(ways)] == late)
    def _():
        add_blocks(
            plan, occ, sources, eps_col, eps_row, ft, wide, buf, acc, dens, turned, raw, sem
        )


def far_kernel(
    ints, occ, eps_col, eps_row, ft, acc_in, dens_in, block, after,
    acc, dens, token, wide, buf, turned, *, ways, total_ways, cells, number,
):
    del acc_in, dens_in, after
    token[...] = jnp.zeros_like(token)
    plan = Plan(ints, acc.shape[0])
    t, at = cell_of(cells, number, ints[plan.at_flip(total_ways)])
    here = needed(plan, 2, t)
    for way in ways:
        here = here & (plan.way(way) == 0)

    @pl.when(here)
    def _():
        clear_margins(buf, block.shape[0] + SUB)
        add_block(plan, occ, 2, t, at, eps_col, eps_row, ft, block, wide, buf, acc, dens, turned)


def send_out(s, tile_of_rows, dens, ready, out, dens_out, sem):
    step = out.shape[1] // OUT_TILES
    pltpu.make_async_copy(dens.at[s], dens_out.at[s], sem.at[s, OUT_TILES]).start()

    def one(i, carry):
        part = pl.ds(pl.multiple_of(i * step, SUB), step)
        ready[s, part, :] = tile_of_rows(i * step, step).astype(ready.dtype)
        pltpu.make_async_copy(ready.at[s, part], out.at[s, part], sem.at[s, i]).start()
        return carry

    lax.fori_loop(0, OUT_TILES, one, 0)


def wait_out(s, dens, ready, out, dens_out, sem):
    step = out.shape[1] // OUT_TILES
    pltpu.make_async_copy(dens.at[s], dens_out.at[s], sem.at[s, OUT_TILES]).wait()
    for i in range(OUT_TILES):
        part = pl.ds(i * step, step)
        pltpu.make_async_copy(ready.at[s, part], out.at[s, part], sem.at[s, i]).wait()


def relayed_kernel(
    ints, occ, eps_col, eps_row, ft, acc_in, dens_in, *refs, numbers, cells
):
    del acc_in, dens_in
    *blocks, _, acc, dens, token, out, dens_out, wide, buf, turned, raw, ready, sem, out_sem = refs
    token[...] = jnp.zeros_like(token)
    owned = acc.shape[0]
    plan = Plan(ints, owned)
    flip = ints[plan.at_flip(len(numbers))]
    last, _ = cell_of(cells, len(cells) - 1, flip)
    for way, (block, number) in enumerate(zip(blocks, numbers)):
        t, at = cell_of(cells, number, flip)

        @pl.when(needed(plan, 2, t) & (plan.way(way) == 1))
        def _():
            copy = pltpu.make_async_copy(block, raw, sem)
            copy.start()
            clear_margins(buf, raw.shape[0] + SUB)
            copy.wait()
            add_block(plan, occ, 2, t, at, eps_col, eps_row, ft, raw, wide, buf, acc, dens, turned)

    for s in range(owned):

        @pl.when(plan.count(plan.slot(2, s, last)) == 0)
        def _():
            send_out(
                s,
                lambda base, n: acc[s, pl.ds(pl.multiple_of(base, SUB), n), :],
                dens, ready, out, dens_out, out_sem,
            )

    for s in range(owned):

        @pl.when(plan.count(plan.slot(2, s, last)) == 0)
        def _():
            wait_out(s, dens, ready, out, dens_out, out_sem)


def last_kernel(
    ints, occ, eps_col, eps_row, ft, acc_in, dens_in, block, out_in, dens_out_in, after,
    acc, dens, out, dens_out, wide, buf, turned, raw, ready, sem, raw_sem, *, total_ways, cells,
):
    del acc_in, dens_in, out_in, dens_out_in, after
    owned, aux, width = out.shape
    plan = Plan(ints, owned)
    t, at = cell_of(cells, len(cells) - 1, ints[plan.at_flip(total_ways)])
    scale = float(width) ** -0.5

    @pl.when(needed(plan, 2, t))
    def _():
        step = aux // LOAD_TILES
        parts = [pl.ds(i * step, step) for i in range(LOAD_TILES)]
        loads = [
            pltpu.make_async_copy(block.at[part], raw.at[part], raw_sem.at[i])
            for i, part in enumerate(parts)
        ]
        for load in loads:
            load.start()
        clear_margins(buf, aux + SUB)
        clear_ends(wide)
        for i, load in enumerate(loads):
            load.wait()
            wide[SUB + i * step : SUB + (i + 1) * step, :] = raw[parts[i], :].astype(jnp.float32)

    def one(s, carry):
        slot = plan.slot(2, s, t)

        @pl.when(plan.count(slot) != 0)
        def _():
            place(plan.lead(slot), wide, buf)
            amplitude, turned[...] = amplitude_of(
                plan, occ, slot, s, 2 * owned + t, at, eps_col, eps_row, ft, buf
            )
            dens[s] += scale * dot(amplitude, turned[...])

            def total(base, n):
                rows = buf[pl.ds(pl.multiple_of(plan.offset(slot) + base, SUB), n), :]
                return acc[s, pl.ds(pl.multiple_of(base, SUB), n), :] + dot(rows, turned[...])

            send_out(s, total, dens, ready, out, dens_out, sem)

        return carry

    lax.fori_loop(0, owned, one, 0)
    for s in range(owned):

        @pl.when(plan.count(plan.slot(2, s, t)) != 0)
        def _():
            wait_out(s, dens, ready, out, dens_out, sem)


def copy_kernel(source, *refs, numbers, cells, devices):
    *outs, buf, sem = refs[-len(numbers) - 2 :]
    owned = source.shape[0]
    flip = jnp.int32(0)
    if any(numbers):
        position = lax.axis_index("row")
        pairs = near_pairs_of(position, refs[0], owned, devices)
        beyond = position + jnp.where(position % 2 == 1, 1, -1)
        used = []
        for t in range(owned):
            total = jnp.int32(0)
            for s in range(owned):
                count = count_between(pairs, position * owned + t, beyond * owned + s)
                total = total + (count != 0).astype(jnp.int32)
            used.append(total)
        flip = flip_of(used)
    places = [cell_of(cells, number, flip) for number in numbers]
    rows, cols = outs[0].shape
    tile = rows // CHUNK_TILES
    parts = [(n, i) for n in range(len(places)) for i in range(CHUNK_TILES)]

    def copies(n, i):
        t, at = places[n]
        part = pl.ds(i * tile, tile)
        held = buf.at[n, part]
        load = pltpu.make_async_copy(source.at[t, part, pl.ds(at, cols)], held, sem.at[0, n, i])
        return load, pltpu.make_async_copy(held, outs[n].at[part], sem.at[1, n, i])

    for n, i in parts:
        copies(n, i)[0].start()
    for n, i in parts:
        load, store = copies(n, i)
        load.wait()
        store.start()
    for n, i in parts:
        copies(n, i)[1].wait()


def copy_first_kernel(source, out, sem):
    rows, cols = out.shape
    tile = rows // CHUNK_TILES
    parts = [pl.ds(i * tile, tile) for i in range(CHUNK_TILES)]
    copies = [
        pltpu.make_async_copy(source.at[0, part, pl.ds(0, cols)], out.at[part], sem.at[i])
        for i, part in enumerate(parts)
    ]
    for copy in copies:
        copy.start()
    for copy in copies:
        copy.wait()


def pass_kernel(source, after, out):
    del source, after, out


def relay_plan(devices, chunks):
    if devices != 16 or chunks != 4:
        return []
    plan = []
    for z, chunk, alone in ((1, 0, True), (0, 0, False), (2, 1, False)):
        high, low = 4 * z + 3, 4 * z + 4
        plan.append((chunk, alone, [(high, low, 0), (low, high, devices - 1)]))
    return plan


def spec(space):
    return pl.BlockSpec(memory_space=space)


def on_device(fitted, fit_start, virt_domain, occ_energy, virt_energy, pair_partner):
    owned, aux, width = fitted.shape
    devices = lax.axis_size("row")
    buf_rows = 2 * REACH + aux
    wide_rows = aux + 2 * SUB + STEP
    smem, vmem, anywhere = spec(pltpu.SMEM), spec(pltpu.VMEM), spec(pl.ANY)

    outward = []
    for i in range(devices):
        to = i + 1 if i % 2 else i - 1
        if 0 <= to < devices:
            outward.append((i, to))
    inward = [(i, i ^ 1) for i in range(devices) if i ^ 1 < devices]

    def in_hbm(array):
        return pltpu.with_memory_space_constraint(array, pltpu.HBM)

    def in_vmem(array):
        return pltpu.with_memory_space_constraint(array, pltpu.VMEM)

    def first_chunk():
        return pl.pallas_call(
            copy_first_kernel,
            out_shape=pltpu.VMEM((aux, COLS), fitted.dtype),
            in_specs=[anywhere],
            out_specs=vmem,
            scratch_shapes=[pltpu.SemaphoreType.DMA((CHUNK_TILES,))],
            compiler_params=pltpu.CompilerParams(vmem_limit_bytes=CHUNK_VMEM),
            name="first_chunk",
        )(in_hbm(fitted))

    def chunks(numbers, *after):
        return pl.pallas_call(
            functools.partial(copy_kernel, numbers=numbers, cells=cells, devices=devices),
            out_shape=[jax.ShapeDtypeStruct((aux, COLS), fitted.dtype)] * len(numbers),
            in_specs=[anywhere, smem] + [vmem] * len(after),
            out_specs=[anywhere] * len(numbers),
            scratch_shapes=[
                pltpu.VMEM((len(numbers), aux, COLS), fitted.dtype),
                pltpu.SemaphoreType.DMA((2, len(numbers), CHUNK_TILES)),
            ],
            compiler_params=pltpu.CompilerParams(vmem_limit_bytes=CHUNK_VMEM),
            name="chunks",
        )(in_hbm(fitted), pair_partner, *map(in_vmem, after))

    def pass_on(block, after):
        return pl.pallas_call(
            pass_kernel,
            out_shape=jax.ShapeDtypeStruct(block.shape, block.dtype),
            in_specs=[anywhere] * 2,
            out_specs=anywhere,
            input_output_aliases={0: 0},
            compiler_params=pltpu.CompilerParams(vmem_limit_bytes=CHUNK_VMEM),
            name="pass_on",
        )(block, after)

    cells = [(t, at) for t in range(owned) for at in range(0, width, COLS)]
    last = len(cells) - 1
    plan = relay_plan(devices, len(cells))
    first_hops = [[(source, by) for source, _, by in pairs] for _, _, pairs in plan]
    second_hops = [[(by, to) for _, to, by in pairs] for _, _, pairs in plan]

    def exchange(number, block):
        pairs = list(outward)
        for (at, alone, group), hop in zip(plan, first_hops):
            if at == number:
                pairs = [pair for pair in pairs if pair not in {(a, b) for a, b, _ in group}]
                pairs += [] if alone else hop
        return lax.ppermute(block, "row", pairs)

    sent = [first_chunk()]
    mate = lax.ppermute(lax.optimization_barrier((fitted, sent[0]))[0], "row", inward)
    far = [exchange(0, sent[0])]
    rest = chunks(list(range(1, len(cells))) + [0] * bool(plan), sent[0])
    sent += rest[:last]
    early = {
        index: lax.ppermute(rest[last], "row", first_hops[index])
        for index, (_, alone, _) in enumerate(plan)
        if alone
    }
    far += [exchange(number, sent[number]) for number in range(1, last + 1)]

    unit = 4 * aux * width * COLS
    acc_shape = pltpu.VMEM((owned, aux, width), jnp.float32)
    dens_shape = pltpu.VMEM((owned, width, width), jnp.float32)
    ft_shape = pltpu.VMEM((owned, width, aux), fitted.dtype)
    token_shape = jax.ShapeDtypeStruct((8, LANES), jnp.int32)
    slots = 3 * owned * owned

    def cost(blocks):
        return pl.CostEstimate(
            flops=100 * unit * blocks * owned, bytes_accessed=8 << 20, transcendentals=0
        )

    ints, occ, eps_col, eps_row, acc, dens, ft, token = pl.pallas_call(
        functools.partial(
            first_kernel,
            devices=devices,
            targets=[[to for _, to, _ in pairs] for _, _, pairs in plan],
            relays=sorted({by for _, _, pairs in plan for _, _, by in pairs}),
        ),
        out_shape=(
            jax.ShapeDtypeStruct((Plan(None, owned).at_flip(len(plan)) + 1,), jnp.int32),
            jax.ShapeDtypeStruct((slots,), jnp.float32),
            pltpu.VMEM((owned, width, 1), jnp.float32),
            pltpu.VMEM((3 * owned, 1, width), jnp.float32),
            acc_shape,
            dens_shape,
            ft_shape,
            token_shape,
        ),
        in_specs=[smem] * 3 + [vmem] * 3 + [anywhere],
        out_specs=(smem,) * 2 + (vmem,) * 6,
        scratch_shapes=[
            pltpu.VMEM((wide_rows, width), jnp.float32),
            pltpu.VMEM((buf_rows, width), fitted.dtype),
            pltpu.VMEM((width, width), fitted.dtype),
        ],
        compiler_params=pltpu.CompilerParams(vmem_limit_bytes=NEAR_VMEM),
        cost_estimate=cost(len(cells)),
        name="first",
    )(
        fit_start, occ_energy, pair_partner, virt_domain, virt_energy.reshape(-1, 1),
        in_hbm(fitted), sent[last - 1],
    )
    state = {"acc": acc, "dens": dens, "token": token}
    hops = []

    def add_pairs(
        kernel, block_specs, blocks, cols, limit, name,
        extra=(), outs=(), aliases={}, scratch=(), token=True,
    ):
        specs = [smem] * 2 + [vmem] * 5 + block_specs
        results = pl.pallas_call(
            kernel,
            out_shape=(acc_shape, dens_shape) + (token_shape,) * token + tuple(outs),
            in_specs=specs + [anywhere] * (1 + len(extra)),
            out_specs=(vmem,) * (2 + token) + (anywhere,) * len(outs),
            input_output_aliases={5: 0, 6: 1, **aliases},
            scratch_shapes=[
                pltpu.VMEM((wide_rows, cols), jnp.float32),
                pltpu.VMEM((buf_rows, cols), fitted.dtype),
                *scratch,
            ],
            compiler_params=pltpu.CompilerParams(vmem_limit_bytes=limit),
            cost_estimate=cost(cols // COLS),
            name=name,
        )(
            ints, occ, in_vmem(eps_col), in_vmem(eps_row), in_vmem(ft), in_vmem(state["acc"]),
            in_vmem(state["dens"]), *blocks, *extra, state["token"],
        )
        state.update(acc=results[0], dens=results[1], token=results[2])
        return results[2 + token :]

    hops = {index: lax.ppermute(early[index], "row", second_hops[index]) for index in early}
    turned_cols = (pltpu.VMEM((COLS, width), fitted.dtype),)

    def near_pairs(late, *extra):
        add_pairs(
            functools.partial(near_kernel, ways=len(plan), late=late),
            [anywhere] * 2, [in_hbm(fitted), mate], width, NEAR_VMEM, f"near_pairs_{late}",
            extra=extra,
            scratch=(
                pltpu.VMEM((width, width), fitted.dtype),
                pltpu.VMEM((2, aux, width), fitted.dtype),
                pltpu.SemaphoreType.DMA((2,)),
            ),
        )

    near_pairs(0, *early.values())
    for number in range(last):
        for index, (at, alone, _) in enumerate(plan):
            if at == number and not alone:
                far[number] = state["token"] = pass_on(far[number], state["token"])
                hops[index] = lax.ppermute(far[number], "row", second_hops[index])
                if index == len(plan) - 1:
                    near_pairs(1)
        ways = [index for index, (at, _, _) in enumerate(plan) if at == number]
        add_pairs(
            functools.partial(
                far_kernel, ways=ways, total_ways=len(plan), cells=cells, number=number
            ),
            [vmem], [far[number]], COLS, FAR_VMEM, f"far_pairs_{number}", scratch=turned_cols,
        )
    results = (
        jax.ShapeDtypeStruct(fitted.shape, fitted.dtype),
        jax.ShapeDtypeStruct((owned, width, width), jnp.float32),
    )
    out_scratch = (
        pltpu.VMEM((owned, aux, width), fitted.dtype),
        pltpu.SemaphoreType.DMA((owned, OUT_TILES + 1)),
    )
    ready = add_pairs(
        functools.partial(
            relayed_kernel, numbers=[at for at, _, _ in plan], cells=cells
        ),
        [anywhere] * len(hops), [hops[index] for index in range(len(plan))], COLS, FAR_VMEM,
        "relayed_pairs",
        outs=results,
        scratch=turned_cols
        + (pltpu.VMEM((aux, COLS), fitted.dtype), out_scratch[0], pltpu.SemaphoreType.DMA)
        + out_scratch[1:],
    )
    gradient, density = add_pairs(
        functools.partial(last_kernel, total_ways=len(plan), cells=cells),
        [anywhere] * 3, [far[last], *ready], COLS, FAR_VMEM, "last_pairs",
        outs=results,
        aliases={8: 2, 9: 3},
        scratch=turned_cols
        + (pltpu.VMEM((aux, COLS), fitted.dtype),)
        + out_scratch
        + (pltpu.SemaphoreType.DMA((LOAD_TILES,)),),
        token=False,
    )
    return gradient, density


def solution(mesh):
    placed = (
        P(("parts", "row"), None, None),
        P("parts"),
        P("parts", None),
        P("parts"),
        P("parts"),
        P("parts"),
    )
    return jax.shard_map(
        on_device,
        mesh=mesh,
        in_specs=placed,
        out_specs=(P(("parts", "row"), None, None), P(("parts", "row"), None, None)),
        check_vma=False,
    )
```

```python
import functools

import jax
import jax.numpy as jnp
from jax import lax
from jax.experimental import pallas as pl
from jax.experimental.pallas import tpu as pltpu
from jax.sharding import PartitionSpec as P

SUB = 16
STEP = 8
LANES = 128
ROW_TILES = 2
OUT_TILES = 4
CHUNK_TILES = 2
COLS = 256
REACH = 1024
NEAR_VMEM = 22 * 1024 * 1024
FAR_VMEM = 16 * 1024 * 1024
CHUNK_VMEM = 6 * 1024 * 1024


class Plan:
    def __init__(self, ref, owned):
        self.ref, self.owned = ref, owned
        self.slots = 3 * owned * owned

    def slot(self, group, s, t):
        return (group * self.owned + s) * self.owned + t

    def at_shift(self, slot):
        return self.slots + slot

    def at_lead(self, slot):
        return 2 * self.slots + slot

    def at_way(self, number):
        return 3 * self.slots + number

    def at_late(self, ways):
        return self.at_way(ways)

    def at_flip(self, ways):
        return self.at_way(ways) + 1

    def count(self, slot):
        return self.ref[slot]

    def offset(self, slot):
        return pl.multiple_of(REACH + self.ref[self.at_shift(slot)], SUB)

    def lead(self, slot):
        return self.ref[self.at_lead(slot)]

    def way(self, number):
        return self.ref[self.at_way(number)]


def dot(a, b):
    return jnp.dot(a, b, preferred_element_type=jnp.float32)


def tile_of(rows):
    return max(n for n in range(SUB, 705, SUB) if rows % n == 0)


def rows_from(load, start, count):
    skip = start % STEP
    base = pl.multiple_of(start - skip, STEP)
    block = load(base, count + STEP)
    width = block.shape[1]
    block = block.reshape(count // STEP + 1, STEP, width)
    turned = pltpu.roll(block, (STEP - skip) % STEP, 1)
    row = lax.broadcasted_iota(jnp.int32, (count // STEP, STEP, width), 1)
    return jnp.where(row < STEP - skip, turned[:-1], turned[1:]).reshape(count, width)


def clear_margins(buf, rows):
    width = buf.shape[1]
    buf[:REACH, :] = jnp.zeros((REACH, width), buf.dtype)
    buf[REACH + rows :, :] = jnp.zeros((buf.shape[0] - REACH - rows, width), buf.dtype)


def clear_ends(wide):
    rows, width = wide.shape
    wide[:SUB, :] = jnp.zeros((SUB, width), jnp.float32)
    wide[rows - SUB - STEP :, :] = jnp.zeros((SUB + STEP, width), jnp.float32)


def widen(source, wide):
    aux = source.shape[0]
    clear_ends(wide)
    tile = tile_of(aux)

    def one(i, carry):
        base = pl.multiple_of(i * tile, SUB)
        wide[pl.ds(pl.multiple_of(SUB + base, SUB), tile), :] = source[
            pl.ds(base, tile), :
        ].astype(jnp.float32)
        return carry

    lax.fori_loop(0, aux // tile, one, 0)


def place(lead, wide, buf, rows, to=REACH):
    step = tile_of(rows)

    def move(i, carry):
        base = pl.multiple_of(i * step, SUB)
        moved = rows_from(lambda at, n: wide[pl.ds(at, n), :], SUB - lead + base, step)
        buf[pl.ds(pl.multiple_of(to + base, SUB), step), :] = moved.astype(buf.dtype)
        return carry

    lax.fori_loop(0, rows // step, move, 0)


def amplitudes(coulomb, denominator, weight):
    amplitude = (coulomb / denominator).astype(jnp.bfloat16)
    weighted = (amplitude.astype(jnp.float32) * weight).astype(jnp.bfloat16)
    return amplitude, weighted.T


def needed(plan, group, t):
    total = jnp.int32(0)
    for s in range(plan.owned):
        total = total + plan.count(plan.slot(group, s, t))
    return total != 0


def amplitude_of(plan, occ, slot, s, partner, at, eps_col, eps_row, ft, buf):
    rows = ft.shape[2]
    cols = buf.shape[1]
    coulomb = dot(ft[s], buf[pl.ds(plan.offset(slot), rows), :])
    denominator = occ[slot] - eps_col[s] - eps_row[partner, :, pl.ds(at, cols)]
    return amplitudes(coulomb, denominator, plan.count(slot).astype(jnp.float32))


def add_block(plan, occ, group, t, at, eps_col, eps_row, ft, source, wide, buf, acc, dens, turned):
    owned, rows, width = acc.shape
    scale = float(width) ** -0.5
    step = rows // ROW_TILES

    @pl.when(needed(plan, group, t))
    def _():
        widen(source, wide)

    def one(s, carry):
        slot = plan.slot(group, s, t)

        @pl.when(plan.count(slot) != 0)
        def _():
            place(plan.lead(slot), wide, buf, rows + SUB)
            amplitude, turned[...] = amplitude_of(
                plan, occ, slot, s, group * owned + t, at, eps_col, eps_row, ft, buf
            )
            dens[s] += scale * dot(amplitude, turned[...])

            def add(i, inner):
                base = pl.multiple_of(i * step, SUB)
                block = buf[pl.ds(pl.multiple_of(plan.offset(slot) + base, SUB), step), :]
                acc[s, pl.ds(base, step), :] += dot(block, turned[...])
                return inner

            lax.fori_loop(0, ROW_TILES, add, 0)

        return carry

    lax.fori_loop(0, owned, one, 0)


def near_pairs_of(position, pair_partner, owned, devices):
    pairs_here = pair_partner.shape[0] // devices
    pairs = []
    for step in (-1, 0, 1):
        group = position + step
        known = (group >= 0) & (group < devices)
        held = jnp.clip(group, 0, devices - 1)
        for n in range(pairs_here):
            pairs.append((known, group * owned + n % owned, pair_partner[held * pairs_here + n]))
    return pairs


def count_between(pairs, one, other):
    total = jnp.int32(0)
    for known, first, second in pairs:
        forth = known & (first == one) & (second == other)
        back = known & (second == one) & (first == other)
        total = total + forth.astype(jnp.int32) + back.astype(jnp.int32)
    return total


def flip_of(used):
    return (used[0] < used[-1]).astype(jnp.int32)


def cell_of(cells, number, flip):
    halves = len([cell for cell in cells if cell[0] == 0])
    flipped = cells[:1] + cells[halves:] + cells[1:halves]
    (t, at), (other_t, other_at) = cells[number], flipped[number]
    if (t, at) == (other_t, other_at):
        return t, at
    return (
        jnp.where(flip == 1, other_t, t),
        pl.multiple_of(jnp.where(flip == 1, other_at, at), COLS),
    )


def make_plan(
    fit_start, occ_energy, pair_partner, domains, energy, ints, occ, eps_col, eps_row,
    *, devices, targets, relays,
):
    owned, width = eps_col.shape[:2]
    orbitals = fit_start.shape[0]
    plan = Plan(ints, owned)
    position = lax.axis_index("row")
    side = jnp.where(position % 2 == 1, 1, -1)
    places = [
        base * owned + t
        for base in (position, position - side, position + side)
        for t in range(owned)
    ]
    inside = [jnp.clip(orbital, 0, orbitals - 1) for orbital in places]
    starts = [fit_start[orbital] for orbital in inside]
    pairs = near_pairs_of(position, pair_partner, owned, devices)
    used = [jnp.int32(0)] * owned
    for group in range(3):
        for s in range(owned):
            for t in range(owned):
                slot = plan.slot(group, s, t)
                other = group * owned + t
                total = count_between(pairs, places[s], places[other])
                ints[slot] = total
                if group == 2:
                    used[t] = used[t] + (total != 0).astype(jnp.int32)
                apart = starts[other] - starts[s]
                ints[plan.at_shift(slot)] = (apart & (SUB - 1)) - apart
                ints[plan.at_lead(slot)] = apart & (SUB - 1)
                occ[slot] = occ_energy[inside[s]] + occ_energy[inside[other]]
    for number, group in enumerate(targets):
        way = jnp.int32(0)
        for to in group:
            way = jnp.where(position == to, 1, way)
        ints[plan.at_way(number)] = way
    late = jnp.int32(0)
    for row in relays:
        late = jnp.where(position == row, 1, late)
    ints[plan.at_late(len(targets))] = late
    ints[plan.at_flip(len(targets))] = flip_of(used)
    entries = energy.shape[0]
    table = lax.broadcasted_iota(jnp.int32, (entries, width), 0)
    for n, orbital in enumerate(inside):
        domain = domains[pl.ds(orbital, 1), :]
        row = jnp.sum(jnp.where(table == domain, energy[...], 0.0), axis=0, keepdims=True)
        eps_row[n] = row
        if n < owned:
            eps_col[n] = jnp.broadcast_to(row, (LANES, width)).T[:, :1]
    return plan


def add_blocks(plan, occ, sources, eps_col, eps_row, ft, wide, buf, acc, dens, turned, raw, sem):
    copies = [
        pltpu.make_async_copy(block, raw.at[n % 2], sem.at[n % 2])
        for n, (_, _, block) in enumerate(sources)
    ]
    copies[0].start()
    clear_margins(buf, raw.shape[1] + SUB)
    for n, (group, t, _) in enumerate(sources):
        if n + 1 < len(copies):
            copies[n + 1].start()
        copies[n].wait()
        add_block(
            plan, occ, group, t, 0, eps_col, eps_row, ft, raw.at[n % 2], wide, buf, acc, dens, turned
        )


def first_kernel(
    fit_start, occ_energy, pair_partner, domains, energy, own, after,
    ints, occ, eps_col, eps_row, acc, dens, ft, token, wide, buf, turned,
    *, devices, targets, relays,
):
    del after
    token[...] = jnp.zeros_like(token)
    plan = make_plan(
        fit_start, occ_energy, pair_partner, domains, energy, ints, occ, eps_col, eps_row,
        devices=devices, targets=targets, relays=relays,
    )
    owned, aux, width = own.shape
    acc[...] = jnp.zeros_like(acc)
    dens[...] = jnp.zeros_like(dens)
    for t in range(owned):

        def turn(i, carry):
            at = pl.multiple_of(i * LANES, LANES)
            ft[t, :, pl.ds(at, LANES)] = own[t, pl.ds(at, LANES), :].T
            return carry

        lax.fori_loop(0, aux // LANES, turn, 0)

    @pl.when(ints[plan.at_late(len(targets))] == 1)
    def _():
        clear_margins(buf, aux + SUB)
        for t in range(owned):
            add_block(
                plan, occ, 0, t, 0, eps_col, eps_row, ft, own.at[t], wide, buf, acc, dens, turned
            )


def near_kernel(
    ints, occ, eps_col, eps_row, ft, acc_in, dens_in, own, mate, *refs, ways, late
):
    del acc_in, dens_in
    acc, dens, token, wide, buf, turned, raw, sem = refs[-8:]
    token[...] = jnp.zeros_like(token)
    owned = own.shape[0]
    plan = Plan(ints, owned)
    groups = ((1, mate),) if late else ((0, own), (1, mate))
    sources = [(group, t, blocks.at[t]) for group, blocks in groups for t in range(owned)]

    @pl.when(ints[plan.at_late(ways)] == late)
    def _():
        add_blocks(
            plan, occ, sources, eps_col, eps_row, ft, wide, buf, acc, dens, turned, raw, sem
        )


def far_kernel(
    ints, occ, eps_col, eps_row, ft, acc_in, dens_in, block, after,
    acc, dens, token, wide, buf, turned, *, ways, total_ways, cells, number,
):
    del acc_in, dens_in, after
    token[...] = jnp.zeros_like(token)
    plan = Plan(ints, acc.shape[0])
    t, at = cell_of(cells, number, ints[plan.at_flip(total_ways)])
    here = needed(plan, 2, t)
    for way in ways:
        here = here & (plan.way(way) == 0)

    @pl.when(here)
    def _():
        clear_margins(buf, block.shape[0] + SUB)
        add_block(plan, occ, 2, t, at, eps_col, eps_row, ft, block, wide, buf, acc, dens, turned)


def send_out(s, tile_of_rows, dens, ready, out, dens_out, sem):
    step = out.shape[1] // OUT_TILES
    pltpu.make_async_copy(dens.at[s], dens_out.at[s], sem.at[s, OUT_TILES]).start()

    def one(i, carry):
        part = pl.ds(pl.multiple_of(i * step, SUB), step)
        ready[s, part, :] = tile_of_rows(i * step, step).astype(ready.dtype)
        pltpu.make_async_copy(ready.at[s, part], out.at[s, part], sem.at[s, i]).start()
        return carry

    lax.fori_loop(0, OUT_TILES, one, 0)


def wait_out(s, dens, ready, out, dens_out, sem):
    step = out.shape[1] // OUT_TILES
    pltpu.make_async_copy(dens.at[s], dens_out.at[s], sem.at[s, OUT_TILES]).wait()
    for i in range(OUT_TILES):
        part = pl.ds(i * step, step)
        pltpu.make_async_copy(ready.at[s, part], out.at[s, part], sem.at[s, i]).wait()


def relayed_kernel(
    ints, occ, eps_col, eps_row, ft, acc_in, dens_in, *refs, numbers, cells
):
    del acc_in, dens_in
    *blocks, _, acc, dens, token, out, dens_out, wide, buf, turned, raw, ready, sem, out_sem = refs
    token[...] = jnp.zeros_like(token)
    owned = acc.shape[0]
    plan = Plan(ints, owned)
    flip = ints[plan.at_flip(len(numbers))]
    last, _ = cell_of(cells, len(cells) - 1, flip)
    for way, (block, number) in enumerate(zip(blocks, numbers)):
        t, at = cell_of(cells, number, flip)

        @pl.when(needed(plan, 2, t) & (plan.way(way) == 1))
        def _():
            copy = pltpu.make_async_copy(block, raw, sem)
            copy.start()
            clear_margins(buf, raw.shape[0] + SUB)
            copy.wait()
            add_block(plan, occ, 2, t, at, eps_col, eps_row, ft, raw, wide, buf, acc, dens, turned)

    for s in range(owned):

        @pl.when(plan.count(plan.slot(2, s, last)) == 0)
        def _():
            send_out(
                s,
                lambda base, n: acc[s, pl.ds(pl.multiple_of(base, SUB), n), :],
                dens, ready, out, dens_out, out_sem,
            )

    for s in range(owned):

        @pl.when(plan.count(plan.slot(2, s, last)) == 0)
        def _():
            wait_out(s, dens, ready, out, dens_out, out_sem)


def last_kernel(
    ints, occ, eps_col, eps_row, ft, acc_in, dens_in, block, out_in, dens_out_in, after,
    acc, dens, out, dens_out, wide, buf, turned, ready, sem, load_sem, *, total_ways, cells,
):
    del acc_in, dens_in, out_in, dens_out_in, after
    owned, aux, width = out.shape
    plan = Plan(ints, owned)
    t, at = cell_of(cells, len(cells) - 1, ints[plan.at_flip(total_ways)])
    scale = float(width) ** -0.5

    rows = block.shape[0]
    aligned = buf.at[pl.ds(REACH, rows)]
    sent_lead = plan.lead(plan.slot(2, owned - 1, t))
    for s in reversed(range(owned - 1)):
        slot = plan.slot(2, s, t)
        sent_lead = jnp.where(plan.count(slot) != 0, plan.lead(slot), sent_lead)

    @pl.when(needed(plan, 2, t))
    def _():
        load = pltpu.make_async_copy(block, aligned, load_sem)
        load.start()
        clear_margins(buf, rows)
        load.wait()

    def one(s, seen):
        slot = plan.slot(2, s, t)
        used = (plan.count(slot) != 0).astype(jnp.int32)

        @pl.when(seen * used == 1)
        def _():
            widen(aligned, wide)
            place(plan.lead(slot) - sent_lead, wide, buf, rows)

        @pl.when(used == 1)
        def _():
            amplitude, turned[...] = amplitude_of(
                plan, occ, slot, s, 2 * owned + t, at, eps_col, eps_row, ft, buf
            )
            dens[s] += scale * dot(amplitude, turned[...])

            def total(base, n):
                rows = buf[pl.ds(pl.multiple_of(plan.offset(slot) + base, SUB), n), :]
                return acc[s, pl.ds(pl.multiple_of(base, SUB), n), :] + dot(rows, turned[...])

            send_out(s, total, dens, ready, out, dens_out, sem)

        return jnp.maximum(seen, used)

    lax.fori_loop(0, owned, one, jnp.int32(0))
    for s in range(owned):

        @pl.when(plan.count(plan.slot(2, s, t)) != 0)
        def _():
            wait_out(s, dens, ready, out, dens_out, sem)


def sent_order(pair_partner, owned, devices):
    position = lax.axis_index("row")
    pairs = near_pairs_of(position, pair_partner, owned, devices)
    beyond = position + jnp.where(position % 2 == 1, 1, -1)
    used, aims = [], []
    for t in range(owned):
        total = jnp.int32(0)
        aim = beyond * owned + owned - 1
        for s in reversed(range(owned)):
            count = count_between(pairs, position * owned + t, beyond * owned + s)
            total = total + (count != 0).astype(jnp.int32)
            aim = jnp.where(count != 0, beyond * owned + s, aim)
        used.append(total)
        aims.append(aim)
    return flip_of(used), aims


def last_chunk_kernel(source, pair_partner, fit_start, after, out, raw, wide, sem, *, cells, devices):
    del after
    owned = source.shape[0]
    position = lax.axis_index("row")
    flip, aims = sent_order(pair_partner, owned, devices)
    t, at = cell_of(cells, len(cells) - 1, flip)
    load = pltpu.make_async_copy(source.at[t, :, pl.ds(at, out.shape[1])], raw, sem)
    load.start()
    aim = aims[-1]
    for n in reversed(range(owned - 1)):
        aim = jnp.where(t == n, aims[n], aim)
    aim = jnp.clip(aim, 0, fit_start.shape[0] - 1)
    lead = (fit_start[position * owned + t] - fit_start[aim]) & (SUB - 1)
    load.wait()
    widen(raw, wide)
    place(lead, wide, out, out.shape[0], 0)


def copy_kernel(source, *refs, numbers, cells, devices):
    *outs, buf, sem = refs[-len(numbers) - 2 :]
    owned = source.shape[0]
    flip = jnp.int32(0)
    if any(numbers):
        flip, _ = sent_order(refs[0], owned, devices)
    places = [cell_of(cells, number, flip) for number in numbers]
    rows, cols = outs[0].shape
    tile = rows // CHUNK_TILES
    parts = [(n, i) for n in range(len(places)) for i in range(CHUNK_TILES)]

    def copies(n, i):
        t, at = places[n]
        part = pl.ds(i * tile, tile)
        held = buf.at[n, part]
        load = pltpu.make_async_copy(source.at[t, part, pl.ds(at, cols)], held, sem.at[0, n, i])
        return load, pltpu.make_async_copy(held, outs[n].at[part], sem.at[1, n, i])

    for n, i in parts:
        copies(n, i)[0].start()
    for n, i in parts:
        load, store = copies(n, i)
        load.wait()
        store.start()
    for n, i in parts:
        copies(n, i)[1].wait()


def pass_kernel(source, after, out):
    del source, after, out


def relay_plan(devices, chunks):
    if devices != 16 or chunks != 4:
        return []
    plan = []
    for z, chunk, alone in ((1, 0, True), (0, 0, False), (2, 1, False)):
        high, low = 4 * z + 3, 4 * z + 4
        plan.append((chunk, alone, [(high, low, 0), (low, high, devices - 1)]))
    return plan


def spec(space):
    return pl.BlockSpec(memory_space=space)


def on_device(fitted, fit_start, virt_domain, occ_energy, virt_energy, pair_partner):
    owned, aux, width = fitted.shape
    devices = lax.axis_size("row")
    buf_rows = 2 * REACH + aux
    wide_rows = aux + 2 * SUB + STEP
    smem, vmem, anywhere = spec(pltpu.SMEM), spec(pltpu.VMEM), spec(pl.ANY)

    outward = []
    for i in range(devices):
        to = i + 1 if i % 2 else i - 1
        if 0 <= to < devices:
            outward.append((i, to))
    inward = [(i, i ^ 1) for i in range(devices) if i ^ 1 < devices]

    def in_hbm(array):
        return pltpu.with_memory_space_constraint(array, pltpu.HBM)

    def in_vmem(array):
        return pltpu.with_memory_space_constraint(array, pltpu.VMEM)

    def chunks(numbers, *after):
        return pl.pallas_call(
            functools.partial(copy_kernel, numbers=numbers, cells=cells, devices=devices),
            out_shape=[jax.ShapeDtypeStruct((aux, COLS), fitted.dtype)] * len(numbers),
            in_specs=[anywhere] + [smem] * any(numbers) + [anywhere] * len(after),
            out_specs=[anywhere] * len(numbers),
            scratch_shapes=[
                pltpu.VMEM((len(numbers), aux, COLS), fitted.dtype),
                pltpu.SemaphoreType.DMA((2, len(numbers), CHUNK_TILES)),
            ],
            compiler_params=pltpu.CompilerParams(vmem_limit_bytes=CHUNK_VMEM),
            name="chunks",
        )(in_hbm(fitted), *[pair_partner] * any(numbers), *after)

    def last_chunk(after):
        return pl.pallas_call(
            functools.partial(last_chunk_kernel, cells=cells, devices=devices),
            out_shape=jax.ShapeDtypeStruct((aux + SUB, COLS), fitted.dtype),
            in_specs=[anywhere, smem, smem, anywhere],
            out_specs=vmem,
            scratch_shapes=[
                pltpu.VMEM((aux, COLS), fitted.dtype),
                pltpu.VMEM((wide_rows, COLS), jnp.float32),
                pltpu.SemaphoreType.DMA,
            ],
            compiler_params=pltpu.CompilerParams(vmem_limit_bytes=CHUNK_VMEM),
            name="last_chunk",
        )(in_hbm(fitted), pair_partner, fit_start, after)

    def pass_on(block, after):
        return pl.pallas_call(
            pass_kernel,
            out_shape=jax.ShapeDtypeStruct(block.shape, block.dtype),
            in_specs=[anywhere] * 2,
            out_specs=anywhere,
            input_output_aliases={0: 0},
            compiler_params=pltpu.CompilerParams(vmem_limit_bytes=CHUNK_VMEM),
            name="pass_on",
        )(block, after)

    cells = [(t, at) for t in range(owned) for at in range(0, width, COLS)]
    last = len(cells) - 1
    plan = relay_plan(devices, len(cells))
    first_hops = [[(source, by) for source, _, by in pairs] for _, _, pairs in plan]
    second_hops = [[(by, to) for _, to, by in pairs] for _, _, pairs in plan]

    def exchange(number, block):
        pairs = list(outward)
        for (at, alone, group), hop in zip(plan, first_hops):
            if at == number:
                pairs = [pair for pair in pairs if pair not in {(a, b) for a, b, _ in group}]
                pairs += [] if alone else hop
        return lax.ppermute(block, "row", pairs)

    sent = list(chunks([0]))
    mate = lax.ppermute(lax.optimization_barrier((fitted, sent[0]))[0], "row", inward)
    far = [exchange(0, sent[0])]
    rest = chunks(list(range(1, last)) + [0] * bool(plan), sent[0])
    sent += rest[: last - 1]
    early = {
        index: lax.ppermute(rest[last - 1], "row", first_hops[index])
        for index, (_, alone, _) in enumerate(plan)
        if alone
    }
    far += [exchange(number, sent[number]) for number in range(1, last)]

    unit = 4 * aux * width * COLS
    acc_shape = pltpu.VMEM((owned, aux, width), jnp.float32)
    dens_shape = pltpu.VMEM((owned, width, width), jnp.float32)
    ft_shape = pltpu.VMEM((owned, width, aux), fitted.dtype)
    token_shape = jax.ShapeDtypeStruct((8, LANES), jnp.int32)
    slots = 3 * owned * owned

    def cost(blocks):
        return pl.CostEstimate(
            flops=100 * unit * blocks * owned, bytes_accessed=8 << 20, transcendentals=0
        )

    ints, occ, eps_col, eps_row, acc, dens, ft, token = pl.pallas_call(
        functools.partial(
            first_kernel,
            devices=devices,
            targets=[[to for _, to, _ in pairs] for _, _, pairs in plan],
            relays=sorted({by for _, _, pairs in plan for _, _, by in pairs}),
        ),
        out_shape=(
            jax.ShapeDtypeStruct((Plan(None, owned).at_flip(len(plan)) + 1,), jnp.int32),
            jax.ShapeDtypeStruct((slots,), jnp.float32),
            pltpu.VMEM((owned, width, 1), jnp.float32),
            pltpu.VMEM((3 * owned, 1, width), jnp.float32),
            acc_shape,
            dens_shape,
            ft_shape,
            token_shape,
        ),
        in_specs=[smem] * 3 + [vmem] * 3 + [anywhere],
        out_specs=(smem,) * 2 + (vmem,) * 6,
        scratch_shapes=[
            pltpu.VMEM((wide_rows, width), jnp.float32),
            pltpu.VMEM((buf_rows, width), fitted.dtype),
            pltpu.VMEM((width, width), fitted.dtype),
        ],
        compiler_params=pltpu.CompilerParams(vmem_limit_bytes=NEAR_VMEM),
        cost_estimate=cost(len(cells)),
        name="first",
    )(
        fit_start, occ_energy, pair_partner, virt_domain, virt_energy.reshape(-1, 1),
        in_hbm(fitted), sent[last - 1],
    )
    state = {"acc": acc, "dens": dens, "token": token}
    hops = []

    def add_pairs(
        kernel, block_specs, blocks, cols, limit, name,
        extra=(), outs=(), aliases={}, scratch=(), token=True, extra_rows=0,
    ):
        specs = [smem] * 2 + [vmem] * 5 + block_specs
        results = pl.pallas_call(
            kernel,
            out_shape=(acc_shape, dens_shape) + (token_shape,) * token + tuple(outs),
            in_specs=specs + [anywhere] * (1 + len(extra)),
            out_specs=(vmem,) * (2 + token) + (anywhere,) * len(outs),
            input_output_aliases={5: 0, 6: 1, **aliases},
            scratch_shapes=[
                pltpu.VMEM((wide_rows + extra_rows, cols), jnp.float32),
                pltpu.VMEM((buf_rows, cols), fitted.dtype),
                *scratch,
            ],
            compiler_params=pltpu.CompilerParams(vmem_limit_bytes=limit),
            cost_estimate=cost(cols // COLS),
            name=name,
        )(
            ints, occ, in_vmem(eps_col), in_vmem(eps_row), in_vmem(ft), in_vmem(state["acc"]),
            in_vmem(state["dens"]), *blocks, *extra, state["token"],
        )
        state.update(acc=results[0], dens=results[1], token=results[2])
        return results[2 + token :]

    state["token"] = last_chunk(token)
    far.append(exchange(last, state["token"]))
    hops = {index: lax.ppermute(early[index], "row", second_hops[index]) for index in early}
    turned_cols = (pltpu.VMEM((COLS, width), fitted.dtype),)

    def near_pairs(late, *extra):
        add_pairs(
            functools.partial(near_kernel, ways=len(plan), late=late),
            [anywhere] * 2, [in_hbm(fitted), mate], width, NEAR_VMEM, f"near_pairs_{late}",
            extra=extra,
            scratch=(
                pltpu.VMEM((width, width), fitted.dtype),
                pltpu.VMEM((2, aux, width), fitted.dtype),
                pltpu.SemaphoreType.DMA((2,)),
            ),
        )

    near_pairs(0, *early.values())
    for number in range(last):
        for index, (at, alone, _) in enumerate(plan):
            if at == number and not alone:
                far[number] = state["token"] = pass_on(far[number], state["token"])
                hops[index] = lax.ppermute(far[number], "row", second_hops[index])
                if index == len(plan) - 1:
                    near_pairs(1)
        ways = [index for index, (at, _, _) in enumerate(plan) if at == number]
        add_pairs(
            functools.partial(
                far_kernel, ways=ways, total_ways=len(plan), cells=cells, number=number
            ),
            [vmem], [far[number]], COLS, FAR_VMEM, f"far_pairs_{number}", scratch=turned_cols,
        )
    results = (
        jax.ShapeDtypeStruct(fitted.shape, fitted.dtype),
        jax.ShapeDtypeStruct((owned, width, width), jnp.float32),
    )
    out_scratch = (
        pltpu.VMEM((owned, aux, width), fitted.dtype),
        pltpu.SemaphoreType.DMA((owned, OUT_TILES + 1)),
    )
    ready = add_pairs(
        functools.partial(
            relayed_kernel, numbers=[at for at, _, _ in plan], cells=cells
        ),
        [anywhere] * len(hops), [hops[index] for index in range(len(plan))], COLS, FAR_VMEM,
        "relayed_pairs",
        outs=results,
        scratch=turned_cols
        + (pltpu.VMEM((aux, COLS), fitted.dtype), out_scratch[0], pltpu.SemaphoreType.DMA)
        + out_scratch[1:],
    )
    gradient, density = add_pairs(
        functools.partial(last_kernel, total_ways=len(plan), cells=cells),
        [anywhere] * 3, [far[last], *ready], COLS, FAR_VMEM, "last_pairs",
        outs=results,
        aliases={8: 2, 9: 3},
        scratch=turned_cols + out_scratch + (pltpu.SemaphoreType.DMA,),
        extra_rows=SUB,
        token=False,
    )
    return gradient, density


def solution(mesh):
    placed = (
        P(("parts", "row"), None, None),
        P("parts"),
        P("parts", None),
        P("parts"),
        P("parts"),
        P("parts"),
    )
    return jax.shard_map(
        on_device,
        mesh=mesh,
        in_specs=placed,
        out_specs=(P(("parts", "row"), None, None), P(("parts", "row"), None, None)),
        check_vma=False,
    )
```

```python
import functools

import jax
import jax.numpy as jnp
from jax import lax
from jax.experimental import pallas as pl
from jax.experimental.pallas import tpu as pltpu
from jax.sharding import PartitionSpec as P

SUB = 16
STEP = 8
LANES = 128
ROW_TILES = 2
OUT_TILES = 4
LOAD_TILES = 4
CHUNK_TILES = 2
COLS = 256
REACH = 1024
NEAR_VMEM = 22 * 1024 * 1024
FAR_VMEM = 16 * 1024 * 1024
CHUNK_VMEM = 6 * 1024 * 1024


class Plan:
    def __init__(self, ref, owned):
        self.ref, self.owned = ref, owned
        self.slots = 3 * owned * owned

    def slot(self, group, s, t):
        return (group * self.owned + s) * self.owned + t

    def at_shift(self, slot):
        return self.slots + slot

    def at_lead(self, slot):
        return 2 * self.slots + slot

    def at_way(self, number):
        return 3 * self.slots + number

    def at_late(self, ways):
        return self.at_way(ways)

    def at_flip(self, ways):
        return self.at_way(ways) + 1

    def count(self, slot):
        return self.ref[slot]

    def offset(self, slot):
        return pl.multiple_of(REACH + self.ref[self.at_shift(slot)], SUB)

    def lead(self, slot):
        return self.ref[self.at_lead(slot)]

    def way(self, number):
        return self.ref[self.at_way(number)]


def dot(a, b):
    return jnp.dot(a, b, preferred_element_type=jnp.float32)


def tile_of(rows):
    return max(n for n in range(SUB, 705, SUB) if rows % n == 0)


def rows_from(load, start, count):
    skip = start % STEP
    base = pl.multiple_of(start - skip, STEP)
    block = load(base, count + STEP)
    width = block.shape[1]
    block = block.reshape(count // STEP + 1, STEP, width)
    turned = pltpu.roll(block, (STEP - skip) % STEP, 1)
    row = lax.broadcasted_iota(jnp.int32, (count // STEP, STEP, width), 1)
    return jnp.where(row < STEP - skip, turned[:-1], turned[1:]).reshape(count, width)


def clear_margins(buf, rows):
    width = buf.shape[1]
    buf[:REACH, :] = jnp.zeros((REACH, width), buf.dtype)
    buf[REACH + rows :, :] = jnp.zeros((buf.shape[0] - REACH - rows, width), buf.dtype)


def clear_ends(wide):
    rows, width = wide.shape
    wide[:SUB, :] = jnp.zeros((SUB, width), jnp.float32)
    wide[rows - SUB - STEP :, :] = jnp.zeros((SUB + STEP, width), jnp.float32)


def widen(source, wide):
    aux = source.shape[0]
    clear_ends(wide)
    tile = aux // ROW_TILES

    def one(i, carry):
        base = pl.multiple_of(i * tile, SUB)
        wide[pl.ds(pl.multiple_of(SUB + base, SUB), tile), :] = source[
            pl.ds(base, tile), :
        ].astype(jnp.float32)
        return carry

    lax.fori_loop(0, ROW_TILES, one, 0)


def place(lead, wide, buf):
    rows = wide.shape[0] - SUB - STEP
    step = tile_of(rows)

    def move(i, carry):
        base = pl.multiple_of(i * step, SUB)
        moved = rows_from(lambda at, n: wide[pl.ds(at, n), :], SUB - lead + base, step)
        buf[pl.ds(pl.multiple_of(REACH + base, SUB), step), :] = moved.astype(buf.dtype)
        return carry

    lax.fori_loop(0, rows // step, move, 0)


def amplitudes(coulomb, denominator, weight):
    amplitude = (coulomb / denominator).astype(jnp.bfloat16)
    weighted = (amplitude.astype(jnp.float32) * weight).astype(jnp.bfloat16)
    return amplitude, weighted.T


def needed(plan, group, t):
    total = jnp.int32(0)
    for s in range(plan.owned):
        total = total + plan.count(plan.slot(group, s, t))
    return total != 0


def amplitude_of(plan, occ, slot, s, partner, at, eps_col, eps_row, ft, buf):
    rows = ft.shape[2]
    cols = buf.shape[1]
    coulomb = dot(ft[s], buf[pl.ds(plan.offset(slot), rows), :])
    denominator = occ[slot] - eps_col[s] - eps_row[partner, :, pl.ds(at, cols)]
    return amplitudes(coulomb, denominator, plan.count(slot).astype(jnp.float32))


def add_block(plan, occ, group, t, at, eps_col, eps_row, ft, source, wide, buf, acc, dens, turned):
    owned, rows, width = acc.shape
    scale = float(width) ** -0.5
    step = rows // ROW_TILES

    @pl.when(needed(plan, group, t))
    def _():
        widen(source, wide)

    def one(s, carry):
        slot = plan.slot(group, s, t)

        @pl.when(plan.count(slot) != 0)
        def _():
            place(plan.lead(slot), wide, buf)
            amplitude, turned[...] = amplitude_of(
                plan, occ, slot, s, group * owned + t, at, eps_col, eps_row, ft, buf
            )
            dens[s] += scale * dot(amplitude, turned[...])

            def add(i, inner):
                base = pl.multiple_of(i * step, SUB)
                block = buf[pl.ds(pl.multiple_of(plan.offset(slot) + base, SUB), step), :]
                acc[s, pl.ds(base, step), :] += dot(block, turned[...])
                return inner

            lax.fori_loop(0, ROW_TILES, add, 0)

        return carry

    lax.fori_loop(0, owned, one, 0)


def near_pairs_of(position, pair_partner, owned, devices):
    pairs_here = pair_partner.shape[0] // devices
    pairs = []
    for step in (-1, 0, 1):
        group = position + step
        known = (group >= 0) & (group < devices)
        held = jnp.clip(group, 0, devices - 1)
        for n in range(pairs_here):
            pairs.append((known, group * owned + n % owned, pair_partner[held * pairs_here + n]))
    return pairs


def count_between(pairs, one, other):
    total = jnp.int32(0)
    for known, first, second in pairs:
        forth = known & (first == one) & (second == other)
        back = known & (second == one) & (first == other)
        total = total + forth.astype(jnp.int32) + back.astype(jnp.int32)
    return total


def flip_of(used):
    return (used[0] < used[-1]).astype(jnp.int32)


def cell_of(cells, number, flip):
    halves = len([cell for cell in cells if cell[0] == 0])
    flipped = cells[:1] + cells[halves:] + cells[1:halves]
    (t, at), (other_t, other_at) = cells[number], flipped[number]
    if (t, at) == (other_t, other_at):
        return t, at
    return (
        jnp.where(flip == 1, other_t, t),
        pl.multiple_of(jnp.where(flip == 1, other_at, at), COLS),
    )


def make_plan(
    fit_start, occ_energy, pair_partner, domains, energy, ints, occ, eps_col, eps_row,
    *, devices, targets, relays,
):
    owned, width = eps_col.shape[:2]
    orbitals = fit_start.shape[0]
    plan = Plan(ints, owned)
    position = lax.axis_index("row")
    side = jnp.where(position % 2 == 1, 1, -1)
    places = [
        base * owned + t
        for base in (position, position - side, position + side)
        for t in range(owned)
    ]
    inside = [jnp.clip(orbital, 0, orbitals - 1) for orbital in places]
    starts = [fit_start[orbital] for orbital in inside]
    pairs = near_pairs_of(position, pair_partner, owned, devices)
    used = [jnp.int32(0)] * owned
    for group in range(3):
        for s in range(owned):
            for t in range(owned):
                slot = plan.slot(group, s, t)
                other = group * owned + t
                total = count_between(pairs, places[s], places[other])
                ints[slot] = total
                if group == 2:
                    used[t] = used[t] + (total != 0).astype(jnp.int32)
                apart = starts[other] - starts[s]
                ints[plan.at_shift(slot)] = (apart & (SUB - 1)) - apart
                ints[plan.at_lead(slot)] = apart & (SUB - 1)
                occ[slot] = occ_energy[inside[s]] + occ_energy[inside[other]]
    for number, group in enumerate(targets):
        way = jnp.int32(0)
        for to in group:
            way = jnp.where(position == to, 1, way)
        ints[plan.at_way(number)] = way
    late = jnp.int32(0)
    for row in relays:
        late = jnp.where(position == row, 1, late)
    ints[plan.at_late(len(targets))] = late
    ints[plan.at_flip(len(targets))] = flip_of(used)
    entries = energy.shape[0]
    table = lax.broadcasted_iota(jnp.int32, (entries, width), 0)
    for n, orbital in enumerate(inside):
        domain = domains[pl.ds(orbital, 1), :]
        row = jnp.sum(jnp.where(table == domain, energy[...], 0.0), axis=0, keepdims=True)
        eps_row[n] = row
        if n < owned:
            eps_col[n] = jnp.broadcast_to(row, (LANES, width)).T[:, :1]
    return plan


def add_blocks(plan, occ, sources, eps_col, eps_row, ft, wide, buf, acc, dens, turned, raw, sem):
    copies = [
        pltpu.make_async_copy(block, raw.at[n % 2], sem.at[n % 2])
        for n, (_, _, block) in enumerate(sources)
    ]
    copies[0].start()
    clear_margins(buf, raw.shape[1] + SUB)
    for n, (group, t, _) in enumerate(sources):
        if n + 1 < len(copies):
            copies[n + 1].start()
        copies[n].wait()
        add_block(
            plan, occ, group, t, 0, eps_col, eps_row, ft, raw.at[n % 2], wide, buf, acc, dens, turned
        )


def first_kernel(
    fit_start, occ_energy, pair_partner, domains, energy, own, after,
    ints, occ, eps_col, eps_row, acc, dens, ft, token, wide, buf, turned,
    *, devices, targets, relays,
):
    del after
    token[...] = jnp.zeros_like(token)
    plan = make_plan(
        fit_start, occ_energy, pair_partner, domains, energy, ints, occ, eps_col, eps_row,
        devices=devices, targets=targets, relays=relays,
    )
    owned, aux, width = own.shape
    acc[...] = jnp.zeros_like(acc)
    dens[...] = jnp.zeros_like(dens)
    for t in range(owned):

        def turn(i, carry):
            at = pl.multiple_of(i * LANES, LANES)
            ft[t, :, pl.ds(at, LANES)] = own[t, pl.ds(at, LANES), :].T
            return carry

        lax.fori_loop(0, aux // LANES, turn, 0)

    @pl.when(ints[plan.at_late(len(targets))] == 1)
    def _():
        clear_margins(buf, aux + SUB)
        for t in range(owned):
            add_block(
                plan, occ, 0, t, 0, eps_col, eps_row, ft, own.at[t], wide, buf, acc, dens, turned
            )


def near_kernel(
    ints, occ, eps_col, eps_row, ft, acc_in, dens_in, own, mate, *refs, ways, late
):
    del acc_in, dens_in
    acc, dens, token, wide, buf, turned, raw, sem = refs[-8:]
    token[...] = jnp.zeros_like(token)
    owned = own.shape[0]
    plan = Plan(ints, owned)
    groups = ((1, mate),) if late else ((0, own), (1, mate))
    sources = [(group, t, blocks.at[t]) for group, blocks in groups for t in range(owned)]

    @pl.when(ints[plan.at_late(ways)] == late)
    def _():
        add_blocks(
            plan, occ, sources, eps_col, eps_row, ft, wide, buf, acc, dens, turned, raw, sem
        )


def far_kernel(
    ints, occ, eps_col, eps_row, ft, acc_in, dens_in, block, after,
    acc, dens, token, wide, buf, turned, *, ways, total_ways, cells, number,
):
    del acc_in, dens_in, after
    token[...] = jnp.zeros_like(token)
    plan = Plan(ints, acc.shape[0])
    t, at = cell_of(cells, number, ints[plan.at_flip(total_ways)])
    here = needed(plan, 2, t)
    for way in ways:
        here = here & (plan.way(way) == 0)

    @pl.when(here)
    def _():
        clear_margins(buf, block.shape[0] + SUB)
        add_block(plan, occ, 2, t, at, eps_col, eps_row, ft, block, wide, buf, acc, dens, turned)


def send_out(s, tile_of_rows, dens, ready, out, dens_out, sem, density=None):
    step = out.shape[1] // OUT_TILES

    def one(i, carry):
        part = pl.ds(pl.multiple_of(i * step, SUB), step)
        ready[s, part, :] = tile_of_rows(i * step, step).astype(ready.dtype)
        pltpu.make_async_copy(ready.at[s, part], out.at[s, part], sem.at[s, i]).start()
        return carry

    lax.fori_loop(0, OUT_TILES, one, 0)
    if density is not None:
        density()
    pltpu.make_async_copy(dens.at[s], dens_out.at[s], sem.at[s, OUT_TILES]).start()


def wait_out(s, dens, ready, out, dens_out, sem):
    step = out.shape[1] // OUT_TILES
    pltpu.make_async_copy(dens.at[s], dens_out.at[s], sem.at[s, OUT_TILES]).wait()
    for i in range(OUT_TILES):
        part = pl.ds(i * step, step)
        pltpu.make_async_copy(ready.at[s, part], out.at[s, part], sem.at[s, i]).wait()


def relayed_kernel(
    ints, occ, eps_col, eps_row, ft, acc_in, dens_in, *refs, numbers, cells
):
    del acc_in, dens_in
    *blocks, _, acc, dens, token, out, dens_out, wide, buf, turned, raw, ready, sem, out_sem = refs
    token[...] = jnp.zeros_like(token)
    owned = acc.shape[0]
    plan = Plan(ints, owned)
    flip = ints[plan.at_flip(len(numbers))]
    last, _ = cell_of(cells, len(cells) - 1, flip)
    for way, (block, number) in enumerate(zip(blocks, numbers)):
        t, at = cell_of(cells, number, flip)

        @pl.when(needed(plan, 2, t) & (plan.way(way) == 1))
        def _():
            copy = pltpu.make_async_copy(block, raw, sem)
            copy.start()
            clear_margins(buf, raw.shape[0] + SUB)
            copy.wait()
            add_block(plan, occ, 2, t, at, eps_col, eps_row, ft, raw, wide, buf, acc, dens, turned)

    for s in range(owned):

        @pl.when(plan.count(plan.slot(2, s, last)) == 0)
        def _():
            send_out(
                s,
                lambda base, n: acc[s, pl.ds(pl.multiple_of(base, SUB), n), :],
                dens, ready, out, dens_out, out_sem,
            )

    for s in range(owned):

        @pl.when(plan.count(plan.slot(2, s, last)) == 0)
        def _():
            wait_out(s, dens, ready, out, dens_out, out_sem)


def last_kernel(
    ints, occ, eps_col, eps_row, ft, acc_in, dens_in, block, out_in, dens_out_in, after,
    acc, dens, out, dens_out, wide, buf, turned, held, raw, ready, sem, raw_sem, *, total_ways, cells,
):
    del acc_in, dens_in, out_in, dens_out_in, after
    owned, aux, width = out.shape
    plan = Plan(ints, owned)
    t, at = cell_of(cells, len(cells) - 1, ints[plan.at_flip(total_ways)])
    scale = float(width) ** -0.5

    @pl.when(needed(plan, 2, t))
    def _():
        step = aux // LOAD_TILES
        parts = [pl.ds(i * step, step) for i in range(LOAD_TILES)]
        loads = [
            pltpu.make_async_copy(block.at[part], raw.at[part], raw_sem.at[i])
            for i, part in enumerate(parts)
        ]
        for load in loads:
            load.start()
        clear_margins(buf, aux + SUB)
        clear_ends(wide)
        for i, load in enumerate(loads):
            load.wait()
            wide[SUB + i * step : SUB + (i + 1) * step, :] = raw[parts[i], :].astype(jnp.float32)

    def one(s, carry):
        slot = plan.slot(2, s, t)

        @pl.when(plan.count(slot) != 0)
        def _():
            place(plan.lead(slot), wide, buf)
            amplitude, turned[...] = amplitude_of(
                plan, occ, slot, s, 2 * owned + t, at, eps_col, eps_row, ft, buf
            )
            held[...] = amplitude

            def density():
                dens[s] += scale * dot(held[...], turned[...])

            def total(base, n):
                rows = buf[pl.ds(pl.multiple_of(plan.offset(slot) + base, SUB), n), :]
                return acc[s, pl.ds(pl.multiple_of(base, SUB), n), :] + dot(rows, turned[...])

            send_out(s, total, dens, ready, out, dens_out, sem, density)

        return carry

    lax.fori_loop(0, owned, one, 0)
    for s in range(owned):

        @pl.when(plan.count(plan.slot(2, s, t)) != 0)
        def _():
            wait_out(s, dens, ready, out, dens_out, sem)


def copy_kernel(source, *refs, numbers, cells, devices):
    *outs, buf, sem = refs[-len(numbers) - 2 :]
    owned = source.shape[0]
    flip = jnp.int32(0)
    if any(numbers):
        position = lax.axis_index("row")
        pairs = near_pairs_of(position, refs[0], owned, devices)
        beyond = position + jnp.where(position % 2 == 1, 1, -1)
        used = []
        for t in range(owned):
            total = jnp.int32(0)
            for s in range(owned):
                count = count_between(pairs, position * owned + t, beyond * owned + s)
                total = total + (count != 0).astype(jnp.int32)
            used.append(total)
        flip = flip_of(used)
    places = [cell_of(cells, number, flip) for number in numbers]
    rows, cols = outs[0].shape
    tile = rows // CHUNK_TILES
    parts = [(n, i) for n in range(len(places)) for i in range(CHUNK_TILES)]

    def copies(n, i):
        t, at = places[n]
        part = pl.ds(i * tile, tile)
        held = buf.at[n, part]
        load = pltpu.make_async_copy(source.at[t, part, pl.ds(at, cols)], held, sem.at[0, n, i])
        return load, pltpu.make_async_copy(held, outs[n].at[part], sem.at[1, n, i])

    for n, i in parts:
        copies(n, i)[0].start()
    for n, i in parts:
        load, store = copies(n, i)
        load.wait()
        store.start()
    for n, i in parts:
        copies(n, i)[1].wait()


def pass_kernel(source, after, out):
    del source, after, out


def relay_plan(devices, chunks):
    if devices != 16 or chunks != 4:
        return []
    plan = []
    for z, chunk, alone in ((1, 0, True), (0, 0, False), (2, 1, False)):
        high, low = 4 * z + 3, 4 * z + 4
        plan.append((chunk, alone, [(high, low, 0), (low, high, devices - 1)]))
    return plan


def spec(space):
    return pl.BlockSpec(memory_space=space)


def on_device(fitted, fit_start, virt_domain, occ_energy, virt_energy, pair_partner):
    owned, aux, width = fitted.shape
    devices = lax.axis_size("row")
    buf_rows = 2 * REACH + aux
    wide_rows = aux + 2 * SUB + STEP
    smem, vmem, anywhere = spec(pltpu.SMEM), spec(pltpu.VMEM), spec(pl.ANY)

    outward = []
    for i in range(devices):
        to = i + 1 if i % 2 else i - 1
        if 0 <= to < devices:
            outward.append((i, to))
    inward = [(i, i ^ 1) for i in range(devices) if i ^ 1 < devices]

    def in_hbm(array):
        return pltpu.with_memory_space_constraint(array, pltpu.HBM)

    def in_vmem(array):
        return pltpu.with_memory_space_constraint(array, pltpu.VMEM)

    def chunks(numbers, *after):
        return pl.pallas_call(
            functools.partial(copy_kernel, numbers=numbers, cells=cells, devices=devices),
            out_shape=[jax.ShapeDtypeStruct((aux, COLS), fitted.dtype)] * len(numbers),
            in_specs=[anywhere] + [smem] * any(numbers) + [anywhere] * len(after),
            out_specs=[anywhere] * len(numbers),
            scratch_shapes=[
                pltpu.VMEM((len(numbers), aux, COLS), fitted.dtype),
                pltpu.SemaphoreType.DMA((2, len(numbers), CHUNK_TILES)),
            ],
            compiler_params=pltpu.CompilerParams(vmem_limit_bytes=CHUNK_VMEM),
            name="chunks",
        )(in_hbm(fitted), *[pair_partner] * any(numbers), *after)

    def pass_on(block, after):
        return pl.pallas_call(
            pass_kernel,
            out_shape=jax.ShapeDtypeStruct(block.shape, block.dtype),
            in_specs=[anywhere] * 2,
            out_specs=anywhere,
            input_output_aliases={0: 0},
            compiler_params=pltpu.CompilerParams(vmem_limit_bytes=CHUNK_VMEM),
            name="pass_on",
        )(block, after)

    cells = [(t, at) for t in range(owned) for at in range(0, width, COLS)]
    last = len(cells) - 1
    plan = relay_plan(devices, len(cells))
    first_hops = [[(source, by) for source, _, by in pairs] for _, _, pairs in plan]
    second_hops = [[(by, to) for _, to, by in pairs] for _, _, pairs in plan]

    def exchange(number, block):
        pairs = list(outward)
        for (at, alone, group), hop in zip(plan, first_hops):
            if at == number:
                pairs = [pair for pair in pairs if pair not in {(a, b) for a, b, _ in group}]
                pairs += [] if alone else hop
        return lax.ppermute(block, "row", pairs)

    sent = list(chunks([0]))
    mate = lax.ppermute(lax.optimization_barrier((fitted, sent[0]))[0], "row", inward)
    far = [exchange(0, sent[0])]
    rest = chunks(list(range(1, len(cells))) + [0] * bool(plan), sent[0])
    sent += rest[:last]
    early = {
        index: lax.ppermute(rest[last], "row", first_hops[index])
        for index, (_, alone, _) in enumerate(plan)
        if alone
    }
    far += [exchange(number, sent[number]) for number in range(1, last + 1)]

    unit = 4 * aux * width * COLS
    acc_shape = pltpu.VMEM((owned, aux, width), jnp.float32)
    dens_shape = pltpu.VMEM((owned, width, width), jnp.float32)
    ft_shape = pltpu.VMEM((owned, width, aux), fitted.dtype)
    token_shape = jax.ShapeDtypeStruct((8, LANES), jnp.int32)
    slots = 3 * owned * owned

    def cost(blocks):
        return pl.CostEstimate(
            flops=100 * unit * blocks * owned, bytes_accessed=8 << 20, transcendentals=0
        )

    ints, occ, eps_col, eps_row, acc, dens, ft, token = pl.pallas_call(
        functools.partial(
            first_kernel,
            devices=devices,
            targets=[[to for _, to, _ in pairs] for _, _, pairs in plan],
            relays=sorted({by for _, _, pairs in plan for _, _, by in pairs}),
        ),
        out_shape=(
            jax.ShapeDtypeStruct((Plan(None, owned).at_flip(len(plan)) + 1,), jnp.int32),
            jax.ShapeDtypeStruct((slots,), jnp.float32),
            pltpu.VMEM((owned, width, 1), jnp.float32),
            pltpu.VMEM((3 * owned, 1, width), jnp.float32),
            acc_shape,
            dens_shape,
            ft_shape,
            token_shape,
        ),
        in_specs=[smem] * 3 + [vmem] * 3 + [anywhere],
        out_specs=(smem,) * 2 + (vmem,) * 6,
        scratch_shapes=[
            pltpu.VMEM((wide_rows, width), jnp.float32),
            pltpu.VMEM((buf_rows, width), fitted.dtype),
            pltpu.VMEM((width, width), fitted.dtype),
        ],
        compiler_params=pltpu.CompilerParams(vmem_limit_bytes=NEAR_VMEM),
        cost_estimate=cost(len(cells)),
        name="first",
    )(
        fit_start, occ_energy, pair_partner, virt_domain, virt_energy.reshape(-1, 1),
        in_hbm(fitted), sent[last - 1],
    )
    state = {"acc": acc, "dens": dens, "token": token}
    hops = []

    def add_pairs(
        kernel, block_specs, blocks, cols, limit, name,
        extra=(), outs=(), aliases={}, scratch=(), token=True,
    ):
        specs = [smem] * 2 + [vmem] * 5 + block_specs
        results = pl.pallas_call(
            kernel,
            out_shape=(acc_shape, dens_shape) + (token_shape,) * token + tuple(outs),
            in_specs=specs + [anywhere] * (1 + len(extra)),
            out_specs=(vmem,) * (2 + token) + (anywhere,) * len(outs),
            input_output_aliases={5: 0, 6: 1, **aliases},
            scratch_shapes=[
                pltpu.VMEM((wide_rows, cols), jnp.float32),
                pltpu.VMEM((buf_rows, cols), fitted.dtype),
                *scratch,
            ],
            compiler_params=pltpu.CompilerParams(vmem_limit_bytes=limit),
            cost_estimate=cost(cols // COLS),
            name=name,
        )(
            ints, occ, in_vmem(eps_col), in_vmem(eps_row), in_vmem(ft), in_vmem(state["acc"]),
            in_vmem(state["dens"]), *blocks, *extra, state["token"],
        )
        state.update(acc=results[0], dens=results[1], token=results[2])
        return results[2 + token :]

    hops = {index: lax.ppermute(early[index], "row", second_hops[index]) for index in early}
    turned_cols = (pltpu.VMEM((COLS, width), fitted.dtype),)

    def near_pairs(late, *extra):
        add_pairs(
            functools.partial(near_kernel, ways=len(plan), late=late),
            [anywhere] * 2, [in_hbm(fitted), mate], width, NEAR_VMEM, f"near_pairs_{late}",
            extra=extra,
            scratch=(
                pltpu.VMEM((width, width), fitted.dtype),
                pltpu.VMEM((2, aux, width), fitted.dtype),
                pltpu.SemaphoreType.DMA((2,)),
            ),
        )

    near_pairs(0, *early.values())
    for number in range(last):
        for index, (at, alone, _) in enumerate(plan):
            if at == number and not alone:
                far[number] = state["token"] = pass_on(far[number], state["token"])
                hops[index] = lax.ppermute(far[number], "row", second_hops[index])
                if index == len(plan) - 1:
                    near_pairs(1)
        ways = [index for index, (at, _, _) in enumerate(plan) if at == number]
        add_pairs(
            functools.partial(
                far_kernel, ways=ways, total_ways=len(plan), cells=cells, number=number
            ),
            [vmem], [far[number]], COLS, FAR_VMEM, f"far_pairs_{number}", scratch=turned_cols,
        )
    results = (
        jax.ShapeDtypeStruct(fitted.shape, fitted.dtype),
        jax.ShapeDtypeStruct((owned, width, width), jnp.float32),
    )
    out_scratch = (
        pltpu.VMEM((owned, aux, width), fitted.dtype),
        pltpu.SemaphoreType.DMA((owned, OUT_TILES + 1)),
    )
    ready = add_pairs(
        functools.partial(
            relayed_kernel, numbers=[at for at, _, _ in plan], cells=cells
        ),
        [anywhere] * len(hops), [hops[index] for index in range(len(plan))], COLS, FAR_VMEM,
        "relayed_pairs",
        outs=results,
        scratch=turned_cols
        + (pltpu.VMEM((aux, COLS), fitted.dtype), out_scratch[0], pltpu.SemaphoreType.DMA)
        + out_scratch[1:],
    )
    gradient, density = add_pairs(
        functools.partial(last_kernel, total_ways=len(plan), cells=cells),
        [anywhere] * 3, [far[last], *ready], COLS, FAR_VMEM, "last_pairs",
        outs=results,
        aliases={8: 2, 9: 3},
        scratch=turned_cols
        + (pltpu.VMEM((width, COLS), fitted.dtype), pltpu.VMEM((aux, COLS), fitted.dtype))
        + out_scratch
        + (pltpu.SemaphoreType.DMA((LOAD_TILES,)),),
        token=False,
    )
    return gradient, density


def solution(mesh):
    placed = (
        P(("parts", "row"), None, None),
        P("parts"),
        P("parts", None),
        P("parts"),
        P("parts"),
        P("parts"),
    )
    return jax.shard_map(
        on_device,
        mesh=mesh,
        in_specs=placed,
        out_specs=(P(("parts", "row"), None, None), P(("parts", "row"), None, None)),
        check_vma=False,
    )
```

```python
import functools

import jax
import jax.numpy as jnp
from jax import lax
from jax.experimental import pallas as pl
from jax.experimental.pallas import tpu as pltpu
from jax.sharding import PartitionSpec as P

SUB = 16
STEP = 8
LANES = 128
ROW_TILES = 1
OUT_TILES = 4
LOAD_TILES = 4
CHUNK_TILES = 2
COLS = 256
REACH = 1024
NEAR_VMEM = 22 * 1024 * 1024
FAR_VMEM = 16 * 1024 * 1024
CHUNK_VMEM = 6 * 1024 * 1024


class Plan:
    def __init__(self, ref, owned):
        self.ref, self.owned = ref, owned
        self.slots = 3 * owned * owned

    def slot(self, group, s, t):
        return (group * self.owned + s) * self.owned + t

    def at_shift(self, slot):
        return self.slots + slot

    def at_lead(self, slot):
        return 2 * self.slots + slot

    def at_way(self, number):
        return 3 * self.slots + number

    def at_late(self, ways):
        return self.at_way(ways)

    def at_flip(self, ways):
        return self.at_way(ways) + 1

    def count(self, slot):
        return self.ref[slot]

    def offset(self, slot):
        return pl.multiple_of(REACH + self.ref[self.at_shift(slot)], SUB)

    def lead(self, slot):
        return self.ref[self.at_lead(slot)]

    def way(self, number):
        return self.ref[self.at_way(number)]


def dot(a, b):
    return jnp.dot(a, b, preferred_element_type=jnp.float32)


def tile_of(rows):
    return max(n for n in range(SUB, 705, SUB) if rows % n == 0)


def rows_from(load, start, count):
    skip = start % STEP
    base = pl.multiple_of(start - skip, STEP)
    block = load(base, count + STEP)
    width = block.shape[1]
    block = block.reshape(count // STEP + 1, STEP, width)
    turned = pltpu.roll(block, (STEP - skip) % STEP, 1)
    row = lax.broadcasted_iota(jnp.int32, (count // STEP, STEP, width), 1)
    return jnp.where(row < STEP - skip, turned[:-1], turned[1:]).reshape(count, width)


def clear_margins(buf, rows):
    width = buf.shape[1]
    buf[:REACH, :] = jnp.zeros((REACH, width), buf.dtype)
    buf[REACH + rows :, :] = jnp.zeros((buf.shape[0] - REACH - rows, width), buf.dtype)


def clear_ends(wide):
    rows, width = wide.shape
    wide[:SUB, :] = jnp.zeros((SUB, width), jnp.float32)
    wide[rows - SUB - STEP :, :] = jnp.zeros((SUB + STEP, width), jnp.float32)


def widen(source, wide):
    aux = source.shape[0]
    clear_ends(wide)
    tile = aux // ROW_TILES

    def one(i, carry):
        base = pl.multiple_of(i * tile, SUB)
        wide[pl.ds(pl.multiple_of(SUB + base, SUB), tile), :] = source[
            pl.ds(base, tile), :
        ].astype(jnp.float32)
        return carry

    lax.fori_loop(0, ROW_TILES, one, 0)


def place(lead, wide, buf):
    rows = wide.shape[0] - SUB - STEP
    step = tile_of(rows)

    def move(i, carry):
        base = pl.multiple_of(i * step, SUB)
        moved = rows_from(lambda at, n: wide[pl.ds(at, n), :], SUB - lead + base, step)
        buf[pl.ds(pl.multiple_of(REACH + base, SUB), step), :] = moved.astype(buf.dtype)
        return carry

    lax.fori_loop(0, rows // step, move, 0)


def amplitudes(coulomb, denominator, weight):
    amplitude = (coulomb / denominator).astype(jnp.bfloat16)
    weighted = (amplitude.astype(jnp.float32) * weight).astype(jnp.bfloat16)
    return amplitude, weighted.T


def needed(plan, group, t):
    total = jnp.int32(0)
    for s in range(plan.owned):
        total = total + plan.count(plan.slot(group, s, t))
    return total != 0


def amplitude_of(plan, occ, slot, s, partner, at, eps_col, eps_row, ft, buf):
    rows = ft.shape[2]
    cols = buf.shape[1]
    coulomb = dot(ft[s], buf[pl.ds(plan.offset(slot), rows), :])
    denominator = occ[slot] - eps_col[s] - eps_row[partner, :, pl.ds(at, cols)]
    return amplitudes(coulomb, denominator, plan.count(slot).astype(jnp.float32))


def add_block(plan, occ, group, t, at, eps_col, eps_row, ft, source, wide, buf, acc, dens, turned):
    owned, rows, width = acc.shape
    scale = float(width) ** -0.5
    step = rows // ROW_TILES

    @pl.when(needed(plan, group, t))
    def _():
        widen(source, wide)

    def one(s, carry):
        slot = plan.slot(group, s, t)

        @pl.when(plan.count(slot) != 0)
        def _():
            place(plan.lead(slot), wide, buf)
            amplitude, turned[...] = amplitude_of(
                plan, occ, slot, s, group * owned + t, at, eps_col, eps_row, ft, buf
            )
            dens[s] += scale * dot(amplitude, turned[...])

            def add(i, inner):
                base = pl.multiple_of(i * step, SUB)
                block = buf[pl.ds(pl.multiple_of(plan.offset(slot) + base, SUB), step), :]
                acc[s, pl.ds(base, step), :] += dot(block, turned[...])
                return inner

            lax.fori_loop(0, ROW_TILES, add, 0)

        return carry

    lax.fori_loop(0, owned, one, 0)


def near_pairs_of(position, pair_partner, owned, devices):
    pairs_here = pair_partner.shape[0] // devices
    pairs = []
    for step in (-1, 0, 1):
        group = position + step
        known = (group >= 0) & (group < devices)
        held = jnp.clip(group, 0, devices - 1)
        for n in range(pairs_here):
            pairs.append((known, group * owned + n % owned, pair_partner[held * pairs_here + n]))
    return pairs


def count_between(pairs, one, other):
    total = jnp.int32(0)
    for known, first, second in pairs:
        forth = known & (first == one) & (second == other)
        back = known & (second == one) & (first == other)
        total = total + forth.astype(jnp.int32) + back.astype(jnp.int32)
    return total


def flip_of(used):
    return (used[0] < used[-1]).astype(jnp.int32)


def cell_of(cells, number, flip):
    halves = len([cell for cell in cells if cell[0] == 0])
    flipped = cells[:1] + cells[halves:] + cells[1:halves]
    (t, at), (other_t, other_at) = cells[number], flipped[number]
    if (t, at) == (other_t, other_at):
        return t, at
    return (
        jnp.where(flip == 1, other_t, t),
        pl.multiple_of(jnp.where(flip == 1, other_at, at), COLS),
    )


def make_plan(
    fit_start, occ_energy, pair_partner, domains, energy, ints, occ, eps_col, eps_row,
    *, devices, targets, relays,
):
    owned, width = eps_col.shape[:2]
    orbitals = fit_start.shape[0]
    plan = Plan(ints, owned)
    position = lax.axis_index("row")
    side = jnp.where(position % 2 == 1, 1, -1)
    places = [
        base * owned + t
        for base in (position, position - side, position + side)
        for t in range(owned)
    ]
    inside = [jnp.clip(orbital, 0, orbitals - 1) for orbital in places]
    starts = [fit_start[orbital] for orbital in inside]
    pairs = near_pairs_of(position, pair_partner, owned, devices)
    used = [jnp.int32(0)] * owned
    for group in range(3):
        for s in range(owned):
            for t in range(owned):
                slot = plan.slot(group, s, t)
                other = group * owned + t
                total = count_between(pairs, places[s], places[other])
                ints[slot] = total
                if group == 2:
                    used[t] = used[t] + (total != 0).astype(jnp.int32)
                apart = starts[other] - starts[s]
                ints[plan.at_shift(slot)] = (apart & (SUB - 1)) - apart
                ints[plan.at_lead(slot)] = apart & (SUB - 1)
                occ[slot] = occ_energy[inside[s]] + occ_energy[inside[other]]
    for number, group in enumerate(targets):
        way = jnp.int32(0)
        for to in group:
            way = jnp.where(position == to, 1, way)
        ints[plan.at_way(number)] = way
    late = jnp.int32(0)
    for row in relays:
        late = jnp.where(position == row, 1, late)
    ints[plan.at_late(len(targets))] = late
    ints[plan.at_flip(len(targets))] = flip_of(used)
    entries = energy.shape[0]
    table = lax.broadcasted_iota(jnp.int32, (entries, width), 0)
    for n, orbital in enumerate(inside):
        domain = domains[pl.ds(orbital, 1), :]
        row = jnp.sum(jnp.where(table == domain, energy[...], 0.0), axis=0, keepdims=True)
        eps_row[n] = row
        if n < owned:
            eps_col[n] = jnp.broadcast_to(row, (LANES, width)).T[:, :1]
    return plan


def add_blocks(plan, occ, sources, eps_col, eps_row, ft, wide, buf, acc, dens, turned, raw, sem):
    copies = [
        pltpu.make_async_copy(block, raw.at[n % 2], sem.at[n % 2])
        for n, (_, _, block) in enumerate(sources)
    ]
    copies[0].start()
    clear_margins(buf, raw.shape[1] + SUB)
    for n, (group, t, _) in enumerate(sources):
        if n + 1 < len(copies):
            copies[n + 1].start()
        copies[n].wait()
        add_block(
            plan, occ, group, t, 0, eps_col, eps_row, ft, raw.at[n % 2], wide, buf, acc, dens, turned
        )


def first_kernel(
    fit_start, occ_energy, pair_partner, domains, energy, own, after,
    ints, occ, eps_col, eps_row, acc, dens, ft, token, wide, buf, turned,
    *, devices, targets, relays,
):
    del after
    token[...] = jnp.zeros_like(token)
    plan = make_plan(
        fit_start, occ_energy, pair_partner, domains, energy, ints, occ, eps_col, eps_row,
        devices=devices, targets=targets, relays=relays,
    )
    owned, aux, width = own.shape
    acc[...] = jnp.zeros_like(acc)
    dens[...] = jnp.zeros_like(dens)
    for t in range(owned):

        def turn(i, carry):
            at = pl.multiple_of(i * LANES, LANES)
            ft[t, :, pl.ds(at, LANES)] = own[t, pl.ds(at, LANES), :].T
            return carry

        lax.fori_loop(0, aux // LANES, turn, 0)

    @pl.when(ints[plan.at_late(len(targets))] == 1)
    def _():
        clear_margins(buf, aux + SUB)
        for t in range(owned):
            add_block(
                plan, occ, 0, t, 0, eps_col, eps_row, ft, own.at[t], wide, buf, acc, dens, turned
            )


def near_kernel(
    ints, occ, eps_col, eps_row, ft, acc_in, dens_in, own, mate, *refs, ways, late
):
    del acc_in, dens_in
    acc, dens, token, wide, buf, turned, raw, sem = refs[-8:]
    token[...] = jnp.zeros_like(token)
    owned = own.shape[0]
    plan = Plan(ints, owned)
    groups = ((1, mate),) if late else ((0, own), (1, mate))
    sources = [(group, t, blocks.at[t]) for group, blocks in groups for t in range(owned)]

    @pl.when(ints[plan.at_late(ways)] == late)
    def _():
        add_blocks(
            plan, occ, sources, eps_col, eps_row, ft, wide, buf, acc, dens, turned, raw, sem
        )


def far_kernel(
    ints, occ, eps_col, eps_row, ft, acc_in, dens_in, block, after,
    acc, dens, token, wide, buf, turned, *, ways, total_ways, cells, number,
):
    del acc_in, dens_in, after
    token[...] = jnp.zeros_like(token)
    plan = Plan(ints, acc.shape[0])
    t, at = cell_of(cells, number, ints[plan.at_flip(total_ways)])
    here = needed(plan, 2, t)
    for way in ways:
        here = here & (plan.way(way) == 0)

    @pl.when(here)
    def _():
        clear_margins(buf, block.shape[0] + SUB)
        add_block(plan, occ, 2, t, at, eps_col, eps_row, ft, block, wide, buf, acc, dens, turned)


def send_out(s, tile_of_rows, dens, ready, out, dens_out, sem):
    step = out.shape[1] // OUT_TILES
    pltpu.make_async_copy(dens.at[s], dens_out.at[s], sem.at[s, OUT_TILES]).start()

    def one(i, carry):
        part = pl.ds(pl.multiple_of(i * step, SUB), step)
        ready[s, part, :] = tile_of_rows(i * step, step).astype(ready.dtype)
        pltpu.make_async_copy(ready.at[s, part], out.at[s, part], sem.at[s, i]).start()
        return carry

    lax.fori_loop(0, OUT_TILES, one, 0)


def wait_out(s, dens, ready, out, dens_out, sem):
    step = out.shape[1] // OUT_TILES
    pltpu.make_async_copy(dens.at[s], dens_out.at[s], sem.at[s, OUT_TILES]).wait()
    for i in range(OUT_TILES):
        part = pl.ds(i * step, step)
        pltpu.make_async_copy(ready.at[s, part], out.at[s, part], sem.at[s, i]).wait()


def relayed_kernel(
    ints, occ, eps_col, eps_row, ft, acc_in, dens_in, *refs, numbers, cells
):
    del acc_in, dens_in
    *blocks, _, acc, dens, token, out, dens_out, wide, buf, turned, raw, ready, sem, out_sem = refs
    token[...] = jnp.zeros_like(token)
    owned = acc.shape[0]
    plan = Plan(ints, owned)
    flip = ints[plan.at_flip(len(numbers))]
    last, _ = cell_of(cells, len(cells) - 1, flip)
    for way, (block, number) in enumerate(zip(blocks, numbers)):
        t, at = cell_of(cells, number, flip)

        @pl.when(needed(plan, 2, t) & (plan.way(way) == 1))
        def _():
            copy = pltpu.make_async_copy(block, raw, sem)
            copy.start()
            clear_margins(buf, raw.shape[0] + SUB)
            copy.wait()
            add_block(plan, occ, 2, t, at, eps_col, eps_row, ft, raw, wide, buf, acc, dens, turned)

    for s in range(owned):

        @pl.when(plan.count(plan.slot(2, s, last)) == 0)
        def _():
            send_out(
                s,
                lambda base, n: acc[s, pl.ds(pl.multiple_of(base, SUB), n), :],
                dens, ready, out, dens_out, out_sem,
            )

    for s in range(owned):

        @pl.when(plan.count(plan.slot(2, s, last)) == 0)
        def _():
            wait_out(s, dens, ready, out, dens_out, out_sem)


def last_kernel(
    ints, occ, eps_col, eps_row, ft, acc_in, dens_in, block, out_in, dens_out_in, after,
    acc, dens, out, dens_out, wide, buf, turned, raw, ready, sem, raw_sem, *, total_ways, cells,
):
    del acc_in, dens_in, out_in, dens_out_in, after
    owned, aux, width = out.shape
    plan = Plan(ints, owned)
    t, at = cell_of(cells, len(cells) - 1, ints[plan.at_flip(total_ways)])
    scale = float(width) ** -0.5

    @pl.when(needed(plan, 2, t))
    def _():
        step = aux // LOAD_TILES
        parts = [pl.ds(i * step, step) for i in range(LOAD_TILES)]
        loads = [
            pltpu.make_async_copy(block.at[part], raw.at[part], raw_sem.at[i])
            for i, part in enumerate(parts)
        ]
        for load in loads:
            load.start()
        clear_margins(buf, aux + SUB)
        clear_ends(wide)
        for i, load in enumerate(loads):
            load.wait()
            wide[SUB + i * step : SUB + (i + 1) * step, :] = raw[parts[i], :].astype(jnp.float32)

    def one(s, carry):
        slot = plan.slot(2, s, t)

        @pl.when(plan.count(slot) != 0)
        def _():
            place(plan.lead(slot), wide, buf)
            amplitude, turned[...] = amplitude_of(
                plan, occ, slot, s, 2 * owned + t, at, eps_col, eps_row, ft, buf
            )
            dens[s] += scale * dot(amplitude, turned[...])

            def total(base, n):
                rows = buf[pl.ds(pl.multiple_of(plan.offset(slot) + base, SUB), n), :]
                return acc[s, pl.ds(pl.multiple_of(base, SUB), n), :] + dot(rows, turned[...])

            send_out(s, total, dens, ready, out, dens_out, sem)

        return carry

    lax.fori_loop(0, owned, one, 0)
    for s in range(owned):

        @pl.when(plan.count(plan.slot(2, s, t)) != 0)
        def _():
            wait_out(s, dens, ready, out, dens_out, sem)


def copy_kernel(source, *refs, numbers, cells, devices):
    *outs, buf, sem = refs[-len(numbers) - 2 :]
    owned = source.shape[0]
    flip = jnp.int32(0)
    if any(numbers):
        position = lax.axis_index("row")
        pairs = near_pairs_of(position, refs[0], owned, devices)
        beyond = position + jnp.where(position % 2 == 1, 1, -1)
        used = []
        for t in range(owned):
            total = jnp.int32(0)
            for s in range(owned):
                count = count_between(pairs, position * owned + t, beyond * owned + s)
                total = total + (count != 0).astype(jnp.int32)
            used.append(total)
        flip = flip_of(used)
    places = [cell_of(cells, number, flip) for number in numbers]
    rows, cols = outs[0].shape
    tile = rows // CHUNK_TILES
    parts = [(n, i) for n in range(len(places)) for i in range(CHUNK_TILES)]

    def copies(n, i):
        t, at = places[n]
        part = pl.ds(i * tile, tile)
        held = buf.at[n, part]
        load = pltpu.make_async_copy(source.at[t, part, pl.ds(at, cols)], held, sem.at[0, n, i])
        return load, pltpu.make_async_copy(held, outs[n].at[part], sem.at[1, n, i])

    for n, i in parts:
        copies(n, i)[0].start()
    for n, i in parts:
        load, store = copies(n, i)
        load.wait()
        store.start()
    for n, i in parts:
        copies(n, i)[1].wait()


def pass_kernel(source, after, out):
    del source, after, out


def relay_plan(devices, chunks):
    if devices != 16 or chunks != 4:
        return []
    plan = []
    for z, chunk, alone in ((1, 0, True), (0, 0, False), (2, 1, False)):
        high, low = 4 * z + 3, 4 * z + 4
        plan.append((chunk, alone, [(high, low, 0), (low, high, devices - 1)]))
    return plan


def spec(space):
    return pl.BlockSpec(memory_space=space)


def on_device(fitted, fit_start, virt_domain, occ_energy, virt_energy, pair_partner):
    owned, aux, width = fitted.shape
    devices = lax.axis_size("row")
    buf_rows = 2 * REACH + aux
    wide_rows = aux + 2 * SUB + STEP
    smem, vmem, anywhere = spec(pltpu.SMEM), spec(pltpu.VMEM), spec(pl.ANY)

    outward = []
    for i in range(devices):
        to = i + 1 if i % 2 else i - 1
        if 0 <= to < devices:
            outward.append((i, to))
    inward = [(i, i ^ 1) for i in range(devices) if i ^ 1 < devices]

    def in_hbm(array):
        return pltpu.with_memory_space_constraint(array, pltpu.HBM)

    def in_vmem(array):
        return pltpu.with_memory_space_constraint(array, pltpu.VMEM)

    def chunks(numbers, *after):
        return pl.pallas_call(
            functools.partial(copy_kernel, numbers=numbers, cells=cells, devices=devices),
            out_shape=[jax.ShapeDtypeStruct((aux, COLS), fitted.dtype)] * len(numbers),
            in_specs=[anywhere] + [smem] * any(numbers) + [anywhere] * len(after),
            out_specs=[anywhere] * len(numbers),
            scratch_shapes=[
                pltpu.VMEM((len(numbers), aux, COLS), fitted.dtype),
                pltpu.SemaphoreType.DMA((2, len(numbers), CHUNK_TILES)),
            ],
            compiler_params=pltpu.CompilerParams(vmem_limit_bytes=CHUNK_VMEM),
            name="chunks",
        )(in_hbm(fitted), *[pair_partner] * any(numbers), *after)

    def pass_on(block, after):
        return pl.pallas_call(
            pass_kernel,
            out_shape=jax.ShapeDtypeStruct(block.shape, block.dtype),
            in_specs=[anywhere] * 2,
            out_specs=anywhere,
            input_output_aliases={0: 0},
            compiler_params=pltpu.CompilerParams(vmem_limit_bytes=CHUNK_VMEM),
            name="pass_on",
        )(block, after)

    cells = [(t, at) for t in range(owned) for at in range(0, width, COLS)]
    last = len(cells) - 1
    plan = relay_plan(devices, len(cells))
    first_hops = [[(source, by) for source, _, by in pairs] for _, _, pairs in plan]
    second_hops = [[(by, to) for _, to, by in pairs] for _, _, pairs in plan]

    def exchange(number, block):
        pairs = list(outward)
        for (at, alone, group), hop in zip(plan, first_hops):
            if at == number:
                pairs = [pair for pair in pairs if pair not in {(a, b) for a, b, _ in group}]
                pairs += [] if alone else hop
        return lax.ppermute(block, "row", pairs)

    sent = list(chunks([0]))
    mate = lax.ppermute(lax.optimization_barrier((fitted, sent[0]))[0], "row", inward)
    far = [exchange(0, sent[0])]
    rest = chunks(list(range(1, len(cells))) + [0] * bool(plan), sent[0])
    sent += rest[:last]
    early = {
        index: lax.ppermute(rest[last], "row", first_hops[index])
        for index, (_, alone, _) in enumerate(plan)
        if alone
    }
    far += [exchange(number, sent[number]) for number in range(1, last + 1)]

    unit = 4 * aux * width * COLS
    acc_shape = pltpu.VMEM((owned, aux, width), jnp.float32)
    dens_shape = pltpu.VMEM((owned, width, width), jnp.float32)
    ft_shape = pltpu.VMEM((owned, width, aux), fitted.dtype)
    token_shape = jax.ShapeDtypeStruct((8, LANES), jnp.int32)
    slots = 3 * owned * owned

    def cost(blocks):
        return pl.CostEstimate(
            flops=100 * unit * blocks * owned, bytes_accessed=8 << 20, transcendentals=0
        )

    ints, occ, eps_col, eps_row, acc, dens, ft, token = pl.pallas_call(
        functools.partial(
            first_kernel,
            devices=devices,
            targets=[[to for _, to, _ in pairs] for _, _, pairs in plan],
            relays=sorted({by for _, _, pairs in plan for _, _, by in pairs}),
        ),
        out_shape=(
            jax.ShapeDtypeStruct((Plan(None, owned).at_flip(len(plan)) + 1,), jnp.int32),
            jax.ShapeDtypeStruct((slots,), jnp.float32),
            pltpu.VMEM((owned, width, 1), jnp.float32),
            pltpu.VMEM((3 * owned, 1, width), jnp.float32),
            acc_shape,
            dens_shape,
            ft_shape,
            token_shape,
        ),
        in_specs=[smem] * 3 + [vmem] * 3 + [anywhere],
        out_specs=(smem,) * 2 + (vmem,) * 6,
        scratch_shapes=[
            pltpu.VMEM((wide_rows, width), jnp.float32),
            pltpu.VMEM((buf_rows, width), fitted.dtype),
            pltpu.VMEM((width, width), fitted.dtype),
        ],
        compiler_params=pltpu.CompilerParams(vmem_limit_bytes=NEAR_VMEM),
        cost_estimate=cost(len(cells)),
        name="first",
    )(
        fit_start, occ_energy, pair_partner, virt_domain, virt_energy.reshape(-1, 1),
        in_hbm(fitted), sent[last - 1],
    )
    state = {"acc": acc, "dens": dens, "token": token}
    hops = []

    def add_pairs(
        kernel, block_specs, blocks, cols, limit, name,
        extra=(), outs=(), aliases={}, scratch=(), token=True,
    ):
        specs = [smem] * 2 + [vmem] * 5 + block_specs
        results = pl.pallas_call(
            kernel,
            out_shape=(acc_shape, dens_shape) + (token_shape,) * token + tuple(outs),
            in_specs=specs + [anywhere] * (1 + len(extra)),
            out_specs=(vmem,) * (2 + token) + (anywhere,) * len(outs),
            input_output_aliases={5: 0, 6: 1, **aliases},
            scratch_shapes=[
                pltpu.VMEM((wide_rows, cols), jnp.float32),
                pltpu.VMEM((buf_rows, cols), fitted.dtype),
                *scratch,
            ],
            compiler_params=pltpu.CompilerParams(vmem_limit_bytes=limit),
            cost_estimate=cost(cols // COLS),
            name=name,
        )(
            ints, occ, in_vmem(eps_col), in_vmem(eps_row), in_vmem(ft), in_vmem(state["acc"]),
            in_vmem(state["dens"]), *blocks, *extra, state["token"],
        )
        state.update(acc=results[0], dens=results[1], token=results[2])
        return results[2 + token :]

    hops = {index: lax.ppermute(early[index], "row", second_hops[index]) for index in early}
    turned_cols = (pltpu.VMEM((COLS, width), fitted.dtype),)

    def near_pairs(late, *extra):
        add_pairs(
            functools.partial(near_kernel, ways=len(plan), late=late),
            [anywhere] * 2, [in_hbm(fitted), mate], width, NEAR_VMEM, f"near_pairs_{late}",
            extra=extra,
            scratch=(
                pltpu.VMEM((width, width), fitted.dtype),
                pltpu.VMEM((2, aux, width), fitted.dtype),
                pltpu.SemaphoreType.DMA((2,)),
            ),
        )

    near_pairs(0, *early.values())
    for number in range(last):
        for index, (at, alone, _) in enumerate(plan):
            if at == number and not alone:
                far[number] = state["token"] = pass_on(far[number], state["token"])
                hops[index] = lax.ppermute(far[number], "row", second_hops[index])
                if index == len(plan) - 1:
                    near_pairs(1)
        ways = [index for index, (at, _, _) in enumerate(plan) if at == number]
        add_pairs(
            functools.partial(
                far_kernel, ways=ways, total_ways=len(plan), cells=cells, number=number
            ),
            [vmem], [far[number]], COLS, FAR_VMEM, f"far_pairs_{number}", scratch=turned_cols,
        )
    results = (
        jax.ShapeDtypeStruct(fitted.shape, fitted.dtype),
        jax.ShapeDtypeStruct((owned, width, width), jnp.float32),
    )
    out_scratch = (
        pltpu.VMEM((owned, aux, width), fitted.dtype),
        pltpu.SemaphoreType.DMA((owned, OUT_TILES + 1)),
    )
    ready = add_pairs(
        functools.partial(
            relayed_kernel, numbers=[at for at, _, _ in plan], cells=cells
        ),
        [anywhere] * len(hops), [hops[index] for index in range(len(plan))], COLS, FAR_VMEM,
        "relayed_pairs",
        outs=results,
        scratch=turned_cols
        + (pltpu.VMEM((aux, COLS), fitted.dtype), out_scratch[0], pltpu.SemaphoreType.DMA)
        + out_scratch[1:],
    )
    gradient, density = add_pairs(
        functools.partial(last_kernel, total_ways=len(plan), cells=cells),
        [anywhere] * 3, [far[last], *ready], COLS, FAR_VMEM, "last_pairs",
        outs=results,
        aliases={8: 2, 9: 3},
        scratch=turned_cols
        + (pltpu.VMEM((aux, COLS), fitted.dtype),)
        + out_scratch
        + (pltpu.SemaphoreType.DMA((LOAD_TILES,)),),
        token=False,
    )
    return gradient, density


def solution(mesh):
    placed = (
        P(("parts", "row"), None, None),
        P("parts"),
        P("parts", None),
        P("parts"),
        P("parts"),
        P("parts"),
    )
    return jax.shard_map(
        on_device,
        mesh=mesh,
        in_specs=placed,
        out_specs=(P(("parts", "row"), None, None), P(("parts", "row"), None, None)),
        check_vma=False,
    )
```

```python
import functools

import jax
import jax.numpy as jnp
from jax import lax
from jax.experimental import pallas as pl
from jax.experimental.pallas import tpu as pltpu
from jax.sharding import PartitionSpec as P

SUB = 16
STEP = 8
LANES = 128
ROW_TILES = 2
OUT_TILES = 4
LOAD_TILES = 4
CHUNK_TILES = 1
COLS = 256
REACH = 1024
NEAR_VMEM = 22 * 1024 * 1024
FAR_VMEM = 16 * 1024 * 1024
CHUNK_VMEM = 6 * 1024 * 1024


class Plan:
    def __init__(self, ref, owned):
        self.ref, self.owned = ref, owned
        self.slots = 3 * owned * owned

    def slot(self, group, s, t):
        return (group * self.owned + s) * self.owned + t

    def at_shift(self, slot):
        return self.slots + slot

    def at_lead(self, slot):
        return 2 * self.slots + slot

    def at_way(self, number):
        return 3 * self.slots + number

    def at_late(self, ways):
        return self.at_way(ways)

    def at_flip(self, ways):
        return self.at_way(ways) + 1

    def count(self, slot):
        return self.ref[slot]

    def offset(self, slot):
        return pl.multiple_of(REACH + self.ref[self.at_shift(slot)], SUB)

    def lead(self, slot):
        return self.ref[self.at_lead(slot)]

    def way(self, number):
        return self.ref[self.at_way(number)]


def dot(a, b):
    return jnp.dot(a, b, preferred_element_type=jnp.float32)


def tile_of(rows):
    return max(n for n in range(SUB, 705, SUB) if rows % n == 0)


def rows_from(load, start, count):
    skip = start % STEP
    base = pl.multiple_of(start - skip, STEP)
    block = load(base, count + STEP)
    width = block.shape[1]
    block = block.reshape(count // STEP + 1, STEP, width)
    turned = pltpu.roll(block, (STEP - skip) % STEP, 1)
    row = lax.broadcasted_iota(jnp.int32, (count // STEP, STEP, width), 1)
    return jnp.where(row < STEP - skip, turned[:-1], turned[1:]).reshape(count, width)


def clear_margins(buf, rows):
    width = buf.shape[1]
    buf[:REACH, :] = jnp.zeros((REACH, width), buf.dtype)
    buf[REACH + rows :, :] = jnp.zeros((buf.shape[0] - REACH - rows, width), buf.dtype)


def clear_ends(wide):
    rows, width = wide.shape
    wide[:SUB, :] = jnp.zeros((SUB, width), jnp.float32)
    wide[rows - SUB - STEP :, :] = jnp.zeros((SUB + STEP, width), jnp.float32)


def widen(source, wide):
    aux = source.shape[0]
    clear_ends(wide)
    tile = aux // ROW_TILES

    def one(i, carry):
        base = pl.multiple_of(i * tile, SUB)
        wide[pl.ds(pl.multiple_of(SUB + base, SUB), tile), :] = source[
            pl.ds(base, tile), :
        ].astype(jnp.float32)
        return carry

    lax.fori_loop(0, ROW_TILES, one, 0)


def place(lead, wide, buf):
    rows = wide.shape[0] - SUB - STEP
    step = tile_of(rows)

    def move(i, carry):
        base = pl.multiple_of(i * step, SUB)
        moved = rows_from(lambda at, n: wide[pl.ds(at, n), :], SUB - lead + base, step)
        buf[pl.ds(pl.multiple_of(REACH + base, SUB), step), :] = moved.astype(buf.dtype)
        return carry

    lax.fori_loop(0, rows // step, move, 0)


def amplitudes(coulomb, denominator, weight):
    amplitude = (coulomb / denominator).astype(jnp.bfloat16)
    weighted = (amplitude.astype(jnp.float32) * weight).astype(jnp.bfloat16)
    return amplitude, weighted.T


def needed(plan, group, t):
    total = jnp.int32(0)
    for s in range(plan.owned):
        total = total + plan.count(plan.slot(group, s, t))
    return total != 0


def amplitude_of(plan, occ, slot, s, partner, at, eps_col, eps_row, ft, buf):
    rows = ft.shape[2]
    cols = buf.shape[1]
    coulomb = dot(ft[s], buf[pl.ds(plan.offset(slot), rows), :])
    denominator = occ[slot] - eps_col[s] - eps_row[partner, :, pl.ds(at, cols)]
    return amplitudes(coulomb, denominator, plan.count(slot).astype(jnp.float32))


def add_block(plan, occ, group, t, at, eps_col, eps_row, ft, source, wide, buf, acc, dens, turned):
    owned, rows, width = acc.shape
    scale = float(width) ** -0.5
    step = rows // ROW_TILES

    @pl.when(needed(plan, group, t))
    def _():
        widen(source, wide)

    def one(s, carry):
        slot = plan.slot(group, s, t)

        @pl.when(plan.count(slot) != 0)
        def _():
            place(plan.lead(slot), wide, buf)
            amplitude, turned[...] = amplitude_of(
                plan, occ, slot, s, group * owned + t, at, eps_col, eps_row, ft, buf
            )
            dens[s] += scale * dot(amplitude, turned[...])

            def add(i, inner):
                base = pl.multiple_of(i * step, SUB)
                block = buf[pl.ds(pl.multiple_of(plan.offset(slot) + base, SUB), step), :]
                acc[s, pl.ds(base, step), :] += dot(block, turned[...])
                return inner

            lax.fori_loop(0, ROW_TILES, add, 0)

        return carry

    lax.fori_loop(0, owned, one, 0)


def near_pairs_of(position, pair_partner, owned, devices):
    pairs_here = pair_partner.shape[0] // devices
    pairs = []
    for step in (-1, 0, 1):
        group = position + step
        known = (group >= 0) & (group < devices)
        held = jnp.clip(group, 0, devices - 1)
        for n in range(pairs_here):
            pairs.append((known, group * owned + n % owned, pair_partner[held * pairs_here + n]))
    return pairs


def count_between(pairs, one, other):
    total = jnp.int32(0)
    for known, first, second in pairs:
        forth = known & (first == one) & (second == other)
        back = known & (second == one) & (first == other)
        total = total + forth.astype(jnp.int32) + back.astype(jnp.int32)
    return total


def flip_of(used):
    return (used[0] < used[-1]).astype(jnp.int32)


def cell_of(cells, number, flip):
    halves = len([cell for cell in cells if cell[0] == 0])
    flipped = cells[:1] + cells[halves:] + cells[1:halves]
    (t, at), (other_t, other_at) = cells[number], flipped[number]
    if (t, at) == (other_t, other_at):
        return t, at
    return (
        jnp.where(flip == 1, other_t, t),
        pl.multiple_of(jnp.where(flip == 1, other_at, at), COLS),
    )


def make_plan(
    fit_start, occ_energy, pair_partner, domains, energy, ints, occ, eps_col, eps_row,
    *, devices, targets, relays,
):
    owned, width = eps_col.shape[:2]
    orbitals = fit_start.shape[0]
    plan = Plan(ints, owned)
    position = lax.axis_index("row")
    side = jnp.where(position % 2 == 1, 1, -1)
    places = [
        base * owned + t
        for base in (position, position - side, position + side)
        for t in range(owned)
    ]
    inside = [jnp.clip(orbital, 0, orbitals - 1) for orbital in places]
    starts = [fit_start[orbital] for orbital in inside]
    pairs = near_pairs_of(position, pair_partner, owned, devices)
    used = [jnp.int32(0)] * owned
    for group in range(3):
        for s in range(owned):
            for t in range(owned):
                slot = plan.slot(group, s, t)
                other = group * owned + t
                total = count_between(pairs, places[s], places[other])
                ints[slot] = total
                if group == 2:
                    used[t] = used[t] + (total != 0).astype(jnp.int32)
                apart = starts[other] - starts[s]
                ints[plan.at_shift(slot)] = (apart & (SUB - 1)) - apart
                ints[plan.at_lead(slot)] = apart & (SUB - 1)
                occ[slot] = occ_energy[inside[s]] + occ_energy[inside[other]]
    for number, group in enumerate(targets):
        way = jnp.int32(0)
        for to in group:
            way = jnp.where(position == to, 1, way)
        ints[plan.at_way(number)] = way
    late = jnp.int32(0)
    for row in relays:
        late = jnp.where(position == row, 1, late)
    ints[plan.at_late(len(targets))] = late
    ints[plan.at_flip(len(targets))] = flip_of(used)
    entries = energy.shape[0]
    table = lax.broadcasted_iota(jnp.int32, (entries, width), 0)
    for n, orbital in enumerate(inside):
        domain = domains[pl.ds(orbital, 1), :]
        row = jnp.sum(jnp.where(table == domain, energy[...], 0.0), axis=0, keepdims=True)
        eps_row[n] = row
        if n < owned:
            eps_col[n] = jnp.broadcast_to(row, (LANES, width)).T[:, :1]
    return plan


def add_blocks(plan, occ, sources, eps_col, eps_row, ft, wide, buf, acc, dens, turned, raw, sem):
    copies = [
        pltpu.make_async_copy(block, raw.at[n % 2], sem.at[n % 2])
        for n, (_, _, block) in enumerate(sources)
    ]
    copies[0].start()
    clear_margins(buf, raw.shape[1] + SUB)
    for n, (group, t, _) in enumerate(sources):
        if n + 1 < len(copies):
            copies[n + 1].start()
        copies[n].wait()
        add_block(
            plan, occ, group, t, 0, eps_col, eps_row, ft, raw.at[n % 2], wide, buf, acc, dens, turned
        )


def first_kernel(
    fit_start, occ_energy, pair_partner, domains, energy, own, after,
    ints, occ, eps_col, eps_row, acc, dens, ft, token, wide, buf, turned,
    *, devices, targets, relays,
):
    del after
    token[...] = jnp.zeros_like(token)
    plan = make_plan(
        fit_start, occ_energy, pair_partner, domains, energy, ints, occ, eps_col, eps_row,
        devices=devices, targets=targets, relays=relays,
    )
    owned, aux, width = own.shape
    acc[...] = jnp.zeros_like(acc)
    dens[...] = jnp.zeros_like(dens)
    for t in range(owned):

        def turn(i, carry):
            at = pl.multiple_of(i * LANES, LANES)
            ft[t, :, pl.ds(at, LANES)] = own[t, pl.ds(at, LANES), :].T
            return carry

        lax.fori_loop(0, aux // LANES, turn, 0)

    @pl.when(ints[plan.at_late(len(targets))] == 1)
    def _():
        clear_margins(buf, aux + SUB)
        for t in range(owned):
            add_block(
                plan, occ, 0, t, 0, eps_col, eps_row, ft, own.at[t], wide, buf, acc, dens, turned
            )


def near_kernel(
    ints, occ, eps_col, eps_row, ft, acc_in, dens_in, own, mate, *refs, ways, late
):
    del acc_in, dens_in
    acc, dens, token, wide, buf, turned, raw, sem = refs[-8:]
    token[...] = jnp.zeros_like(token)
    owned = own.shape[0]
    plan = Plan(ints, owned)
    groups = ((1, mate),) if late else ((0, own), (1, mate))
    sources = [(group, t, blocks.at[t]) for group, blocks in groups for t in range(owned)]

    @pl.when(ints[plan.at_late(ways)] == late)
    def _():
        add_blocks(
            plan, occ, sources, eps_col, eps_row, ft, wide, buf, acc, dens, turned, raw, sem
        )


def far_kernel(
    ints, occ, eps_col, eps_row, ft, acc_in, dens_in, block, after,
    acc, dens, token, wide, buf, turned, *, ways, total_ways, cells, number,
):
    del acc_in, dens_in, after
    token[...] = jnp.zeros_like(token)
    plan = Plan(ints, acc.shape[0])
    t, at = cell_of(cells, number, ints[plan.at_flip(total_ways)])
    here = needed(plan, 2, t)
    for way in ways:
        here = here & (plan.way(way) == 0)

    @pl.when(here)
    def _():
        clear_margins(buf, block.shape[0] + SUB)
        add_block(plan, occ, 2, t, at, eps_col, eps_row, ft, block, wide, buf, acc, dens, turned)


def send_out(s, tile_of_rows, dens, ready, out, dens_out, sem):
    step = out.shape[1] // OUT_TILES
    pltpu.make_async_copy(dens.at[s], dens_out.at[s], sem.at[s, OUT_TILES]).start()

    def one(i, carry):
        part = pl.ds(pl.multiple_of(i * step, SUB), step)
        ready[s, part, :] = tile_of_rows(i * step, step).astype(ready.dtype)
        pltpu.make_async_copy(ready.at[s, part], out.at[s, part], sem.at[s, i]).start()
        return carry

    lax.fori_loop(0, OUT_TILES, one, 0)


def wait_out(s, dens, ready, out, dens_out, sem):
    step = out.shape[1] // OUT_TILES
    pltpu.make_async_copy(dens.at[s], dens_out.at[s], sem.at[s, OUT_TILES]).wait()
    for i in range(OUT_TILES):
        part = pl.ds(i * step, step)
        pltpu.make_async_copy(ready.at[s, part], out.at[s, part], sem.at[s, i]).wait()


def relayed_kernel(
    ints, occ, eps_col, eps_row, ft, acc_in, dens_in, *refs, numbers, cells
):
    del acc_in, dens_in
    *blocks, _, acc, dens, token, out, dens_out, wide, buf, turned, raw, ready, sem, out_sem = refs
    token[...] = jnp.zeros_like(token)
    owned = acc.shape[0]
    plan = Plan(ints, owned)
    flip = ints[plan.at_flip(len(numbers))]
    last, _ = cell_of(cells, len(cells) - 1, flip)
    for way, (block, number) in enumerate(zip(blocks, numbers)):
        t, at = cell_of(cells, number, flip)

        @pl.when(needed(plan, 2, t) & (plan.way(way) == 1))
        def _():
            copy = pltpu.make_async_copy(block, raw, sem)
            copy.start()
            clear_margins(buf, raw.shape[0] + SUB)
            copy.wait()
            add_block(plan, occ, 2, t, at, eps_col, eps_row, ft, raw, wide, buf, acc, dens, turned)

    for s in range(owned):

        @pl.when(plan.count(plan.slot(2, s, last)) == 0)
        def _():
            send_out(
                s,
                lambda base, n: acc[s, pl.ds(pl.multiple_of(base, SUB), n), :],
                dens, ready, out, dens_out, out_sem,
            )

    for s in range(owned):

        @pl.when(plan.count(plan.slot(2, s, last)) == 0)
        def _():
            wait_out(s, dens, ready, out, dens_out, out_sem)


def last_kernel(
    ints, occ, eps_col, eps_row, ft, acc_in, dens_in, block, out_in, dens_out_in, after,
    acc, dens, out, dens_out, wide, buf, turned, raw, ready, sem, raw_sem, *, total_ways, cells,
):
    del acc_in, dens_in, out_in, dens_out_in, after
    owned, aux, width = out.shape
    plan = Plan(ints, owned)
    t, at = cell_of(cells, len(cells) - 1, ints[plan.at_flip(total_ways)])
    scale = float(width) ** -0.5

    @pl.when(needed(plan, 2, t))
    def _():
        step = aux // LOAD_TILES
        parts = [pl.ds(i * step, step) for i in range(LOAD_TILES)]
        loads = [
            pltpu.make_async_copy(block.at[part], raw.at[part], raw_sem.at[i])
            for i, part in enumerate(parts)
        ]
        for load in loads:
            load.start()
        clear_margins(buf, aux + SUB)
        clear_ends(wide)
        for i, load in enumerate(loads):
            load.wait()
            wide[SUB + i * step : SUB + (i + 1) * step, :] = raw[parts[i], :].astype(jnp.float32)

    def one(s, carry):
        slot = plan.slot(2, s, t)

        @pl.when(plan.count(slot) != 0)
        def _():
            place(plan.lead(slot), wide, buf)
            amplitude, turned[...] = amplitude_of(
                plan, occ, slot, s, 2 * owned + t, at, eps_col, eps_row, ft, buf
            )
            dens[s] += scale * dot(amplitude, turned[...])

            def total(base, n):
                rows = buf[pl.ds(pl.multiple_of(plan.offset(slot) + base, SUB), n), :]
                return acc[s, pl.ds(pl.multiple_of(base, SUB), n), :] + dot(rows, turned[...])

            send_out(s, total, dens, ready, out, dens_out, sem)

        return carry

    lax.fori_loop(0, owned, one, 0)
    for s in range(owned):

        @pl.when(plan.count(plan.slot(2, s, t)) != 0)
        def _():
            wait_out(s, dens, ready, out, dens_out, sem)


def copy_kernel(source, *refs, numbers, cells, devices):
    *outs, buf, sem = refs[-len(numbers) - 2 :]
    owned = source.shape[0]
    flip = jnp.int32(0)
    if any(numbers):
        position = lax.axis_index("row")
        pairs = near_pairs_of(position, refs[0], owned, devices)
        beyond = position + jnp.where(position % 2 == 1, 1, -1)
        used = []
        for t in range(owned):
            total = jnp.int32(0)
            for s in range(owned):
                count = count_between(pairs, position * owned + t, beyond * owned + s)
                total = total + (count != 0).astype(jnp.int32)
            used.append(total)
        flip = flip_of(used)
    places = [cell_of(cells, number, flip) for number in numbers]
    rows, cols = outs[0].shape
    tile = rows // CHUNK_TILES
    parts = [(n, i) for n in range(len(places)) for i in range(CHUNK_TILES)]

    def copies(n, i):
        t, at = places[n]
        part = pl.ds(i * tile, tile)
        held = buf.at[n, part]
        load = pltpu.make_async_copy(source.at[t, part, pl.ds(at, cols)], held, sem.at[0, n, i])
        return load, pltpu.make_async_copy(held, outs[n].at[part], sem.at[1, n, i])

    for n, i in parts:
        copies(n, i)[0].start()
    for n, i in parts:
        load, store = copies(n, i)
        load.wait()
        store.start()
    for n, i in parts:
        copies(n, i)[1].wait()


def pass_kernel(source, after, out):
    del source, after, out


def relay_plan(devices, chunks):
    if devices != 16 or chunks != 4:
        return []
    plan = []
    for z, chunk, alone in ((1, 0, True), (0, 0, False), (2, 1, False)):
        high, low = 4 * z + 3, 4 * z + 4
        plan.append((chunk, alone, [(high, low, 0), (low, high, devices - 1)]))
    return plan


def spec(space):
    return pl.BlockSpec(memory_space=space)


def on_device(fitted, fit_start, virt_domain, occ_energy, virt_energy, pair_partner):
    owned, aux, width = fitted.shape
    devices = lax.axis_size("row")
    buf_rows = 2 * REACH + aux
    wide_rows = aux + 2 * SUB + STEP
    smem, vmem, anywhere = spec(pltpu.SMEM), spec(pltpu.VMEM), spec(pl.ANY)

    outward = []
    for i in range(devices):
        to = i + 1 if i % 2 else i - 1
        if 0 <= to < devices:
            outward.append((i, to))
    inward = [(i, i ^ 1) for i in range(devices) if i ^ 1 < devices]

    def in_hbm(array):
        return pltpu.with_memory_space_constraint(array, pltpu.HBM)

    def in_vmem(array):
        return pltpu.with_memory_space_constraint(array, pltpu.VMEM)

    def chunks(numbers, *after):
        return pl.pallas_call(
            functools.partial(copy_kernel, numbers=numbers, cells=cells, devices=devices),
            out_shape=[jax.ShapeDtypeStruct((aux, COLS), fitted.dtype)] * len(numbers),
            in_specs=[anywhere] + [smem] * any(numbers) + [anywhere] * len(after),
            out_specs=[anywhere] * len(numbers),
            scratch_shapes=[
                pltpu.VMEM((len(numbers), aux, COLS), fitted.dtype),
                pltpu.SemaphoreType.DMA((2, len(numbers), CHUNK_TILES)),
            ],
            compiler_params=pltpu.CompilerParams(vmem_limit_bytes=CHUNK_VMEM),
            name="chunks",
        )(in_hbm(fitted), *[pair_partner] * any(numbers), *after)

    def pass_on(block, after):
        return pl.pallas_call(
            pass_kernel,
            out_shape=jax.ShapeDtypeStruct(block.shape, block.dtype),
            in_specs=[anywhere] * 2,
            out_specs=anywhere,
            input_output_aliases={0: 0},
            compiler_params=pltpu.CompilerParams(vmem_limit_bytes=CHUNK_VMEM),
            name="pass_on",
        )(block, after)

    cells = [(t, at) for t in range(owned) for at in range(0, width, COLS)]
    last = len(cells) - 1
    plan = relay_plan(devices, len(cells))
    first_hops = [[(source, by) for source, _, by in pairs] for _, _, pairs in plan]
    second_hops = [[(by, to) for _, to, by in pairs] for _, _, pairs in plan]

    def exchange(number, block):
        pairs = list(outward)
        for (at, alone, group), hop in zip(plan, first_hops):
            if at == number:
                pairs = [pair for pair in pairs if pair not in {(a, b) for a, b, _ in group}]
                pairs += [] if alone else hop
        return lax.ppermute(block, "row", pairs)

    sent = list(chunks([0]))
    mate = lax.ppermute(lax.optimization_barrier((fitted, sent[0]))[0], "row", inward)
    far = [exchange(0, sent[0])]
    rest = chunks(list(range(1, len(cells))) + [0] * bool(plan), sent[0])
    sent += rest[:last]
    early = {
        index: lax.ppermute(rest[last], "row", first_hops[index])
        for index, (_, alone, _) in enumerate(plan)
        if alone
    }
    far += [exchange(number, sent[number]) for number in range(1, last + 1)]

    unit = 4 * aux * width * COLS
    acc_shape = pltpu.VMEM((owned, aux, width), jnp.float32)
    dens_shape = pltpu.VMEM((owned, width, width), jnp.float32)
    ft_shape = pltpu.VMEM((owned, width, aux), fitted.dtype)
    token_shape = jax.ShapeDtypeStruct((8, LANES), jnp.int32)
    slots = 3 * owned * owned

    def cost(blocks):
        return pl.CostEstimate(
            flops=100 * unit * blocks * owned, bytes_accessed=8 << 20, transcendentals=0
        )

    ints, occ, eps_col, eps_row, acc, dens, ft, token = pl.pallas_call(
        functools.partial(
            first_kernel,
            devices=devices,
            targets=[[to for _, to, _ in pairs] for _, _, pairs in plan],
            relays=sorted({by for _, _, pairs in plan for _, _, by in pairs}),
        ),
        out_shape=(
            jax.ShapeDtypeStruct((Plan(None, owned).at_flip(len(plan)) + 1,), jnp.int32),
            jax.ShapeDtypeStruct((slots,), jnp.float32),
            pltpu.VMEM((owned, width, 1), jnp.float32),
            pltpu.VMEM((3 * owned, 1, width), jnp.float32),
            acc_shape,
            dens_shape,
            ft_shape,
            token_shape,
        ),
        in_specs=[smem] * 3 + [vmem] * 3 + [anywhere],
        out_specs=(smem,) * 2 + (vmem,) * 6,
        scratch_shapes=[
            pltpu.VMEM((wide_rows, width), jnp.float32),
            pltpu.VMEM((buf_rows, width), fitted.dtype),
            pltpu.VMEM((width, width), fitted.dtype),
        ],
        compiler_params=pltpu.CompilerParams(vmem_limit_bytes=NEAR_VMEM),
        cost_estimate=cost(len(cells)),
        name="first",
    )(
        fit_start, occ_energy, pair_partner, virt_domain, virt_energy.reshape(-1, 1),
        in_hbm(fitted), sent[last - 1],
    )
    state = {"acc": acc, "dens": dens, "token": token}
    hops = []

    def add_pairs(
        kernel, block_specs, blocks, cols, limit, name,
        extra=(), outs=(), aliases={}, scratch=(), token=True,
    ):
        specs = [smem] * 2 + [vmem] * 5 + block_specs
        results = pl.pallas_call(
            kernel,
            out_shape=(acc_shape, dens_shape) + (token_shape,) * token + tuple(outs),
            in_specs=specs + [anywhere] * (1 + len(extra)),
            out_specs=(vmem,) * (2 + token) + (anywhere,) * len(outs),
            input_output_aliases={5: 0, 6: 1, **aliases},
            scratch_shapes=[
                pltpu.VMEM((wide_rows, cols), jnp.float32),
                pltpu.VMEM((buf_rows, cols), fitted.dtype),
                *scratch,
            ],
            compiler_params=pltpu.CompilerParams(vmem_limit_bytes=limit),
            cost_estimate=cost(cols // COLS),
            name=name,
        )(
            ints, occ, in_vmem(eps_col), in_vmem(eps_row), in_vmem(ft), in_vmem(state["acc"]),
            in_vmem(state["dens"]), *blocks, *extra, state["token"],
        )
        state.update(acc=results[0], dens=results[1], token=results[2])
        return results[2 + token :]

    hops = {index: lax.ppermute(early[index], "row", second_hops[index]) for index in early}
    turned_cols = (pltpu.VMEM((COLS, width), fitted.dtype),)

    def near_pairs(late, *extra):
        add_pairs(
            functools.partial(near_kernel, ways=len(plan), late=late),
            [anywhere] * 2, [in_hbm(fitted), mate], width, NEAR_VMEM, f"near_pairs_{late}",
            extra=extra,
            scratch=(
                pltpu.VMEM((width, width), fitted.dtype),
                pltpu.VMEM((2, aux, width), fitted.dtype),
                pltpu.SemaphoreType.DMA((2,)),
            ),
        )

    near_pairs(0, *early.values())
    for number in range(last):
        for index, (at, alone, _) in enumerate(plan):
            if at == number and not alone:
                far[number] = state["token"] = pass_on(far[number], state["token"])
                hops[index] = lax.ppermute(far[number], "row", second_hops[index])
                if index == len(plan) - 1:
                    near_pairs(1)
        ways = [index for index, (at, _, _) in enumerate(plan) if at == number]
        add_pairs(
            functools.partial(
                far_kernel, ways=ways, total_ways=len(plan), cells=cells, number=number
            ),
            [vmem], [far[number]], COLS, FAR_VMEM, f"far_pairs_{number}", scratch=turned_cols,
        )
    results = (
        jax.ShapeDtypeStruct(fitted.shape, fitted.dtype),
        jax.ShapeDtypeStruct((owned, width, width), jnp.float32),
    )
    out_scratch = (
        pltpu.VMEM((owned, aux, width), fitted.dtype),
        pltpu.SemaphoreType.DMA((owned, OUT_TILES + 1)),
    )
    ready = add_pairs(
        functools.partial(
            relayed_kernel, numbers=[at for at, _, _ in plan], cells=cells
        ),
        [anywhere] * len(hops), [hops[index] for index in range(len(plan))], COLS, FAR_VMEM,
        "relayed_pairs",
        outs=results,
        scratch=turned_cols
        + (pltpu.VMEM((aux, COLS), fitted.dtype), out_scratch[0], pltpu.SemaphoreType.DMA)
        + out_scratch[1:],
    )
    gradient, density = add_pairs(
        functools.partial(last_kernel, total_ways=len(plan), cells=cells),
        [anywhere] * 3, [far[last], *ready], COLS, FAR_VMEM, "last_pairs",
        outs=results,
        aliases={8: 2, 9: 3},
        scratch=turned_cols
        + (pltpu.VMEM((aux, COLS), fitted.dtype),)
        + out_scratch
        + (pltpu.SemaphoreType.DMA((LOAD_TILES,)),),
        token=False,
    )
    return gradient, density


def solution(mesh):
    placed = (
        P(("parts", "row"), None, None),
        P("parts"),
        P("parts", None),
        P("parts"),
        P("parts"),
        P("parts"),
    )
    return jax.shard_map(
        on_device,
        mesh=mesh,
        in_specs=placed,
        out_specs=(P(("parts", "row"), None, None), P(("parts", "row"), None, None)),
        check_vma=False,
    )
```

```python
import functools

import jax
import jax.numpy as jnp
from jax import lax
from jax.experimental import pallas as pl
from jax.experimental.pallas import tpu as pltpu
from jax.sharding import PartitionSpec as P

SUB = 16
STEP = 8
LANES = 128
ROW_TILES = 2
OUT_TILES = 4
LOAD_TILES = 4
CHUNK_TILES = 2
COLS = 256
REACH = 1024
NEAR_VMEM = 22 * 1024 * 1024
FAR_VMEM = 16 * 1024 * 1024
CHUNK_VMEM = 6 * 1024 * 1024


class Plan:
    def __init__(self, ref, owned):
        self.ref, self.owned = ref, owned
        self.slots = 3 * owned * owned

    def slot(self, group, s, t):
        return (group * self.owned + s) * self.owned + t

    def at_shift(self, slot):
        return self.slots + slot

    def at_lead(self, slot):
        return 2 * self.slots + slot

    def at_way(self, number):
        return 3 * self.slots + number

    def at_late(self, ways):
        return self.at_way(ways)

    def at_flip(self, ways):
        return self.at_way(ways) + 1

    def count(self, slot):
        return self.ref[slot]

    def offset(self, slot):
        return pl.multiple_of(REACH + self.ref[self.at_shift(slot)], SUB)

    def lead(self, slot):
        return self.ref[self.at_lead(slot)]

    def way(self, number):
        return self.ref[self.at_way(number)]


def dot(a, b):
    return jnp.dot(a, b, preferred_element_type=jnp.float32)


def tile_of(rows):
    return max(n for n in range(SUB, 705, SUB) if rows % n == 0)


def rows_from(load, start, count):
    skip = start % STEP
    base = pl.multiple_of(start - skip, STEP)
    block = load(base, count + STEP)
    width = block.shape[1]
    block = block.reshape(count // STEP + 1, STEP, width)
    turned = pltpu.roll(block, (STEP - skip) % STEP, 1)
    row = lax.broadcasted_iota(jnp.int32, (count // STEP, STEP, width), 1)
    return jnp.where(row < STEP - skip, turned[:-1], turned[1:]).reshape(count, width)


def clear_margins(buf, rows):
    width = buf.shape[1]
    buf[:REACH, :] = jnp.zeros((REACH, width), buf.dtype)
    buf[REACH + rows :, :] = jnp.zeros((buf.shape[0] - REACH - rows, width), buf.dtype)


def clear_ends(wide):
    rows, width = wide.shape
    wide[:SUB, :] = jnp.zeros((SUB, width), jnp.float32)
    wide[rows - SUB - STEP :, :] = jnp.zeros((SUB + STEP, width), jnp.float32)


def widen(source, wide):
    aux = source.shape[0]
    clear_ends(wide)
    tile = aux // ROW_TILES

    def one(i, carry):
        base = pl.multiple_of(i * tile, SUB)
        wide[pl.ds(pl.multiple_of(SUB + base, SUB), tile), :] = source[
            pl.ds(base, tile), :
        ].astype(jnp.float32)
        return carry

    lax.fori_loop(0, ROW_TILES, one, 0)


def place(lead, wide, buf):
    rows = wide.shape[0] - SUB - STEP
    step = tile_of(rows)

    def move(i, carry):
        base = pl.multiple_of(i * step, SUB)
        moved = rows_from(lambda at, n: wide[pl.ds(at, n), :], SUB - lead + base, step)
        buf[pl.ds(pl.multiple_of(REACH + base, SUB), step), :] = moved.astype(buf.dtype)
        return carry

    lax.fori_loop(0, rows // step, move, 0)


def amplitudes(coulomb, denominator, weight):
    amplitude = (coulomb / denominator).astype(jnp.bfloat16)
    weighted = (amplitude.astype(jnp.float32) * weight).astype(jnp.bfloat16)
    return amplitude, weighted.T


def needed(plan, group, t):
    total = jnp.int32(0)
    for s in range(plan.owned):
        total = total + plan.count(plan.slot(group, s, t))
    return total != 0


def amplitude_of(plan, occ, slot, s, partner, at, eps_col, eps_row, ft, buf):
    rows = ft.shape[2]
    cols = buf.shape[1]
    coulomb = dot(ft[s], buf[pl.ds(plan.offset(slot), rows), :])
    denominator = occ[slot] - eps_col[s] - eps_row[partner, :, pl.ds(at, cols)]
    return amplitudes(coulomb, denominator, plan.count(slot).astype(jnp.float32))


def add_block(plan, occ, group, t, at, eps_col, eps_row, ft, source, wide, buf, acc, dens, turned):
    owned, rows, width = acc.shape
    scale = float(width) ** -0.5
    step = rows // ROW_TILES

    @pl.when(needed(plan, group, t))
    def _():
        widen(source, wide)

    def one(s, carry):
        slot = plan.slot(group, s, t)

        @pl.when(plan.count(slot) != 0)
        def _():
            place(plan.lead(slot), wide, buf)
            amplitude, turned[...] = amplitude_of(
                plan, occ, slot, s, group * owned + t, at, eps_col, eps_row, ft, buf
            )
            dens[s] += scale * dot(amplitude, turned[...])

            def add(i, inner):
                base = pl.multiple_of(i * step, SUB)
                block = buf[pl.ds(pl.multiple_of(plan.offset(slot) + base, SUB), step), :]
                acc[s, pl.ds(base, step), :] += dot(block, turned[...])
                return inner

            lax.fori_loop(0, ROW_TILES, add, 0)

        return carry

    lax.fori_loop(0, owned, one, 0)


def near_pairs_of(position, pair_partner, owned, devices):
    pairs_here = pair_partner.shape[0] // devices
    pairs = []
    for step in (-1, 0, 1):
        group = position + step
        known = (group >= 0) & (group < devices)
        held = jnp.clip(group, 0, devices - 1)
        for n in range(pairs_here):
            pairs.append((known, group * owned + n % owned, pair_partner[held * pairs_here + n]))
    return pairs


def count_between(pairs, one, other):
    total = jnp.int32(0)
    for known, first, second in pairs:
        forth = known & (first == one) & (second == other)
        back = known & (second == one) & (first == other)
        total = total + forth.astype(jnp.int32) + back.astype(jnp.int32)
    return total


def flip_of(used):
    return (used[0] < used[-1]).astype(jnp.int32)


def cell_of(cells, number, flip):
    halves = len([cell for cell in cells if cell[0] == 0])
    flipped = cells[:1] + cells[halves:] + cells[1:halves]
    (t, at), (other_t, other_at) = cells[number], flipped[number]
    if (t, at) == (other_t, other_at):
        return t, at
    return (
        jnp.where(flip == 1, other_t, t),
        pl.multiple_of(jnp.where(flip == 1, other_at, at), COLS),
    )


def make_plan(
    fit_start, occ_energy, pair_partner, domains, energy, ints, occ, eps_col, eps_row,
    *, devices, targets, relays,
):
    owned, width = eps_col.shape[:2]
    orbitals = fit_start.shape[0]
    plan = Plan(ints, owned)
    position = lax.axis_index("row")
    side = jnp.where(position % 2 == 1, 1, -1)
    places = [
        base * owned + t
        for base in (position, position - side, position + side)
        for t in range(owned)
    ]
    inside = [jnp.clip(orbital, 0, orbitals - 1) for orbital in places]
    starts = [fit_start[orbital] for orbital in inside]
    pairs = near_pairs_of(position, pair_partner, owned, devices)
    used = [jnp.int32(0)] * owned
    for group in range(3):
        for s in range(owned):
            for t in range(owned):
                slot = plan.slot(group, s, t)
                other = group * owned + t
                total = count_between(pairs, places[s], places[other])
                ints[slot] = total
                if group == 2:
                    used[t] = used[t] + (total != 0).astype(jnp.int32)
                apart = starts[other] - starts[s]
                ints[plan.at_shift(slot)] = (apart & (SUB - 1)) - apart
                ints[plan.at_lead(slot)] = apart & (SUB - 1)
                occ[slot] = occ_energy[inside[s]] + occ_energy[inside[other]]
    for number, group in enumerate(targets):
        way = jnp.int32(0)
        for to in group:
            way = jnp.where(position == to, 1, way)
        ints[plan.at_way(number)] = way
    late = jnp.int32(0)
    for row in relays:
        late = jnp.where(position == row, 1, late)
    ints[plan.at_late(len(targets))] = late
    ints[plan.at_flip(len(targets))] = flip_of(used)
    entries = energy.shape[0]
    table = lax.broadcasted_iota(jnp.int32, (entries, width), 0)
    for n, orbital in enumerate(inside):
        domain = domains[pl.ds(orbital, 1), :]
        row = jnp.sum(jnp.where(table == domain, energy[...], 0.0), axis=0, keepdims=True)
        eps_row[n] = row
        if n < owned:
            eps_col[n] = jnp.broadcast_to(row, (LANES, width)).T[:, :1]
    return plan


def add_blocks(plan, occ, sources, eps_col, eps_row, ft, wide, buf, acc, dens, turned, raw, sem):
    copies = [
        pltpu.make_async_copy(block, raw.at[n % 2], sem.at[n % 2])
        for n, (_, _, block) in enumerate(sources)
    ]
    copies[0].start()
    clear_margins(buf, raw.shape[1] + SUB)
    for n, (group, t, _) in enumerate(sources):
        if n + 1 < len(copies):
            copies[n + 1].start()
        copies[n].wait()
        add_block(
            plan, occ, group, t, 0, eps_col, eps_row, ft, raw.at[n % 2], wide, buf, acc, dens, turned
        )


def first_kernel(
    fit_start, occ_energy, pair_partner, domains, energy, own, after,
    ints, occ, eps_col, eps_row, acc, dens, ft, token, wide, buf, turned,
    *, devices, targets, relays,
):
    del after
    token[...] = jnp.zeros_like(token)
    plan = make_plan(
        fit_start, occ_energy, pair_partner, domains, energy, ints, occ, eps_col, eps_row,
        devices=devices, targets=targets, relays=relays,
    )
    owned, aux, width = own.shape
    acc[...] = jnp.zeros_like(acc)
    dens[...] = jnp.zeros_like(dens)
    for t in range(owned):

        def turn(i, carry):
            at = pl.multiple_of(i * LANES, LANES)
            ft[t, :, pl.ds(at, LANES)] = own[t, pl.ds(at, LANES), :].T
            return carry

        lax.fori_loop(0, aux // LANES, turn, 0)

    @pl.when(ints[plan.at_late(len(targets))] == 1)
    def _():
        clear_margins(buf, aux + SUB)
        for t in range(owned):
            add_block(
                plan, occ, 0, t, 0, eps_col, eps_row, ft, own.at[t], wide, buf, acc, dens, turned
            )


def near_kernel(
    ints, occ, eps_col, eps_row, ft, acc_in, dens_in, own, mate, *refs, ways, late
):
    del acc_in, dens_in
    acc, dens, token, wide, buf, turned, raw, sem = refs[-8:]
    token[...] = jnp.zeros_like(token)
    owned = own.shape[0]
    plan = Plan(ints, owned)
    groups = ((1, mate),) if late else ((0, own), (1, mate))
    sources = [(group, t, blocks.at[t]) for group, blocks in groups for t in range(owned)]

    @pl.when(ints[plan.at_late(ways)] == late)
    def _():
        add_blocks(
            plan, occ, sources, eps_col, eps_row, ft, wide, buf, acc, dens, turned, raw, sem
        )


def far_kernel(
    ints, occ, eps_col, eps_row, ft, acc_in, dens_in, block, after,
    acc, dens, token, wide, buf, turned, *, ways, total_ways, cells, number,
):
    del acc_in, dens_in, after
    token[...] = jnp.zeros_like(token)
    plan = Plan(ints, acc.shape[0])
    t, at = cell_of(cells, number, ints[plan.at_flip(total_ways)])
    here = needed(plan, 2, t)
    for way in ways:
        here = here & (plan.way(way) == 0)

    @pl.when(here)
    def _():
        clear_margins(buf, block.shape[0] + SUB)
        add_block(plan, occ, 2, t, at, eps_col, eps_row, ft, block, wide, buf, acc, dens, turned)


def send_out(s, tile_of_rows, dens, ready, out, dens_out, sem):
    step = out.shape[1] // OUT_TILES
    pltpu.make_async_copy(dens.at[s], dens_out.at[s], sem.at[s, OUT_TILES]).start()

    def one(i, carry):
        part = pl.ds(pl.multiple_of(i * step, SUB), step)
        ready[s, part, :] = tile_of_rows(i * step, step).astype(ready.dtype)
        pltpu.make_async_copy(ready.at[s, part], out.at[s, part], sem.at[s, i]).start()
        return carry

    lax.fori_loop(0, OUT_TILES, one, 0)


def wait_out(s, dens, ready, out, dens_out, sem):
    step = out.shape[1] // OUT_TILES
    pltpu.make_async_copy(dens.at[s], dens_out.at[s], sem.at[s, OUT_TILES]).wait()
    for i in range(OUT_TILES):
        part = pl.ds(i * step, step)
        pltpu.make_async_copy(ready.at[s, part], out.at[s, part], sem.at[s, i]).wait()


def relayed_kernel(
    ints, occ, eps_col, eps_row, ft, acc_in, dens_in, *refs, numbers, cells
):
    del acc_in, dens_in
    *blocks, _, acc, dens, token, out, dens_out, wide, buf, turned, raw, ready, sem, out_sem = refs
    token[...] = jnp.zeros_like(token)
    owned = acc.shape[0]
    plan = Plan(ints, owned)
    flip = ints[plan.at_flip(len(numbers))]
    last, _ = cell_of(cells, len(cells) - 1, flip)
    for way, (block, number) in enumerate(zip(blocks, numbers)):
        t, at = cell_of(cells, number, flip)

        @pl.when(needed(plan, 2, t) & (plan.way(way) == 1))
        def _():
            copy = pltpu.make_async_copy(block, raw, sem)
            copy.start()
            clear_margins(buf, raw.shape[0] + SUB)
            copy.wait()
            add_block(plan, occ, 2, t, at, eps_col, eps_row, ft, raw, wide, buf, acc, dens, turned)

    for s in range(owned):

        @pl.when(plan.count(plan.slot(2, s, last)) == 0)
        def _():
            send_out(
                s,
                lambda base, n: acc[s, pl.ds(pl.multiple_of(base, SUB), n), :],
                dens, ready, out, dens_out, out_sem,
            )

    for s in range(owned):

        @pl.when(plan.count(plan.slot(2, s, last)) == 0)
        def _():
            wait_out(s, dens, ready, out, dens_out, out_sem)


def last_kernel(
    ints, occ, eps_col, eps_row, ft, acc_in, dens_in, block, out_in, dens_out_in, after,
    acc, dens, out, dens_out, wide, buf, turned, raw, ready, sem, raw_sem, *, total_ways, cells,
):
    del acc_in, dens_in, out_in, dens_out_in, after
    owned, aux, width = out.shape
    plan = Plan(ints, owned)
    t, at = cell_of(cells, len(cells) - 1, ints[plan.at_flip(total_ways)])
    scale = float(width) ** -0.5

    @pl.when(needed(plan, 2, t))
    def _():
        step = aux // LOAD_TILES
        parts = [pl.ds(i * step, step) for i in range(LOAD_TILES)]
        loads = [
            pltpu.make_async_copy(block.at[part], raw.at[part], raw_sem.at[i])
            for i, part in enumerate(parts)
        ]
        for load in loads:
            load.start()
        clear_margins(buf, aux + SUB)
        clear_ends(wide)
        for i, load in enumerate(loads):
            load.wait()
            wide[SUB + i * step : SUB + (i + 1) * step, :] = raw[parts[i], :].astype(jnp.float32)

    def one(s, carry):
        slot = plan.slot(2, s, t)

        @pl.when(plan.count(slot) != 0)
        def _():
            place(plan.lead(slot), wide, buf)
            amplitude, turned[...] = amplitude_of(
                plan, occ, slot, s, 2 * owned + t, at, eps_col, eps_row, ft, buf
            )
            dens[s] += scale * dot(amplitude, turned[...])

            def total(base, n):
                rows = buf[pl.ds(pl.multiple_of(plan.offset(slot) + base, SUB), n), :]
                return acc[s, pl.ds(pl.multiple_of(base, SUB), n), :] + dot(rows, turned[...])

            send_out(s, total, dens, ready, out, dens_out, sem)

        return carry

    lax.fori_loop(0, owned, one, 0)
    for s in range(owned):

        @pl.when(plan.count(plan.slot(2, s, t)) != 0)
        def _():
            wait_out(s, dens, ready, out, dens_out, sem)


def copy_kernel(source, *refs, numbers, cells, devices):
    *outs, buf, sem = refs[-len(numbers) - 2 :]
    owned = source.shape[0]
    flip = jnp.int32(0)
    if any(numbers):
        position = lax.axis_index("row")
        pairs = near_pairs_of(position, refs[0], owned, devices)
        beyond = position + jnp.where(position % 2 == 1, 1, -1)
        used = []
        for t in range(owned):
            total = jnp.int32(0)
            for s in range(owned):
                count = count_between(pairs, position * owned + t, beyond * owned + s)
                total = total + (count != 0).astype(jnp.int32)
            used.append(total)
        flip = flip_of(used)
    places = [cell_of(cells, number, flip) for number in numbers]
    rows, cols = outs[0].shape
    tile = rows // CHUNK_TILES
    parts = [(n, i) for n in range(len(places)) for i in range(CHUNK_TILES)]

    def copies(n, i):
        t, at = places[n]
        part = pl.ds(i * tile, tile)
        held = buf.at[n, part]
        load = pltpu.make_async_copy(source.at[t, part, pl.ds(at, cols)], held, sem.at[0, n, i])
        return load, pltpu.make_async_copy(held, outs[n].at[part], sem.at[1, n, i])

    for n, i in parts:
        copies(n, i)[0].start()
    for n, i in parts:
        load, store = copies(n, i)
        load.wait()
        store.start()
    for n, i in parts:
        copies(n, i)[1].wait()


def pass_kernel(source, after, out):
    del source, after, out


def relay_plan(devices, chunks):
    if devices != 16 or chunks != 4:
        return []
    plan = []
    for z, chunk, alone in ((1, 0, True), (0, 0, False), (2, 1, False)):
        high, low = 4 * z + 3, 4 * z + 4
        plan.append((chunk, alone, [(high, low, 0), (low, high, devices - 1)]))
    return plan


def spec(space):
    return pl.BlockSpec(memory_space=space)


def on_device(fitted, fit_start, virt_domain, occ_energy, virt_energy, pair_partner):
    owned, aux, width = fitted.shape
    devices = lax.axis_size("row")
    buf_rows = 2 * REACH + aux
    wide_rows = aux + 2 * SUB + STEP
    smem, vmem, anywhere = spec(pltpu.SMEM), spec(pltpu.VMEM), spec(pl.ANY)

    outward = []
    for i in range(devices):
        to = i + 1 if i % 2 else i - 1
        if 0 <= to < devices:
            outward.append((i, to))
    inward = [(i, i ^ 1) for i in range(devices) if i ^ 1 < devices]

    def in_hbm(array):
        return pltpu.with_memory_space_constraint(array, pltpu.HBM)

    def in_vmem(array):
        return pltpu.with_memory_space_constraint(array, pltpu.VMEM)

    def chunks(numbers, *after):
        return pl.pallas_call(
            functools.partial(copy_kernel, numbers=numbers, cells=cells, devices=devices),
            out_shape=[jax.ShapeDtypeStruct((aux, COLS), fitted.dtype)] * len(numbers),
            in_specs=[anywhere] + [smem] * any(numbers) + [anywhere] * len(after),
            out_specs=[anywhere] * len(numbers),
            scratch_shapes=[
                pltpu.VMEM((len(numbers), aux, COLS), fitted.dtype),
                pltpu.SemaphoreType.DMA((2, len(numbers), CHUNK_TILES)),
            ],
            compiler_params=pltpu.CompilerParams(vmem_limit_bytes=CHUNK_VMEM),
            name="chunks",
        )(in_hbm(fitted), *[pair_partner] * any(numbers), *after)

    def pass_on(block, after):
        return pl.pallas_call(
            pass_kernel,
            out_shape=jax.ShapeDtypeStruct(block.shape, block.dtype),
            in_specs=[anywhere] * 2,
            out_specs=anywhere,
            input_output_aliases={0: 0},
            compiler_params=pltpu.CompilerParams(vmem_limit_bytes=CHUNK_VMEM),
            name="pass_on",
        )(block, after)

    cells = [(t, at) for t in range(owned) for at in range(0, width, COLS)]
    last = len(cells) - 1
    plan = relay_plan(devices, len(cells))
    first_hops = [[(source, by) for source, _, by in pairs] for _, _, pairs in plan]
    second_hops = [[(by, to) for _, to, by in pairs] for _, _, pairs in plan]

    def exchange(number, block):
        pairs = list(outward)
        for (at, alone, group), hop in zip(plan, first_hops):
            if at == number:
                pairs = [pair for pair in pairs if pair not in {(a, b) for a, b, _ in group}]
                pairs += [] if alone else hop
        return lax.ppermute(block, "row", pairs)

    sent = list(chunks([0]))
    mate = lax.ppermute(fitted, "row", inward)
    far = [exchange(0, sent[0])]
    rest = chunks(list(range(1, len(cells))) + [0] * bool(plan), sent[0])
    sent += rest[:last]
    early = {
        index: lax.ppermute(rest[last], "row", first_hops[index])
        for index, (_, alone, _) in enumerate(plan)
        if alone
    }
    far += [exchange(number, sent[number]) for number in range(1, last + 1)]

    unit = 4 * aux * width * COLS
    acc_shape = pltpu.VMEM((owned, aux, width), jnp.float32)
    dens_shape = pltpu.VMEM((owned, width, width), jnp.float32)
    ft_shape = pltpu.VMEM((owned, width, aux), fitted.dtype)
    token_shape = jax.ShapeDtypeStruct((8, LANES), jnp.int32)
    slots = 3 * owned * owned

    def cost(blocks):
        return pl.CostEstimate(
            flops=100 * unit * blocks * owned, bytes_accessed=8 << 20, transcendentals=0
        )

    ints, occ, eps_col, eps_row, acc, dens, ft, token = pl.pallas_call(
        functools.partial(
            first_kernel,
            devices=devices,
            targets=[[to for _, to, _ in pairs] for _, _, pairs in plan],
            relays=sorted({by for _, _, pairs in plan for _, _, by in pairs}),
        ),
        out_shape=(
            jax.ShapeDtypeStruct((Plan(None, owned).at_flip(len(plan)) + 1,), jnp.int32),
            jax.ShapeDtypeStruct((slots,), jnp.float32),
            pltpu.VMEM((owned, width, 1), jnp.float32),
            pltpu.VMEM((3 * owned, 1, width), jnp.float32),
            acc_shape,
            dens_shape,
            ft_shape,
            token_shape,
        ),
        in_specs=[smem] * 3 + [vmem] * 3 + [anywhere],
        out_specs=(smem,) * 2 + (vmem,) * 6,
        scratch_shapes=[
            pltpu.VMEM((wide_rows, width), jnp.float32),
            pltpu.VMEM((buf_rows, width), fitted.dtype),
            pltpu.VMEM((width, width), fitted.dtype),
        ],
        compiler_params=pltpu.CompilerParams(vmem_limit_bytes=NEAR_VMEM),
        cost_estimate=cost(len(cells)),
        name="first",
    )(
        fit_start, occ_energy, pair_partner, virt_domain, virt_energy.reshape(-1, 1),
        in_hbm(fitted), sent[last - 1],
    )
    state = {"acc": acc, "dens": dens, "token": token}
    hops = []

    def add_pairs(
        kernel, block_specs, blocks, cols, limit, name,
        extra=(), outs=(), aliases={}, scratch=(), token=True,
    ):
        specs = [smem] * 2 + [vmem] * 5 + block_specs
        results = pl.pallas_call(
            kernel,
            out_shape=(acc_shape, dens_shape) + (token_shape,) * token + tuple(outs),
            in_specs=specs + [anywhere] * (1 + len(extra)),
            out_specs=(vmem,) * (2 + token) + (anywhere,) * len(outs),
            input_output_aliases={5: 0, 6: 1, **aliases},
            scratch_shapes=[
                pltpu.VMEM((wide_rows, cols), jnp.float32),
                pltpu.VMEM((buf_rows, cols), fitted.dtype),
                *scratch,
            ],
            compiler_params=pltpu.CompilerParams(vmem_limit_bytes=limit),
            cost_estimate=cost(cols // COLS),
            name=name,
        )(
            ints, occ, in_vmem(eps_col), in_vmem(eps_row), in_vmem(ft), in_vmem(state["acc"]),
            in_vmem(state["dens"]), *blocks, *extra, state["token"],
        )
        state.update(acc=results[0], dens=results[1], token=results[2])
        return results[2 + token :]

    hops = {index: lax.ppermute(early[index], "row", second_hops[index]) for index in early}
    turned_cols = (pltpu.VMEM((COLS, width), fitted.dtype),)

    def near_pairs(late, *extra):
        add_pairs(
            functools.partial(near_kernel, ways=len(plan), late=late),
            [anywhere] * 2, [in_hbm(fitted), mate], width, NEAR_VMEM, f"near_pairs_{late}",
            extra=extra,
            scratch=(
                pltpu.VMEM((width, width), fitted.dtype),
                pltpu.VMEM((2, aux, width), fitted.dtype),
                pltpu.SemaphoreType.DMA((2,)),
            ),
        )

    near_pairs(0, *early.values())
    for number in range(last):
        for index, (at, alone, _) in enumerate(plan):
            if at == number and not alone:
                far[number] = state["token"] = pass_on(far[number], state["token"])
                hops[index] = lax.ppermute(far[number], "row", second_hops[index])
                if index == len(plan) - 1:
                    near_pairs(1)
        ways = [index for index, (at, _, _) in enumerate(plan) if at == number]
        add_pairs(
            functools.partial(
                far_kernel, ways=ways, total_ways=len(plan), cells=cells, number=number
            ),
            [vmem], [far[number]], COLS, FAR_VMEM, f"far_pairs_{number}", scratch=turned_cols,
        )
    results = (
        jax.ShapeDtypeStruct(fitted.shape, fitted.dtype),
        jax.ShapeDtypeStruct((owned, width, width), jnp.float32),
    )
    out_scratch = (
        pltpu.VMEM((owned, aux, width), fitted.dtype),
        pltpu.SemaphoreType.DMA((owned, OUT_TILES + 1)),
    )
    ready = add_pairs(
        functools.partial(
            relayed_kernel, numbers=[at for at, _, _ in plan], cells=cells
        ),
        [anywhere] * len(hops), [hops[index] for index in range(len(plan))], COLS, FAR_VMEM,
        "relayed_pairs",
        outs=results,
        scratch=turned_cols
        + (pltpu.VMEM((aux, COLS), fitted.dtype), out_scratch[0], pltpu.SemaphoreType.DMA)
        + out_scratch[1:],
    )
    gradient, density = add_pairs(
        functools.partial(last_kernel, total_ways=len(plan), cells=cells),
        [anywhere] * 3, [far[last], *ready], COLS, FAR_VMEM, "last_pairs",
        outs=results,
        aliases={8: 2, 9: 3},
        scratch=turned_cols
        + (pltpu.VMEM((aux, COLS), fitted.dtype),)
        + out_scratch
        + (pltpu.SemaphoreType.DMA((LOAD_TILES,)),),
        token=False,
    )
    return gradient, density


def solution(mesh):
    placed = (
        P(("parts", "row"), None, None),
        P("parts"),
        P("parts", None),
        P("parts"),
        P("parts"),
        P("parts"),
    )
    return jax.shard_map(
        on_device,
        mesh=mesh,
        in_specs=placed,
        out_specs=(P(("parts", "row"), None, None), P(("parts", "row"), None, None)),
        check_vma=False,
    )
```
